32 devices in a mesh: dp: 8 (over z, y), rows: 2 (over core), cols: 2 (over x).
Axes of the slice: x: 2, y: 2, z: 4, core: 2. Of those that a mesh axis runs over, the one named last changes fastest.
Arguments:
- tokens: bfloat16 [1536, 16384], P('rows', ('dp', 'cols')), may hold values from -6 to 6
- lengths: int32 [16], P('dp'), may hold values from 256 to 1024, as said below
- mix_gain: float32 [1536], P('rows'), may hold values from 0.5 to 1.5
- rec_weight: bfloat16 [1536, 2048], P('rows', 'cols'), may hold values from -0.15625 to 0.15625
- gate_weight: bfloat16 [1536, 2048], P('rows', 'cols'), may hold values from -0.15625 to 0.15625
- conv_weight: float32 [4, 2048], P(None, 'cols'), may hold values from -3 to 3
- conv_bias: float32 [2048], P('cols'), may hold values from -2 to 2
- recur_weight: bfloat16 [16, 128, 128], P('cols'), may hold values from -0.5 to 0.5
- recur_bias: float32 [2048], P('cols'), may hold values from -3 to 3
- input_weight: bfloat16 [16, 128, 128], P('cols'), may hold values from -0.5 to 0.5
- input_bias: float32 [2048], P('cols'), may hold values from -3 to 3
- decay_param: float32 [2048], P('cols'), may hold values from 1 to 8
- out_weight: bfloat16 [1536, 2048], P('rows', 'cols'), may hold values from -0.5 to 0.5
- ffn_gain: float32 [1536], P('rows'), may hold values from 0.5 to 1.5
- ffn_gate: bfloat16 [1536, 4608], P('rows', 'cols'), may hold values from -0.15625 to 0.15625
- ffn_up: bfloat16 [1536, 4608], P('rows', 'cols'), may hold values from -0.15625 to 0.15625
- ffn_down: bfloat16 [1536, 4608], P('rows', 'cols'), may hold values from -0.125 to 0.125
- cotangent: bfloat16 [1536, 16384], P('rows', ('dp', 'cols')), may hold values from -6 to 6
Outputs:
- result: bfloat16 [1536, 16384], P('rows', ('dp', 'cols'))
- grad_tokens: bfloat16 [1536, 16384], P('rows', ('dp', 'cols'))
- grad_mix_gain: float32 [1536], P('rows')
- grad_rec_weight: float32 [1536, 2048], P('rows', 'cols')
- grad_gate_weight: float32 [1536, 2048], P('rows', 'cols')
- grad_conv_weight: float32 [4, 2048], P(None, 'cols')
- grad_conv_bias: float32 [2048], P('cols')
- grad_recur_weight: float32 [16, 128, 128], P('cols')
- grad_recur_bias: float32 [2048], P('cols')
- grad_input_weight: float32 [16, 128, 128], P('cols')
- grad_input_bias: float32 [2048], P('cols')
- grad_decay_param: float32 [2048], P('cols')
- grad_out_weight: float32 [1536, 2048], P('rows', 'cols')
- grad_ffn_gain: float32 [1536], P('rows')
- grad_ffn_gate: float32 [1536, 4608], P('rows', 'cols')
- grad_ffn_up: float32 [1536, 4608], P('rows', 'cols')
- grad_ffn_down: float32 [1536, 4608], P('rows', 'cols')
The draws below stay inside these ranges and needn't reach their ends.
Inputs may be any that keep to these rules, and one draw needn't show every extreme that they name: `lengths`: live slots of each sequence, counted from its first slot; some sequence has 1024.
All inputs are finite; a program needn't handle non-finite values.
Results may differ from the reference program's by a relative error of at most 0.014.
Values may be sent and summed in bfloat16 or wider, within the bound.
A program may use at most 384 MiB of HBM per device.

```python
import jax
import jax.numpy as jnp
from jax import lax

D = 1536
F = 2048
FF = 4608
H = 16
BLK = 128
KCONV = 4
LEN = 1024
NSEQ = 16
TOKENS = 16384


def draw_lengths(key, part):
    key = jax.random.fold_in(key, 7)
    first_key, second_key = jax.random.split(key)
    drawn = jax.random.randint(first_key, (NSEQ,), LEN // 4, LEN + 1)
    chosen = jax.random.randint(second_key, (), 0, NSEQ)
    return jnp.where(jnp.arange(NSEQ) == chosen, LEN, drawn).astype(jnp.int32)


def shard_levels(rng, extent, pieces, low, high):
    level = 1.0
    for axis_at, blocks in pieces:
        heights = jax.random.uniform(jax.random.fold_in(jax.random.fold_in(rng, 6), axis_at), (blocks,), jnp.float32, low / len(pieces), high / len(pieces))
        level = level * jnp.repeat(jnp.exp(heights), extent[axis_at] // blocks).reshape((-1,) + (1,) * (len(extent) - 1 - axis_at))
    return level


def bell_draw(own_key, shape, scale, reach, pieces=(), kind=jnp.bfloat16):
    entries = jax.random.normal(own_key, shape, jnp.float32) * scale
    if len(pieces) > 0:
        entries = shard_levels(own_key, shape, pieces, -0.22, 0.18) * entries
    return jnp.clip(entries, min=-reach, max=reach).astype(kind)


def setup_inputs(seed: int = 0) -> dict:
    streams_of = jax.random.split(jax.random.key(seed), 19)
    tokens = bell_draw(streams_of[0], (D, TOKENS), 1.0, 6.0, ((0, 2), (1, 16)))
    lengths = draw_lengths(jax.random.fold_in(streams_of[18], 71), 0)
    mix_gain = jnp.clip(1.0 + 0.1 * jax.random.normal(streams_of[2], (D,), jnp.float32), 0.5, 1.5)
    rec_weight = bell_draw(streams_of[3], (D, F), D ** -0.5, 0.15625, ((0, 2), (1, 2)))
    gate_weight = bell_draw(streams_of[4], (D, F), D ** -0.5, 0.15625, ((0, 2), (1, 2)))
    conv_weight = bell_draw(streams_of[5], (KCONV, F), 0.5, 3.0, ((1, 2),), jnp.float32)
    conv_bias = bell_draw(streams_of[6], (F,), 0.3, 2.0, ((0, 2),), jnp.float32)
    recur_weight = bell_draw(streams_of[7], (H, BLK, BLK), BLK ** -0.5, 0.5, ((0, 2),))
    recur_bias = bell_draw(streams_of[8], (F,), 1.0, 3.0, ((0, 2),), jnp.float32)
    input_weight = bell_draw(streams_of[9], (H, BLK, BLK), BLK ** -0.5, 0.5, ((0, 2),))
    input_bias = bell_draw(streams_of[10], (F,), 1.0, 3.0, ((0, 2),), jnp.float32)
    decay_param = jnp.clip(1.0 + 7.0 * jax.random.uniform(streams_of[11], (F,), jnp.float32) ** shard_levels(streams_of[11], (F,), ((0, 2),), -0.2, 0.2), 1.0, 8.0)
    out_weight = bell_draw(streams_of[12], (D, F), (F // 16) ** -0.5, 0.5, ((0, 2), (1, 2)))
    ffn_gain = jnp.clip(1.0 + 0.1 * jax.random.normal(streams_of[13], (D,), jnp.float32), 0.5, 1.5)
    ffn_gate = bell_draw(streams_of[14], (D, FF), D ** -0.5, 0.15625, ((0, 2), (1, 2)))
    ffn_up = bell_draw(streams_of[15], (D, FF), D ** -0.5, 0.15625, ((0, 2), (1, 2)))
    ffn_down = bell_draw(streams_of[16], (D, FF), (FF // 2) ** -0.5, 0.125, ((0, 2), (1, 2)))
    cotangent = bell_draw(streams_of[17], (D, TOKENS), 1.0, 6.0, ((0, 2), (1, 16)))
    return dict(tokens=tokens, lengths=lengths, mix_gain=mix_gain, rec_weight=rec_weight, gate_weight=gate_weight, conv_weight=conv_weight, conv_bias=conv_bias, recur_weight=recur_weight, recur_bias=recur_bias, input_weight=input_weight, input_bias=input_bias, decay_param=decay_param, out_weight=out_weight, ffn_gain=ffn_gain, ffn_gate=ffn_gate, ffn_up=ffn_up, ffn_down=ffn_down, cotangent=cotangent)


EPS = 1e-06
GATE_SCALE = 8.0

@jax.custom_vjp
def low(v):
    return lax.optimization_barrier(v.astype(jnp.bfloat16)).astype(jnp.float32)

@jax.custom_vjp
def low_back(v):
    return v

def low_keep(v):
    return (low(v), None)

def low_pass(kept, grad):
    return (grad,)

def back_keep(v):
    return (v, None)

def back_low(kept, grad):
    return (low(grad),)
low.defvjp(low_keep, low_pass)
low_back.defvjp(back_keep, back_low)

def matmul(left, right):
    return jnp.dot(left, right, precision=lax.Precision.HIGHEST, preferred_element_type=jnp.float32)

def rms_norm(values, gain):
    return values * lax.rsqrt(lax.optimization_barrier(jnp.mean(values * values, axis=-1, keepdims=True)) + EPS) * gain

def linear_step(earlier, latter):
    return (earlier[0] * latter[0], latter[0] * earlier[1] + latter[1])

def block_diag(heads, weight):
    return jnp.einsum('slhi,hij->slhj', heads, weight, precision=lax.Precision.HIGHEST)

def forward(params, block_in, live_mask):
    mix_gain, rec_weight, gate_weight, conv_weight, conv_bias, recur_weight, recur_bias, input_weight, input_bias, decay_param, out_weight, ffn_gain, ffn_gate, ffn_up, ffn_down = params
    seqs = block_in.shape[0] // LEN
    normed_one = low(rms_norm(block_in, mix_gain))
    rec_in = low_back(matmul(normed_one, rec_weight)).reshape(seqs, LEN, F)
    gate_pre = low_back(matmul(normed_one, gate_weight)).reshape(seqs, LEN, F)
    padded = jnp.pad(rec_in, ((0, 0), (KCONV - 1, 0), (0, 0)))
    conv_out = conv_bias + jnp.zeros_like(rec_in)
    for offset in range(KCONV):
        conv_out = conv_out + conv_weight[offset] * padded[:, KCONV - 1 - offset:KCONV - 1 - offset + LEN]
    conv_low = low(conv_out)
    heads = conv_low.reshape(seqs, LEN, H, BLK)
    recur_gate = jax.nn.sigmoid(low_back(block_diag(heads, recur_weight)).reshape(seqs, LEN, F) + recur_bias)
    input_gate = jax.nn.sigmoid(low_back(block_diag(heads, input_weight)).reshape(seqs, LEN, F) + input_bias)
    log_decay = -GATE_SCALE * recur_gate * jax.nn.softplus(-decay_param)
    decay = jnp.exp(log_decay)
    scaling = jnp.sqrt(-jnp.expm1(2.0 * log_decay))
    drive = scaling * input_gate * conv_low
    state = lax.associative_scan(linear_step, (decay, drive), axis=1)[1]
    branch = low(state * jax.nn.gelu(gate_pre, approximate=True)).reshape(-1, F)
    residual_one = block_in + low_back(matmul(branch, out_weight.T))
    normed_two = low(rms_norm(residual_one, ffn_gain))
    ffn_a = low_back(matmul(normed_two, ffn_gate))
    ffn_b = low_back(matmul(normed_two, ffn_up))
    hidden = low(jax.nn.gelu(ffn_a, approximate=True) * ffn_b)
    residual_two = residual_one + low_back(matmul(hidden, ffn_down.T))
    return live_mask[:, None] * residual_two

def reference(tokens, lengths, mix_gain, rec_weight, gate_weight, conv_weight, conv_bias, recur_weight, recur_bias, input_weight, input_bias, decay_param, out_weight, ffn_gain, ffn_gate, ffn_up, ffn_down, cotangent):
    params = tuple((item.astype(jnp.float32) for item in (mix_gain, rec_weight, gate_weight, conv_weight, conv_bias, recur_weight, recur_bias, input_weight, input_bias, decay_param, out_weight, ffn_gain, ffn_gate, ffn_up, ffn_down)))
    groups = lengths.shape[0] // 4
    inputs = tokens.astype(jnp.float32).T.reshape(groups, 4 * LEN, D)
    cots = cotangent.astype(jnp.float32).T.reshape(groups, 4 * LEN, D)
    group_len = lengths.reshape(groups, 4)

    def step(totals, item):
        block_in, block_cot, block_len = item
        live_mask = (jnp.arange(LEN, dtype=jnp.int32)[None, :] < block_len[:, None]).astype(jnp.float32).reshape(-1)

        def run(prm, inp):
            return forward(prm, inp, live_mask)
        output, pullback = jax.vjp(run, params, block_in)
        grad_params, grad_in = pullback(block_cot)
        totals = jax.tree.map(lambda left, right: left + right, totals, grad_params)
        return (totals, (output.astype(jnp.bfloat16), grad_in.astype(jnp.bfloat16)))
    zeros = jax.tree.map(jnp.zeros_like, params)
    totals, (outputs, grad_inputs) = lax.scan(step, zeros, (inputs, cots, group_len))
    result = outputs.reshape(lengths.shape[0] * LEN, D).T
    grad_tokens = grad_inputs.reshape(lengths.shape[0] * LEN, D).T
    return (result, grad_tokens, totals[0], totals[1], totals[2], totals[3], totals[4], totals[5], totals[6], totals[7], totals[8], totals[9], totals[10], totals[11], totals[12], totals[13], totals[14])
```

```python
import functools
import math

import jax
import jax.numpy as jnp
from jax import lax
from jax.experimental import pallas as pl
from jax.experimental.pallas import tpu as pltpu
from jax.sharding import PartitionSpec as P

D = 1536
KCONV = 4
LEN = 1024
EPS = 1e-06
GATE_SCALE = 8.0
TANH_COEF = math.sqrt(2.0 / math.pi)
CUBIC_COEF = 0.044715
F32 = jnp.float32
BF16 = jnp.bfloat16
MIB = 1024 * 1024


def swap(value, axis):
    return lax.ppermute(value, axis, [(0, 1), (1, 0)])


def dot(left, right):
    return lax.dot_general(left, right, (((1,), (0,)), ((), ())), preferred_element_type=F32)


def dot_nt(left, right):
    return lax.dot_general(left, right, (((1,), (1,)), ((), ())), preferred_element_type=F32)


def dot_tn(left, right):
    return lax.dot_general(left, right, (((0,), (0,)), ((), ())), preferred_element_type=F32)


def gelu_act(values):
    inner_arg = TANH_COEF * (values + CUBIC_COEF * values * values * values)
    return 0.5 * values * (1.0 + jnp.tanh(inner_arg))


def gelu_pair(values):
    square = values * values
    tanh_val = jnp.tanh(values * (TANH_COEF + (TANH_COEF * CUBIC_COEF) * square))
    half_up = 0.5 + 0.5 * tanh_val
    slope = half_up + 0.5 * values * (1.0 - tanh_val * tanh_val) * (
        TANH_COEF + (3.0 * TANH_COEF * CUBIC_COEF) * square
    )
    return (values * half_up, slope)


def decay_terms(recur_gate, soft_decay):
    u = (2.0 * GATE_SCALE) * recur_gate * soft_decay
    decay = jnp.exp(-0.5 * u)
    series = u * (
        1.0
        - u
        * (0.5 - u * (1.0 / 6 - u * (1.0 / 24 - u * (1.0 / 120 - u * (1.0 / 720)))))
    )
    em = jnp.where(u < 0.25, series, 1.0 - decay * decay)
    return (decay, em)


def scan_tile(decay, drive, row):
    for shift in (1, 2, 4):
        keep = row >= shift
        before_a = jnp.where(keep, pltpu.roll(decay, shift, 0), 1.0)
        before_b = jnp.where(keep, pltpu.roll(drive, shift, 0), 0.0)
        drive = decay * before_b + drive
        decay = decay * before_a
    return (decay, drive)


def scan_tile_back(decay, drive, row):
    for shift in (1, 2, 4):
        keep = row < 8 - shift
        after_a = jnp.where(keep, pltpu.roll(decay, 8 - shift, 0), 1.0)
        after_b = jnp.where(keep, pltpu.roll(drive, 8 - shift, 0), 0.0)
        drive = decay * after_b + drive
        decay = decay * after_a
    return (decay, drive)


def rec_forward_kernel(
    chunk, width,
    n1, wr0, wr1, wg0, wg1, gw, cw, cb, rb, ib, sp, ow0, ow1,
    rec_o, gate_o, cl_o, r_o, i_o, st_o, br_o, mix_o,
    halo, carry, recpad, pre,
):
    heads = width // 128
    half = wr0.shape[0]

    @pl.when(pl.program_id(0) == 0)
    def _():
        halo[...] = jnp.zeros_like(halo)
        carry[...] = jnp.zeros_like(carry)

    low0 = n1[:, :half]
    low1 = n1[:, half:]
    rec = dot(low0, wr0[...]) + dot(low1, wr1[...])
    recpad[0:8, :] = halo[...]
    recpad[8:, :] = rec
    halo[...] = rec[chunk - 8 :, :]
    rec_o[...] = rec
    gate_o[...] = dot(low0, wg0[...]) + dot(low1, wg1[...])

    def conv_step(i, _):
        base = pl.multiple_of(i * 16, 16)
        for h in range(heads):
            sl = slice(h * 128, (h + 1) * 128)
            window = recpad[pl.ds(base, 24), sl]
            out = cb[:, sl] + cw[0:1, sl] * window[8:]
            for k in range(1, KCONV):
                out = out + cw[k : k + 1, sl] * pltpu.roll(window, k, 0)[8:]
            cl_o[pl.ds(base, 16), sl] = out.astype(BF16)
        return 0

    lax.fori_loop(0, chunk // 16, conv_step, 0)
    for h in range(heads):
        pre[:, h * 256 : (h + 1) * 256] = dot(cl_o[:, h * 128 : (h + 1) * 128], gw[h])
    row = lax.broadcasted_iota(jnp.int32, (8, 128), 0)

    def main_step(i, _):
        base = pl.multiple_of(i * 16, 16)
        rows = pl.ds(base, 16)
        for h in range(heads):
            sl = slice(h * 128, (h + 1) * 128)
            r = jax.nn.sigmoid(pre[rows, h * 256 : h * 256 + 128] + rb[:, sl])
            g = jax.nn.sigmoid(pre[rows, h * 256 + 128 : (h + 1) * 256] + ib[:, sl])
            conv = cl_o[rows, sl].astype(F32)
            decay, em = decay_terms(r, sp[:, sl])
            drive = jnp.sqrt(em) * g * conv
            r_o[rows, sl] = r
            i_o[rows, sl] = g
            held = carry[0:1, sl]
            parts = []
            for p in range(2):
                a, b = scan_tile(decay[p * 8 : p * 8 + 8], drive[p * 8 : p * 8 + 8], row)
                state = a * held + b
                held = state[7:8]
                parts.append(state)
            carry[0:1, sl] = held
            state = jnp.concatenate(parts, axis=0)
            st_o[rows, sl] = state
            br_o[rows, sl] = (state * gelu_act(gate_o[rows, sl])).astype(BF16)
        return 0

    lax.fori_loop(0, chunk // 16, main_step, 0)
    branch = br_o[...]
    mix_o[:, :half] = dot_nt(branch, ow0[...]).astype(BF16)
    mix_o[:, half:] = dot_nt(branch, ow1[...]).astype(BF16)


def rec_forward(n1, wr, wg, gw, cw, cb, rb, ib, sp, ow, chunk=256):
    tokens = n1.shape[0]
    half, width = wr[0].shape
    heads = width // 128
    row_block = lambda cols: pl.BlockSpec((chunk, cols), lambda i: (i, 0))
    whole = lambda shape: pl.BlockSpec(
        shape, lambda i: (0,) * len(shape), pipeline_mode=pl.Buffered(1)
    )
    f32 = jax.ShapeDtypeStruct((tokens, width), F32)
    low = jax.ShapeDtypeStruct((tokens, width), BF16)
    return pl.pallas_call(
        functools.partial(rec_forward_kernel, chunk, width),
        grid=(tokens // chunk,),
        in_specs=[row_block(2 * half)]
        + [whole((half, width))] * 4
        + [whole((heads, 128, 256)), whole((KCONV, width))]
        + [whole((1, width))] * 4
        + [whole((half, width))] * 2,
        out_specs=[row_block(width)] * 7 + [row_block(2 * half)],
        out_shape=[f32, f32, low, f32, f32, f32, low,
                   jax.ShapeDtypeStruct((tokens, 2 * half), BF16)],
        scratch_shapes=[
            pltpu.VMEM((8, width), F32),
            pltpu.VMEM((8, width), F32),
            pltpu.VMEM((chunk + 8, width), F32),
            pltpu.VMEM((chunk, 2 * width), F32),
        ],
        compiler_params=pltpu.CompilerParams(vmem_limit_bytes=56 * MIB),
        name="recurrent_forward",
    )(n1, wr[0], wr[1], wg[0], wg[1], gw, cw, cb, rb, ib, sp, ow[0], ow[1])


def ffn_kernel(
    tile,
    n2, n2t, cot, cott, wg0, wg1, wu0, wu1, wd0, wd1,
    out_o, gn2_o, gg0, gg1, gu0, gu1, gd0, gd1,
    out_acc, gn2_acc, hid_s, ga_s, gb_s,
):
    step = pl.program_id(0)
    tokens = n2.shape[0]
    half = wg0.shape[0]

    @pl.when(step == 0)
    def _():
        out_acc[...] = jnp.zeros_like(out_acc)
        gn2_acc[...] = jnp.zeros_like(gn2_acc)

    def tile_step(i, _):
        rows = pl.ds(pl.multiple_of(i * tile, tile), tile)
        n0, n1 = n2[rows, :half], n2[rows, half:]
        c0, c1 = cot[rows, :half], cot[rows, half:]
        a = dot(n0, wg0[...]) + dot(n1, wg1[...])
        b = dot(n0, wu0[...]) + dot(n1, wu1[...])
        gh = dot(c0, wd0[...]) + dot(c1, wd1[...])
        act, slope = gelu_pair(a)
        hidden = (act * b).astype(BF16)
        ga = (gh * b * slope).astype(BF16)
        gb = (gh * act).astype(BF16)
        hid_s[rows, :] = hidden
        ga_s[rows, :] = ga
        gb_s[rows, :] = gb
        out_acc[rows, :half] += dot_nt(hidden, wd0[...])
        out_acc[rows, half:] += dot_nt(hidden, wd1[...])
        gn2_acc[rows, :half] += dot_nt(ga, wg0[...]) + dot_nt(gb, wu0[...])
        gn2_acc[rows, half:] += dot_nt(ga, wg1[...]) + dot_nt(gb, wu1[...])
        return 0

    lax.fori_loop(0, tokens // tile, tile_step, 0)
    gg0[...] = dot(n2t[:half], ga_s[...]).astype(BF16)
    gg1[...] = dot(n2t[half:], ga_s[...]).astype(BF16)
    gu0[...] = dot(n2t[:half], gb_s[...]).astype(BF16)
    gu1[...] = dot(n2t[half:], gb_s[...]).astype(BF16)
    gd0[...] = dot(cott[:half], hid_s[...]).astype(BF16)
    gd1[...] = dot(cott[half:], hid_s[...]).astype(BF16)

    @pl.when(step == pl.num_programs(0) - 1)
    def _():
        out_o[...] = out_acc[...].astype(BF16)
        gn2_o[...] = gn2_acc[...].astype(BF16)


def ffn(n2, n2t, cot, cott, wg, wu, wd, block=256, tile=256):
    tokens, wide = n2.shape
    half, width = wg[0].shape
    whole = lambda shape: pl.BlockSpec(shape, lambda i: (0, 0), pipeline_mode=pl.Buffered(1))
    col_block = pl.BlockSpec((half, block), lambda i: (0, i))
    act = jax.ShapeDtypeStruct((tokens, wide), BF16)
    grad = jax.ShapeDtypeStruct((half, width), BF16)
    return pl.pallas_call(
        functools.partial(ffn_kernel, tile),
        grid=(width // block,),
        in_specs=[whole((tokens, wide)), whole((wide, tokens))] * 2 + [col_block] * 6,
        out_specs=[whole((tokens, wide))] * 2 + [col_block] * 6,
        out_shape=[act, act] + [grad] * 6,
        scratch_shapes=[
            pltpu.VMEM((tokens, wide), F32),
            pltpu.VMEM((tokens, wide), F32),
            pltpu.VMEM((tokens, block), BF16),
            pltpu.VMEM((tokens, block), BF16),
            pltpu.VMEM((tokens, block), BF16),
        ],
        compiler_params=pltpu.CompilerParams(vmem_limit_bytes=60 * MIB),
        name="ffn",
    )(n2, n2t, cot, cott, wg[0], wg[1], wu[0], wu[1], wd[0], wd[1])


def rec_backward_kernel(
    tile,
    g1, g1t, n1t, st, gate, r_in, i_in, cl, rec, br, ow0, ow1, wr0, wr1, wg0, wg1, gw, cw, sp,
    gn1_o, go0, go1, gr0, gr1, gg0, gg1, ggw, gvec,
    acc, gb_s, gc_s, ggp_s, grp_s, gip_s, grec_s, sums,
):
    step = pl.program_id(0)
    tokens, block = gb_s.shape
    heads = block // 128
    half = ow0.shape[0]
    tiles = tokens // tile
    subs = tile // 8

    @pl.when(step == 0)
    def _():
        acc[...] = jnp.zeros_like(acc)

    gb_s[...] = dot(g1[:, :half], ow0[...]) + dot(g1[:, half:], ow1[...])
    go0[...] = dot(g1t[:half], br[...]).astype(BF16)
    go1[...] = dot(g1t[half:], br[...]).astype(BF16)
    sums[...] = jnp.zeros_like(sums)
    row = lax.broadcasted_iota(jnp.int32, (8, 128), 0)

    def back_step(j, held):
        i = tiles - 1 - j
        base = pl.multiple_of(i * tile, tile)
        rows = pl.ds(base, tile)
        before = pl.ds(pl.multiple_of(jnp.maximum(base - 8, 0), 8), 8)
        out = []
        for h in range(heads):
            sl = slice(h * 128, (h + 1) * 128)
            later_decay, later_carried = held[h]
            grad_branch = gb_s[rows, sl]
            act, slope = gelu_pair(gate[rows, sl])
            state = st[rows, sl]
            ggp_s[rows, sl] = (grad_branch * state * slope).astype(BF16)
            grad_state = grad_branch * act
            r = r_in[rows, sl]
            soft = sp[:, sl]
            decay, em = decay_terms(r, soft)
            parts = [None] * subs
            for p in range(subs - 1, -1, -1):
                own = decay[p * 8 : p * 8 + 8]
                after = jnp.where(row == 7, later_decay, pltpu.roll(own, 7, 0))
                a, b = scan_tile_back(after, grad_state[p * 8 : p * 8 + 8], row)
                carried = a * later_carried + b
                later_decay = own[0:1]
                later_carried = carried[0:1]
                parts[p] = carried
            out.append((later_decay, later_carried))
            carried = jnp.concatenate(parts, axis=0)
            edge = jnp.where(i > 0, st[before, sl][7:8], 0.0)
            prev = []
            for p in range(subs):
                prev.append(jnp.where(row == 0, edge, pltpu.roll(state[p * 8 : p * 8 + 8], 1, 0)))
                edge = state[p * 8 + 7 : p * 8 + 8]
            prev = jnp.concatenate(prev, axis=0)
            g = i_in[rows, sl]
            conv = cl[rows, sl].astype(F32)
            scaling = jnp.sqrt(em)
            gated = g * conv
            grad_log = carried * (prev * decay - gated * (decay * decay) / scaling)
            grad_soft = grad_log * (-GATE_SCALE * r)
            grp = grad_soft * soft * (1.0 - r)
            cs = carried * scaling
            gc_s[rows, sl] = cs * g
            gip = cs * gated * (1.0 - g)
            grp_s[rows, sl] = grp.astype(BF16)
            gip_s[rows, sl] = gip.astype(BF16)
            for n, term in enumerate((grp, gip, grad_soft)):
                total = term[0:8]
                for p in range(1, subs):
                    total = total + term[p * 8 : p * 8 + 8]
                sums[n * 8 : n * 8 + 8, sl] += total
        return tuple(out)

    zero = jnp.zeros((1, 128), F32)
    lax.fori_loop(0, tiles, back_step, tuple((zero, zero) for _ in range(heads)))
    for h in range(heads):
        sl = slice(h * 128, (h + 1) * 128)
        low = cl[:, sl]
        ggw[h, :, 0:128] = dot_tn(low, grp_s[:, sl])
        ggw[h, :, 128:256] = dot_tn(low, gip_s[:, sl])
        gc_s[:, sl] += dot_nt(grp_s[:, sl], gw[h, :, 0:128]) + dot_nt(gip_s[:, sl], gw[h, :, 128:256])

    def conv_step(j, held):
        i = tiles - 1 - j
        base = pl.multiple_of(i * tile, tile)
        rows = pl.ds(base, tile)
        before = pl.ds(pl.multiple_of(jnp.maximum(base - 8, 0), 8), 8)
        out = []
        for h in range(heads):
            sl = slice(h * 128, (h + 1) * 128)
            grad_conv = gc_s[rows, sl]
            window = jnp.concatenate([grad_conv, held[h]], axis=0)
            out.append(grad_conv[0:8])
            grad_rec = cw[0:1, sl] * grad_conv
            for k in range(1, KCONV):
                grad_rec = grad_rec + cw[k : k + 1, sl] * pltpu.roll(window, tile + 8 - k, 0)[:tile]
            grec_s[rows, sl] = grad_rec.astype(BF16)
            edge = jnp.where(i > 0, rec[before, sl], 0.0)
            past = jnp.concatenate([edge, rec[rows, sl]], axis=0)
            terms = [grad_conv * past[8:]]
            for k in range(1, KCONV):
                terms.append(grad_conv * pltpu.roll(past, k, 0)[8:])
            terms.append(grad_conv)
            for n, term in enumerate(terms):
                total = term[0:8]
                for p in range(1, subs):
                    total = total + term[p * 8 : p * 8 + 8]
                sums[24 + n * 8 : 32 + n * 8, sl] += total
        return tuple(out)

    lax.fori_loop(0, tiles, conv_step, tuple(jnp.zeros((8, 128), F32) for _ in range(heads)))
    for n in range(8):
        gvec[n : n + 1, :] = jnp.sum(sums[n * 8 : n * 8 + 8, :], axis=0, keepdims=True)
    grad_rec = grec_s[...]
    grad_gate = ggp_s[...]
    gr0[...] = dot(n1t[:half], grad_rec).astype(BF16)
    gr1[...] = dot(n1t[half:], grad_rec).astype(BF16)
    gg0[...] = dot(n1t[:half], grad_gate).astype(BF16)
    gg1[...] = dot(n1t[half:], grad_gate).astype(BF16)
    acc[:, :half] += dot_nt(grad_rec, wr0[...]) + dot_nt(grad_gate, wg0[...])
    acc[:, half:] += dot_nt(grad_rec, wr1[...]) + dot_nt(grad_gate, wg1[...])

    @pl.when(step == pl.num_programs(0) - 1)
    def _():
        gn1_o[...] = acc[...].astype(BF16)


def rec_backward(g1, g1t, n1t, st, gate, r, g, cl, rec, br, ow, wr, wg, gw, cw, sp, block=256, tile=32):
    tokens, wide = g1.shape
    half, width = wr[0].shape
    heads = block // 128
    whole = lambda shape: pl.BlockSpec(shape, lambda i: (0, 0), pipeline_mode=pl.Buffered(1))
    act = pl.BlockSpec((tokens, block), lambda i: (0, i))
    weight = pl.BlockSpec((half, block), lambda i: (0, i))
    thin = lambda n: pl.BlockSpec((n, block), lambda i: (0, i))
    gate_block = pl.BlockSpec((heads, 128, 256), lambda i: (i, 0, 0))
    grad = jax.ShapeDtypeStruct((half, width), BF16)
    return pl.pallas_call(
        functools.partial(rec_backward_kernel, tile),
        grid=(width // block,),
        in_specs=[whole((tokens, wide)), whole((wide, tokens)), whole((wide, tokens))]
        + [act] * 7
        + [weight] * 6
        + [gate_block, thin(KCONV), thin(1)],
        out_specs=[whole((tokens, wide))] + [weight] * 6 + [gate_block, thin(8)],
        out_shape=[jax.ShapeDtypeStruct((tokens, wide), BF16)]
        + [grad] * 6
        + [
            jax.ShapeDtypeStruct((width // 128, 128, 256), F32),
            jax.ShapeDtypeStruct((8, width), F32),
        ],
        scratch_shapes=[
            pltpu.VMEM((tokens, wide), F32),
            pltpu.VMEM((tokens, block), F32),
            pltpu.VMEM((tokens, block), F32),
            pltpu.VMEM((tokens, block), BF16),
            pltpu.VMEM((tokens, block), BF16),
            pltpu.VMEM((tokens, block), BF16),
            pltpu.VMEM((tokens, block), BF16),
            pltpu.VMEM((64, block), F32),
        ],
        compiler_params=pltpu.CompilerParams(vmem_limit_bytes=60 * MIB),
        name="recurrent_backward",
    )(
        g1, g1t, n1t, st, gate, r, g, cl, rec, br,
        ow[0], ow[1], wr[0], wr[1], wg[0], wg[1], gw, cw, sp,
    )


def body(
    tokens, lengths, mix_gain, rec_weight, gate_weight, conv_weight, conv_bias,
    recur_weight, recur_bias, input_weight, input_bias, decay_param, out_weight,
    ffn_gain, ffn_gate, ffn_up, ffn_down, cotangent,
):
    at_row = lax.axis_index("rows")
    at_col = lax.axis_index("cols")
    diag = at_row == at_col
    half = tokens.shape[0]
    wide = 2 * half

    def to_sequence(own):
        other = swap(own, "cols")
        mine = jnp.where(diag, own, other)
        partner = swap(jnp.where(diag, other, own), "rows")
        return jnp.concatenate([mine, partner], axis=0)

    def from_sequence(whole):
        partner = swap(whole[:, half:], "rows")
        own = whole[:, :half]
        keep = jnp.where(diag, own, partner)
        give = jnp.where(diag, partner, own)
        return keep, swap(give, "cols")

    both = lambda weight: (weight, swap(weight, "rows"))
    gains = lambda gain: jnp.concatenate(both(gain))

    positions = jnp.arange(LEN, dtype=jnp.int32)
    live_core = (positions < lengths[at_row]).astype(BF16)
    live_chip = (positions < lengths[at_col]).astype(F32)

    xt = to_sequence(tokens)
    wr = both(rec_weight)
    wg = both(gate_weight)
    ow = both(out_weight)
    cott = to_sequence(cotangent) * live_core[None, :]
    fg = both(ffn_gate)
    fu = both(ffn_up)
    fd = both(ffn_down)
    gain_one = gains(mix_gain)
    gain_two = gains(ffn_gain)
    x = xt.T
    xf = x.astype(F32)
    scale_one = lax.rsqrt(jnp.mean(xf * xf, axis=1, keepdims=True) + EPS)
    n1 = (xf * scale_one * gain_one).astype(BF16)
    n1t = n1.T
    gw = jnp.concatenate([recur_weight, input_weight], axis=2)
    sp = jax.nn.softplus(-decay_param)[None, :]
    rec, gate, cl, r, g, st, br, mixed = rec_forward(
        n1, wr, wg, gw, conv_weight, conv_bias[None, :], recur_bias[None, :],
        input_bias[None, :], sp, ow,
    )
    res1 = xf + (mixed.astype(F32) + swap(mixed, "cols").astype(F32))
    scale_two = lax.rsqrt(jnp.mean(res1 * res1, axis=1, keepdims=True) + EPS)
    n2 = (res1 * scale_two * gain_two).astype(BF16)
    n2t = n2.T
    cot = cott.T
    ffn_out, gn2_part, gg0, gg1, gu0, gu1, gd0, gd1 = ffn(n2, n2t, cot, cott, fg, fu, fd)
    gn2 = gn2_part.astype(F32) + swap(gn2_part, "cols").astype(F32)
    grad_gain_two = jnp.sum(gn2 * res1 * scale_two, axis=0)
    weighted = gn2 * gain_two
    inner = jnp.sum(weighted * res1, axis=1, keepdims=True)
    grad_one = (
        cot.astype(F32)
        + scale_two * weighted
        - res1 * (scale_two * scale_two * scale_two * inner / wide)
    )
    g1 = grad_one.astype(BF16)
    g1t = g1.T

    def over_rows(own, other):
        return (own.astype(F32) + swap(other, "rows").astype(F32)).astype(BF16)

    sum_gate = lax.psum(over_rows(gg0, gg1), "dp").astype(F32)
    sum_up = lax.psum(over_rows(gu0, gu1), "dp").astype(F32)
    sum_down = lax.psum(over_rows(gd0, gd1), "dp").astype(F32)
    gn1_part, go0, go1, gr0, gr1, gt0, gt1, ggw, gvec = rec_backward(
        g1, g1t, n1t, st, gate, r, g, cl, rec, br, ow, wr, wg, gw, conv_weight, sp
    )
    sum_out = lax.psum(over_rows(go0, go1), "dp").astype(F32)
    sum_rec = lax.psum(over_rows(gr0, gr1), "dp").astype(F32)
    sum_gatew = lax.psum(over_rows(gt0, gt1), "dp").astype(F32)

    with_res = ffn_out.astype(F32) + jnp.where(diag, res1, 0.0)
    keep, came = from_sequence(with_res.astype(BF16))
    result = ((keep.astype(F32) + came.astype(F32)).T * live_chip[None, :]).astype(BF16)

    keep, came = from_sequence(gn1_part)
    gn1 = (keep.astype(F32) + came.astype(F32)).T
    g1_partner = swap(g1[:, half:], "rows")
    g1_here = jnp.where(diag, g1[:, :half], g1_partner).T.astype(F32)
    xh = tokens.astype(F32)
    squares = jnp.sum(xh * xh, axis=0)
    s_here = lax.rsqrt((squares + swap(squares, "rows")) / wide + EPS)[None, :]
    weighted = gn1 * mix_gain[:, None]
    inner = jnp.sum(weighted * xh, axis=0)
    inner = (inner + swap(inner, "rows"))[None, :]
    grad_tokens = (
        g1_here + s_here * weighted - xh * (s_here * s_here * s_here * inner / wide)
    ).astype(BF16)
    grad_gain_one = jnp.sum(gn1 * xh * s_here, axis=1)

    both_gain_two = grad_gain_two[:half] + swap(grad_gain_two[half:], "rows")
    small = lax.psum((gvec, ggw), ("dp", "rows"))
    vec, gates = small
    summed_gain = lax.psum(grad_gain_one, ("dp", "cols"))
    summed_gain_two = lax.psum(both_gain_two, "dp")
    grad_decay = vec[2] * -jax.nn.sigmoid(-decay_param)
    return (
        result,
        grad_tokens,
        summed_gain,
        sum_rec,
        sum_gatew,
        vec[3:7],
        vec[7],
        gates[:, :, :128],
        vec[0],
        gates[:, :, 128:],
        vec[1],
        grad_decay,
        sum_out,
        summed_gain_two,
        sum_gate,
        sum_up,
        sum_down,
    )


def solution(mesh):
    return jax.shard_map(
        body,
        mesh=mesh,
        in_specs=(
            P("rows", ("dp", "cols")),
            P("dp"),
            P("rows"),
            P("rows", "cols"),
            P("rows", "cols"),
            P(None, "cols"),
            P("cols"),
            P("cols", None, None),
            P("cols"),
            P("cols", None, None),
            P("cols"),
            P("cols"),
            P("rows", "cols"),
            P("rows"),
            P("rows", "cols"),
            P("rows", "cols"),
            P("rows", "cols"),
            P("rows", ("dp", "cols")),
        ),
        out_specs=(
            P("rows", ("dp", "cols")),
            P("rows", ("dp", "cols")),
            P("rows"),
            P("rows", "cols"),
            P("rows", "cols"),
            P(None, "cols"),
            P("cols"),
            P("cols", None, None),
            P("cols"),
            P("cols", None, None),
            P("cols"),
            P("cols"),
            P("rows", "cols"),
            P("rows"),
            P("rows", "cols"),
            P("rows", "cols"),
            P("rows", "cols"),
        ),
        check_vma=False,
    )
```

```python
import functools
import math

import jax
import jax.numpy as jnp
from jax import lax
from jax.experimental import pallas as pl
from jax.experimental.pallas import tpu as pltpu
from jax.sharding import PartitionSpec as P

D = 1536
KCONV = 4
LEN = 1024
OFFLOAD = 1536
EPS = 1e-06
GATE_SCALE = 8.0
TANH_COEF = math.sqrt(2.0 / math.pi)
CUBIC_COEF = 0.044715
F32 = jnp.float32
BF16 = jnp.bfloat16
MIB = 1024 * 1024


def swap(value, axis):
    return lax.ppermute(value, axis, [(0, 1), (1, 0)])


def dot(left, right):
    return lax.dot_general(left, right, (((1,), (0,)), ((), ())), preferred_element_type=F32)


def dot_nt(left, right):
    return lax.dot_general(left, right, (((1,), (1,)), ((), ())), preferred_element_type=F32)


def dot_tn(left, right):
    return lax.dot_general(left, right, (((0,), (0,)), ((), ())), preferred_element_type=F32)


def gelu_act(values):
    inner_arg = TANH_COEF * (values + CUBIC_COEF * values * values * values)
    return 0.5 * values * (1.0 + jnp.tanh(inner_arg))


def gelu_pair(values):
    square = values * values
    tanh_val = jnp.tanh(values * (TANH_COEF + (TANH_COEF * CUBIC_COEF) * square))
    half_up = 0.5 + 0.5 * tanh_val
    slope = half_up + 0.5 * values * (1.0 - tanh_val * tanh_val) * (
        TANH_COEF + (3.0 * TANH_COEF * CUBIC_COEF) * square
    )
    return (values * half_up, slope)


def decay_terms(recur_gate, soft_decay):
    u = (2.0 * GATE_SCALE) * recur_gate * soft_decay
    decay = jnp.exp(-0.5 * u)
    series = u * (
        1.0
        - u
        * (0.5 - u * (1.0 / 6 - u * (1.0 / 24 - u * (1.0 / 120 - u * (1.0 / 720)))))
    )
    em = jnp.where(u < 0.25, series, 1.0 - decay * decay)
    return (decay, em)


def scan_tile(decay, drive, row):
    for shift in (1, 2, 4):
        keep = row >= shift
        before_a = jnp.where(keep, pltpu.roll(decay, shift, 0), 1.0)
        before_b = jnp.where(keep, pltpu.roll(drive, shift, 0), 0.0)
        drive = decay * before_b + drive
        decay = decay * before_a
    return (decay, drive)


def scan_tile_back(decay, drive, row):
    for shift in (1, 2, 4):
        keep = row < 8 - shift
        after_a = jnp.where(keep, pltpu.roll(decay, 8 - shift, 0), 1.0)
        after_b = jnp.where(keep, pltpu.roll(drive, 8 - shift, 0), 0.0)
        drive = decay * after_b + drive
        decay = decay * after_a
    return (decay, drive)


def group_barrier(core, chip):
    barrier = pltpu.get_barrier_semaphore()
    for peer in ((1 - core, chip), (core, 1 - chip), (1 - core, 1 - chip)):
        pl.semaphore_signal(barrier, inc=1, device_id={"rows": peer[0], "cols": peer[1]})
    pl.semaphore_wait(barrier, 3)


def rec_forward_kernel(
    chunk, count, cot_parts,
    tokens, cotangent, wr_h, wg_h, ow_h, gain_h, rw, iw, cw, cb, rb, ib, sp,
    x_o, n1t_o, rec_o, gate_o, cl_o, r_o, i_o, st_o, br_o, mix_o, cot_o, far_o,
    tok_b, mix_s, wr, wg, ow, gain, gw, halo, carry, recpad, pre,
    tok_send, tok_recv, w_send, w_recv, w_own, cot_send, cot_recv, mix_send, mix_recv,
):
    step = pl.program_id(0)
    width = wr_h.shape[1]
    half = wr_h.shape[0]
    heads = width // 128
    core = lax.axis_index("rows")
    chip = lax.axis_index("cols")
    slot = lax.select(core == chip, 0, 1)
    near = {"rows": 1 - core}
    far = {"rows": chip, "cols": 1 - chip}

    def piece_moves(src, dst, send, recv):
        return (
            pltpu.make_async_copy(src, dst, recv),
            pltpu.make_async_remote_copy(src, dst, send.at[0], recv, device_id=near),
            pltpu.make_async_remote_copy(src, dst, send.at[1], recv, device_id=far),
        )

    def token_moves(k):
        return piece_moves(
            tokens.at[:, pl.ds(k * chunk, chunk)], tok_b.at[k, slot], tok_send.at[k], tok_recv.at[k, slot]
        )

    def cot_moves(k):
        return piece_moves(
            cotangent.at[:, pl.ds(k * chunk, chunk)],
            cot_o.at[slot, :, pl.ds(k * chunk, chunk)],
            cot_send.at[k],
            cot_recv.at[k, slot],
        )

    def mix_move(k):
        return pltpu.make_async_remote_copy(
            mix_s.at[k],
            far_o.at[pl.ds(k * chunk, chunk), :],
            mix_send.at[k],
            mix_recv.at[k],
            device_id={"cols": 1 - chip},
        )

    def start(moves):
        moves[2].start()

        @pl.when(core == chip)
        def _():
            moves[0].start()

        @pl.when(core != chip)
        def _():
            moves[1].start()

    def finish_send(moves):
        moves[2].wait_send()

        @pl.when(core != chip)
        def _():
            moves[1].wait_send()

    weights = ((wr_h, wr), (wg_h, wg), (ow_h, ow), (gain_h, gain))

    def weight_moves(n):
        src, dst = weights[n]
        return (
            pltpu.make_async_copy(src, dst.at[0], w_own.at[n]),
            pltpu.make_async_remote_copy(src, dst.at[1], w_send.at[n], w_recv.at[n], device_id=near),
        )

    def wait_weight(n):
        own, other = weight_moves(n)
        own.wait()
        other.wait_recv()

    @pl.when(step == 0)
    def _():
        group_barrier(core, chip)
        start(token_moves(0))
        for n in (3, 0, 1, 2):
            for move in weight_moves(n):
                move.start()
        for k in range(1, count):
            start(token_moves(k))
        halo[...] = jnp.zeros_like(halo)
        carry[...] = jnp.zeros_like(carry)
        for h in range(heads):
            gw[h, :, 0:128] = rw[h]
            gw[h, :, 128:256] = iw[h]
        wait_weight(3)

    for s in range(2):
        pltpu.make_async_copy(
            tokens.at[:, pl.ds(0, chunk)], tok_b.at[step, s], tok_recv.at[step, s]
        ).wait()

    @pl.when(step == count - 2)
    def _():
        for k in range(cot_parts):
            start(cot_moves(k))

    xt0 = tok_b[step, 0].astype(F32)
    xt1 = tok_b[step, 1].astype(F32)
    squares = jnp.sum(xt0 * xt0, axis=0, keepdims=True) + jnp.sum(xt1 * xt1, axis=0, keepdims=True)
    scale = lax.rsqrt(squares / (2 * half) + EPS)
    nt0 = (xt0 * scale * gain[0]).astype(BF16)
    nt1 = (xt1 * scale * gain[1]).astype(BF16)
    n1t_o[0:half, :] = nt0
    n1t_o[half:, :] = nt1
    x_o[:, 0:half] = tok_b[step, 0].T
    x_o[:, half:] = tok_b[step, 1].T
    low0 = nt0.T
    low1 = nt1.T

    @pl.when(step == 0)
    def _():
        wait_weight(0)
        wait_weight(1)

    rec = dot(low0, wr[0]) + dot(low1, wr[1])
    recpad[0:8, :] = halo[...]
    recpad[8:, :] = rec
    halo[...] = rec[chunk - 8 :, :]
    rec_o[...] = rec
    gate_o[...] = dot(low0, wg[0]) + dot(low1, wg[1])

    def conv_step(i, _):
        base = pl.multiple_of(i * 16, 16)
        for h in range(heads):
            sl = slice(h * 128, (h + 1) * 128)
            window = recpad[pl.ds(base, 24), sl]
            out = cb[:, sl] + cw[0:1, sl] * window[8:]
            for k in range(1, KCONV):
                out = out + cw[k : k + 1, sl] * pltpu.roll(window, k, 0)[8:]
            cl_o[pl.ds(base, 16), sl] = out.astype(BF16)
        return 0

    lax.fori_loop(0, chunk // 16, conv_step, 0)
    for h in range(heads):
        pre[:, h * 256 : (h + 1) * 256] = dot(cl_o[:, h * 128 : (h + 1) * 128], gw[h])
    row = lax.broadcasted_iota(jnp.int32, (8, 128), 0)

    def main_step(i, _):
        base = pl.multiple_of(i * 16, 16)
        rows = pl.ds(base, 16)
        for h in range(heads):
            sl = slice(h * 128, (h + 1) * 128)
            r = jax.nn.sigmoid(pre[rows, h * 256 : h * 256 + 128] + rb[:, sl])
            g = jax.nn.sigmoid(pre[rows, h * 256 + 128 : (h + 1) * 256] + ib[:, sl])
            conv = cl_o[rows, sl].astype(F32)
            decay, em = decay_terms(r, sp[:, sl])
            drive = jnp.sqrt(em) * g * conv
            r_o[rows, sl] = r
            i_o[rows, sl] = g
            held = carry[0:1, sl]
            parts = []
            for p in range(2):
                a, b = scan_tile(decay[p * 8 : p * 8 + 8], drive[p * 8 : p * 8 + 8], row)
                state = a * held + b
                held = state[7:8]
                parts.append(state)
            carry[0:1, sl] = held
            state = jnp.concatenate(parts, axis=0)
            st_o[rows, sl] = state
            br_o[rows, sl] = (state * gelu_act(gate_o[rows, sl])).astype(BF16)
        return 0

    lax.fori_loop(0, chunk // 16, main_step, 0)

    @pl.when(step == 0)
    def _():
        wait_weight(2)

    branch = br_o[...]
    mix_o[:, :half] = dot_nt(branch, ow[0]).astype(BF16)
    mix_o[:, half:] = dot_nt(branch, ow[1]).astype(BF16)

    for k in range(cot_parts):

        @pl.when(step == k)
        def _():
            mix_s[k] = mix_o[...]
            mix_move(k).start()

    @pl.when(step == count - 1)
    def _():
        for k in range(cot_parts):
            for s in range(2):
                pltpu.make_async_copy(
                    cotangent.at[:, pl.ds(0, chunk)],
                    cot_o.at[s, :, pl.ds(k * chunk, chunk)],
                    cot_recv.at[k, s],
                ).wait()
            finish_send(cot_moves(k))
            mix_move(k).wait()
        for k in range(count):
            finish_send(token_moves(k))
        for n in range(4):
            weight_moves(n)[1].wait_send()


def rec_forward(tokens, cotangent, wr, wg, ow, gain, rw, iw, cw, cb, rb, ib, sp, chunk=256):
    half, length = tokens.shape
    width = wr.shape[1]
    heads = width // 128
    count = length // chunk
    cot_parts = count // 2
    wide = 2 * half
    row_block = lambda cols: pl.BlockSpec((chunk, cols), lambda i: (i, 0))
    whole = lambda shape: pl.BlockSpec(
        shape, lambda i: (0,) * len(shape), pipeline_mode=pl.Buffered(1)
    )
    hbm = pl.BlockSpec(memory_space=pl.ANY)
    f32 = jax.ShapeDtypeStruct((length, width), F32)
    low = jax.ShapeDtypeStruct((length, width), BF16)
    dma = pltpu.SemaphoreType.DMA
    return pl.pallas_call(
        functools.partial(rec_forward_kernel, chunk, count, cot_parts),
        grid=(count,),
        in_specs=[hbm] * 6
        + [whole((heads, 128, 128))] * 2
        + [whole((KCONV, width))]
        + [whole((1, width))] * 4,
        out_specs=[row_block(wide), pl.BlockSpec((wide, chunk), lambda i: (0, i))]
        + [row_block(width)] * 7
        + [row_block(wide), hbm, hbm],
        out_shape=[
            jax.ShapeDtypeStruct((length, wide), BF16),
            jax.ShapeDtypeStruct((wide, length), BF16),
            f32, f32, low, f32, f32, f32, low,
            jax.ShapeDtypeStruct((length, wide), BF16),
            jax.ShapeDtypeStruct((2, half, cot_parts * chunk), BF16),
            jax.ShapeDtypeStruct((cot_parts * chunk, wide), BF16),
        ],
        scratch_shapes=[
            pltpu.VMEM((count, 2, half, chunk), BF16),
            pltpu.VMEM((cot_parts, chunk, wide), BF16),
            pltpu.VMEM((2, half, width), BF16),
            pltpu.VMEM((2, half, width), BF16),
            pltpu.VMEM((2, half, width), BF16),
            pltpu.VMEM((2, half, 1), F32),
            pltpu.VMEM((heads, 128, 256), BF16),
            pltpu.VMEM((8, width), F32),
            pltpu.VMEM((8, width), F32),
            pltpu.VMEM((chunk + 8, width), F32),
            pltpu.VMEM((chunk, 2 * width), F32),
            dma((count, 2)),
            dma((count, 2)),
            dma((4,)),
            dma((4,)),
            dma((4,)),
            dma((count, 2)),
            dma((count, 2)),
            dma((cot_parts,)),
            dma((cot_parts,)),
        ],
        compiler_params=pltpu.CompilerParams(
            vmem_limit_bytes=60 * MIB, collective_id=2, has_side_effects=True
        ),
        name="recurrent_forward",
    )(tokens, cotangent, wr, wg, ow, gain, rw, iw, cw, cb, rb, ib, sp)


def exchange(srcs, dsts, send, recv, at, core, chip):
    def moves(m):
        src, dst = srcs[m], dsts[m]
        if len(dst.shape) == 2:
            return (
                pltpu.make_async_remote_copy(src, dst, send.at[m, 0], recv.at[m, 0], device_id={"cols": 1 - chip}),
            )
        slot = lax.select(core == chip, 0, 1)
        there = dst.at[slot]
        return (
            pltpu.make_async_copy(src, there, recv.at[m, slot]),
            pltpu.make_async_remote_copy(
                src, there, send.at[m, 0], recv.at[m, slot], device_id={"rows": 1 - core}
            ),
            pltpu.make_async_remote_copy(
                src, there, send.at[m, 1], recv.at[m, slot], device_id={"rows": chip, "cols": 1 - chip}
            ),
        )

    @pl.when(at == 0)
    def _():
        group_barrier(core, chip)
        for m in range(len(srcs)):
            move = moves(m)
            move[-1].start()
            if len(move) > 1:

                @pl.when(core == chip)
                def _():
                    move[0].start()

                @pl.when(core != chip)
                def _():
                    move[1].start()

    def finish():
        for m in range(len(srcs)):
            move = moves(m)
            if len(move) == 1:
                move[0].wait()
                continue
            for s in range(2):
                pltpu.make_async_copy(srcs[m], dsts[m].at[s], recv.at[m, s]).wait()
            move[2].wait_send()

            @pl.when(core != chip)
            def _():
                move[1].wait_send()

    return finish


def ffn_kernel(
    tile, moved,
    x, mix, mix_far, ct, live, gain, keep, wg0, wg1, wu0, wu1, wd0, wd1, *refs
):
    srcs, refs = refs[:moved], refs[moved:]
    (res_o, n2t_o, cott_o, cot_o, out_o, gn2_o, hid_o, ga_o, gb_o), refs = refs[:9], refs[9:]
    dsts, (n2_s, out_acc, gn2_acc, send, recv) = refs[:moved], refs[moved:]
    finish = exchange(
        srcs, dsts, send, recv, pl.program_id(0), lax.axis_index("rows"), lax.axis_index("cols")
    )
    step = pl.program_id(0)
    tokens, wide = x.shape
    half = wide // 2

    @pl.when(step == 0)
    def _():
        out_acc[...] = jnp.zeros_like(out_acc)
        gn2_acc[...] = jnp.zeros_like(gn2_acc)
        cott_o[:half] = ct[0] * live[...]
        cott_o[half:] = ct[1] * live[...]
        cot_o[...] = cott_o[...].T

        def norm_step(i, _):
            rows = pl.ds(pl.multiple_of(i * 16, 16), 16)
            res = x[rows, :].astype(F32) + (mix[rows, :].astype(F32) + mix_far[rows, :].astype(F32))
            res_o[rows, :] = res
            scale = lax.rsqrt(jnp.sum(res * res, axis=1, keepdims=True) / wide + EPS)
            n2_s[rows, :] = (res * scale * gain[...]).astype(BF16)
            return 0

        lax.fori_loop(0, tokens // 16, norm_step, 0)
        n2t_o[...] = n2_s[...].T

    def tile_step(i, _):
        rows = pl.ds(pl.multiple_of(i * tile, tile), tile)
        n0, n1 = n2_s[rows, :half], n2_s[rows, half:]
        c0, c1 = cot_o[rows, :half], cot_o[rows, half:]
        a = dot(n0, wg0[...]) + dot(n1, wg1[...])
        b = dot(n0, wu0[...]) + dot(n1, wu1[...])
        gh = dot(c0, wd0[...]) + dot(c1, wd1[...])
        act, slope = gelu_pair(a)
        hidden = (act * b).astype(BF16)
        ga = (gh * b * slope).astype(BF16)
        gb = (gh * act).astype(BF16)
        hid_o[rows, :] = hidden
        ga_o[rows, :] = ga
        gb_o[rows, :] = gb
        out_acc[rows, :half] += dot_nt(hidden, wd0[...])
        out_acc[rows, half:] += dot_nt(hidden, wd1[...])
        gn2_acc[rows, :half] += dot_nt(ga, wg0[...]) + dot_nt(gb, wu0[...])
        gn2_acc[rows, half:] += dot_nt(ga, wg1[...]) + dot_nt(gb, wu1[...])
        return 0

    lax.fori_loop(0, tokens // tile, tile_step, 0)

    @pl.when(step == pl.num_programs(0) - 1)
    def _():
        out_o[...] = (out_acc[...] + keep[...] * res_o[...]).astype(BF16)
        gn2_o[...] = gn2_acc[...].astype(BF16)
        finish()


def ffn(part, tokens, x, mix, mix_far, cott, live, gain, keep, wg, wu, wd, srcs, dsts, collective_id, block=256, tile=256):
    wide = x.shape[1]
    half, width = wg[0].shape
    whole = lambda shape, at=(0, 0): pl.BlockSpec(
        shape, lambda i: at, pipeline_mode=pl.Buffered(1)
    )
    hbm = pl.BlockSpec(memory_space=pl.ANY)
    rows = whole((tokens, wide), (part, 0))
    act = whole((tokens, wide))
    across = whole((wide, tokens))
    weight = pl.BlockSpec((half, block), lambda i: (0, i))
    mid = pl.BlockSpec((tokens, block), lambda i: (0, i))
    low = jax.ShapeDtypeStruct((tokens, wide), BF16)
    turned = jax.ShapeDtypeStruct((wide, tokens), BF16)
    hidden = jax.ShapeDtypeStruct((tokens, width), BF16)
    sems = pltpu.SemaphoreType.DMA((len(srcs), 2))
    return pl.pallas_call(
        functools.partial(ffn_kernel, tile, len(srcs)),
        grid=(width // block,),
        in_specs=[rows, rows, act, whole((2, half, tokens), (0, 0, 0)), whole((1, tokens), (0, part))]
        + [whole((1, wide)), whole((1, 1))]
        + [weight] * 6
        + [hbm] * len(srcs),
        out_specs=[act, across, across, act, act, act, mid, mid, mid] + [hbm] * len(srcs),
        out_shape=[
            jax.ShapeDtypeStruct((tokens, wide), F32),
            turned, turned, low, low, low, hidden, hidden, hidden,
        ]
        + [jax.ShapeDtypeStruct(shape, BF16) for shape in dsts],
        scratch_shapes=[
            pltpu.VMEM((tokens, wide), BF16),
            pltpu.VMEM((tokens, wide), F32),
            pltpu.VMEM((tokens, wide), F32),
            sems,
            sems,
        ],
        compiler_params=pltpu.CompilerParams(
            vmem_limit_bytes=60 * MIB, collective_id=collective_id, has_side_effects=True
        ),
        name=f"ffn_{part}",
    )(x, mix, mix_far, cott, live, gain, keep, wg[0], wg[1], wu[0], wu[1], wd[0], wd[1], *srcs)


def ffn_weights_kernel(parts, *refs):
    n2t, cott, hid, ga, gb = (refs[i * parts : (i + 1) * parts] for i in range(5))
    src, gg0, gg1, gu0, gu1, gd0, gd1, dst, send, recv = refs[5 * parts :]
    finish = exchange(
        [src], [dst], send, recv, pl.program_id(0), lax.axis_index("rows"), lax.axis_index("cols")
    )
    half = gg0.shape[0]
    total = lambda pairs: sum(dot(left, right) for left, right in pairs).astype(BF16)
    for left, right, out0, out1 in ((n2t, ga, gg0, gg1), (n2t, gb, gu0, gu1), (cott, hid, gd0, gd1)):
        out0[...] = total([(a[:half], b[...]) for a, b in zip(left, right)])
        out1[...] = total([(a[half:], b[...]) for a, b in zip(left, right)])

    @pl.when(pl.program_id(0) == pl.num_programs(0) - 1)
    def _():
        finish()


def ffn_weights(n2t, cott, hid, ga, gb, src, collective_id, block=256):
    parts = len(n2t)
    wide, tokens = n2t[0].shape
    half, width = wide // 2, hid[0].shape[1]
    whole = lambda shape: pl.BlockSpec(shape, lambda i: (0, 0), pipeline_mode=pl.Buffered(1))
    mid = pl.BlockSpec((tokens, block), lambda i: (0, i))
    grad = jax.ShapeDtypeStruct((half, width), BF16)
    hbm = pl.BlockSpec(memory_space=pl.ANY)
    sems = pltpu.SemaphoreType.DMA((1, 2))
    return pl.pallas_call(
        functools.partial(ffn_weights_kernel, parts),
        grid=(width // block,),
        in_specs=[whole((wide, tokens))] * (2 * parts) + [mid] * (3 * parts) + [hbm],
        out_specs=[pl.BlockSpec((half, block), lambda i: (0, i))] * 6 + [hbm],
        out_shape=[grad] * 6 + [jax.ShapeDtypeStruct(src.shape, src.dtype)],
        scratch_shapes=[sems, sems],
        compiler_params=pltpu.CompilerParams(
            vmem_limit_bytes=60 * MIB, collective_id=collective_id, has_side_effects=True
        ),
        name="ffn_weights",
    )(*n2t, *cott, *hid, *ga, *gb, src)


def norm_back_kernel(gn, gn_far, res, cot, gain, g1_o, g1t_o, gain_o):
    rows_all, wide = gn.shape

    @pl.when(pl.program_id(0) == 0)
    def _():
        gain_o[...] = jnp.zeros_like(gain_o)

    def step(i, _):
        rows = pl.ds(pl.multiple_of(i * 16, 16), 16)
        grad = gn[rows, :].astype(F32) + gn_far[rows, :].astype(F32)
        held = res[rows, :]
        scale = lax.rsqrt(jnp.sum(held * held, axis=1, keepdims=True) / wide + EPS)
        product = grad * held
        by_gain = product * scale
        gain_o[...] += by_gain[0:8] + by_gain[8:16]
        inner = jnp.sum(product * gain[...], axis=1, keepdims=True)
        grad_one = (
            cot[rows, :].astype(F32)
            + scale * (grad * gain[...])
            - held * (scale * scale * scale * inner / wide)
        )
        g1_o[rows, :] = grad_one.astype(BF16)
        return 0

    lax.fori_loop(0, rows_all // 16, step, 0)
    g1t_o[...] = g1_o[...].T


def norm_back(gn, gn_far, res, cot, gain, chunk=256):
    tokens, wide = gn.shape
    rows = pl.BlockSpec((chunk, wide), lambda i: (i, 0))
    return pl.pallas_call(
        norm_back_kernel,
        grid=(tokens // chunk,),
        in_specs=[rows] * 4 + [pl.BlockSpec((1, wide), lambda i: (0, 0))],
        out_specs=[
            rows,
            pl.BlockSpec((wide, chunk), lambda i: (0, i)),
            pl.BlockSpec((8, wide), lambda i: (0, 0)),
        ],
        out_shape=[
            jax.ShapeDtypeStruct((tokens, wide), BF16),
            jax.ShapeDtypeStruct((wide, tokens), BF16),
            jax.ShapeDtypeStruct((8, wide), F32),
        ],
        compiler_params=pltpu.CompilerParams(vmem_limit_bytes=48 * MIB),
        name="norm_back",
    )(gn, gn_far, res, cot, gain)


def rec_backward_kernel(
    tile,
    g1a, g1b, g1ta, g1tb, n1t, st, gate, r_in, i_in, cl, rec, br, ow0, ow1, wr0, wr1, wg0, wg1, gw, cw, sp,
    x, gain, gain_a, gain_b,
    gn1_o, go0, go1, gr0, gr1, gg0, gg1, ggw, sums, stat, gains0, gains1,
    acc, gb_s, gc_s, ggp_s, grp_s, gip_s, grec_s, gain_s,
):
    step = pl.program_id(0)
    tokens, block = gb_s.shape
    wide = n1t.shape[0]
    heads = block // 128
    half = ow0.shape[0]
    tiles = tokens // tile
    subs = tile // 8

    @pl.when(step == 0)
    def _():
        acc[...] = jnp.zeros_like(acc)

    mid = tokens // 2
    gb_s[:mid] = dot(g1a[:, :half], ow0[...]) + dot(g1a[:, half:], ow1[...])
    gb_s[mid:] = dot(g1b[:, :half], ow0[...]) + dot(g1b[:, half:], ow1[...])
    go0[...] = (dot(g1ta[:half], br[:mid]) + dot(g1tb[:half], br[mid:])).astype(BF16)
    go1[...] = (dot(g1ta[half:], br[:mid]) + dot(g1tb[half:], br[mid:])).astype(BF16)
    sums[...] = jnp.zeros_like(sums)
    row = lax.broadcasted_iota(jnp.int32, (8, 128), 0)

    def back_step(j, held):
        i = tiles - 1 - j
        base = pl.multiple_of(i * tile, tile)
        rows = pl.ds(base, tile)
        before = pl.ds(pl.multiple_of(jnp.maximum(base - 8, 0), 8), 8)
        out = []
        for h in range(heads):
            sl = slice(h * 128, (h + 1) * 128)
            later_decay, later_carried = held[h]
            grad_branch = gb_s[rows, sl]
            act, slope = gelu_pair(gate[rows, sl])
            state = st[rows, sl]
            ggp_s[rows, sl] = (grad_branch * state * slope).astype(BF16)
            grad_state = grad_branch * act
            r = r_in[rows, sl]
            soft = sp[:, sl]
            decay, em = decay_terms(r, soft)
            parts = [None] * subs
            for p in range(subs - 1, -1, -1):
                own = decay[p * 8 : p * 8 + 8]
                after = jnp.where(row == 7, later_decay, pltpu.roll(own, 7, 0))
                a, b = scan_tile_back(after, grad_state[p * 8 : p * 8 + 8], row)
                carried = a * later_carried + b
                later_decay = own[0:1]
                later_carried = carried[0:1]
                parts[p] = carried
            out.append((later_decay, later_carried))
            carried = jnp.concatenate(parts, axis=0)
            edge = jnp.where(i > 0, st[before, sl][7:8], 0.0)
            prev = []
            for p in range(subs):
                prev.append(jnp.where(row == 0, edge, pltpu.roll(state[p * 8 : p * 8 + 8], 1, 0)))
                edge = state[p * 8 + 7 : p * 8 + 8]
            prev = jnp.concatenate(prev, axis=0)
            g = i_in[rows, sl]
            conv = cl[rows, sl].astype(F32)
            scaling = jnp.sqrt(em)
            gated = g * conv
            grad_log = carried * (prev * decay - gated * (decay * decay) / scaling)
            grad_soft = grad_log * (-GATE_SCALE * r)
            grp = grad_soft * soft * (1.0 - r)
            cs = carried * scaling
            gc_s[rows, sl] = cs * g
            gip = cs * gated * (1.0 - g)
            grp_s[rows, sl] = grp.astype(BF16)
            gip_s[rows, sl] = gip.astype(BF16)
            for n, term in enumerate((grp, gip, grad_soft)):
                total = term[0:8]
                for p in range(1, subs):
                    total = total + term[p * 8 : p * 8 + 8]
                sums[n * 8 : n * 8 + 8, sl] += total
        return tuple(out)

    zero = jnp.zeros((1, 128), F32)
    lax.fori_loop(0, tiles, back_step, tuple((zero, zero) for _ in range(heads)))
    for h in range(heads):
        sl = slice(h * 128, (h + 1) * 128)
        low = cl[:, sl]
        ggw[h, :, 0:128] = dot_tn(low, grp_s[:, sl]).astype(BF16)
        ggw[h, :, 128:256] = dot_tn(low, gip_s[:, sl]).astype(BF16)
        gc_s[:, sl] += dot_nt(grp_s[:, sl], gw[h, :, 0:128]) + dot_nt(gip_s[:, sl], gw[h, :, 128:256])

    def conv_step(j, held):
        i = tiles - 1 - j
        base = pl.multiple_of(i * tile, tile)
        rows = pl.ds(base, tile)
        before = pl.ds(pl.multiple_of(jnp.maximum(base - 8, 0), 8), 8)
        out = []
        for h in range(heads):
            sl = slice(h * 128, (h + 1) * 128)
            grad_conv = gc_s[rows, sl]
            window = jnp.concatenate([grad_conv, held[h]], axis=0)
            out.append(grad_conv[0:8])
            grad_rec = cw[0:1, sl] * grad_conv
            for k in range(1, KCONV):
                grad_rec = grad_rec + cw[k : k + 1, sl] * pltpu.roll(window, tile + 8 - k, 0)[:tile]
            grec_s[rows, sl] = grad_rec.astype(BF16)
            edge = jnp.where(i > 0, rec[before, sl], 0.0)
            past = jnp.concatenate([edge, rec[rows, sl]], axis=0)
            terms = [grad_conv * past[8:]]
            for k in range(1, KCONV):
                terms.append(grad_conv * pltpu.roll(past, k, 0)[8:])
            terms.append(grad_conv)
            for n, term in enumerate(terms):
                total = term[0:8]
                for p in range(1, subs):
                    total = total + term[p * 8 : p * 8 + 8]
                sums[24 + n * 8 : 32 + n * 8, sl] += total
        return tuple(out)

    lax.fori_loop(0, tiles, conv_step, tuple(jnp.zeros((8, 128), F32) for _ in range(heads)))
    grad_rec = grec_s[...]
    grad_gate = ggp_s[...]
    gr0[...] = dot(n1t[:half], grad_rec).astype(BF16)
    gr1[...] = dot(n1t[half:], grad_rec).astype(BF16)
    gg0[...] = dot(n1t[:half], grad_gate).astype(BF16)
    gg1[...] = dot(n1t[half:], grad_gate).astype(BF16)
    acc[:, :half] += dot_nt(grad_rec, wr0[...]) + dot_nt(grad_gate, wg0[...])
    acc[:, half:] += dot_nt(grad_rec, wr1[...]) + dot_nt(grad_gate, wg1[...])

    @pl.when(step == pl.num_programs(0) - 1)
    def _():
        gain_s[...] = jnp.zeros_like(gain_s)

        def stat_step(i, _):
            rows = pl.ds(pl.multiple_of(i * 16, 16), 16)
            part = acc[rows, :]
            gn1_o[rows, :] = part.astype(BF16)
            held = x[rows, :].astype(F32)
            scale = lax.rsqrt(jnp.sum(held * held, axis=1, keepdims=True) / wide + EPS)
            product = part * held
            by_gain = product * scale
            gain_s[...] += by_gain[0:8] + by_gain[8:16]
            inner = jnp.sum(product * gain[...], axis=1, keepdims=True)
            stat[rows, 0:64] = jnp.broadcast_to(inner, (16, 64))
            stat[rows, 64:128] = jnp.broadcast_to(scale, (16, 64))
            return 0

        lax.fori_loop(0, tokens // 16, stat_step, 0)
        both = gain_a[...] + gain_b[...]
        for out, sl in ((gains0, slice(0, half)), (gains1, slice(half, wide))):
            out[...] = jnp.zeros_like(out)
            out[0:8, :] = gain_s[:, sl]
            out[8:16, :] = both[:, sl]


def rec_backward(
    g1, g1t, n1t, st, gate, r, g, cl, rec, br, ow, wr, wg, gw, cw, sp, x, gain, gain_a, gain_b, block=256, tile=32
):
    wide, tokens = n1t.shape
    half, width = wr[0].shape
    heads = block // 128
    mid = tokens // 2
    whole = lambda shape: pl.BlockSpec(shape, lambda i: (0, 0), pipeline_mode=pl.Buffered(1))
    act = pl.BlockSpec((tokens, block), lambda i: (0, i))
    weight = pl.BlockSpec((half, block), lambda i: (0, i))
    thin = lambda n: pl.BlockSpec((n, block), lambda i: (0, i))
    gate_block = pl.BlockSpec((heads, 128, 256), lambda i: (i, 0, 0))
    grad = jax.ShapeDtypeStruct((half, width), BF16)
    return pl.pallas_call(
        functools.partial(rec_backward_kernel, tile),
        grid=(width // block,),
        in_specs=[whole((mid, wide))] * 2 + [whole((wide, mid))] * 2 + [whole((wide, tokens))]
        + [act] * 7
        + [weight] * 6
        + [gate_block, thin(KCONV), thin(1)]
        + [whole((tokens, wide)), whole((1, wide)), whole((8, wide)), whole((8, wide))],
        out_specs=[whole((tokens, wide))]
        + [weight] * 6
        + [gate_block, thin(64), whole((tokens, 128)), whole((64, half)), whole((64, half))],
        out_shape=[jax.ShapeDtypeStruct((tokens, wide), BF16)]
        + [grad] * 6
        + [
            jax.ShapeDtypeStruct((width // 128, 128, 256), BF16),
            jax.ShapeDtypeStruct((64, width), F32),
            jax.ShapeDtypeStruct((tokens, 128), F32),
            jax.ShapeDtypeStruct((64, half), F32),
            jax.ShapeDtypeStruct((64, half), F32),
        ],
        scratch_shapes=[
            pltpu.VMEM((tokens, wide), F32),
            pltpu.VMEM((tokens, block), F32),
            pltpu.VMEM((tokens, block), F32),
            pltpu.VMEM((tokens, block), BF16),
            pltpu.VMEM((tokens, block), BF16),
            pltpu.VMEM((tokens, block), BF16),
            pltpu.VMEM((tokens, block), BF16),
            pltpu.VMEM((8, wide), F32),
        ],
        compiler_params=pltpu.CompilerParams(vmem_limit_bytes=60 * MIB),
        name="recurrent_backward",
    )(
        g1[0], g1[1], g1t[0], g1t[1], n1t, st, gate, r, g, cl, rec, br,
        ow[0], ow[1], wr[0], wr[1], wg[0], wg[1], gw, cw, sp, x, gain, gain_a, gain_b,
    )


def ring_kernel(n, count, *refs):
    own, other, refs = refs[:count], refs[count : 2 * count], refs[2 * count :]
    (gn1, out_a, out_b, stat, g1_a, g1_b), refs = refs[:6], refs[6:]
    outs, refs = refs[:count], refs[count:]
    (gn1_p, out_p, stat_p, g1_p), scratch = refs[:4], refs[4:]
    piece_send, piece_recv = scratch[-2:]
    scratch = scratch[:-2]
    own_b, part_b, ring_b = scratch[:count], scratch[count : 2 * count], scratch[2 * count : 3 * count]
    own_sem, part_send, part_recv, rs_send, rs_recv, ag_send, ag_recv, put_sem = scratch[3 * count :]
    at = lax.axis_index("dp")
    core = lax.axis_index("rows")
    chip = lax.axis_index("cols")

    def place_of(index):
        return lax.select(index % 2 == 0, index // 2, n - 1 - index // 2)

    def index_of(place):
        return lax.select(place < n // 2, 2 * place, 2 * (n - 1 - place) + 1)

    me = place_of(at)
    nexts = (index_of(lax.rem(me + 1, n)), index_of(lax.rem(me + n - 1, n)))
    barrier = pltpu.get_barrier_semaphore()
    for neighbour in nexts:
        pl.semaphore_signal(barrier, inc=1, device_id={"dp": neighbour})
    for peer in ((1 - core, chip), (core, 1 - chip), (1 - core, 1 - chip)):
        pl.semaphore_signal(barrier, inc=1, device_id={"rows": peer[0], "cols": peer[1]})
    pl.semaphore_wait(barrier, 5)

    half = gn1_p.shape[2]
    part = out_a.shape[0]
    first, second = slice(0, half), slice(half, 2 * half)
    everything = slice(None)
    pieces = [
        (gn1, gn1_p, slice(None), first, second),
        (out_a, out_p, slice(0, part), first, second),
        (out_b, out_p, slice(part, 2 * part), first, second),
        (stat, stat_p, slice(None), everything, everything),
    ]
    singles = [(g1_a, slice(0, part)), (g1_b, slice(part, 2 * part))]
    diag = core == chip

    def piece_moves(m):
        src, dst, rows, mine, theirs = pieces[m]
        there = dst.at[chip, rows, :]
        sems = lambda w: (piece_send.at[m, w], piece_recv.at[m, chip])
        near = src.at[:, mine]
        away = src.at[:, theirs]
        return (
            pltpu.make_async_copy(near, there, piece_recv.at[m, chip]),
            pltpu.make_async_remote_copy(near, there, *sems(0), device_id={"cols": 1 - chip}),
            pltpu.make_async_remote_copy(away, there, *sems(1), device_id={"rows": 1 - core}),
            pltpu.make_async_remote_copy(
                away, there, *sems(1), device_id={"rows": 1 - core, "cols": 1 - chip}
            ),
        )

    def single_moves(m):
        src, rows = singles[m]
        there = g1_p.at[rows, :]
        at = len(pieces) + m
        return (
            pltpu.make_async_copy(src.at[:, first], there, piece_recv.at[at, 0]),
            pltpu.make_async_remote_copy(
                src.at[:, second], there, piece_send.at[at, 1], piece_recv.at[at, 0],
                device_id={"rows": 1 - core},
            ),
        )

    @pl.when(diag)
    def _():
        for m in range(len(pieces)):
            moves = piece_moves(m)
            moves[0].start()
            moves[2].start()
        for m in range(len(singles)):
            moves = single_moves(m)
            moves[0].start()
            moves[1].start()

    @pl.when(jnp.logical_not(diag))
    def _():
        for m in range(len(pieces)):
            moves = piece_moves(m)
            moves[1].start()
            moves[3].start()

    def chunk_of(way, s):
        return lax.rem(me + n - s, n) if way == 0 else lax.rem(me + s, n)

    def rows_of(k, way, s):
        size = own[k].shape[0] // n
        return pl.ds(pl.multiple_of(chunk_of(way, s) * size, size), size)

    def cols_of(k, way):
        wide = own[k].shape[1] // 2
        return pl.ds(way * wide, wide)

    def own_copy(k, way, s):
        return pltpu.make_async_copy(
            own[k].at[rows_of(k, way, s), cols_of(k, way)], own_b[k].at[way, s], own_sem.at[k, way, s]
        )

    def part_copy(k, way, s):
        return pltpu.make_async_remote_copy(
            src_ref=other[k].at[rows_of(k, way, s), cols_of(k, way)],
            dst_ref=part_b[k].at[way, s],
            send_sem=part_send.at[k, way],
            recv_sem=part_recv.at[k, way, s],
            device_id={"rows": 1 - core},
        )

    def sum_copy(k, way, s):
        return pltpu.make_async_remote_copy(
            src_ref=ring_b[k].at[way, s],
            dst_ref=ring_b[k].at[way, s + 1],
            send_sem=rs_send.at[k, way],
            recv_sem=rs_recv.at[k, way, s],
            device_id={"dp": nexts[way]},
        )

    def first_gather(k, way):
        rows = rows_of(k, way, n - 1)
        return pltpu.make_async_remote_copy(
            src_ref=ring_b[k].at[way, n - 1],
            dst_ref=outs[k].at[rows, cols_of(k, way)],
            send_sem=ag_send.at[k, way, 0],
            recv_sem=ag_recv.at[k, way, 0],
            device_id={"dp": nexts[way]},
        )

    def gather_copy(k, way, s):
        rows = rows_of(k, way, s - 1)
        there = outs[k].at[rows, cols_of(k, way)]
        return pltpu.make_async_remote_copy(
            src_ref=there,
            dst_ref=there,
            send_sem=ag_send.at[k, way, s],
            recv_sem=ag_recv.at[k, way, s],
            device_id={"dp": nexts[way]},
        )

    def put_copy(k, way):
        return pltpu.make_async_copy(
            ring_b[k].at[way, n - 1],
            outs[k].at[rows_of(k, way, n - 1), cols_of(k, way)],
            put_sem.at[k, way],
        )

    both = [(k, way) for k in range(count) for way in range(2)]

    def load_step(s, _):
        for k, way in both:
            part_copy(k, way, s).start()
            own_copy(k, way, s).start()
        return 0

    lax.fori_loop(0, n, load_step, 0)

    def add_step(k, way, s, received):
        own_copy(k, way, s).wait()
        part_copy(k, way, s).wait_recv()
        total = own_b[k][way, s].astype(F32) + part_b[k][way, s].astype(F32)
        if received:
            sum_copy(k, way, s - 1).wait_recv()
            total = total + ring_b[k][way, s].astype(F32)
        ring_b[k][way, s] = total.astype(ring_b[k].dtype)

    for k, way in both:
        add_step(k, way, 0, False)
        sum_copy(k, way, 0).start()

    def sum_step(s, _):
        for k, way in both:
            add_step(k, way, s, True)
            sum_copy(k, way, s).start()
        return 0

    lax.fori_loop(1, n - 1, sum_step, 0)
    for k, way in both:
        add_step(k, way, n - 1, True)
        first_gather(k, way).start()
        put_copy(k, way).start()

    def gather_step(s, _):
        for k, way in both:
            gather_copy(k, way, s - 1).wait_recv()
            gather_copy(k, way, s).start()
        return 0

    for k, way in both:
        first_gather(k, way).wait_recv()
        gather_copy(k, way, 1).start()
    lax.fori_loop(2, n - 1, gather_step, 0)
    for k, way in both:
        gather_copy(k, way, n - 2).wait_recv()
        put_copy(k, way).wait()
        first_gather(k, way).wait_send()

    def drain_step(s, _):
        for k, way in both:
            gather_copy(k, way, s).wait_send()
        return 0

    lax.fori_loop(1, n - 1, drain_step, 0)
    for k, way in both:
        pltpu.make_async_remote_copy(
            ring_b[k].at[way, pl.ds(0, n - 1)],
            ring_b[k].at[way, pl.ds(1, n - 1)],
            rs_send.at[k, way],
            rs_recv.at[k, way, 0],
            device_id={"dp": nexts[way]},
        ).wait_send()
        pltpu.make_async_remote_copy(
            own_b[k].at[way],
            part_b[k].at[way],
            part_send.at[k, way],
            part_recv.at[k, way, 0],
            device_id={"rows": 1 - core},
        ).wait_send()

    for m in range(len(pieces)):
        src, dst, rows, mine, _ = pieces[m]
        for c in range(2):
            pltpu.make_async_copy(src.at[:, mine], dst.at[c, rows, :], piece_recv.at[m, c]).wait()
    for m in range(len(singles)):
        single_moves(m)[0].wait()

    @pl.when(diag)
    def _():
        for m in range(len(pieces)):
            piece_moves(m)[2].wait_send()
        for m in range(len(singles)):
            single_moves(m)[1].wait_send()

    @pl.when(jnp.logical_not(diag))
    def _():
        for m in range(len(pieces)):
            moves = piece_moves(m)
            moves[1].wait_send()
            moves[3].wait_send()


def ring_sum(n, own, other, pieces):
    count = len(own)
    own, other = list(own), list(other)
    rows = [a.shape[0] for a in own]
    unit = lambda a: (16 if a.dtype == BF16 else 8) * n
    pad = [-a.shape[0] % unit(a) for a in own]
    fit = lambda a, extra: jnp.pad(a, ((0, extra), (0, 0))) if extra else a
    own = [fit(a, e) for a, e in zip(own, pad)]
    other = [fit(a, e) for a, e in zip(other, pad)]
    slots = [pltpu.VMEM((2, n, a.shape[0] // n, a.shape[1] // 2), a.dtype) for a in own]
    sems = pltpu.SemaphoreType.DMA((count, 2, n))
    pair = pltpu.SemaphoreType.DMA((count, 2))
    tokens, wide = pieces[0].shape
    piece = jax.ShapeDtypeStruct((2, tokens, wide // 2), BF16)
    hbm = pl.BlockSpec(memory_space=pl.ANY)
    outs = pl.pallas_call(
        functools.partial(ring_kernel, n, count),
        in_specs=[hbm] * (2 * count + len(pieces)),
        out_specs=[hbm] * (count + 4),
        out_shape=[jax.ShapeDtypeStruct(a.shape, a.dtype) for a in own]
        + [
            piece,
            piece,
            jax.ShapeDtypeStruct((2, tokens, 128), F32),
            jax.ShapeDtypeStruct((tokens, wide // 2), BF16),
        ],
        scratch_shapes=slots * 3
        + [sems, pair, sems, pair] + [sems] * 3 + [pair]
        + [pltpu.SemaphoreType.DMA((6, 2))] * 2,
        compiler_params=pltpu.CompilerParams(
            collective_id=0, has_side_effects=True, vmem_limit_bytes=60 * MIB
        ),
        name="ring_sum",
    )(*own, *other, *pieces)
    return [a[:r] for a, r in zip(outs, rows)], outs[count:]


def final_kernel(gn, out, stat, g1, tokens, gain, live, result_o, grad_o):
    wide = 2 * tokens.shape[0]
    low = lambda ref: ref[0].astype(F32) + ref[1].astype(F32)
    result_o[...] = (low(out).T * live[...]).astype(BF16)
    grad = low(gn).T
    held = tokens[...].astype(F32)
    inner = (stat[0] + stat[1]).T[0:1, :]
    scale = stat[0].T[64:65, :]
    grad_o[...] = (
        g1[...].astype(F32).T
        + (scale * gain[...]) * grad
        - held * (scale * scale * scale * inner / wide)
    ).astype(BF16)


def final(gn, out, stat, g1, tokens, gain, live, chunk=256):
    half, length = tokens.shape
    pair = lambda cols: pl.BlockSpec((2, chunk, cols), lambda i: (0, i, 0))
    across = pl.BlockSpec((half, chunk), lambda i: (0, i))
    shape = jax.ShapeDtypeStruct((half, length), BF16)
    return pl.pallas_call(
        final_kernel,
        grid=(length // chunk,),
        in_specs=[
            pair(half), pair(half), pair(128),
            pl.BlockSpec((chunk, half), lambda i: (i, 0)),
            across,
            pl.BlockSpec((half, 1), lambda i: (0, 0)),
            pl.BlockSpec((1, chunk), lambda i: (0, i)),
        ],
        out_specs=[across, across],
        out_shape=[shape, shape],
        compiler_params=pltpu.CompilerParams(vmem_limit_bytes=48 * MIB),
        name="final",
    )(gn, out, stat, g1, tokens, gain, live)


def body(
    dp, tokens, lengths, mix_gain, rec_weight, gate_weight, conv_weight, conv_bias,
    recur_weight, recur_bias, input_weight, input_bias, decay_param, out_weight,
    ffn_gain, ffn_gate, ffn_up, ffn_down, cotangent,
):
    at_row = lax.axis_index("rows")
    at_col = lax.axis_index("cols")
    diag = at_row == at_col
    half = tokens.shape[0]
    wide = 2 * half

    def over_rows(own, other):
        return (own.astype(F32) + swap(other, "rows").astype(F32)).astype(BF16)

    both = lambda weight: (weight, swap(weight, "rows"))

    positions = jnp.arange(LEN, dtype=jnp.int32)
    live_core = (positions < lengths[at_row]).astype(BF16)[None, :]
    live_chip = (positions < lengths[at_col]).astype(F32)
    part = LEN // 2

    sp = jax.nn.softplus(-decay_param)[None, :]
    (x, n1t, rec, gate, cl, r, g, st, br, mixed, cot_a, far_a) = rec_forward(
        tokens, cotangent, rec_weight, gate_weight, out_weight, mix_gain[:, None],
        recur_weight, input_weight, conv_weight, conv_bias[None, :], recur_bias[None, :],
        input_bias[None, :], sp,
    )
    wr = both(rec_weight)
    wg = both(gate_weight)
    ow = both(out_weight)
    fg = both(ffn_gate)
    fu = both(ffn_up)
    fd = both(ffn_down)
    gain_two = jnp.concatenate(both(ffn_gain))[None, :]
    gain_one = jnp.concatenate(both(mix_gain))[None, :]
    keep = diag.astype(F32).reshape(1, 1)
    gw = jnp.concatenate([recur_weight, input_weight], axis=2)

    half_shape = (part, 2 * half)
    res_a, n2t_a, cott_a, ctok_a, out_a, gn2_a, hid_a, ga_a, gb_a, far_b, cot_b = ffn(
        0, part, x, mixed, far_a, cot_a, live_core, gain_two, keep, fg, fu, fd,
        [mixed[part:], cotangent[:, part:]], [half_shape, (2, half, part)], 3,
    )
    res_b, n2t_b, cott_b, ctok_b, out_b, gn2_b, hid_b, ga_b, gb_b, gn2_far_a = ffn(
        1, part, x, mixed, far_b, cot_b, live_core, gain_two, keep, fg, fu, fd,
        [gn2_a], [half_shape], 4,
    )
    gg0, gg1, gu0, gu1, gd0, gd1, gn2_far_b = ffn_weights(
        [n2t_a, n2t_b], [cott_a, cott_b], [hid_a, hid_b], [ga_a, ga_b], [gb_a, gb_b], gn2_b, 5
    )
    g1_a, g1t_a, gain_a = norm_back(gn2_a, gn2_far_a, res_a, ctok_a, gain_two)
    g1_b, g1t_b, gain_b = norm_back(gn2_b, gn2_far_b, res_b, ctok_b, gain_two)
    cut = OFFLOAD
    sum_gate = lax.psum(over_rows(gg0[:, :cut], gg1[:, :cut]), "dp")
    gn1_part, go0, go1, gr0, gr1, gt0, gt1, ggw, sums, stat, gains0, gains1 = rec_backward(
        [g1_a, g1_b], [g1t_a, g1t_b], n1t, st, gate, r, g, cl, rec, br, ow, wr, wg, gw,
        conv_weight, sp, x, gain_one, gain_a, gain_b,
    )
    sum_gate, gu0 = lax.optimization_barrier((sum_gate, gu0))
    gates = ggw.reshape(-1, 256)
    own = [gu0, gd0, go0, gr0, gt0, gates, sums, gains0]
    other = [gu1, gd1, go1, gr1, gt1, gates, sums, gains1]
    if cut < gg0.shape[1]:
        own.append(gg0[:, cut:])
        other.append(gg1[:, cut:])
    total, moved = ring_sum(dp, own, other, [gn1_part, out_a, out_b, stat, g1_a, g1_b])
    sum_up, sum_down, sum_out, sum_rec, sum_gatew, gates, sums, gains = total[:8]
    sum_gate = jnp.concatenate([sum_gate] + total[8:], axis=1)
    result, grad_tokens = final(*moved, tokens, mix_gain[:, None], live_chip[None, :])
    gates = gates.astype(F32).reshape(ggw.shape)
    vec = jnp.sum(sums.reshape(8, 8, -1), axis=1)
    gains = jnp.sum(gains[:16].reshape(2, 8, half), axis=1)
    grad_gain_one = gains[0] + swap(gains[0], "cols")
    grad_decay = vec[2] * -jax.nn.sigmoid(-decay_param)
    return (
        result,
        grad_tokens,
        grad_gain_one,
        sum_rec.astype(F32),
        sum_gatew.astype(F32),
        vec[3:7],
        vec[7],
        gates[:, :, :128],
        vec[0],
        gates[:, :, 128:],
        vec[1],
        grad_decay,
        sum_out.astype(F32),
        gains[1],
        sum_gate.astype(F32),
        sum_up.astype(F32),
        sum_down.astype(F32),
    )


def solution(mesh):
    return jax.shard_map(
        functools.partial(body, mesh.shape["dp"]),
        mesh=mesh,
        in_specs=(
            P("rows", ("dp", "cols")),
            P("dp"),
            P("rows"),
            P("rows", "cols"),
            P("rows", "cols"),
            P(None, "cols"),
            P("cols"),
            P("cols", None, None),
            P("cols"),
            P("cols", None, None),
            P("cols"),
            P("cols"),
            P("rows", "cols"),
            P("rows"),
            P("rows", "cols"),
            P("rows", "cols"),
            P("rows", "cols"),
            P("rows", ("dp", "cols")),
        ),
        out_specs=(
            P("rows", ("dp", "cols")),
            P("rows", ("dp", "cols")),
            P("rows"),
            P("rows", "cols"),
            P("rows", "cols"),
            P(None, "cols"),
            P("cols"),
            P("cols", None, None),
            P("cols"),
            P("cols", None, None),
            P("cols"),
            P("cols"),
            P("rows", "cols"),
            P("rows"),
            P("rows", "cols"),
            P("rows", "cols"),
            P("rows", "cols"),
        ),
        check_vma=False,
    )
```

```python
import functools
import math

import jax
import jax.numpy as jnp
from jax import lax
from jax.experimental import pallas as pl
from jax.experimental.pallas import tpu as pltpu
from jax.sharding import PartitionSpec as P

D = 1536
KCONV = 4
LEN = 1024
EPS = 1e-06
GATE_SCALE = 8.0
TANH_COEF = math.sqrt(2.0 / math.pi)
CUBIC_COEF = 0.044715
F32 = jnp.float32
BF16 = jnp.bfloat16
MIB = 1024 * 1024


def swap(value, axis):
    return lax.ppermute(value, axis, [(0, 1), (1, 0)])


def dot(left, right):
    return lax.dot_general(left, right, (((1,), (0,)), ((), ())), preferred_element_type=F32)


def dot_nt(left, right):
    return lax.dot_general(left, right, (((1,), (1,)), ((), ())), preferred_element_type=F32)


def dot_tn(left, right):
    return lax.dot_general(left, right, (((0,), (0,)), ((), ())), preferred_element_type=F32)


def gelu_act(values):
    inner_arg = TANH_COEF * (values + CUBIC_COEF * values * values * values)
    return 0.5 * values * (1.0 + jnp.tanh(inner_arg))


def gelu_pair(values):
    square = values * values
    tanh_val = jnp.tanh(values * (TANH_COEF + (TANH_COEF * CUBIC_COEF) * square))
    half_up = 0.5 + 0.5 * tanh_val
    slope = half_up + 0.5 * values * (1.0 - tanh_val * tanh_val) * (
        TANH_COEF + (3.0 * TANH_COEF * CUBIC_COEF) * square
    )
    return (values * half_up, slope)


def decay_terms(recur_gate, soft_decay):
    u = (2.0 * GATE_SCALE) * recur_gate * soft_decay
    decay = jnp.exp(-0.5 * u)
    series = u * (
        1.0
        - u
        * (0.5 - u * (1.0 / 6 - u * (1.0 / 24 - u * (1.0 / 120 - u * (1.0 / 720)))))
    )
    em = jnp.where(u < 0.25, series, 1.0 - decay * decay)
    return (decay, em)


def scan_tile(decay, drive, row):
    for shift in (1, 2, 4):
        keep = row >= shift
        before_a = jnp.where(keep, pltpu.roll(decay, shift, 0), 1.0)
        before_b = jnp.where(keep, pltpu.roll(drive, shift, 0), 0.0)
        drive = decay * before_b + drive
        decay = decay * before_a
    return (decay, drive)


def scan_tile_back(decay, drive, row):
    for shift in (1, 2, 4):
        keep = row < 8 - shift
        after_a = jnp.where(keep, pltpu.roll(decay, 8 - shift, 0), 1.0)
        after_b = jnp.where(keep, pltpu.roll(drive, 8 - shift, 0), 0.0)
        drive = decay * after_b + drive
        decay = decay * after_a
    return (decay, drive)


def group_barrier(core, chip):
    barrier = pltpu.get_barrier_semaphore()
    for peer in ((1 - core, chip), (core, 1 - chip), (1 - core, 1 - chip)):
        pl.semaphore_signal(barrier, inc=1, device_id={"rows": peer[0], "cols": peer[1]})
    pl.semaphore_wait(barrier, 3)


def rec_forward_kernel(
    chunk, count, cot_parts,
    tokens, cotangent, wr_h, wg_h, ow_h, gain_h, rw, iw, cw, cb, rb, ib, sp,
    x_o, n1t_o, rec_o, gate_o, cl_o, r_o, i_o, st_o, br_o, mix_o, cot_o, far_o, wr_o, wg_o, ow_o,
    tok_b, mix_s, wr, wg, ow, gain, gw, halo, carry, recpad, pre,
    tok_send, tok_recv, w_send, w_recv, w_own, cot_send, cot_recv, mix_send, mix_recv, put,
):
    step = pl.program_id(0)
    width = wr_h.shape[1]
    half = wr_h.shape[0]
    heads = width // 128
    core = lax.axis_index("rows")
    chip = lax.axis_index("cols")
    slot = lax.select(core == chip, 0, 1)
    near = {"rows": 1 - core}
    far = {"rows": chip, "cols": 1 - chip}

    def piece_moves(src, dst, send, recv):
        return (
            pltpu.make_async_copy(src, dst, recv),
            pltpu.make_async_remote_copy(src, dst, send.at[0], recv, device_id=near),
            pltpu.make_async_remote_copy(src, dst, send.at[1], recv, device_id=far),
        )

    def token_moves(k):
        return piece_moves(
            tokens.at[:, pl.ds(k * chunk, chunk)], tok_b.at[k, slot], tok_send.at[k], tok_recv.at[k, slot]
        )

    def cot_moves(k):
        return piece_moves(
            cotangent.at[:, pl.ds(k * chunk, chunk)],
            cot_o.at[slot, :, pl.ds(k * chunk, chunk)],
            cot_send.at[k],
            cot_recv.at[k, slot],
        )

    def mix_move(k):
        return pltpu.make_async_remote_copy(
            mix_s.at[k],
            far_o.at[pl.ds(k * chunk, chunk), :],
            mix_send.at[k],
            mix_recv.at[k],
            device_id={"cols": 1 - chip},
        )

    def start(moves):
        moves[2].start()

        @pl.when(core == chip)
        def _():
            moves[0].start()

        @pl.when(core != chip)
        def _():
            moves[1].start()

    def finish_send(moves):
        moves[2].wait_send()

        @pl.when(core != chip)
        def _():
            moves[1].wait_send()

    weights = ((wr_h, wr), (wg_h, wg), (ow_h, ow), (gain_h, gain))

    def weight_moves(n):
        src, dst = weights[n]
        return (
            pltpu.make_async_copy(src, dst.at[0], w_own.at[n]),
            pltpu.make_async_remote_copy(src, dst.at[1], w_send.at[n], w_recv.at[n], device_id=near),
        )

    def wait_weight(n):
        own, other = weight_moves(n)
        own.wait()
        other.wait_recv()

    @pl.when(step == 0)
    def _():
        group_barrier(core, chip)
        start(token_moves(0))
        for n in (3, 0, 1, 2):
            for move in weight_moves(n):
                move.start()
        for k in range(1, count):
            start(token_moves(k))
        halo[...] = jnp.zeros_like(halo)
        carry[...] = jnp.zeros_like(carry)
        for h in range(heads):
            gw[h, :, 0:128] = rw[h]
            gw[h, :, 128:256] = iw[h]
        wait_weight(3)

    for s in range(2):
        pltpu.make_async_copy(
            tokens.at[:, pl.ds(0, chunk)], tok_b.at[step, s], tok_recv.at[step, s]
        ).wait()

    @pl.when(step == count - 2)
    def _():
        for k in range(cot_parts):
            start(cot_moves(k))

    xt0 = tok_b[step, 0].astype(F32)
    xt1 = tok_b[step, 1].astype(F32)
    squares = jnp.sum(xt0 * xt0, axis=0, keepdims=True) + jnp.sum(xt1 * xt1, axis=0, keepdims=True)
    scale = lax.rsqrt(squares / (2 * half) + EPS)
    nt0 = (xt0 * scale * gain[0]).astype(BF16)
    nt1 = (xt1 * scale * gain[1]).astype(BF16)
    n1t_o[0:half, :] = nt0
    n1t_o[half:, :] = nt1
    x_o[:, 0:half] = tok_b[step, 0].T
    x_o[:, half:] = tok_b[step, 1].T
    low0 = nt0.T
    low1 = nt1.T

    @pl.when(step == 0)
    def _():
        wait_weight(0)
        wait_weight(1)

    rec = dot(low0, wr[0]) + dot(low1, wr[1])
    recpad[0:8, :] = halo[...]
    recpad[8:, :] = rec
    halo[...] = rec[chunk - 8 :, :]
    rec_o[...] = rec
    gate_o[...] = dot(low0, wg[0]) + dot(low1, wg[1])

    def conv_step(i, _):
        base = pl.multiple_of(i * 16, 16)
        for h in range(heads):
            sl = slice(h * 128, (h + 1) * 128)
            window = recpad[pl.ds(base, 24), sl]
            out = cb[:, sl] + cw[0:1, sl] * window[8:]
            for k in range(1, KCONV):
                out = out + cw[k : k + 1, sl] * pltpu.roll(window, k, 0)[8:]
            cl_o[pl.ds(base, 16), sl] = out.astype(BF16)
        return 0

    lax.fori_loop(0, chunk // 16, conv_step, 0)
    for h in range(heads):
        pre[:, h * 256 : (h + 1) * 256] = dot(cl_o[:, h * 128 : (h + 1) * 128], gw[h])
    row = lax.broadcasted_iota(jnp.int32, (8, 128), 0)

    def main_step(i, _):
        base = pl.multiple_of(i * 16, 16)
        rows = pl.ds(base, 16)
        for h in range(heads):
            sl = slice(h * 128, (h + 1) * 128)
            r = jax.nn.sigmoid(pre[rows, h * 256 : h * 256 + 128] + rb[:, sl])
            g = jax.nn.sigmoid(pre[rows, h * 256 + 128 : (h + 1) * 256] + ib[:, sl])
            conv = cl_o[rows, sl].astype(F32)
            decay, em = decay_terms(r, sp[:, sl])
            drive = jnp.sqrt(em) * g * conv
            r_o[rows, sl] = r
            i_o[rows, sl] = g
            held = carry[0:1, sl]
            parts = []
            for p in range(2):
                a, b = scan_tile(decay[p * 8 : p * 8 + 8], drive[p * 8 : p * 8 + 8], row)
                state = a * held + b
                held = state[7:8]
                parts.append(state)
            carry[0:1, sl] = held
            state = jnp.concatenate(parts, axis=0)
            st_o[rows, sl] = state
            br_o[rows, sl] = (state * gelu_act(gate_o[rows, sl])).astype(BF16)
        return 0

    lax.fori_loop(0, chunk // 16, main_step, 0)

    @pl.when(step == 0)
    def _():
        wait_weight(2)

    def put_moves():
        return [
            pltpu.make_async_copy(held.at[1], out, put.at[n])
            for n, (held, out) in enumerate(((wr, wr_o), (wg, wg_o), (ow, ow_o)))
        ]

    @pl.when(step == 0)
    def _():
        for move in put_moves():
            move.start()

    branch = br_o[...]
    mix_o[:, :half] = dot_nt(branch, ow[0]).astype(BF16)
    mix_o[:, half:] = dot_nt(branch, ow[1]).astype(BF16)

    for k in range(cot_parts):

        @pl.when(step == k)
        def _():
            mix_s[k] = mix_o[...]
            mix_move(k).start()

    @pl.when(step == count - 1)
    def _():
        for k in range(cot_parts):
            for s in range(2):
                pltpu.make_async_copy(
                    cotangent.at[:, pl.ds(0, chunk)],
                    cot_o.at[s, :, pl.ds(k * chunk, chunk)],
                    cot_recv.at[k, s],
                ).wait()
            finish_send(cot_moves(k))
            mix_move(k).wait()
        for k in range(count):
            finish_send(token_moves(k))
        for n in range(4):
            weight_moves(n)[1].wait_send()
        for move in put_moves():
            move.wait()


def rec_forward(tokens, cotangent, wr, wg, ow, gain, rw, iw, cw, cb, rb, ib, sp, chunk=256):
    half, length = tokens.shape
    width = wr.shape[1]
    heads = width // 128
    count = length // chunk
    cot_parts = count // 2
    wide = 2 * half
    row_block = lambda cols: pl.BlockSpec((chunk, cols), lambda i: (i, 0))
    whole = lambda shape: pl.BlockSpec(
        shape, lambda i: (0,) * len(shape), pipeline_mode=pl.Buffered(1)
    )
    hbm = pl.BlockSpec(memory_space=pl.ANY)
    f32 = jax.ShapeDtypeStruct((length, width), F32)
    low = jax.ShapeDtypeStruct((length, width), BF16)
    dma = pltpu.SemaphoreType.DMA
    return pl.pallas_call(
        functools.partial(rec_forward_kernel, chunk, count, cot_parts),
        grid=(count,),
        in_specs=[hbm] * 6
        + [whole((heads, 128, 128))] * 2
        + [whole((KCONV, width))]
        + [whole((1, width))] * 4,
        out_specs=[row_block(wide), pl.BlockSpec((wide, chunk), lambda i: (0, i))]
        + [row_block(width)] * 7
        + [row_block(wide)]
        + [hbm] * 5,
        out_shape=[
            jax.ShapeDtypeStruct((length, wide), BF16),
            jax.ShapeDtypeStruct((wide, length), BF16),
            f32, f32, low, f32, f32, f32, low,
            jax.ShapeDtypeStruct((length, wide), BF16),
            jax.ShapeDtypeStruct((2, half, cot_parts * chunk), BF16),
            jax.ShapeDtypeStruct((cot_parts * chunk, wide), BF16),
        ]
        + [jax.ShapeDtypeStruct((half, width), BF16)] * 3,
        scratch_shapes=[
            pltpu.VMEM((count, 2, half, chunk), BF16),
            pltpu.VMEM((cot_parts, chunk, wide), BF16),
            pltpu.VMEM((2, half, width), BF16),
            pltpu.VMEM((2, half, width), BF16),
            pltpu.VMEM((2, half, width), BF16),
            pltpu.VMEM((2, half, 1), F32),
            pltpu.VMEM((heads, 128, 256), BF16),
            pltpu.VMEM((8, width), F32),
            pltpu.VMEM((8, width), F32),
            pltpu.VMEM((chunk + 8, width), F32),
            pltpu.VMEM((chunk, 2 * width), F32),
            dma((count, 2)),
            dma((count, 2)),
            dma((4,)),
            dma((4,)),
            dma((4,)),
            dma((count, 2)),
            dma((count, 2)),
            dma((cot_parts,)),
            dma((cot_parts,)),
            dma((3,)),
        ],
        compiler_params=pltpu.CompilerParams(
            vmem_limit_bytes=60 * MIB, collective_id=2, has_side_effects=True
        ),
        name="recurrent_forward",
    )(tokens, cotangent, wr, wg, ow, gain, rw, iw, cw, cb, rb, ib, sp)


def exchange(srcs, dsts, send, recv, at, core, chip):
    def moves(m):
        src, dst = srcs[m], dsts[m]
        if len(dst.shape) == 2:
            return (
                pltpu.make_async_remote_copy(src, dst, send.at[m, 0], recv.at[m, 0], device_id={"cols": 1 - chip}),
            )
        slot = lax.select(core == chip, 0, 1)
        there = dst.at[slot]
        return (
            pltpu.make_async_copy(src, there, recv.at[m, slot]),
            pltpu.make_async_remote_copy(
                src, there, send.at[m, 0], recv.at[m, slot], device_id={"rows": 1 - core}
            ),
            pltpu.make_async_remote_copy(
                src, there, send.at[m, 1], recv.at[m, slot], device_id={"rows": chip, "cols": 1 - chip}
            ),
        )

    @pl.when(at == 0)
    def _():
        group_barrier(core, chip)
        for m in range(len(srcs)):
            move = moves(m)
            move[-1].start()
            if len(move) > 1:

                @pl.when(core == chip)
                def _():
                    move[0].start()

                @pl.when(core != chip)
                def _():
                    move[1].start()

    def finish():
        for m in range(len(srcs)):
            move = moves(m)
            if len(move) == 1:
                move[0].wait()
                continue
            for s in range(2):
                pltpu.make_async_copy(srcs[m], dsts[m].at[s], recv.at[m, s]).wait()
            move[2].wait_send()

            @pl.when(core != chip)
            def _():
                move[1].wait_send()

    return finish


def ffn_kernel(
    tile, moved,
    x, mix, mix_far, ct, live, gain, keep, wg0, wg1, wu0, wu1, wd0, wd1, *refs
):
    srcs, refs = refs[:moved], refs[moved:]
    (res_o, n2t_o, cott_o, cot_o, out_o, gn2_o, hid_o, ga_o, gb_o), refs = refs[:9], refs[9:]
    dsts, (n2_s, out_acc, gn2_acc, send, recv) = refs[:moved], refs[moved:]
    later = pl.ds(x.shape[0], x.shape[0])
    if moved == 2:
        views = [srcs[0].at[later, :], srcs[1].at[:, later]]
    else:
        views = [srcs[0].at[...]]
    finish = exchange(
        views, dsts, send, recv, pl.program_id(0), lax.axis_index("rows"), lax.axis_index("cols")
    )
    step = pl.program_id(0)
    tokens, wide = x.shape
    half = wide // 2

    @pl.when(step == 0)
    def _():
        out_acc[...] = jnp.zeros_like(out_acc)
        gn2_acc[...] = jnp.zeros_like(gn2_acc)
        cott_o[:half] = ct[0] * live[...]
        cott_o[half:] = ct[1] * live[...]
        cot_o[...] = cott_o[...].T

        def norm_step(i, _):
            rows = pl.ds(pl.multiple_of(i * 16, 16), 16)
            res = x[rows, :].astype(F32) + (mix[rows, :].astype(F32) + mix_far[rows, :].astype(F32))
            res_o[rows, :] = res
            scale = lax.rsqrt(jnp.sum(res * res, axis=1, keepdims=True) / wide + EPS)
            n2_s[rows, :] = (res * scale * gain[...]).astype(BF16)
            return 0

        lax.fori_loop(0, tokens // 16, norm_step, 0)
        n2t_o[...] = n2_s[...].T

    def tile_step(i, _):
        rows = pl.ds(i * tile, tile)
        n0, n1 = n2_s[rows, :half], n2_s[rows, half:]
        c0, c1 = cot_o[rows, :half], cot_o[rows, half:]
        a = dot(n0, wg0[...]) + dot(n1, wg1[...])
        b = dot(n0, wu0[...]) + dot(n1, wu1[...])
        gh = dot(c0, wd0[...]) + dot(c1, wd1[...])
        act, slope = gelu_pair(a)
        hidden = (act * b).astype(BF16)
        ga = (gh * b * slope).astype(BF16)
        gb = (gh * act).astype(BF16)
        hid_o[rows, :] = hidden
        ga_o[rows, :] = ga
        gb_o[rows, :] = gb
        out_acc[rows, :half] += dot_nt(hidden, wd0[...])
        out_acc[rows, half:] += dot_nt(hidden, wd1[...])
        gn2_acc[rows, :half] += dot_nt(ga, wg0[...]) + dot_nt(gb, wu0[...])
        gn2_acc[rows, half:] += dot_nt(ga, wg1[...]) + dot_nt(gb, wu1[...])
        return 0

    for i in range(tokens // tile):
        tile_step(i, 0)

    @pl.when(step == pl.num_programs(0) - 1)
    def _():
        out_o[...] = (out_acc[...] + keep[...] * res_o[...]).astype(BF16)
        gn2_o[...] = gn2_acc[...].astype(BF16)
        finish()


def ffn(part, tokens, x, mix, mix_far, cott, live, gain, keep, wg, wu, wd, srcs, dsts, collective_id, block=256, tile=256):
    wide = x.shape[1]
    half, width = wg[0].shape
    whole = lambda shape, at=(0, 0): pl.BlockSpec(
        shape, lambda i: at, pipeline_mode=pl.Buffered(1)
    )
    hbm = pl.BlockSpec(memory_space=pl.ANY)
    rows = whole((tokens, wide), (part, 0))
    act = whole((tokens, wide))
    across = whole((wide, tokens))
    weight = pl.BlockSpec((half, block), lambda i: (0, i))
    mid = pl.BlockSpec((tokens, block), lambda i: (0, i))
    low = jax.ShapeDtypeStruct((tokens, wide), BF16)
    turned = jax.ShapeDtypeStruct((wide, tokens), BF16)
    hidden = jax.ShapeDtypeStruct((tokens, width), BF16)
    sems = pltpu.SemaphoreType.DMA((len(srcs), 2))
    return pl.pallas_call(
        functools.partial(ffn_kernel, tile, len(srcs)),
        grid=(width // block,),
        in_specs=[rows, rows, act, whole((2, half, tokens), (0, 0, 0)), whole((1, tokens), (0, part))]
        + [whole((1, wide)), whole((1, 1))]
        + [weight] * 6
        + [hbm] * len(srcs),
        out_specs=[act, across, across, act, act, act, mid, mid, mid] + [hbm] * len(srcs),
        out_shape=[
            jax.ShapeDtypeStruct((tokens, wide), F32),
            turned, turned, low, low, low, hidden, hidden, hidden,
        ]
        + [jax.ShapeDtypeStruct(shape, BF16) for shape in dsts],
        scratch_shapes=[
            pltpu.VMEM((tokens, wide), BF16),
            pltpu.VMEM((tokens, wide), F32),
            pltpu.VMEM((tokens, wide), F32),
            sems,
            sems,
        ],
        compiler_params=pltpu.CompilerParams(
            vmem_limit_bytes=60 * MIB, collective_id=collective_id, has_side_effects=True
        ),
        name=f"ffn_{part}",
    )(x, mix, mix_far, cott, live, gain, keep, wg[0], wg[1], wu[0], wu[1], wd[0], wd[1], *srcs)


def norm_back(gn, gn_far, res, cot, gain, g1_o, g1t_o, gain_o):
    rows_all, wide = g1_o.shape

    def step(i, _):
        rows = pl.ds(pl.multiple_of(i * 16, 16), 16)
        grad = gn[rows, :].astype(F32) + gn_far[rows, :].astype(F32)
        held = res[rows, :]
        scale = lax.rsqrt(jnp.sum(held * held, axis=1, keepdims=True) / wide + EPS)
        product = grad * held
        by_gain = product * scale
        gain_o[...] += by_gain[0:8] + by_gain[8:16]
        inner = jnp.sum(product * gain[...], axis=1, keepdims=True)
        grad_one = (
            cot[rows, :].astype(F32)
            + scale * (grad * gain[...])
            - held * (scale * scale * scale * inner / wide)
        )
        g1_o[rows, :] = grad_one.astype(BF16)
        return 0

    lax.fori_loop(0, rows_all // 16, step, 0)
    g1t_o[...] = g1_o[...].T


def ffn_back_kernel(
    n2t_a, n2t_b, cott_a, cott_b, hid_a, hid_b, ga_a, ga_b, gb_a, gb_b,
    gn_a, gn_far_a, gn_b, res_a, res_b, cot_a, cot_b, gain,
    gu_sum, gg0, gg1, gd0, gd1, g1_a, g1t_a, g1_b, g1t_b, gain_o,
    gn_far_b, keep_s, give_s, got_s, send, recv, up_send, up_recv,
):
    step = pl.program_id(0)
    last = pl.num_programs(0) - 1
    core, chip = lax.axis_index("rows"), lax.axis_index("cols")
    finish = exchange([gn_b.at[...]], [gn_far_b], send, recv, step, core, chip)
    half, block = gg0.shape

    def give(k):
        return pltpu.make_async_remote_copy(
            give_s.at[k], got_s.at[k], up_send.at[k], up_recv.at[k], device_id={"rows": 1 - core}
        )

    def join(k):
        give(k).wait()
        total = keep_s[k].astype(F32) + got_s[k].astype(F32)
        gu_sum[:, pl.ds(pl.multiple_of(k * block, block), block)] = total.astype(BF16)

    @pl.when(step == 0)
    def _():
        gain_o[...] = jnp.zeros_like(gain_o)
        norm_back(gn_a, gn_far_a, res_a, cot_a, gain, g1_a, g1t_a, gain_o)

    def product(left_a, left_b, right_a, right_b, top):
        sl = slice(0, half) if top else slice(half, 2 * half)
        return (dot(left_a[sl], right_a[...]) + dot(left_b[sl], right_b[...])).astype(BF16)

    give_s[step] = product(n2t_a, n2t_b, gb_a, gb_b, False)
    give(step).start()
    keep_s[step] = product(n2t_a, n2t_b, gb_a, gb_b, True)
    gg0[...] = product(n2t_a, n2t_b, ga_a, ga_b, True)
    gg1[...] = product(n2t_a, n2t_b, ga_a, ga_b, False)
    gd0[...] = product(cott_a, cott_b, hid_a, hid_b, True)
    gd1[...] = product(cott_a, cott_b, hid_a, hid_b, False)

    @pl.when(step > 0)
    def _():
        join(step - 1)

    @pl.when(step == last)
    def _():
        finish()
        norm_back(gn_b, gn_far_b, res_b, cot_b, gain, g1_b, g1t_b, gain_o)
        join(step)


def ffn_back(n2t, cott, hid, ga, gb, gn, gn_far_a, res, cot, gain, collective_id, block=256):
    wide, tokens = n2t[0].shape
    half, width = wide // 2, hid[0].shape[1]
    count = width // block
    whole = lambda shape: pl.BlockSpec(shape, lambda i: (0, 0), pipeline_mode=pl.Buffered(1))
    mid = pl.BlockSpec((tokens, block), lambda i: (0, i))
    grad = jax.ShapeDtypeStruct((half, width), BF16)
    act, across = whole((tokens, wide)), whole((wide, tokens))
    weight = pl.BlockSpec((half, block), lambda i: (0, i))
    sems = pltpu.SemaphoreType.DMA((1, 2))
    up_sems = pltpu.SemaphoreType.DMA((count,))
    low = jax.ShapeDtypeStruct((tokens, wide), BF16)
    turned = jax.ShapeDtypeStruct((wide, tokens), BF16)
    blocks = pltpu.VMEM((count, half, block), BF16)
    return pl.pallas_call(
        ffn_back_kernel,
        grid=(count,),
        in_specs=[across] * 4 + [mid] * 6 + [act] * 7 + [whole((1, wide))],
        out_specs=[whole((half, width))]
        + [weight] * 4
        + [act, across, act, across, whole((8, wide))],
        out_shape=[grad] * 5 + [low, turned, low, turned, jax.ShapeDtypeStruct((8, wide), F32)],
        scratch_shapes=[
            pltpu.VMEM((tokens, wide), BF16), blocks, blocks, blocks, sems, sems, up_sems, up_sems,
        ],
        compiler_params=pltpu.CompilerParams(
            vmem_limit_bytes=60 * MIB, collective_id=collective_id, has_side_effects=True
        ),
        name="ffn_back",
    )(*n2t, *cott, *hid, *ga, *gb, gn[0], gn_far_a, gn[1], *res, *cot, gain)


def ring_place(n, at):
    def index_of(place):
        return lax.select(place < n // 2, 2 * place, 2 * (n - 1 - place) + 1)

    me = lax.select(at % 2 == 0, at // 2, n - 1 - at // 2)
    return me, (index_of(lax.rem(me + 1, n)), index_of(lax.rem(me + n - 1, n)))


def ring_rows(n, me, total, way, s):
    size = total // n
    chunk = lax.rem(me + n - s, n) if way == 0 else lax.rem(me + s, n)
    return pl.ds(pl.multiple_of(chunk * size, size), size)


def ring_beside(n, own, out, own_b, ring_b, own_sem, rs_send, rs_recv, ag_send, ag_recv, put_sem):
    me, nexts = ring_place(n, lax.axis_index("dp"))
    wide = own.shape[1] // 2
    cut = (wide // 128 + 1) // 2 * 128
    groups = (pl.ds(0, cut), pl.ds(cut, wide - cut))
    both = [(g, way) for g in range(2) for way in range(2)]
    per = -(-n // 8)
    per_gather = -(-(n - 2) // 6)
    rows_of = lambda way, s: ring_rows(n, me, own.shape[0], way, s)
    cols_of = lambda g, way: pl.ds(way * wide + g * cut, wide - cut if g else cut)

    def own_copy(way, s):
        return pltpu.make_async_copy(
            own.at[rows_of(way, s), pl.ds(way * wide, wide)], own_b.at[way, s], own_sem.at[way, s]
        )

    def sum_copy(g, way, s):
        return pltpu.make_async_remote_copy(
            ring_b.at[way, s, :, groups[g]], ring_b.at[way, s + 1, :, groups[g]],
            rs_send.at[g, way], rs_recv.at[g, way, s], device_id={"dp": nexts[way]},
        )

    def first_gather(g, way):
        return pltpu.make_async_remote_copy(
            ring_b.at[way, n - 1, :, groups[g]], out.at[rows_of(way, n - 1), cols_of(g, way)],
            ag_send.at[g, way, 0], ag_recv.at[g, way, 0], device_id={"dp": nexts[way]},
        )

    def gather_copy(g, way, s):
        there = out.at[rows_of(way, s - 1), cols_of(g, way)]
        return pltpu.make_async_remote_copy(
            there, there, ag_send.at[g, way, s], ag_recv.at[g, way, s], device_id={"dp": nexts[way]}
        )

    def put_copy(g, way):
        return pltpu.make_async_copy(
            ring_b.at[way, n - 1, :, groups[g]],
            out.at[rows_of(way, n - 1), cols_of(g, way)],
            put_sem.at[g, way],
        )

    def begin():
        barrier = pltpu.get_barrier_semaphore()
        for neighbour in nexts:
            pl.semaphore_signal(barrier, inc=1, device_id={"dp": neighbour})

        def load(s, _):
            for way in range(2):
                own_copy(way, s).start()
            return 0

        lax.fori_loop(0, n, load, 0)
        pl.semaphore_wait(barrier, 2)

    def tick(g, t):
        def sum_step(s, _):
            for way in range(2):
                if g == 0:
                    own_copy(way, s).wait()

                @pl.when(s == 0)
                def _():
                    ring_b[way, s, :, groups[g]] = own_b[way, s, :, groups[g]]

                @pl.when(s > 0)
                def _():
                    sum_copy(g, way, s - 1).wait_recv()
                    total = ring_b[way, s, :, groups[g]].astype(F32) + own_b[
                        way, s, :, groups[g]
                    ].astype(F32)
                    ring_b[way, s, :, groups[g]] = total.astype(BF16)

                @pl.when(s < n - 1)
                def _():
                    sum_copy(g, way, s).start()

                @pl.when(s == n - 1)
                def _():
                    first_gather(g, way).start()
                    put_copy(g, way).start()
            return 0

        def gather_step(s, _):
            for way in range(2):

                @pl.when(s == 1)
                def _():
                    first_gather(g, way).wait_recv()

                @pl.when(s > 1)
                def _():
                    gather_copy(g, way, s - 1).wait_recv()

                gather_copy(g, way, s).start()
            return 0

        @pl.when(t < 8)
        def _():
            lax.fori_loop(t * per, jnp.minimum((t + 1) * per, n), sum_step, 0)

        @pl.when(t >= 8)
        def _():
            start = 1 + (t - 8) * per_gather
            lax.fori_loop(start, jnp.minimum(start + per_gather, n - 1), gather_step, 0)

    def end():
        for g, way in both:
            gather_copy(g, way, n - 2).wait_recv()
            put_copy(g, way).wait()
            first_gather(g, way).wait_send()
            pltpu.make_async_remote_copy(
                ring_b.at[way, pl.ds(0, n - 1), :, groups[g]],
                ring_b.at[way, pl.ds(1, n - 1), :, groups[g]],
                rs_send.at[g, way], rs_recv.at[g, way, 0], device_id={"dp": nexts[way]},
            ).wait_send()

        def drain(s, _):
            for g, way in both:
                gather_copy(g, way, s).wait_send()
            return 0

        lax.fori_loop(1, n - 1, drain, 0)

    return begin, tick, end


def rec_backward_kernel(
    tile, n,
    g1a, g1b, g1ta, g1tb, n1t, st, gate, r_in, i_in, cl, rec, br, ow0, ow1, wr0, wr1, wg0, wg1, rw, iw, cw, sp,
    x, gain, gain_two, up,
    gn1_o, go0, go1, gr0, gr1, gg0, gg1, ggw, sums, stat, gains0, gains1, up_o,
    acc, gb_s, gc_s, ggp_s, grp_s, gip_s, grec_s, gain_s, *ring_refs
):
    step = pl.program_id(0)
    tokens, block = gb_s.shape
    wide = n1t.shape[0]
    heads = block // 128
    half = ow0.shape[0]
    tiles = tokens // tile
    subs = tile // 8

    begin, tick, end = ring_beside(n, up, up_o, *ring_refs)

    @pl.when(step == 0)
    def _():
        begin()
        acc[...] = jnp.zeros_like(acc)

    beat = lambda at: tick(at % 2, step * 3 + at // 2)
    beat(0)
    mid = tokens // 2
    gb_s[:mid] = dot(g1a[:, :half], ow0[...]) + dot(g1a[:, half:], ow1[...])
    gb_s[mid:] = dot(g1b[:, :half], ow0[...]) + dot(g1b[:, half:], ow1[...])
    beat(1)
    go0[...] = (dot(g1ta[:half], br[:mid]) + dot(g1tb[:half], br[mid:])).astype(BF16)
    go1[...] = (dot(g1ta[half:], br[:mid]) + dot(g1tb[half:], br[mid:])).astype(BF16)
    beat(2)
    sums[...] = jnp.zeros_like(sums)
    row = lax.broadcasted_iota(jnp.int32, (8, 128), 0)

    def back_step(j, held):
        @pl.when(j == tiles // 2)
        def _():
            beat(3)

        i = tiles - 1 - j
        base = pl.multiple_of(i * tile, tile)
        rows = pl.ds(base, tile)
        before = pl.ds(pl.multiple_of(jnp.maximum(base - 8, 0), 8), 8)
        out = []
        for h in range(heads):
            sl = slice(h * 128, (h + 1) * 128)
            later_decay, later_carried = held[h]
            grad_branch = gb_s[rows, sl]
            act, slope = gelu_pair(gate[rows, sl])
            state = st[rows, sl]
            ggp_s[rows, sl] = (grad_branch * state * slope).astype(BF16)
            grad_state = grad_branch * act
            r = r_in[rows, sl]
            soft = sp[:, sl]
            decay, em = decay_terms(r, soft)
            parts = [None] * subs
            for p in range(subs - 1, -1, -1):
                own = decay[p * 8 : p * 8 + 8]
                after = jnp.where(row == 7, later_decay, pltpu.roll(own, 7, 0))
                a, b = scan_tile_back(after, grad_state[p * 8 : p * 8 + 8], row)
                carried = a * later_carried + b
                later_decay = own[0:1]
                later_carried = carried[0:1]
                parts[p] = carried
            out.append((later_decay, later_carried))
            carried = jnp.concatenate(parts, axis=0)
            edge = jnp.where(i > 0, st[before, sl][7:8], 0.0)
            prev = []
            for p in range(subs):
                prev.append(jnp.where(row == 0, edge, pltpu.roll(state[p * 8 : p * 8 + 8], 1, 0)))
                edge = state[p * 8 + 7 : p * 8 + 8]
            prev = jnp.concatenate(prev, axis=0)
            g = i_in[rows, sl]
            conv = cl[rows, sl].astype(F32)
            scaling = jnp.sqrt(em)
            gated = g * conv
            grad_log = carried * (prev * decay - gated * (decay * decay) / scaling)
            grad_soft = grad_log * (-GATE_SCALE * r)
            grp = grad_soft * soft * (1.0 - r)
            cs = carried * scaling
            gc_s[rows, sl] = cs * g
            gip = cs * gated * (1.0 - g)
            grp_s[rows, sl] = grp.astype(BF16)
            gip_s[rows, sl] = gip.astype(BF16)
            for n, term in enumerate((grp, gip, grad_soft)):
                total = term[0:8]
                for p in range(1, subs):
                    total = total + term[p * 8 : p * 8 + 8]
                sums[n * 8 : n * 8 + 8, sl] += total
        return tuple(out)

    zero = jnp.zeros((1, 128), F32)
    lax.fori_loop(0, tiles, back_step, tuple((zero, zero) for _ in range(heads)))
    beat(4)
    for h in range(heads):
        sl = slice(h * 128, (h + 1) * 128)
        low = cl[:, sl]
        ggw[h, :, 0:128] = dot_tn(low, grp_s[:, sl]).astype(BF16)
        ggw[h, :, 128:256] = dot_tn(low, gip_s[:, sl]).astype(BF16)
        gc_s[:, sl] += dot_nt(grp_s[:, sl], rw[h]) + dot_nt(gip_s[:, sl], iw[h])

    def conv_step(j, held):
        i = tiles - 1 - j
        base = pl.multiple_of(i * tile, tile)
        rows = pl.ds(base, tile)
        before = pl.ds(pl.multiple_of(jnp.maximum(base - 8, 0), 8), 8)
        out = []
        for h in range(heads):
            sl = slice(h * 128, (h + 1) * 128)
            grad_conv = gc_s[rows, sl]
            window = jnp.concatenate([grad_conv, held[h]], axis=0)
            out.append(grad_conv[0:8])
            grad_rec = cw[0:1, sl] * grad_conv
            for k in range(1, KCONV):
                grad_rec = grad_rec + cw[k : k + 1, sl] * pltpu.roll(window, tile + 8 - k, 0)[:tile]
            grec_s[rows, sl] = grad_rec.astype(BF16)
            edge = jnp.where(i > 0, rec[before, sl], 0.0)
            past = jnp.concatenate([edge, rec[rows, sl]], axis=0)
            terms = [grad_conv * past[8:]]
            for k in range(1, KCONV):
                terms.append(grad_conv * pltpu.roll(past, k, 0)[8:])
            terms.append(grad_conv)
            for n, term in enumerate(terms):
                total = term[0:8]
                for p in range(1, subs):
                    total = total + term[p * 8 : p * 8 + 8]
                sums[24 + n * 8 : 32 + n * 8, sl] += total
        return tuple(out)

    lax.fori_loop(0, tiles, conv_step, tuple(jnp.zeros((8, 128), F32) for _ in range(heads)))
    beat(5)
    grad_rec = grec_s[...]
    grad_gate = ggp_s[...]
    gr0[...] = dot(n1t[:half], grad_rec).astype(BF16)
    gr1[...] = dot(n1t[half:], grad_rec).astype(BF16)
    gg0[...] = dot(n1t[:half], grad_gate).astype(BF16)
    gg1[...] = dot(n1t[half:], grad_gate).astype(BF16)
    acc[:, :half] += dot_nt(grad_rec, wr0[...]) + dot_nt(grad_gate, wg0[...])
    acc[:, half:] += dot_nt(grad_rec, wr1[...]) + dot_nt(grad_gate, wg1[...])

    @pl.when(step == pl.num_programs(0) - 1)
    def _():
        gain_s[...] = jnp.zeros_like(gain_s)
        for g in range(2):
            tick(g, 12)

        def stat_step(i, _):
            @pl.when(i == tokens // 32)
            def _():
                for g in range(2):
                    tick(g, 13)

            rows = pl.ds(pl.multiple_of(i * 16, 16), 16)
            part = acc[rows, :]
            gn1_o[rows, :] = part.astype(BF16)
            held = x[rows, :].astype(F32)
            scale = lax.rsqrt(jnp.sum(held * held, axis=1, keepdims=True) / wide + EPS)
            product = part * held
            by_gain = product * scale
            gain_s[...] += by_gain[0:8] + by_gain[8:16]
            inner = jnp.sum(product * gain[...], axis=1, keepdims=True)
            stat[rows, 0:64] = jnp.broadcast_to(inner, (16, 64))
            stat[rows, 64:128] = jnp.broadcast_to(scale, (16, 64))
            return 0

        lax.fori_loop(0, tokens // 16, stat_step, 0)
        both = gain_two[...]
        for out, sl in ((gains0, slice(0, half)), (gains1, slice(half, wide))):
            out[...] = jnp.zeros_like(out)
            out[0:8, :] = gain_s[:, sl]
            out[8:16, :] = both[:, sl]
        end()


def rec_backward(
    g1, g1t, n1t, st, gate, r, g, cl, rec, br, ow, wr, wg, rw, iw, cw, sp, x, gain, gain_two, up, n, block=256, tile=64
):
    wide, tokens = n1t.shape
    half, width = wr[0].shape
    heads = block // 128
    mid = tokens // 2
    rows = up.shape[0]
    up = jnp.pad(up, ((0, -rows % (16 * n)), (0, 0)))
    slots = pltpu.VMEM((2, n, up.shape[0] // n, up.shape[1] // 2), BF16)
    dma = pltpu.SemaphoreType.DMA
    hbm = pl.BlockSpec(memory_space=pl.ANY)
    whole = lambda shape: pl.BlockSpec(shape, lambda i: (0, 0), pipeline_mode=pl.Buffered(1))
    act = pl.BlockSpec((tokens, block), lambda i: (0, i))
    weight = pl.BlockSpec((half, block), lambda i: (0, i))
    thin = lambda n: pl.BlockSpec((n, block), lambda i: (0, i))
    gate_block = pl.BlockSpec((heads, 128, 256), lambda i: (i, 0, 0))
    grad = jax.ShapeDtypeStruct((half, width), BF16)
    outs = pl.pallas_call(
        functools.partial(rec_backward_kernel, tile, n),
        grid=(width // block,),
        in_specs=[whole((mid, wide))] * 2 + [whole((wide, mid))] * 2 + [whole((wide, tokens))]
        + [act] * 7
        + [weight] * 6
        + [pl.BlockSpec((heads, 128, 128), lambda i: (i, 0, 0))] * 2
        + [thin(KCONV), thin(1)]
        + [whole((tokens, wide)), whole((1, wide)), whole((8, wide)), hbm],
        out_specs=[whole((tokens, wide))]
        + [weight] * 6
        + [gate_block, thin(64), whole((tokens, 128)), whole((64, half)), whole((64, half)), hbm],
        out_shape=[jax.ShapeDtypeStruct((tokens, wide), BF16)]
        + [grad] * 6
        + [
            jax.ShapeDtypeStruct((width // 128, 128, 256), BF16),
            jax.ShapeDtypeStruct((64, width), F32),
            jax.ShapeDtypeStruct((tokens, 128), F32),
            jax.ShapeDtypeStruct((64, half), F32),
            jax.ShapeDtypeStruct((64, half), F32),
            jax.ShapeDtypeStruct(up.shape, BF16),
        ],
        scratch_shapes=[
            pltpu.VMEM((tokens, wide), F32),
            pltpu.VMEM((tokens, block), F32),
            pltpu.VMEM((tokens, block), F32),
            pltpu.VMEM((tokens, block), BF16),
            pltpu.VMEM((tokens, block), BF16),
            pltpu.VMEM((tokens, block), BF16),
            pltpu.VMEM((tokens, block), BF16),
            pltpu.VMEM((8, wide), F32),
            slots, slots,
            dma((2, n)), dma((2, 2)), dma((2, 2, n)), dma((2, 2, n)), dma((2, 2, n)), dma((2, 2)),
        ],
        compiler_params=pltpu.CompilerParams(
            vmem_limit_bytes=62 * MIB, collective_id=6, has_side_effects=True
        ),
        name="recurrent_backward",
    )(
        g1[0], g1[1], g1t[0], g1t[1], n1t, st, gate, r, g, cl, rec, br,
        ow[0], ow[1], wr[0], wr[1], wg[0], wg[1], rw, iw, cw, sp, x, gain, gain_two, up,
    )
    return (*outs[:-1], outs[-1][:rows])


def ring_kernel(n, count, *refs):
    own, other, refs = refs[:count], refs[count : 2 * count], refs[2 * count :]
    (gn1, out_a, out_b, stat, g1_a, g1_b), refs = refs[:6], refs[6:]
    outs, refs = refs[:count], refs[count:]
    (gn1_p, out_p, stat_p, g1_p), scratch = refs[:4], refs[4:]
    piece_send, piece_recv = scratch[-2:]
    scratch = scratch[:-2]
    own_b, part_b, ring_b = scratch[:count], scratch[count : 2 * count], scratch[2 * count : 3 * count]
    own_sem, part_send, part_recv, rs_send, rs_recv, ag_send, ag_recv, put_sem = scratch[3 * count :]
    at = lax.axis_index("dp")
    core = lax.axis_index("rows")
    chip = lax.axis_index("cols")

    me, nexts = ring_place(n, at)
    barrier = pltpu.get_barrier_semaphore()
    for neighbour in nexts:
        pl.semaphore_signal(barrier, inc=1, device_id={"dp": neighbour})
    for peer in ((1 - core, chip), (core, 1 - chip), (1 - core, 1 - chip)):
        pl.semaphore_signal(barrier, inc=1, device_id={"rows": peer[0], "cols": peer[1]})
    pl.semaphore_wait(barrier, 5)

    half = gn1_p.shape[2]
    part = out_a.shape[0]
    first, second = slice(0, half), slice(half, 2 * half)
    everything = slice(None)
    pieces = [
        (gn1, gn1_p, slice(None), first, second),
        (out_a, out_p, slice(0, part), first, second),
        (out_b, out_p, slice(part, 2 * part), first, second),
        (stat, stat_p, slice(None), everything, everything),
    ]
    singles = [(g1_a, slice(0, part)), (g1_b, slice(part, 2 * part))]
    diag = core == chip

    def piece_moves(m):
        src, dst, rows, mine, theirs = pieces[m]
        there = dst.at[chip, rows, :]
        sems = lambda w: (piece_send.at[m, w], piece_recv.at[m, chip])
        near = src.at[:, mine]
        away = src.at[:, theirs]
        return (
            pltpu.make_async_copy(near, there, piece_recv.at[m, chip]),
            pltpu.make_async_remote_copy(near, there, *sems(0), device_id={"cols": 1 - chip}),
            pltpu.make_async_remote_copy(away, there, *sems(1), device_id={"rows": 1 - core}),
            pltpu.make_async_remote_copy(
                away, there, *sems(1), device_id={"rows": 1 - core, "cols": 1 - chip}
            ),
        )

    def single_moves(m):
        src, rows = singles[m]
        there = g1_p.at[rows, :]
        at = len(pieces) + m
        return (
            pltpu.make_async_copy(src.at[:, first], there, piece_recv.at[at, 0]),
            pltpu.make_async_remote_copy(
                src.at[:, second], there, piece_send.at[at, 1], piece_recv.at[at, 0],
                device_id={"rows": 1 - core},
            ),
        )

    @pl.when(diag)
    def _():
        for m in range(len(pieces)):
            moves = piece_moves(m)
            moves[0].start()
            moves[2].start()
        for m in range(len(singles)):
            moves = single_moves(m)
            moves[0].start()
            moves[1].start()

    @pl.when(jnp.logical_not(diag))
    def _():
        for m in range(len(pieces)):
            moves = piece_moves(m)
            moves[1].start()
            moves[3].start()

    def rows_of(k, way, s):
        return ring_rows(n, me, own[k].shape[0], way, s)

    def cols_of(k, way):
        wide = own[k].shape[1] // 2
        return pl.ds(way * wide, wide)

    def own_copy(k, way, s):
        return pltpu.make_async_copy(
            own[k].at[rows_of(k, way, s), cols_of(k, way)], own_b[k].at[way, s], own_sem.at[k, way, s]
        )

    def part_copy(k, way, s):
        return pltpu.make_async_remote_copy(
            src_ref=other[k].at[rows_of(k, way, s), cols_of(k, way)],
            dst_ref=part_b[k].at[way, s],
            send_sem=part_send.at[k, way],
            recv_sem=part_recv.at[k, way, s],
            device_id={"rows": 1 - core},
        )

    def sum_copy(k, way, s):
        return pltpu.make_async_remote_copy(
            src_ref=ring_b[k].at[way, s],
            dst_ref=ring_b[k].at[way, s + 1],
            send_sem=rs_send.at[k, way],
            recv_sem=rs_recv.at[k, way, s],
            device_id={"dp": nexts[way]},
        )

    def first_gather(k, way):
        rows = rows_of(k, way, n - 1)
        return pltpu.make_async_remote_copy(
            src_ref=ring_b[k].at[way, n - 1],
            dst_ref=outs[k].at[rows, cols_of(k, way)],
            send_sem=ag_send.at[k, way, 0],
            recv_sem=ag_recv.at[k, way, 0],
            device_id={"dp": nexts[way]},
        )

    def gather_copy(k, way, s):
        rows = rows_of(k, way, s - 1)
        there = outs[k].at[rows, cols_of(k, way)]
        return pltpu.make_async_remote_copy(
            src_ref=there,
            dst_ref=there,
            send_sem=ag_send.at[k, way, s],
            recv_sem=ag_recv.at[k, way, s],
            device_id={"dp": nexts[way]},
        )

    def put_copy(k, way):
        return pltpu.make_async_copy(
            ring_b[k].at[way, n - 1],
            outs[k].at[rows_of(k, way, n - 1), cols_of(k, way)],
            put_sem.at[k, way],
        )

    both = [(k, way) for k in range(count) for way in range(2)]

    def load_step(s, _):
        for k, way in both:
            part_copy(k, way, s).start()
            own_copy(k, way, s).start()
        return 0

    lax.fori_loop(0, n, load_step, 0)

    def add_step(k, way, s, received):
        own_copy(k, way, s).wait()
        part_copy(k, way, s).wait_recv()
        total = own_b[k][way, s].astype(F32) + part_b[k][way, s].astype(F32)
        if received:
            sum_copy(k, way, s - 1).wait_recv()
            total = total + ring_b[k][way, s].astype(F32)
        ring_b[k][way, s] = total.astype(ring_b[k].dtype)

    for k, way in both:
        add_step(k, way, 0, False)
        sum_copy(k, way, 0).start()

    def sum_step(s, _):
        for k, way in both:
            add_step(k, way, s, True)
            sum_copy(k, way, s).start()
        return 0

    lax.fori_loop(1, n - 1, sum_step, 0)
    for k, way in both:
        add_step(k, way, n - 1, True)
        first_gather(k, way).start()
        put_copy(k, way).start()

    def gather_step(s, _):
        for k, way in both:
            gather_copy(k, way, s - 1).wait_recv()
            gather_copy(k, way, s).start()
        return 0

    for k, way in both:
        first_gather(k, way).wait_recv()
        gather_copy(k, way, 1).start()
    lax.fori_loop(2, n - 1, gather_step, 0)
    for k, way in both:
        gather_copy(k, way, n - 2).wait_recv()
        put_copy(k, way).wait()
        first_gather(k, way).wait_send()

    def drain_step(s, _):
        for k, way in both:
            gather_copy(k, way, s).wait_send()
        return 0

    lax.fori_loop(1, n - 1, drain_step, 0)
    for k, way in both:
        pltpu.make_async_remote_copy(
            ring_b[k].at[way, pl.ds(0, n - 1)],
            ring_b[k].at[way, pl.ds(1, n - 1)],
            rs_send.at[k, way],
            rs_recv.at[k, way, 0],
            device_id={"dp": nexts[way]},
        ).wait_send()
        pltpu.make_async_remote_copy(
            own_b[k].at[way],
            part_b[k].at[way],
            part_send.at[k, way],
            part_recv.at[k, way, 0],
            device_id={"rows": 1 - core},
        ).wait_send()

    for m in range(len(pieces)):
        src, dst, rows, mine, _ = pieces[m]
        for c in range(2):
            pltpu.make_async_copy(src.at[:, mine], dst.at[c, rows, :], piece_recv.at[m, c]).wait()
    for m in range(len(singles)):
        single_moves(m)[0].wait()

    @pl.when(diag)
    def _():
        for m in range(len(pieces)):
            piece_moves(m)[2].wait_send()
        for m in range(len(singles)):
            single_moves(m)[1].wait_send()

    @pl.when(jnp.logical_not(diag))
    def _():
        for m in range(len(pieces)):
            moves = piece_moves(m)
            moves[1].wait_send()
            moves[3].wait_send()


def ring_sum(n, own, other, pieces):
    count = len(own)
    own, other = list(own), list(other)
    rows = [a.shape[0] for a in own]
    unit = lambda a: (16 if a.dtype == BF16 else 8) * n
    pad = [-a.shape[0] % unit(a) for a in own]
    fit = lambda a, extra: jnp.pad(a, ((0, extra), (0, 0))) if extra else a
    own = [fit(a, e) for a, e in zip(own, pad)]
    other = [fit(a, e) for a, e in zip(other, pad)]
    slots = [pltpu.VMEM((2, n, a.shape[0] // n, a.shape[1] // 2), a.dtype) for a in own]
    sems = pltpu.SemaphoreType.DMA((count, 2, n))
    pair = pltpu.SemaphoreType.DMA((count, 2))
    tokens, wide = pieces[0].shape
    piece = jax.ShapeDtypeStruct((2, tokens, wide // 2), BF16)
    hbm = pl.BlockSpec(memory_space=pl.ANY)
    outs = pl.pallas_call(
        functools.partial(ring_kernel, n, count),
        in_specs=[hbm] * (2 * count + len(pieces)),
        out_specs=[hbm] * (count + 4),
        out_shape=[jax.ShapeDtypeStruct(a.shape, a.dtype) for a in own]
        + [
            piece,
            piece,
            jax.ShapeDtypeStruct((2, tokens, 128), F32),
            jax.ShapeDtypeStruct((tokens, wide // 2), BF16),
        ],
        scratch_shapes=slots * 3
        + [sems, pair, sems, pair] + [sems] * 3 + [pair]
        + [pltpu.SemaphoreType.DMA((6, 2))] * 2,
        compiler_params=pltpu.CompilerParams(
            collective_id=0, has_side_effects=True, vmem_limit_bytes=60 * MIB
        ),
        name="ring_sum",
    )(*own, *other, *pieces)
    return [a[:r] for a, r in zip(outs, rows)], outs[count:]


def final_kernel(gn, out, stat, g1, tokens, gain, live, result_o, grad_o):
    wide = 2 * tokens.shape[0]
    low = lambda ref: ref[0].astype(F32) + ref[1].astype(F32)
    result_o[...] = (low(out).T * live[...]).astype(BF16)
    grad = low(gn).T
    held = tokens[...].astype(F32)
    inner = (stat[0] + stat[1]).T[0:1, :]
    scale = stat[0].T[64:65, :]
    grad_o[...] = (
        g1[...].astype(F32).T
        + (scale * gain[...]) * grad
        - held * (scale * scale * scale * inner / wide)
    ).astype(BF16)


def final(gn, out, stat, g1, tokens, gain, live, chunk=256):
    half, length = tokens.shape
    pair = lambda cols: pl.BlockSpec((2, chunk, cols), lambda i: (0, i, 0))
    across = pl.BlockSpec((half, chunk), lambda i: (0, i))
    shape = jax.ShapeDtypeStruct((half, length), BF16)
    return pl.pallas_call(
        final_kernel,
        grid=(length // chunk,),
        in_specs=[
            pair(half), pair(half), pair(128),
            pl.BlockSpec((chunk, half), lambda i: (i, 0)),
            across,
            pl.BlockSpec((half, 1), lambda i: (0, 0)),
            pl.BlockSpec((1, chunk), lambda i: (0, i)),
        ],
        out_specs=[across, across],
        out_shape=[shape, shape],
        compiler_params=pltpu.CompilerParams(vmem_limit_bytes=48 * MIB),
        name="final",
    )(gn, out, stat, g1, tokens, gain, live)


def body(
    dp, tokens, lengths, mix_gain, rec_weight, gate_weight, conv_weight, conv_bias,
    recur_weight, recur_bias, input_weight, input_bias, decay_param, out_weight,
    ffn_gain, ffn_gate, ffn_up, ffn_down, cotangent,
):
    at_row = lax.axis_index("rows")
    at_col = lax.axis_index("cols")
    diag = at_row == at_col
    half = tokens.shape[0]
    wide = 2 * half

    both = lambda weight: (weight, swap(weight, "rows"))

    positions = jnp.arange(LEN, dtype=jnp.int32)
    live_core = (positions < lengths[at_row]).astype(BF16)[None, :]
    live_chip = (positions < lengths[at_col]).astype(F32)
    part = LEN // 2

    sp = jax.nn.softplus(-decay_param)[None, :]
    (x, n1t, rec, gate, cl, r, g, st, br, mixed, cot_a, far_a, wr_far, wg_far, ow_far) = rec_forward(
        tokens, cotangent, rec_weight, gate_weight, out_weight, mix_gain[:, None],
        recur_weight, input_weight, conv_weight, conv_bias[None, :], recur_bias[None, :],
        input_bias[None, :], sp,
    )
    wr = (rec_weight, wr_far)
    wg = (gate_weight, wg_far)
    ow = (out_weight, ow_far)
    fg = both(ffn_gate)
    fu = both(ffn_up)
    fd = both(ffn_down)
    gain_two = jnp.concatenate(both(ffn_gain))[None, :]
    gain_one = jnp.concatenate(both(mix_gain))[None, :]
    keep = diag.astype(F32).reshape(1, 1)

    half_shape = (part, 2 * half)
    res_a, n2t_a, cott_a, ctok_a, out_a, gn2_a, hid_a, ga_a, gb_a, far_b, cot_b = ffn(
        0, part, x, mixed, far_a, cot_a, live_core, gain_two, keep, fg, fu, fd,
        [mixed, cotangent], [half_shape, (2, half, part)], 3,
    )
    res_b, n2t_b, cott_b, ctok_b, out_b, gn2_b, hid_b, ga_b, gb_b, gn2_far_a = ffn(
        1, part, x, mixed, far_b, cot_b, live_core, gain_two, keep, fg, fu, fd,
        [gn2_a], [half_shape], 4,
    )
    up_sum, gg0, gg1, gd0, gd1, g1_a, g1t_a, g1_b, g1t_b, grad_gain_two = ffn_back(
        [n2t_a, n2t_b], [cott_a, cott_b], [hid_a, hid_b], [ga_a, ga_b], [gb_a, gb_b],
        [gn2_a, gn2_b], gn2_far_a, [res_a, res_b], [ctok_a, ctok_b], gain_two, 5,
    )
    gn1_part, go0, go1, gr0, gr1, gt0, gt1, ggw, sums, stat, gains0, gains1, sum_up = rec_backward(
        [g1_a, g1_b], [g1t_a, g1t_b], n1t, st, gate, r, g, cl, rec, br, ow, wr, wg, recur_weight,
        input_weight, conv_weight, sp, x, gain_one, grad_gain_two, up_sum, dp,
    )
    gates = ggw.reshape(-1, 256)
    own = [gd0, gg0, go0, gr0, gt0, gates, sums, gains0]
    other = [gd1, gg1, go1, gr1, gt1, gates, sums, gains1]
    total, moved = ring_sum(dp, own, other, [gn1_part, out_a, out_b, stat, g1_a, g1_b])
    sum_down, sum_gate, sum_out, sum_rec, sum_gatew, gates, sums, gains = total
    result, grad_tokens = final(*moved, tokens, mix_gain[:, None], live_chip[None, :])
    gates = gates.astype(F32).reshape(ggw.shape)
    vec = jnp.sum(sums.reshape(8, 8, -1), axis=1)
    gains = jnp.sum(gains[:16].reshape(2, 8, half), axis=1)
    grad_gain_one = gains[0] + swap(gains[0], "cols")
    grad_decay = vec[2] * -jax.nn.sigmoid(-decay_param)
    return (
        result,
        grad_tokens,
        grad_gain_one,
        sum_rec.astype(F32),
        sum_gatew.astype(F32),
        vec[3:7],
        vec[7],
        gates[:, :, :128],
        vec[0],
        gates[:, :, 128:],
        vec[1],
        grad_decay,
        sum_out.astype(F32),
        gains[1],
        sum_gate.astype(F32),
        sum_up.astype(F32),
        sum_down.astype(F32),
    )


def solution(mesh):
    return jax.shard_map(
        functools.partial(body, mesh.shape["dp"]),
        mesh=mesh,
        in_specs=(
            P("rows", ("dp", "cols")),
            P("dp"),
            P("rows"),
            P("rows", "cols"),
            P("rows", "cols"),
            P(None, "cols"),
            P("cols"),
            P("cols", None, None),
            P("cols"),
            P("cols", None, None),
            P("cols"),
            P("cols"),
            P("rows", "cols"),
            P("rows"),
            P("rows", "cols"),
            P("rows", "cols"),
            P("rows", "cols"),
            P("rows", ("dp", "cols")),
        ),
        out_specs=(
            P("rows", ("dp", "cols")),
            P("rows", ("dp", "cols")),
            P("rows"),
            P("rows", "cols"),
            P("rows", "cols"),
            P(None, "cols"),
            P("cols"),
            P("cols", None, None),
            P("cols"),
            P("cols", None, None),
            P("cols"),
            P("cols"),
            P("rows", "cols"),
            P("rows"),
            P("rows", "cols"),
            P("rows", "cols"),
            P("rows", "cols"),
        ),
        check_vma=False,
    )
```

```python
import functools
import math

import jax
import jax.numpy as jnp
from jax import lax
from jax.experimental import pallas as pl
from jax.experimental.pallas import tpu as pltpu
from jax.sharding import PartitionSpec as P

D = 1536
KCONV = 4
LEN = 1024
EPS = 1e-06
GATE_SCALE = 8.0
TANH_COEF = math.sqrt(2.0 / math.pi)
CUBIC_COEF = 0.044715
F32 = jnp.float32
BF16 = jnp.bfloat16
MIB = 1024 * 1024


def swap(value, axis):
    return lax.ppermute(value, axis, [(0, 1), (1, 0)])


def dot(left, right):
    return lax.dot_general(left, right, (((1,), (0,)), ((), ())), preferred_element_type=F32)


def dot_nt(left, right):
    return lax.dot_general(left, right, (((1,), (1,)), ((), ())), preferred_element_type=F32)


def dot_tn(left, right):
    return lax.dot_general(left, right, (((0,), (0,)), ((), ())), preferred_element_type=F32)


def gelu_act(values):
    inner_arg = TANH_COEF * (values + CUBIC_COEF * values * values * values)
    return 0.5 * values * (1.0 + jnp.tanh(inner_arg))


def gelu_pair(values):
    square = values * values
    tanh_val = jnp.tanh(values * (TANH_COEF + (TANH_COEF * CUBIC_COEF) * square))
    half_up = 0.5 + 0.5 * tanh_val
    slope = half_up + 0.5 * values * (1.0 - tanh_val * tanh_val) * (
        TANH_COEF + (3.0 * TANH_COEF * CUBIC_COEF) * square
    )
    return (values * half_up, slope)


def decay_terms(recur_gate, soft_decay):
    u = (2.0 * GATE_SCALE) * recur_gate * soft_decay
    decay = jnp.exp(-0.5 * u)
    series = u * (
        1.0
        - u
        * (0.5 - u * (1.0 / 6 - u * (1.0 / 24 - u * (1.0 / 120 - u * (1.0 / 720)))))
    )
    em = jnp.where(u < 0.25, series, 1.0 - decay * decay)
    return (decay, em)


def scan_tile(decay, drive, row):
    for shift in (1, 2, 4):
        keep = row >= shift
        before_a = jnp.where(keep, pltpu.roll(decay, shift, 0), 1.0)
        before_b = jnp.where(keep, pltpu.roll(drive, shift, 0), 0.0)
        drive = decay * before_b + drive
        decay = decay * before_a
    return (decay, drive)


def scan_tile_back(decay, drive, row):
    for shift in (1, 2, 4):
        keep = row < 8 - shift
        after_a = jnp.where(keep, pltpu.roll(decay, 8 - shift, 0), 1.0)
        after_b = jnp.where(keep, pltpu.roll(drive, 8 - shift, 0), 0.0)
        drive = decay * after_b + drive
        decay = decay * after_a
    return (decay, drive)


def group_barrier(core, chip):
    barrier = pltpu.get_barrier_semaphore()
    for peer in ((1 - core, chip), (core, 1 - chip), (1 - core, 1 - chip)):
        pl.semaphore_signal(barrier, inc=1, device_id={"rows": peer[0], "cols": peer[1]})
    pl.semaphore_wait(barrier, 3)


def rec_forward_kernel(
    chunk, count, cot_parts,
    tokens, cotangent, wr_h, wg_h, ow_h, gain_h, rw, iw, cw, cb, rb, ib, sp,
    x_o, n1t_o, rec_o, gate_o, cl_o, r_o, i_o, st_o, br_o, mix_o, cot_o, far_o, wr_o, wg_o, ow_o,
    tok_b, mix_s, wr, wg, ow, gain, gw, halo, carry, recpad, pre,
    tok_send, tok_recv, w_send, w_recv, w_own, cot_send, cot_recv, mix_send, mix_recv, put,
):
    step = pl.program_id(0)
    width = wr_h.shape[1]
    half = wr_h.shape[0]
    heads = width // 128
    core = lax.axis_index("rows")
    chip = lax.axis_index("cols")
    slot = lax.select(core == chip, 0, 1)
    near = {"rows": 1 - core}
    far = {"rows": chip, "cols": 1 - chip}

    def piece_moves(src, dst, send, recv):
        return (
            pltpu.make_async_copy(src, dst, recv),
            pltpu.make_async_remote_copy(src, dst, send.at[0], recv, device_id=near),
            pltpu.make_async_remote_copy(src, dst, send.at[1], recv, device_id=far),
        )

    def token_moves(k):
        return piece_moves(
            tokens.at[:, pl.ds(k * chunk, chunk)], tok_b.at[k, slot], tok_send.at[k], tok_recv.at[k, slot]
        )

    def cot_moves(k):
        return piece_moves(
            cotangent.at[:, pl.ds(k * chunk, chunk)],
            cot_o.at[slot, :, pl.ds(k * chunk, chunk)],
            cot_send.at[k],
            cot_recv.at[k, slot],
        )

    def mix_move(k):
        return pltpu.make_async_remote_copy(
            mix_s.at[k],
            far_o.at[pl.ds(k * chunk, chunk), :],
            mix_send.at[k],
            mix_recv.at[k],
            device_id={"cols": 1 - chip},
        )

    def start(moves):
        moves[2].start()

        @pl.when(core == chip)
        def _():
            moves[0].start()

        @pl.when(core != chip)
        def _():
            moves[1].start()

    def finish_send(moves):
        moves[2].wait_send()

        @pl.when(core != chip)
        def _():
            moves[1].wait_send()

    weights = ((wr_h, wr), (wg_h, wg), (ow_h, ow), (gain_h, gain))

    def weight_moves(n):
        src, dst = weights[n]
        return (
            pltpu.make_async_copy(src, dst.at[0], w_own.at[n]),
            pltpu.make_async_remote_copy(src, dst.at[1], w_send.at[n], w_recv.at[n], device_id=near),
        )

    def wait_weight(n):
        own, other = weight_moves(n)
        own.wait()
        other.wait_recv()

    @pl.when(step == 0)
    def _():
        group_barrier(core, chip)
        start(token_moves(0))
        for n in (3, 0, 1, 2):
            for move in weight_moves(n):
                move.start()
        for k in range(1, count):
            start(token_moves(k))
        halo[...] = jnp.zeros_like(halo)
        carry[...] = jnp.zeros_like(carry)
        for h in range(heads):
            gw[h, :, 0:128] = rw[h]
            gw[h, :, 128:256] = iw[h]
        wait_weight(3)

    for s in range(2):
        pltpu.make_async_copy(
            tokens.at[:, pl.ds(0, chunk)], tok_b.at[step, s], tok_recv.at[step, s]
        ).wait()

    @pl.when(step == count - 2)
    def _():
        for k in range(cot_parts):
            start(cot_moves(k))

    xt0 = tok_b[step, 0].astype(F32)
    xt1 = tok_b[step, 1].astype(F32)
    squares = jnp.sum(xt0 * xt0, axis=0, keepdims=True) + jnp.sum(xt1 * xt1, axis=0, keepdims=True)
    scale = lax.rsqrt(squares / (2 * half) + EPS)
    nt0 = (xt0 * scale * gain[0]).astype(BF16)
    nt1 = (xt1 * scale * gain[1]).astype(BF16)
    n1t_o[0:half, :] = nt0
    n1t_o[half:, :] = nt1
    x_o[:, 0:half] = tok_b[step, 0].T
    x_o[:, half:] = tok_b[step, 1].T
    low0 = nt0.T
    low1 = nt1.T

    @pl.when(step == 0)
    def _():
        wait_weight(0)
        wait_weight(1)

    rec = dot(low0, wr[0]) + dot(low1, wr[1])
    recpad[0:8, :] = halo[...]
    recpad[8:, :] = rec
    halo[...] = rec[chunk - 8 :, :]
    rec_o[...] = rec
    gate_o[...] = dot(low0, wg[0]) + dot(low1, wg[1])

    def conv_step(i, _):
        base = pl.multiple_of(i * 16, 16)
        for h in range(heads):
            sl = slice(h * 128, (h + 1) * 128)
            window = recpad[pl.ds(base, 24), sl]
            out = cb[:, sl] + cw[0:1, sl] * window[8:]
            for k in range(1, KCONV):
                out = out + cw[k : k + 1, sl] * pltpu.roll(window, k, 0)[8:]
            cl_o[pl.ds(base, 16), sl] = out.astype(BF16)
        return 0

    lax.fori_loop(0, chunk // 16, conv_step, 0)
    for h in range(heads):
        pre[:, h * 256 : (h + 1) * 256] = dot(cl_o[:, h * 128 : (h + 1) * 128], gw[h])
    row = lax.broadcasted_iota(jnp.int32, (8, 128), 0)

    def main_step(i, _):
        base = pl.multiple_of(i * 16, 16)
        rows = pl.ds(base, 16)
        for h in range(heads):
            sl = slice(h * 128, (h + 1) * 128)
            r = jax.nn.sigmoid(pre[rows, h * 256 : h * 256 + 128] + rb[:, sl])
            g = jax.nn.sigmoid(pre[rows, h * 256 + 128 : (h + 1) * 256] + ib[:, sl])
            conv = cl_o[rows, sl].astype(F32)
            decay, em = decay_terms(r, sp[:, sl])
            drive = jnp.sqrt(em) * g * conv
            r_o[rows, sl] = r
            i_o[rows, sl] = g
            held = carry[0:1, sl]
            parts = []
            for p in range(2):
                a, b = scan_tile(decay[p * 8 : p * 8 + 8], drive[p * 8 : p * 8 + 8], row)
                state = a * held + b
                held = state[7:8]
                parts.append(state)
            carry[0:1, sl] = held
            state = jnp.concatenate(parts, axis=0)
            st_o[rows, sl] = state
            br_o[rows, sl] = (state * gelu_act(gate_o[rows, sl])).astype(BF16)
        return 0

    lax.fori_loop(0, chunk // 16, main_step, 0)

    @pl.when(step == 0)
    def _():
        wait_weight(2)

    def put_moves():
        return [
            pltpu.make_async_copy(held.at[1], out, put.at[n])
            for n, (held, out) in enumerate(((wr, wr_o), (wg, wg_o), (ow, ow_o)))
        ]

    @pl.when(step == 0)
    def _():
        for move in put_moves():
            move.start()

    branch = br_o[...]
    mix_o[:, :half] = dot_nt(branch, ow[0]).astype(BF16)
    mix_o[:, half:] = dot_nt(branch, ow[1]).astype(BF16)

    for k in range(cot_parts):

        @pl.when(step == k)
        def _():
            mix_s[k] = mix_o[...]
            mix_move(k).start()

    @pl.when(step == count - 1)
    def _():
        for k in range(cot_parts):
            for s in range(2):
                pltpu.make_async_copy(
                    cotangent.at[:, pl.ds(0, chunk)],
                    cot_o.at[s, :, pl.ds(k * chunk, chunk)],
                    cot_recv.at[k, s],
                ).wait()
            finish_send(cot_moves(k))
            mix_move(k).wait()
        for k in range(count):
            finish_send(token_moves(k))
        for n in range(4):
            weight_moves(n)[1].wait_send()
        for move in put_moves():
            move.wait()


def rec_forward(tokens, cotangent, wr, wg, ow, gain, rw, iw, cw, cb, rb, ib, sp, chunk=256):
    half, length = tokens.shape
    width = wr.shape[1]
    heads = width // 128
    count = length // chunk
    cot_parts = 1
    wide = 2 * half
    row_block = lambda cols: pl.BlockSpec((chunk, cols), lambda i: (i, 0))
    whole = lambda shape: pl.BlockSpec(
        shape, lambda i: (0,) * len(shape), pipeline_mode=pl.Buffered(1)
    )
    hbm = pl.BlockSpec(memory_space=pl.ANY)
    f32 = jax.ShapeDtypeStruct((length, width), F32)
    low = jax.ShapeDtypeStruct((length, width), BF16)
    dma = pltpu.SemaphoreType.DMA
    return pl.pallas_call(
        functools.partial(rec_forward_kernel, chunk, count, cot_parts),
        grid=(count,),
        in_specs=[hbm] * 6
        + [whole((heads, 128, 128))] * 2
        + [whole((KCONV, width))]
        + [whole((1, width))] * 4,
        out_specs=[row_block(wide), pl.BlockSpec((wide, chunk), lambda i: (0, i))]
        + [row_block(width)] * 7
        + [row_block(wide)]
        + [hbm] * 5,
        out_shape=[
            jax.ShapeDtypeStruct((length, wide), BF16),
            jax.ShapeDtypeStruct((wide, length), BF16),
            f32, f32, low, f32, f32, f32, low,
            jax.ShapeDtypeStruct((length, wide), BF16),
            jax.ShapeDtypeStruct((2, half, cot_parts * chunk), BF16),
            jax.ShapeDtypeStruct((cot_parts * chunk, wide), BF16),
        ]
        + [jax.ShapeDtypeStruct((half, width), BF16)] * 3,
        scratch_shapes=[
            pltpu.VMEM((count, 2, half, chunk), BF16),
            pltpu.VMEM((cot_parts, chunk, wide), BF16),
            pltpu.VMEM((2, half, width), BF16),
            pltpu.VMEM((2, half, width), BF16),
            pltpu.VMEM((2, half, width), BF16),
            pltpu.VMEM((2, half, 1), F32),
            pltpu.VMEM((heads, 128, 256), BF16),
            pltpu.VMEM((8, width), F32),
            pltpu.VMEM((8, width), F32),
            pltpu.VMEM((chunk + 8, width), F32),
            pltpu.VMEM((chunk, 2 * width), F32),
            dma((count, 2)),
            dma((count, 2)),
            dma((4,)),
            dma((4,)),
            dma((4,)),
            dma((count, 2)),
            dma((count, 2)),
            dma((cot_parts,)),
            dma((cot_parts,)),
            dma((3,)),
        ],
        compiler_params=pltpu.CompilerParams(
            vmem_limit_bytes=60 * MIB, collective_id=2, has_side_effects=True
        ),
        name="recurrent_forward",
    )(tokens, cotangent, wr, wg, ow, gain, rw, iw, cw, cb, rb, ib, sp)


def ffn_kernel(
    count, blocks,
    x, mix, live, gain, keep, wg0, wg1, wu0, wu1, wd0, wd1, mixed, cotangent, far_first, cot_first,
    out_o, gu_sum, gg0, gg1, gd0, gd1, g1_o, g1t_o, gain_o,
    far_s, ct_s, ctok_s, n2_s, n2t_s, hid_s, ga_s, gb_s, out_acc, gn_acc, gn_s, gn_far,
    keep_s, give_s, got_s,
    far_send, far_recv, ct_send, ct_recv, gn_send, gn_recv, up_send, up_recv, free_sem,
):
    step = pl.program_id(0)
    core, chip = lax.axis_index("rows"), lax.axis_index("cols")
    chunk, wide = n2_s.shape
    half, block = gg0.shape
    first_part = count * blocks
    slot = lax.select(core == chip, 0, 1)
    beside = {"cols": 1 - chip}

    def far_move(c):
        return pltpu.make_async_remote_copy(
            mixed.at[pl.ds(c * chunk, chunk), :], far_s.at[c], far_send.at[c], far_recv.at[c], device_id=beside
        )

    def far_load():
        return pltpu.make_async_copy(far_first, far_s.at[0], far_recv.at[0])

    def cot_moves(c):
        src = cotangent.at[:, pl.ds(c * chunk, chunk)]
        there = ct_s.at[slot, :, pl.ds(c * chunk, chunk)]
        return (
            pltpu.make_async_copy(src, there, ct_recv.at[c, slot]),
            pltpu.make_async_remote_copy(
                src, there, ct_send.at[c, 0], ct_recv.at[c, slot], device_id={"rows": 1 - core}
            ),
            pltpu.make_async_remote_copy(
                src, there, ct_send.at[c, 1], ct_recv.at[c, slot],
                device_id={"rows": chip, "cols": 1 - chip},
            ),
        )

    def cot_load(s):
        return pltpu.make_async_copy(
            cot_first.at[s], ct_s.at[s, :, pl.ds(0, chunk)], ct_recv.at[0, s]
        )

    def gn_move(c):
        return pltpu.make_async_remote_copy(
            gn_s.at[c], gn_far.at[c], gn_send.at[c], gn_recv.at[c], device_id=beside
        )

    def send_part(c):
        far_move(c).start()
        moves = cot_moves(c)
        moves[2].start()

        @pl.when(core == chip)
        def _():
            moves[0].start()

        @pl.when(core != chip)
        def _():
            moves[1].start()

    @pl.when(step == 0)
    def _():
        far_load().start()
        for s in range(2):
            cot_load(s).start()
        group_barrier(core, chip)
        for c in range(1, count):
            send_part(c)
        gain_o[...] = jnp.zeros_like(gain_o)

    def turned_cot(c):
        cols = pl.ds(pl.multiple_of(c * chunk, chunk), chunk)
        for s in range(2):
            ctok_s[:, s * half : (s + 1) * half] = ct_s[s, :, cols].T

    def norm_forward(c):
        cols = pl.ds(pl.multiple_of(c * chunk, chunk), chunk)
        pltpu.make_async_copy(far_first, far_s.at[c], far_recv.at[c]).wait()
        for s in range(2):
            pltpu.make_async_copy(
                cot_first.at[s], ct_s.at[s, :, cols], ct_recv.at[c, s]
            ).wait()
            ct_s[s, :, cols] = ct_s[s, :, cols] * live[:, cols]
        turned_cot(c)
        gn_acc[...] = jnp.zeros_like(gn_acc)

        def rows_step(i, _):
            rows = pl.ds(pl.multiple_of(i * 16, 16), 16)
            res = x[rows, :].astype(F32) + (mix[rows, :].astype(F32) + far_s[c, rows, :].astype(F32))
            out_acc[rows, :] = keep[...] * res
            scale = lax.rsqrt(jnp.sum(res * res, axis=1, keepdims=True) / wide + EPS)
            n2_s[rows, :] = (res * scale * gain[...]).astype(BF16)
            return 0

        lax.fori_loop(0, chunk // 16, rows_step, 0)
        n2t_s[:, cols] = n2_s[...].T

    @pl.when(step < first_part)
    def _():
        c = step // blocks
        blk = step % blocks
        rows = pl.ds(pl.multiple_of(c * chunk, chunk), chunk)

        @pl.when(blk == 0)
        def _():
            norm_forward(c)

        n0, n1 = n2_s[:, :half], n2_s[:, half:]
        c0, c1 = ctok_s[:, :half], ctok_s[:, half:]
        a = dot(n0, wg0[...]) + dot(n1, wg1[...])
        b = dot(n0, wu0[...]) + dot(n1, wu1[...])
        gh = dot(c0, wd0[...]) + dot(c1, wd1[...])
        act, slope = gelu_pair(a)
        hidden = (act * b).astype(BF16)
        ga = (gh * b * slope).astype(BF16)
        gb = (gh * act).astype(BF16)
        hid_s[blk, rows, :] = hidden
        ga_s[blk, rows, :] = ga
        gb_s[blk, rows, :] = gb
        out_acc[:, :half] += dot_nt(hidden, wd0[...])
        out_acc[:, half:] += dot_nt(hidden, wd1[...])
        gn_acc[:, :half] += dot_nt(ga, wg0[...]) + dot_nt(gb, wu0[...])
        gn_acc[:, half:] += dot_nt(ga, wg1[...]) + dot_nt(gb, wu1[...])

        @pl.when(blk == blocks - 1)
        def _():
            out_o[...] = out_acc[...].astype(BF16)
            gn_s[c] = gn_acc[...].astype(BF16)
            gn_move(c).start()

    def norm_back(c):
        turned_cot(c)
        gn_move(c).wait_recv()

        def rows_step(i, _):
            rows = pl.ds(pl.multiple_of(i * 16, 16), 16)
            grad = gn_s[c, rows, :].astype(F32) + gn_far[c, rows, :].astype(F32)
            held = x[rows, :].astype(F32) + (mix[rows, :].astype(F32) + far_s[c, rows, :].astype(F32))
            scale = lax.rsqrt(jnp.sum(held * held, axis=1, keepdims=True) / wide + EPS)
            product = grad * held
            by_gain = product * scale
            gain_o[...] += by_gain[0:8] + by_gain[8:16]
            inner = jnp.sum(product * gain[...], axis=1, keepdims=True)
            grad_one = (
                ctok_s[rows, :].astype(F32)
                + scale * (grad * gain[...])
                - held * (scale * scale * scale * inner / wide)
            )
            g1_o[rows, :] = grad_one.astype(BF16)
            return 0

        lax.fori_loop(0, chunk // 16, rows_step, 0)
        g1t_o[...] = g1_o[...].T

    def give(k):
        at = k % 2
        return pltpu.make_async_remote_copy(
            give_s.at[at], got_s.at[at], up_send.at[at], up_recv.at[at], device_id={"rows": 1 - core}
        )

    k = step - first_part

    @pl.when(jnp.logical_and(k > 0, k <= blocks))
    def _():
        give(k - 1).wait()
        total = keep_s[(k - 1) % 2].astype(F32) + got_s[(k - 1) % 2].astype(F32)
        gu_sum[...] = total.astype(BF16)

        @pl.when(k - 1 < blocks - 2)
        def _():
            pl.semaphore_signal(free_sem, inc=1, device_id={"rows": 1 - core})

    @pl.when(jnp.logical_and(k >= 0, k < blocks))
    def _():
        up, down, gate = gb_s[k], hid_s[k], ga_s[k]
        give_s[k % 2] = dot(n2t_s[half:], up).astype(BF16)

        @pl.when(k >= 2)
        def _():
            pl.semaphore_wait(free_sem, 1)

        give(k).start()
        keep_s[k % 2] = dot(n2t_s[:half], up).astype(BF16)
        gg0[...] = dot(n2t_s[:half], gate).astype(BF16)
        gg1[...] = dot(n2t_s[half:], gate).astype(BF16)
        gd0[...] = dot(ct_s[0], down).astype(BF16)
        gd1[...] = dot(ct_s[1], down).astype(BF16)

    for c in range(count):

        @pl.when(k == (2 * c + 1 if c < count - 1 else blocks))
        def _():
            norm_back(c)

    @pl.when(k == blocks)
    def _():
        for c in range(count):
            gn_move(c).wait_send()
        for c in range(1, count):
            far_move(c).wait_send()
            moves = cot_moves(c)
            moves[2].wait_send()

            @pl.when(core != chip)
            def _():
                moves[1].wait_send()


def ffn(x, mix, live, gain, keep, wg, wu, wd, cotangent, far_first, cot_first, chunk=256, block=256):
    tokens, wide = x.shape
    half, width = wg[0].shape
    count, blocks = tokens // chunk, width // block
    first_part = count * blocks
    whole = lambda shape: pl.BlockSpec(
        shape, lambda i: (0,) * len(shape), pipeline_mode=pl.Buffered(1)
    )
    hbm = pl.BlockSpec(memory_space=pl.ANY)

    def back_chunk(i):
        return jnp.clip((i - first_part) // 2, 0, count - 1)

    def chunk_at(i):
        return jnp.where(i < first_part, i // blocks, back_chunk(i))

    rows = pl.BlockSpec((chunk, wide), lambda i: (chunk_at(i), 0))
    weight = pl.BlockSpec(
        (half, block), lambda i: (0, jnp.where(i < first_part, i % blocks, blocks - 1))
    )
    grad_at = lambda late: pl.BlockSpec(
        (half, block), lambda i: (0, jnp.clip(i - first_part - late, 0, blocks - 1))
    )
    grad = jax.ShapeDtypeStruct((half, width), BF16)
    low = jax.ShapeDtypeStruct((tokens, wide), BF16)
    part = pltpu.VMEM((count, chunk, wide), BF16)
    middle = pltpu.VMEM((blocks, tokens, block), BF16)
    pair = pltpu.VMEM((2, half, block), BF16)
    dma = pltpu.SemaphoreType.DMA
    return pl.pallas_call(
        functools.partial(ffn_kernel, count, blocks),
        grid=(first_part + blocks + 1,),
        in_specs=[rows, rows, whole((1, tokens)), whole((1, wide)), whole((1, 1))]
        + [weight] * 6
        + [hbm] * 4,
        out_specs=[
            pl.BlockSpec((chunk, wide), lambda i: (jnp.minimum(i // blocks, count - 1), 0)),
            grad_at(1),
        ]
        + [grad_at(0)] * 4
        + [
            pl.BlockSpec((chunk, wide), lambda i: (back_chunk(i), 0)),
            pl.BlockSpec((wide, chunk), lambda i: (0, back_chunk(i))),
            whole((8, wide)),
        ],
        out_shape=[low]
        + [grad] * 5
        + [low, jax.ShapeDtypeStruct((wide, tokens), BF16), jax.ShapeDtypeStruct((8, wide), F32)],
        scratch_shapes=[
            part,
            pltpu.VMEM((2, half, tokens), BF16),
            pltpu.VMEM((chunk, wide), BF16),
            pltpu.VMEM((chunk, wide), BF16),
            pltpu.VMEM((wide, tokens), BF16),
            middle, middle, middle,
            pltpu.VMEM((chunk, wide), F32),
            pltpu.VMEM((chunk, wide), F32),
            part, part,
            pair, pair, pair,
            dma((count,)), dma((count,)),
            dma((count, 2)), dma((count, 2)),
            dma((count,)), dma((count,)),
            dma((2,)), dma((2,)),
            pltpu.SemaphoreType.REGULAR,
        ],
        compiler_params=pltpu.CompilerParams(
            vmem_limit_bytes=62 * MIB, collective_id=3, has_side_effects=True
        ),
        name="ffn",
    )(
        x, mix, live, gain, keep, wg[0], wg[1], wu[0], wu[1], wd[0], wd[1],
        mix, cotangent, far_first, cot_first,
    )


def ring_place(n, at):
    def index_of(place):
        return lax.select(place < n // 2, 2 * place, 2 * (n - 1 - place) + 1)

    me = lax.select(at % 2 == 0, at // 2, n - 1 - at // 2)
    return me, (index_of(lax.rem(me + 1, n)), index_of(lax.rem(me + n - 1, n)))


def ring_rows(n, me, total, way, s):
    size = total // n
    chunk = lax.rem(me + n - s, n) if way == 0 else lax.rem(me + s, n)
    return pl.ds(pl.multiple_of(chunk * size, size), size)


def ring_beside(n, own, out, own_b, ring_b, own_sem, rs_send, rs_recv, ag_send, ag_recv, put_sem):
    me, nexts = ring_place(n, lax.axis_index("dp"))
    wide = own.shape[1] // 2
    cut = (wide // 128 + 1) // 2 * 128
    groups = (pl.ds(0, cut), pl.ds(cut, wide - cut))
    both = [(g, way) for g in range(2) for way in range(2)]
    per = -(-n // 8)
    per_gather = -(-(n - 2) // 6)
    rows_of = lambda way, s: ring_rows(n, me, own.shape[0], way, s)
    cols_of = lambda g, way: pl.ds(way * wide + g * cut, wide - cut if g else cut)

    def own_copy(way, s):
        return pltpu.make_async_copy(
            own.at[rows_of(way, s), pl.ds(way * wide, wide)], own_b.at[way, s], own_sem.at[way, s]
        )

    def sum_copy(g, way, s):
        return pltpu.make_async_remote_copy(
            ring_b.at[way, s, :, groups[g]], ring_b.at[way, s + 1, :, groups[g]],
            rs_send.at[g, way], rs_recv.at[g, way, s], device_id={"dp": nexts[way]},
        )

    def first_gather(g, way):
        return pltpu.make_async_remote_copy(
            ring_b.at[way, n - 1, :, groups[g]], out.at[rows_of(way, n - 1), cols_of(g, way)],
            ag_send.at[g, way, 0], ag_recv.at[g, way, 0], device_id={"dp": nexts[way]},
        )

    def gather_copy(g, way, s):
        there = out.at[rows_of(way, s - 1), cols_of(g, way)]
        return pltpu.make_async_remote_copy(
            there, there, ag_send.at[g, way, s], ag_recv.at[g, way, s], device_id={"dp": nexts[way]}
        )

    def put_copy(g, way):
        return pltpu.make_async_copy(
            ring_b.at[way, n - 1, :, groups[g]],
            out.at[rows_of(way, n - 1), cols_of(g, way)],
            put_sem.at[g, way],
        )

    def begin():
        barrier = pltpu.get_barrier_semaphore()
        for neighbour in nexts:
            pl.semaphore_signal(barrier, inc=1, device_id={"dp": neighbour})

        def load(s, _):
            for way in range(2):
                own_copy(way, s).start()
            return 0

        lax.fori_loop(0, n, load, 0)
        pl.semaphore_wait(barrier, 2)

    def tick(g, t):
        def sum_step(s, _):
            for way in range(2):
                if g == 0:
                    own_copy(way, s).wait()

                @pl.when(s == 0)
                def _():
                    ring_b[way, s, :, groups[g]] = own_b[way, s, :, groups[g]]

                @pl.when(s > 0)
                def _():
                    sum_copy(g, way, s - 1).wait_recv()
                    total = ring_b[way, s, :, groups[g]].astype(F32) + own_b[
                        way, s, :, groups[g]
                    ].astype(F32)
                    ring_b[way, s, :, groups[g]] = total.astype(BF16)

                @pl.when(s < n - 1)
                def _():
                    sum_copy(g, way, s).start()

                @pl.when(s == n - 1)
                def _():
                    first_gather(g, way).start()
                    put_copy(g, way).start()
            return 0

        def gather_step(s, _):
            for way in range(2):

                @pl.when(s == 1)
                def _():
                    first_gather(g, way).wait_recv()

                @pl.when(s > 1)
                def _():
                    gather_copy(g, way, s - 1).wait_recv()

                gather_copy(g, way, s).start()
            return 0

        @pl.when(t < 8)
        def _():
            lax.fori_loop(t * per, jnp.minimum((t + 1) * per, n), sum_step, 0)

        @pl.when(t >= 8)
        def _():
            start = 1 + (t - 8) * per_gather
            lax.fori_loop(start, jnp.minimum(start + per_gather, n - 1), gather_step, 0)

    def end():
        for g, way in both:
            gather_copy(g, way, n - 2).wait_recv()
            put_copy(g, way).wait()
            first_gather(g, way).wait_send()
            pltpu.make_async_remote_copy(
                ring_b.at[way, pl.ds(0, n - 1), :, groups[g]],
                ring_b.at[way, pl.ds(1, n - 1), :, groups[g]],
                rs_send.at[g, way], rs_recv.at[g, way, 0], device_id={"dp": nexts[way]},
            ).wait_send()

        def drain(s, _):
            for g, way in both:
                gather_copy(g, way, s).wait_send()
            return 0

        lax.fori_loop(1, n - 1, drain, 0)

    return begin, tick, end


def rec_backward_kernel(
    tile, n,
    g1, g1t, n1t, st, gate, r_in, i_in, cl, rec, br, ow0, ow1, wr0, wr1, wg0, wg1, rw, iw, cw, sp,
    x, gain, gain_two, up,
    gn1_o, go0, go1, gr0, gr1, gg0, gg1, ggw, sums, stat, gains0, gains1, up_o,
    acc, gb_s, gc_s, ggp_s, grp_s, gip_s, grec_s, gain_s, *ring_refs
):
    step = pl.program_id(0)
    tokens, block = gb_s.shape
    wide = n1t.shape[0]
    heads = block // 128
    half = ow0.shape[0]
    tiles = tokens // tile
    subs = tile // 8

    begin, tick, end = ring_beside(n, up, up_o, *ring_refs)

    @pl.when(step == 0)
    def _():
        begin()
        acc[...] = jnp.zeros_like(acc)

    beat = lambda at: tick(at % 2, step * 3 + at // 2)
    beat(0)
    gb_s[...] = dot(g1[:, :half], ow0[...]) + dot(g1[:, half:], ow1[...])
    beat(1)
    go0[...] = dot(g1t[:half], br[...]).astype(BF16)
    go1[...] = dot(g1t[half:], br[...]).astype(BF16)
    beat(2)
    sums[...] = jnp.zeros_like(sums)
    row = lax.broadcasted_iota(jnp.int32, (8, 128), 0)

    def back_step(j, held):
        @pl.when(j == tiles // 2)
        def _():
            beat(3)

        i = tiles - 1 - j
        base = pl.multiple_of(i * tile, tile)
        rows = pl.ds(base, tile)
        before = pl.ds(pl.multiple_of(jnp.maximum(base - 8, 0), 8), 8)
        out = []
        for h in range(heads):
            sl = slice(h * 128, (h + 1) * 128)
            later_decay, later_carried = held[h]
            grad_branch = gb_s[rows, sl]
            act, slope = gelu_pair(gate[rows, sl])
            state = st[rows, sl]
            ggp_s[rows, sl] = (grad_branch * state * slope).astype(BF16)
            grad_state = grad_branch * act
            r = r_in[rows, sl]
            soft = sp[:, sl]
            decay, em = decay_terms(r, soft)
            parts = [None] * subs
            for p in range(subs - 1, -1, -1):
                own = decay[p * 8 : p * 8 + 8]
                after = jnp.where(row == 7, later_decay, pltpu.roll(own, 7, 0))
                a, b = scan_tile_back(after, grad_state[p * 8 : p * 8 + 8], row)
                carried = a * later_carried + b
                later_decay = own[0:1]
                later_carried = carried[0:1]
                parts[p] = carried
            out.append((later_decay, later_carried))
            carried = jnp.concatenate(parts, axis=0)
            edge = jnp.where(i > 0, st[before, sl][7:8], 0.0)
            prev = []
            for p in range(subs):
                prev.append(jnp.where(row == 0, edge, pltpu.roll(state[p * 8 : p * 8 + 8], 1, 0)))
                edge = state[p * 8 + 7 : p * 8 + 8]
            prev = jnp.concatenate(prev, axis=0)
            g = i_in[rows, sl]
            conv = cl[rows, sl].astype(F32)
            scaling = jnp.sqrt(em)
            gated = g * conv
            grad_log = carried * (prev * decay - gated * (decay * decay) / scaling)
            grad_soft = grad_log * (-GATE_SCALE * r)
            grp = grad_soft * soft * (1.0 - r)
            cs = carried * scaling
            gc_s[rows, sl] = cs * g
            gip = cs * gated * (1.0 - g)
            grp_s[rows, sl] = grp.astype(BF16)
            gip_s[rows, sl] = gip.astype(BF16)
            for n, term in enumerate((grp, gip, grad_soft)):
                total = term[0:8]
                for p in range(1, subs):
                    total = total + term[p * 8 : p * 8 + 8]
                sums[n * 8 : n * 8 + 8, sl] += total
        return tuple(out)

    zero = jnp.zeros((1, 128), F32)
    lax.fori_loop(0, tiles, back_step, tuple((zero, zero) for _ in range(heads)))
    beat(4)
    for h in range(heads):
        sl = slice(h * 128, (h + 1) * 128)
        low = cl[:, sl]
        ggw[h, :, 0:128] = dot_tn(low, grp_s[:, sl]).astype(BF16)
        ggw[h, :, 128:256] = dot_tn(low, gip_s[:, sl]).astype(BF16)
        gc_s[:, sl] += dot_nt(grp_s[:, sl], rw[h]) + dot_nt(gip_s[:, sl], iw[h])

    def conv_step(j, held):
        i = tiles - 1 - j
        base = pl.multiple_of(i * tile, tile)
        rows = pl.ds(base, tile)
        before = pl.ds(pl.multiple_of(jnp.maximum(base - 8, 0), 8), 8)
        out = []
        for h in range(heads):
            sl = slice(h * 128, (h + 1) * 128)
            grad_conv = gc_s[rows, sl]
            window = jnp.concatenate([grad_conv, held[h]], axis=0)
            out.append(grad_conv[0:8])
            grad_rec = cw[0:1, sl] * grad_conv
            for k in range(1, KCONV):
                grad_rec = grad_rec + cw[k : k + 1, sl] * pltpu.roll(window, tile + 8 - k, 0)[:tile]
            grec_s[rows, sl] = grad_rec.astype(BF16)
            edge = jnp.where(i > 0, rec[before, sl], 0.0)
            past = jnp.concatenate([edge, rec[rows, sl]], axis=0)
            terms = [grad_conv * past[8:]]
            for k in range(1, KCONV):
                terms.append(grad_conv * pltpu.roll(past, k, 0)[8:])
            terms.append(grad_conv)
            for n, term in enumerate(terms):
                total = term[0:8]
                for p in range(1, subs):
                    total = total + term[p * 8 : p * 8 + 8]
                sums[24 + n * 8 : 32 + n * 8, sl] += total
        return tuple(out)

    lax.fori_loop(0, tiles, conv_step, tuple(jnp.zeros((8, 128), F32) for _ in range(heads)))
    beat(5)
    grad_rec = grec_s[...]
    grad_gate = ggp_s[...]
    gr0[...] = dot(n1t[:half], grad_rec).astype(BF16)
    gr1[...] = dot(n1t[half:], grad_rec).astype(BF16)
    gg0[...] = dot(n1t[:half], grad_gate).astype(BF16)
    gg1[...] = dot(n1t[half:], grad_gate).astype(BF16)
    acc[:, :half] += dot_nt(grad_rec, wr0[...]) + dot_nt(grad_gate, wg0[...])
    acc[:, half:] += dot_nt(grad_rec, wr1[...]) + dot_nt(grad_gate, wg1[...])

    @pl.when(step == pl.num_programs(0) - 1)
    def _():
        gain_s[...] = jnp.zeros_like(gain_s)
        for g in range(2):
            tick(g, 12)

        def stat_step(i, _):
            @pl.when(i == tokens // 32)
            def _():
                for g in range(2):
                    tick(g, 13)

            rows = pl.ds(pl.multiple_of(i * 16, 16), 16)
            part = acc[rows, :]
            gn1_o[rows, :] = part.astype(BF16)
            held = x[rows, :].astype(F32)
            scale = lax.rsqrt(jnp.sum(held * held, axis=1, keepdims=True) / wide + EPS)
            product = part * held
            by_gain = product * scale
            gain_s[...] += by_gain[0:8] + by_gain[8:16]
            inner = jnp.sum(product * gain[...], axis=1, keepdims=True)
            stat[rows, 0:64] = jnp.broadcast_to(inner, (16, 64))
            stat[rows, 64:128] = jnp.broadcast_to(scale, (16, 64))
            return 0

        lax.fori_loop(0, tokens // 16, stat_step, 0)
        both = gain_two[...]
        for out, sl in ((gains0, slice(0, half)), (gains1, slice(half, wide))):
            out[...] = jnp.zeros_like(out)
            out[0:8, :] = gain_s[:, sl]
            out[8:16, :] = both[:, sl]
        end()


def rec_backward(
    g1, g1t, n1t, st, gate, r, g, cl, rec, br, ow, wr, wg, rw, iw, cw, sp, x, gain, gain_two, up, n, block=256, tile=64
):
    wide, tokens = n1t.shape
    half, width = wr[0].shape
    heads = block // 128
    rows = up.shape[0]
    up = jnp.pad(up, ((0, -rows % (16 * n)), (0, 0)))
    slots = pltpu.VMEM((2, n, up.shape[0] // n, up.shape[1] // 2), BF16)
    dma = pltpu.SemaphoreType.DMA
    hbm = pl.BlockSpec(memory_space=pl.ANY)
    whole = lambda shape: pl.BlockSpec(shape, lambda i: (0, 0), pipeline_mode=pl.Buffered(1))
    act = pl.BlockSpec((tokens, block), lambda i: (0, i))
    weight = pl.BlockSpec((half, block), lambda i: (0, i))
    thin = lambda n: pl.BlockSpec((n, block), lambda i: (0, i))
    gate_block = pl.BlockSpec((heads, 128, 256), lambda i: (i, 0, 0))
    grad = jax.ShapeDtypeStruct((half, width), BF16)
    outs = pl.pallas_call(
        functools.partial(rec_backward_kernel, tile, n),
        grid=(width // block,),
        in_specs=[whole((tokens, wide))] + [whole((wide, tokens))] * 2
        + [act] * 7
        + [weight] * 6
        + [pl.BlockSpec((heads, 128, 128), lambda i: (i, 0, 0))] * 2
        + [thin(KCONV), thin(1)]
        + [whole((tokens, wide)), whole((1, wide)), whole((8, wide)), hbm],
        out_specs=[whole((tokens, wide))]
        + [weight] * 6
        + [gate_block, thin(64), whole((tokens, 128)), whole((64, half)), whole((64, half)), hbm],
        out_shape=[jax.ShapeDtypeStruct((tokens, wide), BF16)]
        + [grad] * 6
        + [
            jax.ShapeDtypeStruct((width // 128, 128, 256), BF16),
            jax.ShapeDtypeStruct((64, width), F32),
            jax.ShapeDtypeStruct((tokens, 128), F32),
            jax.ShapeDtypeStruct((64, half), F32),
            jax.ShapeDtypeStruct((64, half), F32),
            jax.ShapeDtypeStruct(up.shape, BF16),
        ],
        scratch_shapes=[
            pltpu.VMEM((tokens, wide), F32),
            pltpu.VMEM((tokens, block), F32),
            pltpu.VMEM((tokens, block), F32),
            pltpu.VMEM((tokens, block), BF16),
            pltpu.VMEM((tokens, block), BF16),
            pltpu.VMEM((tokens, block), BF16),
            pltpu.VMEM((tokens, block), BF16),
            pltpu.VMEM((8, wide), F32),
            slots, slots,
            dma((2, n)), dma((2, 2)), dma((2, 2, n)), dma((2, 2, n)), dma((2, 2, n)), dma((2, 2)),
        ],
        compiler_params=pltpu.CompilerParams(
            vmem_limit_bytes=62 * MIB, collective_id=6, has_side_effects=True
        ),
        name="recurrent_backward",
    )(
        g1, g1t, n1t, st, gate, r, g, cl, rec, br,
        ow[0], ow[1], wr[0], wr[1], wg[0], wg[1], rw, iw, cw, sp, x, gain, gain_two, up,
    )
    return (*outs[:-1], outs[-1][:rows])


def ring_kernel(n, count, *refs):
    own, other, refs = refs[:count], refs[count : 2 * count], refs[2 * count :]
    (gn1, out, stat, g1), refs = refs[:4], refs[4:]
    outs, refs = refs[:count], refs[count:]
    (gn1_p, out_p, stat_p, g1_p), scratch = refs[:4], refs[4:]
    piece_send, piece_recv = scratch[-2:]
    scratch = scratch[:-2]
    own_b, part_b, ring_b = scratch[:count], scratch[count : 2 * count], scratch[2 * count : 3 * count]
    own_sem, part_send, part_recv, rs_send, rs_recv, ag_send, ag_recv, put_sem = scratch[3 * count :]
    at = lax.axis_index("dp")
    core = lax.axis_index("rows")
    chip = lax.axis_index("cols")

    me, nexts = ring_place(n, at)
    barrier = pltpu.get_barrier_semaphore()
    for neighbour in nexts:
        pl.semaphore_signal(barrier, inc=1, device_id={"dp": neighbour})
    for peer in ((1 - core, chip), (core, 1 - chip), (1 - core, 1 - chip)):
        pl.semaphore_signal(barrier, inc=1, device_id={"rows": peer[0], "cols": peer[1]})
    pl.semaphore_wait(barrier, 5)

    half = gn1_p.shape[2]
    first, second = slice(0, half), slice(half, 2 * half)
    everything = slice(None)
    pieces = [
        (gn1, gn1_p, slice(None), first, second),
        (out, out_p, slice(None), first, second),
        (stat, stat_p, slice(None), everything, everything),
    ]
    singles = [(g1, slice(None))]
    diag = core == chip

    def piece_moves(m):
        src, dst, rows, mine, theirs = pieces[m]
        there = dst.at[chip, rows, :]
        sems = lambda w: (piece_send.at[m, w], piece_recv.at[m, chip])
        near = src.at[:, mine]
        away = src.at[:, theirs]
        return (
            pltpu.make_async_copy(near, there, piece_recv.at[m, chip]),
            pltpu.make_async_remote_copy(near, there, *sems(0), device_id={"cols": 1 - chip}),
            pltpu.make_async_remote_copy(away, there, *sems(1), device_id={"rows": 1 - core}),
            pltpu.make_async_remote_copy(
                away, there, *sems(1), device_id={"rows": 1 - core, "cols": 1 - chip}
            ),
        )

    def single_moves(m):
        src, rows = singles[m]
        there = g1_p.at[rows, :]
        at = len(pieces) + m
        return (
            pltpu.make_async_copy(src.at[:, first], there, piece_recv.at[at, 0]),
            pltpu.make_async_remote_copy(
                src.at[:, second], there, piece_send.at[at, 1], piece_recv.at[at, 0],
                device_id={"rows": 1 - core},
            ),
        )

    @pl.when(diag)
    def _():
        for m in range(len(pieces)):
            moves = piece_moves(m)
            moves[0].start()
            moves[2].start()
        for m in range(len(singles)):
            moves = single_moves(m)
            moves[0].start()
            moves[1].start()

    @pl.when(jnp.logical_not(diag))
    def _():
        for m in range(len(pieces)):
            moves = piece_moves(m)
            moves[1].start()
            moves[3].start()

    def rows_of(k, way, s):
        return ring_rows(n, me, own[k].shape[0], way, s)

    def cols_of(k, way):
        wide = own[k].shape[1] // 2
        return pl.ds(way * wide, wide)

    def own_copy(k, way, s):
        return pltpu.make_async_copy(
            own[k].at[rows_of(k, way, s), cols_of(k, way)], own_b[k].at[way, s], own_sem.at[k, way, s]
        )

    def part_copy(k, way, s):
        return pltpu.make_async_remote_copy(
            src_ref=other[k].at[rows_of(k, way, s), cols_of(k, way)],
            dst_ref=part_b[k].at[way, s],
            send_sem=part_send.at[k, way],
            recv_sem=part_recv.at[k, way, s],
            device_id={"rows": 1 - core},
        )

    def sum_copy(k, way, s):
        return pltpu.make_async_remote_copy(
            src_ref=ring_b[k].at[way, s],
            dst_ref=ring_b[k].at[way, s + 1],
            send_sem=rs_send.at[k, way],
            recv_sem=rs_recv.at[k, way, s],
            device_id={"dp": nexts[way]},
        )

    def first_gather(k, way):
        rows = rows_of(k, way, n - 1)
        return pltpu.make_async_remote_copy(
            src_ref=ring_b[k].at[way, n - 1],
            dst_ref=outs[k].at[rows, cols_of(k, way)],
            send_sem=ag_send.at[k, way, 0],
            recv_sem=ag_recv.at[k, way, 0],
            device_id={"dp": nexts[way]},
        )

    def gather_copy(k, way, s):
        rows = rows_of(k, way, s - 1)
        there = outs[k].at[rows, cols_of(k, way)]
        return pltpu.make_async_remote_copy(
            src_ref=there,
            dst_ref=there,
            send_sem=ag_send.at[k, way, s],
            recv_sem=ag_recv.at[k, way, s],
            device_id={"dp": nexts[way]},
        )

    def put_copy(k, way):
        return pltpu.make_async_copy(
            ring_b[k].at[way, n - 1],
            outs[k].at[rows_of(k, way, n - 1), cols_of(k, way)],
            put_sem.at[k, way],
        )

    both = [(k, way) for k in range(count) for way in range(2)]

    def load_step(s, _):
        for k, way in both:
            part_copy(k, way, s).start()
            own_copy(k, way, s).start()
        return 0

    lax.fori_loop(0, n, load_step, 0)

    def add_step(k, way, s, received):
        own_copy(k, way, s).wait()
        part_copy(k, way, s).wait_recv()
        total = own_b[k][way, s].astype(F32) + part_b[k][way, s].astype(F32)
        if received:
            sum_copy(k, way, s - 1).wait_recv()
            total = total + ring_b[k][way, s].astype(F32)
        ring_b[k][way, s] = total.astype(ring_b[k].dtype)

    for k, way in both:
        add_step(k, way, 0, False)
        sum_copy(k, way, 0).start()

    def sum_step(s, _):
        for k, way in both:
            add_step(k, way, s, True)
            sum_copy(k, way, s).start()
        return 0

    lax.fori_loop(1, n - 1, sum_step, 0)
    for k, way in both:
        add_step(k, way, n - 1, True)
        first_gather(k, way).start()
        put_copy(k, way).start()

    def gather_step(s, _):
        for k, way in both:
            gather_copy(k, way, s - 1).wait_recv()
            gather_copy(k, way, s).start()
        return 0

    for k, way in both:
        first_gather(k, way).wait_recv()
        gather_copy(k, way, 1).start()
    lax.fori_loop(2, n - 1, gather_step, 0)
    for k, way in both:
        gather_copy(k, way, n - 2).wait_recv()
        put_copy(k, way).wait()
        first_gather(k, way).wait_send()

    def drain_step(s, _):
        for k, way in both:
            gather_copy(k, way, s).wait_send()
        return 0

    lax.fori_loop(1, n - 1, drain_step, 0)
    for k, way in both:
        pltpu.make_async_remote_copy(
            ring_b[k].at[way, pl.ds(0, n - 1)],
            ring_b[k].at[way, pl.ds(1, n - 1)],
            rs_send.at[k, way],
            rs_recv.at[k, way, 0],
            device_id={"dp": nexts[way]},
        ).wait_send()
        pltpu.make_async_remote_copy(
            own_b[k].at[way],
            part_b[k].at[way],
            part_send.at[k, way],
            part_recv.at[k, way, 0],
            device_id={"rows": 1 - core},
        ).wait_send()

    for m in range(len(pieces)):
        src, dst, rows, mine, _ = pieces[m]
        for c in range(2):
            pltpu.make_async_copy(src.at[:, mine], dst.at[c, rows, :], piece_recv.at[m, c]).wait()
    for m in range(len(singles)):
        single_moves(m)[0].wait()

    @pl.when(diag)
    def _():
        for m in range(len(pieces)):
            piece_moves(m)[2].wait_send()
        for m in range(len(singles)):
            single_moves(m)[1].wait_send()

    @pl.when(jnp.logical_not(diag))
    def _():
        for m in range(len(pieces)):
            moves = piece_moves(m)
            moves[1].wait_send()
            moves[3].wait_send()


def ring_sum(n, own, other, pieces):
    count = len(own)
    own, other = list(own), list(other)
    rows = [a.shape[0] for a in own]
    unit = lambda a: (16 if a.dtype == BF16 else 8) * n
    pad = [-a.shape[0] % unit(a) for a in own]
    fit = lambda a, extra: jnp.pad(a, ((0, extra), (0, 0))) if extra else a
    own = [fit(a, e) for a, e in zip(own, pad)]
    other = [fit(a, e) for a, e in zip(other, pad)]
    slots = [pltpu.VMEM((2, n, a.shape[0] // n, a.shape[1] // 2), a.dtype) for a in own]
    sems = pltpu.SemaphoreType.DMA((count, 2, n))
    pair = pltpu.SemaphoreType.DMA((count, 2))
    tokens, wide = pieces[0].shape
    piece = jax.ShapeDtypeStruct((2, tokens, wide // 2), BF16)
    hbm = pl.BlockSpec(memory_space=pl.ANY)
    outs = pl.pallas_call(
        functools.partial(ring_kernel, n, count),
        in_specs=[hbm] * (2 * count + len(pieces)),
        out_specs=[hbm] * (count + 4),
        out_shape=[jax.ShapeDtypeStruct(a.shape, a.dtype) for a in own]
        + [
            piece,
            piece,
            jax.ShapeDtypeStruct((2, tokens, 128), F32),
            jax.ShapeDtypeStruct((tokens, wide // 2), BF16),
        ],
        scratch_shapes=slots * 3
        + [sems, pair, sems, pair] + [sems] * 3 + [pair]
        + [pltpu.SemaphoreType.DMA((4, 2))] * 2,
        compiler_params=pltpu.CompilerParams(
            collective_id=0, has_side_effects=True, vmem_limit_bytes=60 * MIB
        ),
        name="ring_sum",
    )(*own, *other, *pieces)
    return [a[:r] for a, r in zip(outs, rows)], outs[count:]


def final_kernel(gn, out, stat, g1, tokens, gain, live, result_o, grad_o):
    wide = 2 * tokens.shape[0]
    low = lambda ref: ref[0].astype(F32) + ref[1].astype(F32)
    result_o[...] = (low(out).T * live[...]).astype(BF16)
    grad = low(gn).T
    held = tokens[...].astype(F32)
    inner = (stat[0] + stat[1]).T[0:1, :]
    scale = stat[0].T[64:65, :]
    grad_o[...] = (
        g1[...].astype(F32).T
        + (scale * gain[...]) * grad
        - held * (scale * scale * scale * inner / wide)
    ).astype(BF16)


def final(gn, out, stat, g1, tokens, gain, live, chunk=256):
    half, length = tokens.shape
    pair = lambda cols: pl.BlockSpec((2, chunk, cols), lambda i: (0, i, 0))
    across = pl.BlockSpec((half, chunk), lambda i: (0, i))
    shape = jax.ShapeDtypeStruct((half, length), BF16)
    return pl.pallas_call(
        final_kernel,
        grid=(length // chunk,),
        in_specs=[
            pair(half), pair(half), pair(128),
            pl.BlockSpec((chunk, half), lambda i: (i, 0)),
            across,
            pl.BlockSpec((half, 1), lambda i: (0, 0)),
            pl.BlockSpec((1, chunk), lambda i: (0, i)),
        ],
        out_specs=[across, across],
        out_shape=[shape, shape],
        compiler_params=pltpu.CompilerParams(vmem_limit_bytes=48 * MIB),
        name="final",
    )(gn, out, stat, g1, tokens, gain, live)


def body(
    dp, tokens, lengths, mix_gain, rec_weight, gate_weight, conv_weight, conv_bias,
    recur_weight, recur_bias, input_weight, input_bias, decay_param, out_weight,
    ffn_gain, ffn_gate, ffn_up, ffn_down, cotangent,
):
    at_row = lax.axis_index("rows")
    at_col = lax.axis_index("cols")
    diag = at_row == at_col
    half = tokens.shape[0]
    wide = 2 * half

    both = lambda weight: (weight, swap(weight, "rows"))

    positions = jnp.arange(LEN, dtype=jnp.int32)
    live_core = (positions < lengths[at_row]).astype(BF16)[None, :]
    live_chip = (positions < lengths[at_col]).astype(F32)

    sp = jax.nn.softplus(-decay_param)[None, :]
    (x, n1t, rec, gate, cl, r, g, st, br, mixed, cot_a, far_a, wr_far, wg_far, ow_far) = rec_forward(
        tokens, cotangent, rec_weight, gate_weight, out_weight, mix_gain[:, None],
        recur_weight, input_weight, conv_weight, conv_bias[None, :], recur_bias[None, :],
        input_bias[None, :], sp,
    )
    wr = (rec_weight, wr_far)
    wg = (gate_weight, wg_far)
    ow = (out_weight, ow_far)
    fg = both(ffn_gate)
    fu = both(ffn_up)
    fd = both(ffn_down)
    gain_two = jnp.concatenate(both(ffn_gain))[None, :]
    gain_one = jnp.concatenate(both(mix_gain))[None, :]
    keep = diag.astype(F32).reshape(1, 1)

    out, up_sum, gg0, gg1, gd0, gd1, g1, g1t, grad_gain_two = ffn(
        x, mixed, live_core, gain_two, keep, fg, fu, fd, cotangent, far_a, cot_a
    )
    gn1_part, go0, go1, gr0, gr1, gt0, gt1, ggw, sums, stat, gains0, gains1, sum_up = rec_backward(
        g1, g1t, n1t, st, gate, r, g, cl, rec, br, ow, wr, wg, recur_weight,
        input_weight, conv_weight, sp, x, gain_one, grad_gain_two, up_sum, dp,
    )
    gates = ggw.reshape(-1, 256)
    own = [gd0, gg0, go0, gr0, gt0, gates, sums, gains0]
    other = [gd1, gg1, go1, gr1, gt1, gates, sums, gains1]
    total, moved = ring_sum(dp, own, other, [gn1_part, out, stat, g1])
    sum_down, sum_gate, sum_out, sum_rec, sum_gatew, gates, sums, gains = total
    result, grad_tokens = final(*moved, tokens, mix_gain[:, None], live_chip[None, :])
    gates = gates.astype(F32).reshape(ggw.shape)
    vec = jnp.sum(sums.reshape(8, 8, -1), axis=1)
    gains = jnp.sum(gains[:16].reshape(2, 8, half), axis=1)
    grad_gain_one = gains[0] + swap(gains[0], "cols")
    grad_decay = vec[2] * -jax.nn.sigmoid(-decay_param)
    return (
        result,
        grad_tokens,
        grad_gain_one,
        sum_rec.astype(F32),
        sum_gatew.astype(F32),
        vec[3:7],
        vec[7],
        gates[:, :, :128],
        vec[0],
        gates[:, :, 128:],
        vec[1],
        grad_decay,
        sum_out.astype(F32),
        gains[1],
        sum_gate.astype(F32),
        sum_up.astype(F32),
        sum_down.astype(F32),
    )


def solution(mesh):
    return jax.shard_map(
        functools.partial(body, mesh.shape["dp"]),
        mesh=mesh,
        in_specs=(
            P("rows", ("dp", "cols")),
            P("dp"),
            P("rows"),
            P("rows", "cols"),
            P("rows", "cols"),
            P(None, "cols"),
            P("cols"),
            P("cols", None, None),
            P("cols"),
            P("cols", None, None),
            P("cols"),
            P("cols"),
            P("rows", "cols"),
            P("rows"),
            P("rows", "cols"),
            P("rows", "cols"),
            P("rows", "cols"),
            P("rows", ("dp", "cols")),
        ),
        out_specs=(
            P("rows", ("dp", "cols")),
            P("rows", ("dp", "cols")),
            P("rows"),
            P("rows", "cols"),
            P("rows", "cols"),
            P(None, "cols"),
            P("cols"),
            P("cols", None, None),
            P("cols"),
            P("cols", None, None),
            P("cols"),
            P("cols"),
            P("rows", "cols"),
            P("rows"),
            P("rows", "cols"),
            P("rows", "cols"),
            P("rows", "cols"),
        ),
        check_vma=False,
    )
```

```python
import functools
import math

import jax
import jax.numpy as jnp
from jax import lax
from jax.experimental import pallas as pl
from jax.experimental.pallas import tpu as pltpu
from jax.sharding import PartitionSpec as P

D = 1536
KCONV = 4
LEN = 1024
BLOCK = 256
SEND_STEPS = (0, 8, 17)
GN_STEPS = (0, 6, 11)
BESIDE = 3
EPS = 1e-06
GATE_SCALE = 8.0
TANH_COEF = math.sqrt(2.0 / math.pi)
CUBIC_COEF = 0.044715
F32 = jnp.float32
BF16 = jnp.bfloat16
MIB = 1024 * 1024


def swap(value, axis):
    return lax.ppermute(value, axis, [(0, 1), (1, 0)])


def dot(left, right):
    return lax.dot_general(left, right, (((1,), (0,)), ((), ())), preferred_element_type=F32)


def dot_nt(left, right):
    return lax.dot_general(left, right, (((1,), (1,)), ((), ())), preferred_element_type=F32)


def dot_tn(left, right):
    return lax.dot_general(left, right, (((0,), (0,)), ((), ())), preferred_element_type=F32)


def gelu_act(values):
    inner_arg = TANH_COEF * (values + CUBIC_COEF * values * values * values)
    return 0.5 * values * (1.0 + jnp.tanh(inner_arg))


def gelu_pair(values):
    square = values * values
    tanh_val = jnp.tanh(values * (TANH_COEF + (TANH_COEF * CUBIC_COEF) * square))
    half_up = 0.5 + 0.5 * tanh_val
    slope = half_up + 0.5 * values * (1.0 - tanh_val * tanh_val) * (
        TANH_COEF + (3.0 * TANH_COEF * CUBIC_COEF) * square
    )
    return (values * half_up, slope)


def decay_terms(recur_gate, soft_decay):
    u = (2.0 * GATE_SCALE) * recur_gate * soft_decay
    decay = jnp.exp(-0.5 * u)
    series = u * (
        1.0
        - u
        * (0.5 - u * (1.0 / 6 - u * (1.0 / 24 - u * (1.0 / 120 - u * (1.0 / 720)))))
    )
    em = jnp.where(u < 0.25, series, 1.0 - decay * decay)
    return (decay, em)


def scan_tile(decay, drive, row):
    for shift in (1, 2, 4):
        keep = row >= shift
        before_a = jnp.where(keep, pltpu.roll(decay, shift, 0), 1.0)
        before_b = jnp.where(keep, pltpu.roll(drive, shift, 0), 0.0)
        drive = decay * before_b + drive
        decay = decay * before_a
    return (decay, drive)


def scan_tile_back(decay, drive, row):
    for shift in (1, 2, 4):
        keep = row < 8 - shift
        after_a = jnp.where(keep, pltpu.roll(decay, 8 - shift, 0), 1.0)
        after_b = jnp.where(keep, pltpu.roll(drive, 8 - shift, 0), 0.0)
        drive = decay * after_b + drive
        decay = decay * after_a
    return (decay, drive)


def group_barrier(core, chip):
    barrier = pltpu.get_barrier_semaphore()
    for peer in ((1 - core, chip), (core, 1 - chip), (1 - core, 1 - chip)):
        pl.semaphore_signal(barrier, inc=1, device_id={"rows": peer[0], "cols": peer[1]})
    pl.semaphore_wait(barrier, 3)


def rec_forward_kernel(
    chunk, count, cot_parts,
    tokens, cotangent, wr_h, wg_h, ow_h, gain_h, rw, iw, cw, cb, rb, ib, sp,
    x_o, n1t_o, rec_o, gate_o, cl_o, r_o, i_o, st_o, br_o, mix_o, cot_o, far_o, wr_o, wg_o, ow_o,
    tok_b, mix_s, wr, wg, ow, gain, gw, halo, carry, recpad, pre,
    tok_send, tok_recv, w_send, w_recv, w_own, cot_send, cot_recv, mix_send, mix_recv, put,
):
    step = pl.program_id(0)
    width = wr_h.shape[1]
    half = wr_h.shape[0]
    heads = width // 128
    core = lax.axis_index("rows")
    chip = lax.axis_index("cols")
    slot = lax.select(core == chip, 0, 1)
    near = {"rows": 1 - core}
    far = {"rows": chip, "cols": 1 - chip}

    def piece_moves(src, dst, send, recv):
        return (
            pltpu.make_async_copy(src, dst, recv),
            pltpu.make_async_remote_copy(src, dst, send.at[0], recv, device_id=near),
            pltpu.make_async_remote_copy(src, dst, send.at[1], recv, device_id=far),
        )

    def token_moves(k):
        return piece_moves(
            tokens.at[:, pl.ds(k * chunk, chunk)], tok_b.at[k, slot], tok_send.at[k], tok_recv.at[k, slot]
        )

    def cot_moves(k):
        return piece_moves(
            cotangent.at[:, pl.ds(k * chunk, chunk)],
            cot_o.at[slot, :, pl.ds(k * chunk, chunk)],
            cot_send.at[k],
            cot_recv.at[k, slot],
        )

    def mix_move(k):
        return pltpu.make_async_remote_copy(
            mix_s.at[k],
            far_o.at[pl.ds(k * chunk, chunk), :],
            mix_send.at[k],
            mix_recv.at[k],
            device_id={"cols": 1 - chip},
        )

    def start(moves):
        moves[2].start()

        @pl.when(core == chip)
        def _():
            moves[0].start()

        @pl.when(core != chip)
        def _():
            moves[1].start()

    def finish_send(moves):
        moves[2].wait_send()

        @pl.when(core != chip)
        def _():
            moves[1].wait_send()

    weights = ((wr_h, wr), (wg_h, wg), (ow_h, ow), (gain_h, gain))

    def weight_moves(n):
        src, dst = weights[n]
        return (
            pltpu.make_async_copy(src, dst.at[0], w_own.at[n]),
            pltpu.make_async_remote_copy(src, dst.at[1], w_send.at[n], w_recv.at[n], device_id=near),
        )

    def wait_weight(n):
        own, other = weight_moves(n)
        own.wait()
        other.wait_recv()

    @pl.when(step == 0)
    def _():
        group_barrier(core, chip)
        start(token_moves(0))
        for n in (3, 0, 1, 2):
            for move in weight_moves(n):
                move.start()
        for k in range(1, count):
            start(token_moves(k))
        halo[...] = jnp.zeros_like(halo)
        carry[...] = jnp.zeros_like(carry)
        for h in range(heads):
            gw[h, :, 0:128] = rw[h]
            gw[h, :, 128:256] = iw[h]
        wait_weight(3)

    for s in range(2):
        pltpu.make_async_copy(
            tokens.at[:, pl.ds(0, chunk)], tok_b.at[step, s], tok_recv.at[step, s]
        ).wait()

    @pl.when(step == count - 2)
    def _():
        for k in range(cot_parts):
            start(cot_moves(k))

    xt0 = tok_b[step, 0].astype(F32)
    xt1 = tok_b[step, 1].astype(F32)
    squares = jnp.sum(xt0 * xt0, axis=0, keepdims=True) + jnp.sum(xt1 * xt1, axis=0, keepdims=True)
    scale = lax.rsqrt(squares / (2 * half) + EPS)
    nt0 = (xt0 * scale * gain[0]).astype(BF16)
    nt1 = (xt1 * scale * gain[1]).astype(BF16)
    n1t_o[0:half, :] = nt0
    n1t_o[half:, :] = nt1
    x_o[:, 0:half] = tok_b[step, 0].T
    x_o[:, half:] = tok_b[step, 1].T
    low0 = nt0.T
    low1 = nt1.T

    @pl.when(step == 0)
    def _():
        wait_weight(0)
        wait_weight(1)

    rec = dot(low0, wr[0]) + dot(low1, wr[1])
    recpad[0:8, :] = halo[...]
    recpad[8:, :] = rec
    halo[...] = rec[chunk - 8 :, :]
    rec_o[...] = rec
    gate_o[...] = dot(low0, wg[0]) + dot(low1, wg[1])

    def conv_step(i, _):
        base = pl.multiple_of(i * 16, 16)
        for h in range(heads):
            sl = slice(h * 128, (h + 1) * 128)
            window = recpad[pl.ds(base, 24), sl]
            out = cb[:, sl] + cw[0:1, sl] * window[8:]
            for k in range(1, KCONV):
                out = out + cw[k : k + 1, sl] * pltpu.roll(window, k, 0)[8:]
            cl_o[pl.ds(base, 16), sl] = out.astype(BF16)
        return 0

    lax.fori_loop(0, chunk // 16, conv_step, 0)
    for h in range(heads):
        pre[:, h * 256 : (h + 1) * 256] = dot(cl_o[:, h * 128 : (h + 1) * 128], gw[h])
    row = lax.broadcasted_iota(jnp.int32, (8, 128), 0)

    def main_step(i, _):
        base = pl.multiple_of(i * 16, 16)
        rows = pl.ds(base, 16)
        for h in range(heads):
            sl = slice(h * 128, (h + 1) * 128)
            r = jax.nn.sigmoid(pre[rows, h * 256 : h * 256 + 128] + rb[:, sl])
            g = jax.nn.sigmoid(pre[rows, h * 256 + 128 : (h + 1) * 256] + ib[:, sl])
            conv = cl_o[rows, sl].astype(F32)
            decay, em = decay_terms(r, sp[:, sl])
            drive = jnp.sqrt(em) * g * conv
            r_o[rows, sl] = r
            i_o[rows, sl] = g
            held = carry[0:1, sl]
            parts = []
            for p in range(2):
                a, b = scan_tile(decay[p * 8 : p * 8 + 8], drive[p * 8 : p * 8 + 8], row)
                state = a * held + b
                held = state[7:8]
                parts.append(state)
            carry[0:1, sl] = held
            state = jnp.concatenate(parts, axis=0)
            st_o[rows, sl] = state
            br_o[rows, sl] = (state * gelu_act(gate_o[rows, sl])).astype(BF16)
        return 0

    lax.fori_loop(0, chunk // 16, main_step, 0)

    @pl.when(step == 0)
    def _():
        wait_weight(2)

    def put_moves():
        return [
            pltpu.make_async_copy(held.at[1], out, put.at[n])
            for n, (held, out) in enumerate(((wr, wr_o), (wg, wg_o), (ow, ow_o)))
        ]

    @pl.when(step == 0)
    def _():
        for move in put_moves():
            move.start()

    branch = br_o[...]
    mix_o[:, :half] = dot_nt(branch, ow[0]).astype(BF16)
    mix_o[:, half:] = dot_nt(branch, ow[1]).astype(BF16)

    for k in range(cot_parts):

        @pl.when(step == k)
        def _():
            mix_s[k] = mix_o[...]
            mix_move(k).start()

    @pl.when(step == count - 1)
    def _():
        for k in range(cot_parts):
            for s in range(2):
                pltpu.make_async_copy(
                    cotangent.at[:, pl.ds(0, chunk)],
                    cot_o.at[s, :, pl.ds(k * chunk, chunk)],
                    cot_recv.at[k, s],
                ).wait()
            finish_send(cot_moves(k))
            mix_move(k).wait()
        for k in range(count):
            finish_send(token_moves(k))
        for n in range(4):
            weight_moves(n)[1].wait_send()
        for move in put_moves():
            move.wait()


def rec_forward(tokens, cotangent, wr, wg, ow, gain, rw, iw, cw, cb, rb, ib, sp, chunk=256):
    half, length = tokens.shape
    width = wr.shape[1]
    heads = width // 128
    count = length // chunk
    cot_parts = 1
    wide = 2 * half
    row_block = lambda cols: pl.BlockSpec((chunk, cols), lambda i: (i, 0))
    whole = lambda shape: pl.BlockSpec(
        shape, lambda i: (0,) * len(shape), pipeline_mode=pl.Buffered(1)
    )
    hbm = pl.BlockSpec(memory_space=pl.ANY)
    f32 = jax.ShapeDtypeStruct((length, width), F32)
    low = jax.ShapeDtypeStruct((length, width), BF16)
    dma = pltpu.SemaphoreType.DMA
    return pl.pallas_call(
        functools.partial(rec_forward_kernel, chunk, count, cot_parts),
        grid=(count,),
        in_specs=[hbm] * 6
        + [whole((heads, 128, 128))] * 2
        + [whole((KCONV, width))]
        + [whole((1, width))] * 4,
        out_specs=[row_block(wide), pl.BlockSpec((wide, chunk), lambda i: (0, i))]
        + [row_block(width)] * 7
        + [row_block(wide)]
        + [hbm] * 5,
        out_shape=[
            jax.ShapeDtypeStruct((length, wide), BF16),
            jax.ShapeDtypeStruct((wide, length), BF16),
            f32, f32, low, f32, f32, f32, low,
            jax.ShapeDtypeStruct((length, wide), BF16),
            jax.ShapeDtypeStruct((2, half, cot_parts * chunk), BF16),
            jax.ShapeDtypeStruct((cot_parts * chunk, wide), BF16),
        ]
        + [jax.ShapeDtypeStruct((half, width), BF16)] * 3,
        scratch_shapes=[
            pltpu.VMEM((count, 2, half, chunk), BF16),
            pltpu.VMEM((cot_parts, chunk, wide), BF16),
            pltpu.VMEM((2, half, width), BF16),
            pltpu.VMEM((2, half, width), BF16),
            pltpu.VMEM((2, half, width), BF16),
            pltpu.VMEM((2, half, 1), F32),
            pltpu.VMEM((heads, 128, 256), BF16),
            pltpu.VMEM((8, width), F32),
            pltpu.VMEM((8, width), F32),
            pltpu.VMEM((chunk + 8, width), F32),
            pltpu.VMEM((chunk, 2 * width), F32),
            dma((count, 2)),
            dma((count, 2)),
            dma((4,)),
            dma((4,)),
            dma((4,)),
            dma((count, 2)),
            dma((count, 2)),
            dma((cot_parts,)),
            dma((cot_parts,)),
            dma((3,)),
        ],
        compiler_params=pltpu.CompilerParams(
            vmem_limit_bytes=60 * MIB, collective_id=2, has_side_effects=True
        ),
        name="recurrent_forward",
    )(tokens, cotangent, wr, wg, ow, gain, rw, iw, cw, cb, rb, ib, sp)


def norm_back_rows(rows, grad, held, cot, gain, gain_o, g1_o):
    wide = held.shape[1]
    scale = lax.rsqrt(jnp.sum(held * held, axis=1, keepdims=True) / wide + EPS)
    product = grad * held
    by_gain = product * scale
    gain_o[...] += by_gain[0:8] + by_gain[8:16]
    inner = jnp.sum(product * gain[...], axis=1, keepdims=True)
    grad_one = (
        cot.astype(F32)
        + scale * (grad * gain[...])
        - held * (scale * scale * scale * inner / wide)
    )
    g1_o[rows, :] = grad_one.astype(BF16)


def ffn_kernel(
    count, blocks,
    x, mix, lengths, gain, keep, wg0, wg1, wu0, wu1, wd0, wd1, mixed, cotangent, far_first, cot_first,
    out_o, gu_sum, gg_sum, gg0, gg1, gd0, gd1, g1_o, g1t_o, gain_o, gn_last, far_last, cot_last,
    far_s, ct_s, ctok_s, n2_s, n2t_s, hid_s, ga_s, gb_s, out_acc, gn_acc, gn_s, gn_far,
    keep_s, give_s, got_s,
    far_send, far_recv, ct_send, ct_recv, gn_send, gn_recv, up_send, up_recv, free_sem,
):
    step = pl.program_id(0)
    core, chip = lax.axis_index("rows"), lax.axis_index("cols")
    chunk, wide = n2_s.shape
    half, block = gg0.shape
    first_part = count * blocks
    slot = lax.select(core == chip, 0, 1)
    beside = {"cols": 1 - chip}

    def far_move(c):
        return pltpu.make_async_remote_copy(
            mixed.at[pl.ds(c * chunk, chunk), :], far_s.at[c], far_send.at[c], far_recv.at[c], device_id=beside
        )

    def far_load():
        return pltpu.make_async_copy(far_first, far_s.at[0], far_recv.at[0])

    def cot_moves(c):
        src = cotangent.at[:, pl.ds(c * chunk, chunk)]
        there = ct_s.at[slot, :, pl.ds(c * chunk, chunk)]
        return (
            pltpu.make_async_copy(src, there, ct_recv.at[c, slot]),
            pltpu.make_async_remote_copy(
                src, there, ct_send.at[c, 0], ct_recv.at[c, slot], device_id={"rows": 1 - core}
            ),
            pltpu.make_async_remote_copy(
                src, there, ct_send.at[c, 1], ct_recv.at[c, slot],
                device_id={"rows": chip, "cols": 1 - chip},
            ),
        )

    def cot_load(s):
        return pltpu.make_async_copy(
            cot_first.at[s], ct_s.at[s, :, pl.ds(0, chunk)], ct_recv.at[0, s]
        )

    def gn_move(c):
        return pltpu.make_async_remote_copy(
            gn_s.at[c], gn_far.at[c], gn_send.at[c], gn_recv.at[c], device_id=beside
        )

    def send_part(c):
        far_move(c).start()
        moves = cot_moves(c)
        moves[2].start()

        @pl.when(core == chip)
        def _():
            moves[0].start()

        @pl.when(core != chip)
        def _():
            moves[1].start()

    @pl.when(step == 0)
    def _():
        far_load().start()
        for s in range(2):
            cot_load(s).start()
        group_barrier(core, chip)
        gain_o[...] = jnp.zeros_like(gain_o)

    for c, at in enumerate(SEND_STEPS):

        @pl.when(step == at)
        def _():
            send_part(c + 1)

    def turned_cot(c):
        cols = pl.ds(pl.multiple_of(c * chunk, chunk), chunk)
        for s in range(2):
            ctok_s[:, s * half : (s + 1) * half] = ct_s[s, :, cols].T

    def norm_forward(c):
        cols = pl.ds(pl.multiple_of(c * chunk, chunk), chunk)
        slots = c * chunk + lax.broadcasted_iota(jnp.int32, (1, chunk), 1)
        live = (slots < lengths[core]).astype(F32).astype(BF16)
        pltpu.make_async_copy(far_first, far_s.at[c], far_recv.at[c]).wait()
        for s in range(2):
            pltpu.make_async_copy(
                cot_first.at[s], ct_s.at[s, :, cols], ct_recv.at[c, s]
            ).wait()
            ct_s[s, :, cols] = ct_s[s, :, cols] * live
        turned_cot(c)
        gn_acc[...] = jnp.zeros_like(gn_acc)

        def rows_step(i, _):
            rows = pl.ds(pl.multiple_of(i * 16, 16), 16)
            res = x[rows, :].astype(F32) + (mix[rows, :].astype(F32) + far_s[c, rows, :].astype(F32))
            out_acc[rows, :] = keep[...] * res
            scale = lax.rsqrt(jnp.sum(res * res, axis=1, keepdims=True) / wide + EPS)
            n2_s[rows, :] = (res * scale * gain[...]).astype(BF16)
            return 0

        lax.fori_loop(0, chunk // 16, rows_step, 0)
        n2t_s[:, cols] = n2_s[...].T

    @pl.when(step < first_part)
    def _():
        c = step // blocks
        blk = step % blocks
        rows = pl.ds(pl.multiple_of(c * chunk, chunk), chunk)

        @pl.when(blk == 0)
        def _():
            norm_forward(c)

        n0, n1 = n2_s[:, :half], n2_s[:, half:]
        c0, c1 = ctok_s[:, :half], ctok_s[:, half:]
        a = dot(n0, wg0[...]) + dot(n1, wg1[...])
        b = dot(n0, wu0[...]) + dot(n1, wu1[...])
        gh = dot(c0, wd0[...]) + dot(c1, wd1[...])
        act, slope = gelu_pair(a)
        hidden = (act * b).astype(BF16)
        ga = (gh * b * slope).astype(BF16)
        gb = (gh * act).astype(BF16)
        hid_s[blk, rows, :] = hidden
        ga_s[blk, rows, :] = ga
        gb_s[blk, rows, :] = gb
        out_acc[:, :half] += dot_nt(hidden, wd0[...])
        out_acc[:, half:] += dot_nt(hidden, wd1[...])
        gn_acc[:, :half] += dot_nt(ga, wg0[...]) + dot_nt(gb, wu0[...])
        gn_acc[:, half:] += dot_nt(ga, wg1[...]) + dot_nt(gb, wu1[...])

        @pl.when(blk == blocks - 1)
        def _():
            out_o[...] = out_acc[...].astype(BF16)
            gn_s[c] = gn_acc[...].astype(BF16)

        @pl.when(step == first_part - 1)
        def _():
            gn_last[...] = gn_s[count - 1]
            far_last[...] = far_s[count - 1]
            cot_last[...] = ctok_s[...]

    for c, at in enumerate(GN_STEPS):

        @pl.when(step == first_part - blocks + at)
        def _():
            gn_move(c).start()

    def norm_back(c):
        turned_cot(c)
        gn_move(c).wait_recv()

        def rows_step(i, _):
            rows = pl.ds(pl.multiple_of(i * 16, 16), 16)
            grad = gn_s[c, rows, :].astype(F32) + gn_far[c, rows, :].astype(F32)
            held = x[rows, :].astype(F32) + (mix[rows, :].astype(F32) + far_s[c, rows, :].astype(F32))
            norm_back_rows(rows, grad, held, ctok_s[rows, :], gain, gain_o, g1_o)
            return 0

        lax.fori_loop(0, chunk // 16, rows_step, 0)
        g1t_o[...] = g1_o[...].T

    def give(a, k):
        at = k % 2
        return pltpu.make_async_remote_copy(
            give_s.at[a, at], got_s.at[a, at], up_send.at[a, at], up_recv.at[a, at],
            device_id={"rows": 1 - core},
        )

    k = step - first_part
    shared = ((gb_s, gu_sum, blocks), (ga_s, gg_sum, BESIDE))
    for a, (_, total_o, many) in enumerate(shared):

        @pl.when(jnp.logical_and(k > 0, k <= many))
        def _():
            give(a, k - 1).wait()
            at = (k - 1) % 2
            total_o[...] = (keep_s[a, at].astype(F32) + got_s[a, at].astype(F32)).astype(BF16)

            @pl.when(k - 1 < many - 2)
            def _():
                pl.semaphore_signal(free_sem.at[a], inc=1, device_id={"rows": 1 - core})

        @pl.when(jnp.logical_and(k >= 0, k < many))
        def _():
            grad = shared[a][0][k]
            give_s[a, k % 2] = dot(n2t_s[half:], grad).astype(BF16)

            @pl.when(k >= 2)
            def _():
                pl.semaphore_wait(free_sem.at[a], 1)

            give(a, k).start()
            keep_s[a, k % 2] = dot(n2t_s[:half], grad).astype(BF16)

    @pl.when(jnp.logical_and(k >= BESIDE, k < blocks))
    def _():
        gg0[...] = dot(n2t_s[:half], ga_s[k]).astype(BF16)
        gg1[...] = dot(n2t_s[half:], ga_s[k]).astype(BF16)

    @pl.when(jnp.logical_and(k >= 0, k < blocks))
    def _():
        gd0[...] = dot(ct_s[0], hid_s[k]).astype(BF16)
        gd1[...] = dot(ct_s[1], hid_s[k]).astype(BF16)

    for c in range(count - 1):

        @pl.when(k == 3 * (c + 1))
        def _():
            norm_back(c)

    @pl.when(k == blocks)
    def _():
        for c in range(count - 1):
            gn_move(c).wait_send()
        for c in range(1, count):
            far_move(c).wait_send()
            moves = cot_moves(c)
            moves[2].wait_send()

            @pl.when(core != chip)
            def _():
                moves[1].wait_send()


def ffn(x, mix, lengths, gain, keep, wg, wu, wd, cotangent, far_first, cot_first, chunk=256, block=BLOCK):
    tokens, wide = x.shape
    half, width = wg[0].shape
    count, blocks = tokens // chunk, width // block
    first_part = count * blocks
    whole = lambda shape: pl.BlockSpec(
        shape, lambda i: (0,) * len(shape), pipeline_mode=pl.Buffered(1)
    )
    hbm = pl.BlockSpec(memory_space=pl.ANY)

    def back_chunk(i):
        return jnp.clip((i - first_part - 1) // 3, 0, count - 2)

    def chunk_at(i):
        return jnp.where(i < first_part, i // blocks, back_chunk(i))

    rows = pl.BlockSpec((chunk, wide), lambda i: (chunk_at(i), 0))
    weight = pl.BlockSpec(
        (half, block), lambda i: (0, jnp.where(i < first_part, i % blocks, blocks - 1))
    )
    grad_at = lambda late, many: pl.BlockSpec(
        (half, block), lambda i: (0, jnp.clip(i - first_part - late, 0, many - 1))
    )
    grad = lambda many: jax.ShapeDtypeStruct((half, many * block), BF16)
    low = jax.ShapeDtypeStruct((tokens, wide), BF16)
    part = pltpu.VMEM((count, chunk, wide), BF16)
    middle = pltpu.VMEM((blocks, tokens, block), BF16)
    pair = pltpu.VMEM((2, 2, half, block), BF16)
    dma = pltpu.SemaphoreType.DMA
    return pl.pallas_call(
        functools.partial(ffn_kernel, count, blocks),
        grid=(first_part + blocks + 1,),
        in_specs=[rows, rows, pl.BlockSpec(memory_space=pltpu.SMEM), whole((1, wide)), whole((1, 1))]
        + [weight] * 6
        + [hbm] * 4,
        out_specs=[
            pl.BlockSpec((chunk, wide), lambda i: (jnp.minimum(i // blocks, count - 1), 0)),
            grad_at(1, blocks),
            grad_at(1, BESIDE),
        ]
        + [grad_at(BESIDE, blocks - BESIDE)] * 2
        + [grad_at(0, blocks)] * 2
        + [
            pl.BlockSpec((chunk, wide), lambda i: (back_chunk(i), 0)),
            pl.BlockSpec((wide, chunk), lambda i: (0, back_chunk(i))),
            whole((8, wide)),
        ]
        + [whole((chunk, wide))] * 3,
        out_shape=[low]
        + [grad(blocks), grad(BESIDE)]
        + [grad(blocks - BESIDE)] * 2
        + [grad(blocks)] * 2
        + [
            jax.ShapeDtypeStruct((tokens - chunk, wide), BF16),
            jax.ShapeDtypeStruct((wide, tokens - chunk), BF16),
            jax.ShapeDtypeStruct((8, wide), F32),
        ]
        + [jax.ShapeDtypeStruct((chunk, wide), BF16)] * 3,
        scratch_shapes=[
            part,
            pltpu.VMEM((2, half, tokens), BF16),
            pltpu.VMEM((chunk, wide), BF16),
            pltpu.VMEM((chunk, wide), BF16),
            pltpu.VMEM((wide, tokens), BF16),
            middle, middle, middle,
            pltpu.VMEM((chunk, wide), F32),
            pltpu.VMEM((chunk, wide), F32),
            part, part,
            pair, pair, pair,
            dma((count,)), dma((count,)),
            dma((count, 2)), dma((count, 2)),
            dma((count,)), dma((count,)),
            dma((2, 2)), dma((2, 2)),
            pltpu.SemaphoreType.REGULAR((2,)),
        ],
        compiler_params=pltpu.CompilerParams(
            vmem_limit_bytes=62 * MIB, collective_id=3, has_side_effects=True
        ),
        name="ffn",
    )(
        x, mix, lengths, gain, keep, wg[0], wg[1], wu[0], wu[1], wd[0], wd[1],
        mix, cotangent, far_first, cot_first,
    )


def ring_place(n, at):
    def index_of(place):
        return lax.select(place < n // 2, 2 * place, 2 * (n - 1 - place) + 1)

    me = lax.select(at % 2 == 0, at // 2, n - 1 - at // 2)
    return me, (index_of(lax.rem(me + 1, n)), index_of(lax.rem(me + n - 1, n)))


def ring_rows(n, me, total, way, s):
    size = total // n
    chunk = lax.rem(me + n - s, n) if way == 0 else lax.rem(me + s, n)
    return pl.ds(pl.multiple_of(chunk * size, size), size)


def ring_beside(n, owns, out, own_b, ring_b, own_sem, rs_send, rs_recv, ag_send, ag_recv, put_sem):
    me, nexts = ring_place(n, lax.axis_index("dp"))
    wide = out.shape[1] // 2
    cut = (wide // 128 + 1) // 2 * 128
    groups = (pl.ds(0, cut), pl.ds(cut, wide - cut))
    both = [(g, way) for g in range(2) for way in range(2)]
    per = -(-n // 8)
    per_gather = -(-(n - 2) // 6)
    rows_of = lambda way, s: ring_rows(n, me, out.shape[0], way, s)
    cols_of = lambda g, way: pl.ds(way * wide + g * cut, wide - cut if g else cut)

    def own_copies(way, s):
        moves, at = [], 0
        for m, own in enumerate(owns):
            size = own.shape[1] // 2
            moves.append(
                pltpu.make_async_copy(
                    own.at[rows_of(way, s), pl.ds(way * size, size)],
                    own_b.at[way, s % 2, :, pl.ds(at, size)],
                    own_sem.at[m, way, s % 2],
                )
            )
            at += size
        return moves

    def sum_copy(g, way, s):
        return pltpu.make_async_remote_copy(
            ring_b.at[way, s, :, groups[g]], ring_b.at[way, s + 1, :, groups[g]],
            rs_send.at[g, way], rs_recv.at[g, way, s], device_id={"dp": nexts[way]},
        )

    def first_gather(g, way):
        return pltpu.make_async_remote_copy(
            ring_b.at[way, n - 1, :, groups[g]], out.at[rows_of(way, n - 1), cols_of(g, way)],
            ag_send.at[g, way, 0], ag_recv.at[g, way, 0], device_id={"dp": nexts[way]},
        )

    def gather_copy(g, way, s):
        there = out.at[rows_of(way, s - 1), cols_of(g, way)]
        return pltpu.make_async_remote_copy(
            there, there, ag_send.at[g, way, s], ag_recv.at[g, way, s], device_id={"dp": nexts[way]}
        )

    def put_copy(g, way):
        return pltpu.make_async_copy(
            ring_b.at[way, n - 1, :, groups[g]],
            out.at[rows_of(way, n - 1), cols_of(g, way)],
            put_sem.at[g, way],
        )

    def begin(chip):
        barrier = pltpu.get_barrier_semaphore()
        for neighbour in nexts:
            pl.semaphore_signal(barrier, inc=1, device_id={"dp": neighbour})
        pl.semaphore_signal(barrier, inc=1, device_id={"cols": 1 - chip})
        for s in range(2):
            for way in range(2):
                for move in own_copies(way, s):
                    move.start()
        pl.semaphore_wait(barrier, 3)

    def sum_step(g, s):
        for way in range(2):
            if g == 0:
                for move in own_copies(way, s):
                    move.wait()

            @pl.when(s == 0)
            def _():
                ring_b[way, s, :, groups[g]] = own_b[way, s % 2, :, groups[g]]

            @pl.when(s > 0)
            def _():
                sum_copy(g, way, s - 1).wait_recv()
                total = ring_b[way, s, :, groups[g]].astype(F32) + own_b[
                    way, s % 2, :, groups[g]
                ].astype(F32)
                ring_b[way, s, :, groups[g]] = total.astype(BF16)

            @pl.when(s < n - 1)
            def _():
                sum_copy(g, way, s).start()

            @pl.when(s == n - 1)
            def _():
                first_gather(g, way).start()
                put_copy(g, way).start()

            if g == 1:

                @pl.when(s < n - 2)
                def _():
                    for move in own_copies(way, s + 2):
                        move.start()

    def gather_step(g, s):
        for way in range(2):

            @pl.when(s == 1)
            def _():
                first_gather(g, way).wait_recv()

            @pl.when(s > 1)
            def _():
                gather_copy(g, way, s - 1).wait_recv()

            gather_copy(g, way, s).start()

    def tick(g, t):
        if per > 1 and g == 0:
            return
        turns = (0, 1) if per > 1 else (g,)

        def run(step):
            def once(s, _):
                for turn in turns:
                    step(turn, s)
                return 0

            return once

        @pl.when(t < 8)
        def _():
            lax.fori_loop(t * per, jnp.minimum((t + 1) * per, n), run(sum_step), 0)

        @pl.when(t >= 8)
        def _():
            start = 1 + (t - 8) * per_gather
            lax.fori_loop(start, jnp.minimum(start + per_gather, n - 1), run(gather_step), 0)

    def end():
        for g, way in both:
            gather_copy(g, way, n - 2).wait_recv()
            put_copy(g, way).wait()
            first_gather(g, way).wait_send()
            pltpu.make_async_remote_copy(
                ring_b.at[way, pl.ds(0, n - 1), :, groups[g]],
                ring_b.at[way, pl.ds(1, n - 1), :, groups[g]],
                rs_send.at[g, way], rs_recv.at[g, way, 0], device_id={"dp": nexts[way]},
            ).wait_send()

        def drain(s, _):
            for g, way in both:
                gather_copy(g, way, s).wait_send()
            return 0

        lax.fori_loop(1, n - 1, drain, 0)

    return begin, tick, end


def rec_backward_kernel(
    tile, n,
    n1t, st, gate, r_in, i_in, cl, rec, br, ow0, ow1, wr0, wr1, wg0, wg1, rw, iw, cw, sp,
    x, gain, gain_second, gain_two, up, gate_own, g1_head, g1t_head, mixed, gn_last, far_last, cot_last,
    gn1_o, go0, go1, gr0, gr1, gg0, gg1, ggw, small0, small1, stat, up_o, g1_last,
    acc, gb_s, gc_s, ggp_s, grp_s, gip_s, grec_s, gain_s, sums, g1, g1t, gain_b,
    gn_s, gn_far, mix_s, far_s, cot_s, load_sem, gn_send, gn_recv, put_last, *ring_refs
):
    step = pl.program_id(0)
    tokens, block = gb_s.shape
    wide = n1t.shape[0]
    heads = block // 128
    half = ow0.shape[0]
    tiles = tokens // tile
    subs = tile // 8

    begin, tick, end = ring_beside(n, (up, gate_own), up_o, *ring_refs)

    chunk = gn_s.shape[0]
    head = tokens - chunk
    chip = lax.axis_index("cols")
    gn_move = pltpu.make_async_remote_copy(
        gn_last, gn_far, gn_send.at[0], gn_recv.at[0], device_id={"cols": 1 - chip}
    )
    last_put = pltpu.make_async_copy(g1.at[pl.ds(head, chunk), :], g1_last, put_last.at[0])
    beat = lambda at: tick(at % 2, 3 + step * 3 + at // 2)

    @pl.when(step == 0)
    def _():
        loads = [
            pltpu.make_async_copy(src, dst, load_sem.at[m])
            for m, (src, dst) in enumerate(
                (
                    (mixed.at[pl.ds(head, chunk), :], mix_s),
                    (far_last, far_s),
                    (cot_last, cot_s),
                    (gn_last, gn_s),
                    (g1_head, g1.at[pl.ds(0, head), :]),
                    (g1t_head, g1t.at[:, pl.ds(0, head)]),
                )
            )
        ]
        for move in loads:
            move.start()
        begin(chip)
        gn_move.start()
        acc[...] = jnp.zeros_like(acc)
        small0[...] = jnp.zeros_like(small0)
        small1[...] = jnp.zeros_like(small1)
        gain_b[...] = gain_two[...]
        for t in range(3):
            for g in range(2):
                tick(g, t)
        for move in loads:
            move.wait()
        gn_move.wait()

        def rows_step(i, _):
            base = pl.multiple_of(i * 16, 16)
            rows = pl.ds(base, 16)
            grad = gn_s[rows, :].astype(F32) + gn_far[rows, :].astype(F32)
            held = x[pl.ds(head + base, 16), :].astype(F32) + (
                mix_s[rows, :].astype(F32) + far_s[rows, :].astype(F32)
            )
            norm_back_rows(pl.ds(head + base, 16), grad, held, cot_s[rows, :], gain_second, gain_b, g1)
            return 0

        lax.fori_loop(0, chunk // 16, rows_step, 0)
        g1t[:, head:] = g1[head:, :].T
        last_put.start()

    beat(0)
    gb_s[...] = dot(g1[:, :half], ow0[...]) + dot(g1[:, half:], ow1[...])
    beat(1)
    go0[...] = dot(g1t[:half], br[...]).astype(BF16)
    go1[...] = dot(g1t[half:], br[...]).astype(BF16)
    beat(2)
    sums[...] = jnp.zeros_like(sums)
    row = lax.broadcasted_iota(jnp.int32, (8, 128), 0)

    def back_step(j, held):
        @pl.when(j == tiles // 2)
        def _():
            beat(3)

        i = tiles - 1 - j
        base = pl.multiple_of(i * tile, tile)
        rows = pl.ds(base, tile)
        before = pl.ds(pl.multiple_of(jnp.maximum(base - 8, 0), 8), 8)
        out = []
        for h in range(heads):
            sl = slice(h * 128, (h + 1) * 128)
            later_decay, later_carried = held[h]
            grad_branch = gb_s[rows, sl]
            act, slope = gelu_pair(gate[rows, sl])
            state = st[rows, sl]
            ggp_s[rows, sl] = (grad_branch * state * slope).astype(BF16)
            grad_state = grad_branch * act
            r = r_in[rows, sl]
            soft = sp[:, sl]
            decay, em = decay_terms(r, soft)
            parts = [None] * subs
            for p in range(subs - 1, -1, -1):
                own = decay[p * 8 : p * 8 + 8]
                after = jnp.where(row == 7, later_decay, pltpu.roll(own, 7, 0))
                a, b = scan_tile_back(after, grad_state[p * 8 : p * 8 + 8], row)
                carried = a * later_carried + b
                later_decay = own[0:1]
                later_carried = carried[0:1]
                parts[p] = carried
            out.append((later_decay, later_carried))
            carried = jnp.concatenate(parts, axis=0)
            edge = jnp.where(i > 0, st[before, sl][7:8], 0.0)
            prev = []
            for p in range(subs):
                prev.append(jnp.where(row == 0, edge, pltpu.roll(state[p * 8 : p * 8 + 8], 1, 0)))
                edge = state[p * 8 + 7 : p * 8 + 8]
            prev = jnp.concatenate(prev, axis=0)
            g = i_in[rows, sl]
            conv = cl[rows, sl].astype(F32)
            scaling = jnp.sqrt(em)
            gated = g * conv
            grad_log = carried * (prev * decay - gated * (decay * decay) / scaling)
            grad_soft = grad_log * (-GATE_SCALE * r)
            grp = grad_soft * soft * (1.0 - r)
            cs = carried * scaling
            gc_s[rows, sl] = cs * g
            gip = cs * gated * (1.0 - g)
            grp_s[rows, sl] = grp.astype(BF16)
            gip_s[rows, sl] = gip.astype(BF16)
            for n, term in enumerate((grp, gip, grad_soft)):
                total = term[0:8]
                for p in range(1, subs):
                    total = total + term[p * 8 : p * 8 + 8]
                sums[n * 8 : n * 8 + 8, sl] += total
        return tuple(out)

    zero = jnp.zeros((1, 128), F32)
    lax.fori_loop(0, tiles, back_step, tuple((zero, zero) for _ in range(heads)))
    beat(4)
    for h in range(heads):
        sl = slice(h * 128, (h + 1) * 128)
        low = cl[:, sl]
        ggw[h, :, 0:128] = dot_tn(low, grp_s[:, sl]).astype(BF16)
        ggw[h, :, 128:256] = dot_tn(low, gip_s[:, sl]).astype(BF16)
        gc_s[:, sl] += dot_nt(grp_s[:, sl], rw[h]) + dot_nt(gip_s[:, sl], iw[h])

    def conv_step(j, held):
        i = tiles - 1 - j
        base = pl.multiple_of(i * tile, tile)
        rows = pl.ds(base, tile)
        before = pl.ds(pl.multiple_of(jnp.maximum(base - 8, 0), 8), 8)
        out = []
        for h in range(heads):
            sl = slice(h * 128, (h + 1) * 128)
            grad_conv = gc_s[rows, sl]
            window = jnp.concatenate([grad_conv, held[h]], axis=0)
            out.append(grad_conv[0:8])
            grad_rec = cw[0:1, sl] * grad_conv
            for k in range(1, KCONV):
                grad_rec = grad_rec + cw[k : k + 1, sl] * pltpu.roll(window, tile + 8 - k, 0)[:tile]
            grec_s[rows, sl] = grad_rec.astype(BF16)
            edge = jnp.where(i > 0, rec[before, sl], 0.0)
            past = jnp.concatenate([edge, rec[rows, sl]], axis=0)
            terms = [grad_conv * past[8:]]
            for k in range(1, KCONV):
                terms.append(grad_conv * pltpu.roll(past, k, 0)[8:])
            terms.append(grad_conv)
            for n, term in enumerate(terms):
                total = term[0:8]
                for p in range(1, subs):
                    total = total + term[p * 8 : p * 8 + 8]
                sums[24 + n * 8 : 32 + n * 8, sl] += total
        return tuple(out)

    lax.fori_loop(0, tiles, conv_step, tuple(jnp.zeros((8, 128), F32) for _ in range(heads)))
    beat(5)
    all_heads = small0.shape[0] // 8
    head_row = lax.broadcasted_iota(jnp.int32, (all_heads, 128), 0)
    for n in range(8):
        vector = jnp.sum(sums[n * 8 : n * 8 + 8, :], axis=0, keepdims=True)
        for h in range(heads):
            at = slice(n * all_heads, (n + 1) * all_heads)
            mine = vector[:, h * 128 : (h + 1) * 128]
            tile_now = jnp.where(head_row == step * heads + h, mine, small0[at, 0:128])
            small0[at, 0:128] = tile_now
            small1[at, 0:128] = tile_now
    grad_rec = grec_s[...]
    grad_gate = ggp_s[...]
    gr0[...] = dot(n1t[:half], grad_rec).astype(BF16)
    gr1[...] = dot(n1t[half:], grad_rec).astype(BF16)
    gg0[...] = dot(n1t[:half], grad_gate).astype(BF16)
    gg1[...] = dot(n1t[half:], grad_gate).astype(BF16)
    acc[:, :half] += dot_nt(grad_rec, wr0[...]) + dot_nt(grad_gate, wg0[...])
    acc[:, half:] += dot_nt(grad_rec, wr1[...]) + dot_nt(grad_gate, wg1[...])

    @pl.when(step == pl.num_programs(0) - 1)
    def _():
        gain_s[...] = jnp.zeros_like(gain_s)

        def stat_step(i, _):
            rows = pl.ds(pl.multiple_of(i * 32, 32), 32)
            part = acc[rows, :]
            gn1_o[rows, :] = part.astype(BF16)
            held = x[rows, :].astype(F32)
            scale = lax.rsqrt(jnp.sum(held * held, axis=1, keepdims=True) / wide + EPS)
            product = part * held
            by_gain = product * scale
            gain_s[...] += (by_gain[0:8] + by_gain[8:16]) + (by_gain[16:24] + by_gain[24:32])
            inner = jnp.sum(product * gain[...], axis=1, keepdims=True)
            stat[rows, 0:64] = jnp.broadcast_to(inner, (32, 64))
            stat[rows, 64:128] = jnp.broadcast_to(scale, (32, 64))
            return 0

        lax.fori_loop(0, tokens // 32, stat_step, 0)
        for n, held in enumerate((gain_s, gain_b)):
            vector = jnp.sum(held[...], axis=0, keepdims=True)
            for m in range(half // 128):
                at = n * 8 + m
                small0[at : at + 1, 128:] = vector[:, m * 128 : (m + 1) * 128]
                small1[at : at + 1, 128:] = vector[:, half + m * 128 : half + (m + 1) * 128]
        last_put.wait()
        end()


def rec_backward(
    n1t, st, gate, r, g, cl, rec, br, ow, wr, wg, rw, iw, cw, sp, x, gain, gain_second, gain_two,
    up, gate_own, lasts, n, block=256, tile=64
):
    wide, tokens = n1t.shape
    half, width = wr[0].shape
    heads = block // 128
    rows = up.shape[0]
    up, gate_own = (jnp.pad(a, ((0, -rows % (16 * n)), (0, 0))) for a in (up, gate_own))
    side = (up.shape[0], up.shape[1] + gate_own.shape[1])
    small = (8 * (width // 128), 256)
    chunk = lasts[-1].shape[0]
    slots = lambda many: pltpu.VMEM((2, many, side[0] // n, side[1] // 2), BF16)
    dma = pltpu.SemaphoreType.DMA
    hbm = pl.BlockSpec(memory_space=pl.ANY)
    whole = lambda shape: pl.BlockSpec(shape, lambda i: (0, 0), pipeline_mode=pl.Buffered(1))
    act = pl.BlockSpec((tokens, block), lambda i: (0, i))
    weight = pl.BlockSpec((half, block), lambda i: (0, i))
    thin = lambda n: pl.BlockSpec((n, block), lambda i: (0, i))
    gate_block = pl.BlockSpec((heads, 128, 256), lambda i: (i, 0, 0))
    grad = jax.ShapeDtypeStruct((half, width), BF16)
    outs = pl.pallas_call(
        functools.partial(rec_backward_kernel, tile, n),
        grid=(width // block,),
        in_specs=[whole((wide, tokens))]
        + [act] * 7
        + [weight] * 6
        + [pl.BlockSpec((heads, 128, 128), lambda i: (i, 0, 0))] * 2
        + [thin(KCONV), thin(1)]
        + [whole((tokens, wide)), whole((1, wide)), whole((1, wide)), whole((8, wide))]
        + [hbm] * 8,
        out_specs=[whole((tokens, wide))]
        + [weight] * 6
        + [gate_block, whole(small), whole(small), whole((tokens, 128)), hbm, hbm],
        out_shape=[jax.ShapeDtypeStruct((tokens, wide), BF16)]
        + [grad] * 6
        + [
            jax.ShapeDtypeStruct((width // 128, 128, 256), BF16),
            jax.ShapeDtypeStruct(small, F32),
            jax.ShapeDtypeStruct(small, F32),
            jax.ShapeDtypeStruct((tokens, 128), F32),
            jax.ShapeDtypeStruct(side, BF16),
            jax.ShapeDtypeStruct((chunk, wide), BF16),
        ],
        scratch_shapes=[
            pltpu.VMEM((tokens, wide), F32),
            pltpu.VMEM((tokens, block), F32),
            pltpu.VMEM((tokens, block), F32),
            pltpu.VMEM((tokens, block), BF16),
            pltpu.VMEM((tokens, block), BF16),
            pltpu.VMEM((tokens, block), BF16),
            pltpu.VMEM((tokens, block), BF16),
            pltpu.VMEM((8, wide), F32),
            pltpu.VMEM((64, block), F32),
            pltpu.VMEM((tokens, wide), BF16),
            pltpu.VMEM((wide, tokens), BF16),
            pltpu.VMEM((8, wide), F32),
        ]
        + [pltpu.VMEM((chunk, wide), BF16)] * 5
        + [
            dma((6,)), dma((1,)), dma((1,)), dma((1,)),
            slots(2), slots(n),
            dma((2, 2, 2)), dma((2, 2)), dma((2, 2, n)), dma((2, 2, n)), dma((2, 2, n)), dma((2, 2)),
        ],
        compiler_params=pltpu.CompilerParams(
            vmem_limit_bytes=62 * MIB, collective_id=6, has_side_effects=True
        ),
        name="recurrent_backward",
    )(
        n1t, st, gate, r, g, cl, rec, br,
        ow[0], ow[1], wr[0], wr[1], wg[0], wg[1], rw, iw, cw, sp, x, gain, gain_second, gain_two,
        up, gate_own, *lasts,
    )
    return (*outs[:-2], outs[-2][:rows], outs[-1])


def ring_kernel(n, count, *refs):
    own, other, refs = refs[:count], refs[count : 2 * count], refs[2 * count :]
    (gn1, out, stat, g1_head, g1_last), refs = refs[:5], refs[5:]
    outs, refs = refs[:count], refs[count:]
    (gn1_p, out_p, stat_p, g1_p), scratch = refs[:4], refs[4:]
    piece_send, piece_recv = scratch[-2:]
    scratch = scratch[:-2]
    own_b, part_b, ring_b = scratch[:count], scratch[count : 2 * count], scratch[2 * count : 3 * count]
    own_sem, part_send, part_recv, rs_send, rs_recv, ag_send, ag_recv, put_sem = scratch[3 * count :]
    at = lax.axis_index("dp")
    core = lax.axis_index("rows")
    chip = lax.axis_index("cols")

    me, nexts = ring_place(n, at)
    barrier = pltpu.get_barrier_semaphore()
    for neighbour in nexts:
        pl.semaphore_signal(barrier, inc=1, device_id={"dp": neighbour})
    for peer in ((1 - core, chip), (core, 1 - chip), (1 - core, 1 - chip)):
        pl.semaphore_signal(barrier, inc=1, device_id={"rows": peer[0], "cols": peer[1]})
    pl.semaphore_wait(barrier, 5)

    half = gn1_p.shape[2]
    first, second = slice(0, half), slice(half, 2 * half)
    everything = slice(None)
    pieces = [
        (gn1, gn1_p, slice(None), first, second),
        (out, out_p, slice(None), first, second),
        (stat, stat_p, slice(None), everything, everything),
    ]
    head = g1_head.shape[0]
    singles = [(g1_head, slice(0, head)), (g1_last, slice(head, gn1.shape[0]))]
    diag = core == chip

    def piece_moves(m):
        src, dst, rows, mine, theirs = pieces[m]
        there = dst.at[chip, rows, :]
        sems = lambda w: (piece_send.at[m, w], piece_recv.at[m, chip])
        near = src.at[:, mine]
        away = src.at[:, theirs]
        return (
            pltpu.make_async_copy(near, there, piece_recv.at[m, chip]),
            pltpu.make_async_remote_copy(near, there, *sems(0), device_id={"cols": 1 - chip}),
            pltpu.make_async_remote_copy(away, there, *sems(1), device_id={"rows": 1 - core}),
            pltpu.make_async_remote_copy(
                away, there, *sems(1), device_id={"rows": 1 - core, "cols": 1 - chip}
            ),
        )

    def single_moves(m):
        src, rows = singles[m]
        there = g1_p.at[rows, :]
        at = len(pieces) + m
        return (
            pltpu.make_async_copy(src.at[:, first], there, piece_recv.at[at, 0]),
            pltpu.make_async_remote_copy(
                src.at[:, second], there, piece_send.at[at, 1], piece_recv.at[at, 0],
                device_id={"rows": 1 - core},
            ),
        )

    @pl.when(diag)
    def _():
        for m in range(len(pieces)):
            moves = piece_moves(m)
            moves[0].start()
            moves[2].start()
        for m in range(len(singles)):
            moves = single_moves(m)
            moves[0].start()
            moves[1].start()

    @pl.when(jnp.logical_not(diag))
    def _():
        for m in range(len(pieces)):
            moves = piece_moves(m)
            moves[1].start()
            moves[3].start()

    def rows_of(k, way, s):
        return ring_rows(n, me, own[k].shape[0], way, s)

    def cols_of(k, way):
        wide = own[k].shape[1] // 2
        return pl.ds(way * wide, wide)

    def own_copy(k, way, s):
        return pltpu.make_async_copy(
            own[k].at[rows_of(k, way, s), cols_of(k, way)], own_b[k].at[way, s], own_sem.at[k, way, s]
        )

    def part_copy(k, way, s):
        return pltpu.make_async_remote_copy(
            src_ref=other[k].at[rows_of(k, way, s), cols_of(k, way)],
            dst_ref=part_b[k].at[way, s],
            send_sem=part_send.at[k, way],
            recv_sem=part_recv.at[k, way, s],
            device_id={"rows": 1 - core},
        )

    def sum_copy(k, way, s):
        return pltpu.make_async_remote_copy(
            src_ref=ring_b[k].at[way, s],
            dst_ref=ring_b[k].at[way, s + 1],
            send_sem=rs_send.at[k, way],
            recv_sem=rs_recv.at[k, way, s],
            device_id={"dp": nexts[way]},
        )

    def first_gather(k, way):
        rows = rows_of(k, way, n - 1)
        return pltpu.make_async_remote_copy(
            src_ref=ring_b[k].at[way, n - 1],
            dst_ref=outs[k].at[rows, cols_of(k, way)],
            send_sem=ag_send.at[k, way, 0],
            recv_sem=ag_recv.at[k, way, 0],
            device_id={"dp": nexts[way]},
        )

    def gather_copy(k, way, s):
        rows = rows_of(k, way, s - 1)
        there = outs[k].at[rows, cols_of(k, way)]
        return pltpu.make_async_remote_copy(
            src_ref=there,
            dst_ref=there,
            send_sem=ag_send.at[k, way, s],
            recv_sem=ag_recv.at[k, way, s],
            device_id={"dp": nexts[way]},
        )

    def put_copy(k, way):
        return pltpu.make_async_copy(
            ring_b[k].at[way, n - 1],
            outs[k].at[rows_of(k, way, n - 1), cols_of(k, way)],
            put_sem.at[k, way],
        )

    both = [(k, way) for k in range(count) for way in range(2)]

    def load_step(s, _):
        for k, way in both:
            part_copy(k, way, s).start()
            own_copy(k, way, s).start()
        return 0

    lax.fori_loop(0, n, load_step, 0)

    def add_step(k, way, s, received):
        own_copy(k, way, s).wait()
        part_copy(k, way, s).wait_recv()
        total = own_b[k][way, s].astype(F32) + part_b[k][way, s].astype(F32)
        if received:
            sum_copy(k, way, s - 1).wait_recv()
            total = total + ring_b[k][way, s].astype(F32)
        ring_b[k][way, s] = total.astype(ring_b[k].dtype)

    for k, way in both:
        add_step(k, way, 0, False)
        sum_copy(k, way, 0).start()

    def sum_step(s, _):
        for k, way in both:
            add_step(k, way, s, True)
            sum_copy(k, way, s).start()
        return 0

    lax.fori_loop(1, n - 1, sum_step, 0)
    for k, way in both:
        add_step(k, way, n - 1, True)
        first_gather(k, way).start()
        put_copy(k, way).start()

    def gather_step(s, _):
        for k, way in both:
            gather_copy(k, way, s - 1).wait_recv()
            gather_copy(k, way, s).start()
        return 0

    for k, way in both:
        first_gather(k, way).wait_recv()
        gather_copy(k, way, 1).start()
    lax.fori_loop(2, n - 1, gather_step, 0)
    for k, way in both:
        gather_copy(k, way, n - 2).wait_recv()
        put_copy(k, way).wait()
        first_gather(k, way).wait_send()

    def drain_step(s, _):
        for k, way in both:
            gather_copy(k, way, s).wait_send()
        return 0

    lax.fori_loop(1, n - 1, drain_step, 0)
    for k, way in both:
        pltpu.make_async_remote_copy(
            ring_b[k].at[way, pl.ds(0, n - 1)],
            ring_b[k].at[way, pl.ds(1, n - 1)],
            rs_send.at[k, way],
            rs_recv.at[k, way, 0],
            device_id={"dp": nexts[way]},
        ).wait_send()
        pltpu.make_async_remote_copy(
            own_b[k].at[way],
            part_b[k].at[way],
            part_send.at[k, way],
            part_recv.at[k, way, 0],
            device_id={"rows": 1 - core},
        ).wait_send()

    for m in range(len(pieces)):
        src, dst, rows, mine, _ = pieces[m]
        for c in range(2):
            pltpu.make_async_copy(src.at[:, mine], dst.at[c, rows, :], piece_recv.at[m, c]).wait()
    for m in range(len(singles)):
        single_moves(m)[0].wait()

    @pl.when(diag)
    def _():
        for m in range(len(pieces)):
            piece_moves(m)[2].wait_send()
        for m in range(len(singles)):
            single_moves(m)[1].wait_send()

    @pl.when(jnp.logical_not(diag))
    def _():
        for m in range(len(pieces)):
            moves = piece_moves(m)
            moves[1].wait_send()
            moves[3].wait_send()


def ring_sum(n, own, other, pieces):
    count = len(own)
    own, other = list(own), list(other)
    rows = [a.shape[0] for a in own]
    unit = lambda a: (16 if a.dtype == BF16 else 8) * n
    pad = [-a.shape[0] % unit(a) for a in own]
    fit = lambda a, extra: jnp.pad(a, ((0, extra), (0, 0))) if extra else a
    own = [fit(a, e) for a, e in zip(own, pad)]
    other = [fit(a, e) for a, e in zip(other, pad)]
    slots = [pltpu.VMEM((2, n, a.shape[0] // n, a.shape[1] // 2), a.dtype) for a in own]
    sems = pltpu.SemaphoreType.DMA((count, 2, n))
    pair = pltpu.SemaphoreType.DMA((count, 2))
    tokens, wide = pieces[0].shape
    piece = jax.ShapeDtypeStruct((2, tokens, wide // 2), BF16)
    hbm = pl.BlockSpec(memory_space=pl.ANY)
    outs = pl.pallas_call(
        functools.partial(ring_kernel, n, count),
        in_specs=[hbm] * (2 * count + len(pieces)),
        out_specs=[hbm] * (count + 4),
        out_shape=[jax.ShapeDtypeStruct(a.shape, a.dtype) for a in own]
        + [
            piece,
            piece,
            jax.ShapeDtypeStruct((2, tokens, 128), F32),
            jax.ShapeDtypeStruct((tokens, wide // 2), BF16),
        ],
        scratch_shapes=slots * 3
        + [sems, pair, sems, pair] + [sems] * 3 + [pair]
        + [pltpu.SemaphoreType.DMA((5, 2))] * 2,
        compiler_params=pltpu.CompilerParams(
            collective_id=0, has_side_effects=True, vmem_limit_bytes=60 * MIB
        ),
        name="ring_sum",
    )(*own, *other, *pieces)
    return [a[:r] for a, r in zip(outs, rows)], outs[count:]


def final_kernel(
    gn, out, stat, g1, tokens, gain, lengths, beside, down, gate, out_w, rec_w, gate_w,
    result_o, grad_o, up_o, gate_o, down_o, out_w_o, rec_w_o, gate_w_o,
):
    wide = 2 * tokens.shape[0]
    low = lambda ref: ref[0].astype(F32) + ref[1].astype(F32)
    chunk = tokens.shape[1]
    slots = pl.program_id(0) * chunk + lax.broadcasted_iota(jnp.int32, (1, chunk), 1)
    live = (slots < lengths[lax.axis_index("cols")]).astype(F32)
    result_o[...] = (low(out).T * live).astype(BF16)
    grad = low(gn).T
    held = tokens[...].astype(F32)
    inner = (stat[0] + stat[1]).T[0:1, :]
    scale = stat[0].T[64:65, :]
    grad_o[...] = (
        g1[...].astype(F32).T
        + (scale * gain[...]) * grad
        - held * (scale * scale * scale * inner / wide)
    ).astype(BF16)
    side = beside.shape[1] // 2
    up_half = up_o.shape[1] // 2
    gate_half = side - up_half
    for way in range(2):
        at = way * side
        up_o[:, way * up_half : (way + 1) * up_half] = beside[:, at : at + up_half].astype(F32)
        gate_o[:, way * gate_half : (way + 1) * gate_half] = beside[:, at + up_half : at + side].astype(F32)
    gate_o[:, 2 * gate_half :] = gate[...].astype(F32)
    for src, dst in ((down, down_o), (out_w, out_w_o), (rec_w, rec_w_o), (gate_w, gate_w_o)):
        dst[...] = src[...].astype(F32)


def final(gn, out, stat, g1, tokens, gain, lengths, beside, down, gate, out_w, rec_w, gate_w, steps=8):
    half, length = tokens.shape
    chunk, size = length // steps, half // steps
    pair = lambda cols: pl.BlockSpec((2, chunk, cols), lambda i: (0, i, 0))
    across = pl.BlockSpec((half, chunk), lambda i: (0, i))
    rows = lambda cols: pl.BlockSpec((size, cols), lambda i: (i, 0))
    shape = jax.ShapeDtypeStruct((half, length), BF16)
    ffn_wide, wide = down.shape[1], out_w.shape[1]
    grads = [ffn_wide] * 3 + [wide] * 3
    return pl.pallas_call(
        final_kernel,
        grid=(steps,),
        in_specs=[
            pair(half), pair(half), pair(128),
            pl.BlockSpec((chunk, half), lambda i: (i, 0)),
            across,
            pl.BlockSpec((half, 1), lambda i: (0, 0)),
            pl.BlockSpec(memory_space=pltpu.SMEM),
        ]
        + [rows(a.shape[1]) for a in (beside, down, gate, out_w, rec_w, gate_w)],
        out_specs=[across, across] + [rows(cols) for cols in grads],
        out_shape=[shape, shape] + [jax.ShapeDtypeStruct((half, cols), F32) for cols in grads],
        compiler_params=pltpu.CompilerParams(vmem_limit_bytes=56 * MIB),
        name="final",
    )(gn, out, stat, g1, tokens, gain, lengths, beside, down, gate, out_w, rec_w, gate_w)


def body(
    dp, tokens, lengths, mix_gain, rec_weight, gate_weight, conv_weight, conv_bias,
    recur_weight, recur_bias, input_weight, input_bias, decay_param, out_weight,
    ffn_gain, ffn_gate, ffn_up, ffn_down, cotangent,
):
    at_row = lax.axis_index("rows")
    at_col = lax.axis_index("cols")
    diag = at_row == at_col
    half = tokens.shape[0]
    wide = 2 * half

    both = lambda weight: (weight, swap(weight, "rows"))

    sp = jax.nn.softplus(-decay_param)[None, :]
    (x, n1t, rec, gate, cl, r, g, st, br, mixed, cot_a, far_a, wr_far, wg_far, ow_far) = rec_forward(
        tokens, cotangent, rec_weight, gate_weight, out_weight, mix_gain[:, None],
        recur_weight, input_weight, conv_weight, conv_bias[None, :], recur_bias[None, :],
        input_bias[None, :], sp,
    )
    wr = (rec_weight, wr_far)
    wg = (gate_weight, wg_far)
    ow = (out_weight, ow_far)
    fg = both(ffn_gate)
    fu = both(ffn_up)
    fd = both(ffn_down)
    gain_two = jnp.concatenate(both(ffn_gain))[None, :]
    gain_one = jnp.concatenate(both(mix_gain))[None, :]
    keep = diag.astype(F32).reshape(1, 1)

    out, up_own, gate_own, gg0, gg1, gd0, gd1, g1_head, g1t_head, grad_gain_two, *lasts = ffn(
        x, mixed, lengths, gain_two, keep, fg, fu, fd, cotangent, far_a, cot_a
    )
    gn1_part, go0, go1, gr0, gr1, gt0, gt1, ggw, small0, small1, stat, beside, g1_last = rec_backward(
        n1t, st, gate, r, g, cl, rec, br, ow, wr, wg, recur_weight, input_weight, conv_weight, sp,
        x, gain_one, gain_two, grad_gain_two, up_own, gate_own, [g1_head, g1t_head, mixed, *lasts], dp,
    )
    gates = ggw.reshape(-1, 256)
    total, moved = ring_sum(
        dp,
        [gd0, gg0, go0, gr0, gt0, gates, small0],
        [gd1, gg1, go1, gr1, gt1, gates, small1],
        [gn1_part, out, stat, g1_head, g1_last],
    )
    gates, small = total[5:]
    result, grad_tokens, sum_up, sum_gate, sum_down, sum_out, sum_rec, sum_gatew = final(
        *moved, tokens, mix_gain[:, None], lengths, beside, *total[:5]
    )
    gates = gates.astype(F32).reshape(ggw.shape)
    vec = small[:, :128].reshape(8, -1)
    gains = small[:16, 128:].reshape(2, -1)[:, :half]
    grad_gain_one = gains[0] + swap(gains[0], "cols")
    grad_decay = vec[2] * -jax.nn.sigmoid(-decay_param)
    return (
        result,
        grad_tokens,
        grad_gain_one,
        sum_rec,
        sum_gatew,
        vec[3:7],
        vec[7],
        gates[:, :, :128],
        vec[0],
        gates[:, :, 128:],
        vec[1],
        grad_decay,
        sum_out,
        gains[1],
        sum_gate,
        sum_up,
        sum_down,
    )


def solution(mesh):
    return jax.shard_map(
        functools.partial(body, mesh.shape["dp"]),
        mesh=mesh,
        in_specs=(
            P("rows", ("dp", "cols")),
            P("dp"),
            P("rows"),
            P("rows", "cols"),
            P("rows", "cols"),
            P(None, "cols"),
            P("cols"),
            P("cols", None, None),
            P("cols"),
            P("cols", None, None),
            P("cols"),
            P("cols"),
            P("rows", "cols"),
            P("rows"),
            P("rows", "cols"),
            P("rows", "cols"),
            P("rows", "cols"),
            P("rows", ("dp", "cols")),
        ),
        out_specs=(
            P("rows", ("dp", "cols")),
            P("rows", ("dp", "cols")),
            P("rows"),
            P("rows", "cols"),
            P("rows", "cols"),
            P(None, "cols"),
            P("cols"),
            P("cols", None, None),
            P("cols"),
            P("cols", None, None),
            P("cols"),
            P("cols"),
            P("rows", "cols"),
            P("rows"),
            P("rows", "cols"),
            P("rows", "cols"),
            P("rows", "cols"),
        ),
        check_vma=False,
    )
```

```python
import functools
import math

import jax
import jax.numpy as jnp
from jax import lax
from jax.experimental import pallas as pl
from jax.experimental.pallas import tpu as pltpu
from jax.sharding import PartitionSpec as P

D = 1536
KCONV = 4
LEN = 1024
BLOCK = 256
SEND_STEPS = (0, 8, 17)
GN_STEPS = (0, 6, 11)
BESIDE = 3
EPS = 1e-06
GATE_SCALE = 8.0
TANH_COEF = math.sqrt(2.0 / math.pi)
CUBIC_COEF = 0.044715
F32 = jnp.float32
BF16 = jnp.bfloat16
MIB = 1024 * 1024


def swap(value, axis):
    return lax.ppermute(value, axis, [(0, 1), (1, 0)])


def dot(left, right):
    return lax.dot_general(left, right, (((1,), (0,)), ((), ())), preferred_element_type=F32)


def dot_nt(left, right):
    return lax.dot_general(left, right, (((1,), (1,)), ((), ())), preferred_element_type=F32)


def dot_tn(left, right):
    return lax.dot_general(left, right, (((0,), (0,)), ((), ())), preferred_element_type=F32)


def gelu_act(values):
    inner_arg = TANH_COEF * (values + CUBIC_COEF * values * values * values)
    return 0.5 * values * (1.0 + jnp.tanh(inner_arg))


def gelu_pair(values):
    square = values * values
    tanh_val = jnp.tanh(values * (TANH_COEF + (TANH_COEF * CUBIC_COEF) * square))
    half_up = 0.5 + 0.5 * tanh_val
    slope = half_up + 0.5 * values * (1.0 - tanh_val * tanh_val) * (
        TANH_COEF + (3.0 * TANH_COEF * CUBIC_COEF) * square
    )
    return (values * half_up, slope)


def decay_terms(recur_gate, soft_decay):
    u = (2.0 * GATE_SCALE) * recur_gate * soft_decay
    decay = jnp.exp(-0.5 * u)
    series = u * (
        1.0
        - u
        * (0.5 - u * (1.0 / 6 - u * (1.0 / 24 - u * (1.0 / 120 - u * (1.0 / 720)))))
    )
    em = jnp.where(u < 0.25, series, 1.0 - decay * decay)
    return (decay, em)


def scan_tile(decay, drive, row):
    for shift in (1, 2, 4):
        keep = row >= shift
        before_a = jnp.where(keep, pltpu.roll(decay, shift, 0), 1.0)
        before_b = jnp.where(keep, pltpu.roll(drive, shift, 0), 0.0)
        drive = decay * before_b + drive
        decay = decay * before_a
    return (decay, drive)


def scan_tile_back(decay, drive, row):
    for shift in (1, 2, 4):
        keep = row < 8 - shift
        after_a = jnp.where(keep, pltpu.roll(decay, 8 - shift, 0), 1.0)
        after_b = jnp.where(keep, pltpu.roll(drive, 8 - shift, 0), 0.0)
        drive = decay * after_b + drive
        decay = decay * after_a
    return (decay, drive)


def group_barrier(core, chip):
    barrier = pltpu.get_barrier_semaphore()
    for peer in ((1 - core, chip), (core, 1 - chip), (1 - core, 1 - chip)):
        pl.semaphore_signal(barrier, inc=1, device_id={"rows": peer[0], "cols": peer[1]})
    pl.semaphore_wait(barrier, 3)


def rec_forward_kernel(
    chunk, count, cot_parts,
    tokens, cotangent, wr_h, wg_h, ow_h, gain_h, rw, iw, cw, cb, rb, ib, sp,
    x_o, n1t_o, rec_o, gate_o, cl_o, r_o, i_o, st_o, br_o, mix_o, cot_o, far_o, wr_o, wg_o, ow_o,
    tok_b, mix_s, wr, wg, ow, gain, gw, halo, carry, recpad, pre,
    tok_send, tok_recv, w_send, w_recv, w_own, cot_send, cot_recv, mix_send, mix_recv, put,
):
    step = pl.program_id(0)
    width = wr_h.shape[1]
    half = wr_h.shape[0]
    heads = width // 128
    core = lax.axis_index("rows")
    chip = lax.axis_index("cols")
    slot = lax.select(core == chip, 0, 1)
    near = {"rows": 1 - core}
    far = {"rows": chip, "cols": 1 - chip}

    def piece_moves(src, dst, send, recv):
        return (
            pltpu.make_async_copy(src, dst, recv),
            pltpu.make_async_remote_copy(src, dst, send.at[0], recv, device_id=near),
            pltpu.make_async_remote_copy(src, dst, send.at[1], recv, device_id=far),
        )

    def token_moves(k):
        return piece_moves(
            tokens.at[:, pl.ds(k * chunk, chunk)], tok_b.at[k, slot], tok_send.at[k], tok_recv.at[k, slot]
        )

    def cot_moves(k):
        return piece_moves(
            cotangent.at[:, pl.ds(k * chunk, chunk)],
            cot_o.at[slot, :, pl.ds(k * chunk, chunk)],
            cot_send.at[k],
            cot_recv.at[k, slot],
        )

    def mix_move(k):
        return pltpu.make_async_remote_copy(
            mix_s.at[k],
            far_o.at[pl.ds(k * chunk, chunk), :],
            mix_send.at[k],
            mix_recv.at[k],
            device_id={"cols": 1 - chip},
        )

    def start(moves):
        moves[2].start()

        @pl.when(core == chip)
        def _():
            moves[0].start()

        @pl.when(core != chip)
        def _():
            moves[1].start()

    def finish_send(moves):
        moves[2].wait_send()

        @pl.when(core != chip)
        def _():
            moves[1].wait_send()

    weights = ((wr_h, wr), (wg_h, wg), (ow_h, ow), (gain_h, gain))

    def weight_moves(n):
        src, dst = weights[n]
        return (
            pltpu.make_async_copy(src, dst.at[0], w_own.at[n]),
            pltpu.make_async_remote_copy(src, dst.at[1], w_send.at[n], w_recv.at[n], device_id=near),
        )

    def wait_weight(n):
        own, other = weight_moves(n)
        own.wait()
        other.wait_recv()

    @pl.when(step == 0)
    def _():
        group_barrier(core, chip)
        start(token_moves(0))
        for n in (3, 0, 1, 2):
            for move in weight_moves(n):
                move.start()
        for k in range(1, count):
            start(token_moves(k))
        halo[...] = jnp.zeros_like(halo)
        carry[...] = jnp.zeros_like(carry)
        for h in range(heads):
            gw[h, :, 0:128] = rw[h]
            gw[h, :, 128:256] = iw[h]
        wait_weight(3)

    for s in range(2):
        pltpu.make_async_copy(
            tokens.at[:, pl.ds(0, chunk)], tok_b.at[step, s], tok_recv.at[step, s]
        ).wait()

    @pl.when(step == count - 2)
    def _():
        for k in range(cot_parts):
            start(cot_moves(k))

    xt0 = tok_b[step, 0].astype(F32)
    xt1 = tok_b[step, 1].astype(F32)
    squares = jnp.sum(xt0 * xt0, axis=0, keepdims=True) + jnp.sum(xt1 * xt1, axis=0, keepdims=True)
    scale = lax.rsqrt(squares / (2 * half) + EPS)
    nt0 = (xt0 * scale * gain[0]).astype(BF16)
    nt1 = (xt1 * scale * gain[1]).astype(BF16)
    n1t_o[0:half, :] = nt0
    n1t_o[half:, :] = nt1
    x_o[:, 0:half] = tok_b[step, 0].T
    x_o[:, half:] = tok_b[step, 1].T
    low0 = nt0.T
    low1 = nt1.T

    @pl.when(step == 0)
    def _():
        wait_weight(0)
        wait_weight(1)

    rec = dot(low0, wr[0]) + dot(low1, wr[1])
    recpad[0:8, :] = halo[...]
    recpad[8:, :] = rec
    halo[...] = rec[chunk - 8 :, :]
    rec_o[...] = rec
    gate_o[...] = dot(low0, wg[0]) + dot(low1, wg[1])

    def conv_step(i, _):
        base = pl.multiple_of(i * 16, 16)
        for h in range(heads):
            sl = slice(h * 128, (h + 1) * 128)
            window = recpad[pl.ds(base, 24), sl]
            out = cb[:, sl] + cw[0:1, sl] * window[8:]
            for k in range(1, KCONV):
                out = out + cw[k : k + 1, sl] * pltpu.roll(window, k, 0)[8:]
            cl_o[pl.ds(base, 16), sl] = out.astype(BF16)
        return 0

    lax.fori_loop(0, chunk // 16, conv_step, 0)
    for h in range(heads):
        pre[:, h * 256 : (h + 1) * 256] = dot(cl_o[:, h * 128 : (h + 1) * 128], gw[h])
    row = lax.broadcasted_iota(jnp.int32, (8, 128), 0)

    def main_step(i, _):
        base = pl.multiple_of(i * 16, 16)
        rows = pl.ds(base, 16)
        for h in range(heads):
            sl = slice(h * 128, (h + 1) * 128)
            r = jax.nn.sigmoid(pre[rows, h * 256 : h * 256 + 128] + rb[:, sl])
            g = jax.nn.sigmoid(pre[rows, h * 256 + 128 : (h + 1) * 256] + ib[:, sl])
            conv = cl_o[rows, sl].astype(F32)
            decay, em = decay_terms(r, sp[:, sl])
            drive = jnp.sqrt(em) * g * conv
            r_o[rows, sl] = r
            i_o[rows, sl] = g
            held = carry[0:1, sl]
            parts = []
            for p in range(2):
                a, b = scan_tile(decay[p * 8 : p * 8 + 8], drive[p * 8 : p * 8 + 8], row)
                state = a * held + b
                held = state[7:8]
                parts.append(state)
            carry[0:1, sl] = held
            state = jnp.concatenate(parts, axis=0)
            st_o[rows, sl] = state
            br_o[rows, sl] = (state * gelu_act(gate_o[rows, sl])).astype(BF16)
        return 0

    lax.fori_loop(0, chunk // 16, main_step, 0)

    @pl.when(step == 0)
    def _():
        wait_weight(2)

    def put_moves():
        return [
            pltpu.make_async_copy(held.at[1], out, put.at[n])
            for n, (held, out) in enumerate(((wr, wr_o), (wg, wg_o), (ow, ow_o)))
        ]

    @pl.when(step == 0)
    def _():
        for move in put_moves():
            move.start()

    branch = br_o[...]
    mix_o[:, :half] = dot_nt(branch, ow[0]).astype(BF16)
    mix_o[:, half:] = dot_nt(branch, ow[1]).astype(BF16)

    for k in range(cot_parts):

        @pl.when(step == k)
        def _():
            mix_s[k] = mix_o[...]
            mix_move(k).start()

    @pl.when(step == count - 1)
    def _():
        for k in range(cot_parts):
            for s in range(2):
                pltpu.make_async_copy(
                    cotangent.at[:, pl.ds(0, chunk)],
                    cot_o.at[s, :, pl.ds(k * chunk, chunk)],
                    cot_recv.at[k, s],
                ).wait()
            finish_send(cot_moves(k))
            mix_move(k).wait()
        for k in range(count):
            finish_send(token_moves(k))
        for n in range(4):
            weight_moves(n)[1].wait_send()
        for move in put_moves():
            move.wait()


def rec_forward(tokens, cotangent, wr, wg, ow, gain, rw, iw, cw, cb, rb, ib, sp, chunk=256):
    half, length = tokens.shape
    width = wr.shape[1]
    heads = width // 128
    count = length // chunk
    cot_parts = 1
    wide = 2 * half
    row_block = lambda cols: pl.BlockSpec((chunk, cols), lambda i: (i, 0))
    whole = lambda shape: pl.BlockSpec(
        shape, lambda i: (0,) * len(shape), pipeline_mode=pl.Buffered(1)
    )
    hbm = pl.BlockSpec(memory_space=pl.ANY)
    f32 = jax.ShapeDtypeStruct((length, width), F32)
    low = jax.ShapeDtypeStruct((length, width), BF16)
    dma = pltpu.SemaphoreType.DMA
    return pl.pallas_call(
        functools.partial(rec_forward_kernel, chunk, count, cot_parts),
        grid=(count,),
        in_specs=[hbm] * 6
        + [whole((heads, 128, 128))] * 2
        + [whole((KCONV, width))]
        + [whole((1, width))] * 4,
        out_specs=[row_block(wide), pl.BlockSpec((wide, chunk), lambda i: (0, i))]
        + [row_block(width)] * 7
        + [row_block(wide)]
        + [hbm] * 5,
        out_shape=[
            jax.ShapeDtypeStruct((length, wide), BF16),
            jax.ShapeDtypeStruct((wide, length), BF16),
            f32, f32, low, f32, f32, f32, low,
            jax.ShapeDtypeStruct((length, wide), BF16),
            jax.ShapeDtypeStruct((2, half, cot_parts * chunk), BF16),
            jax.ShapeDtypeStruct((cot_parts * chunk, wide), BF16),
        ]
        + [jax.ShapeDtypeStruct((half, width), BF16)] * 3,
        scratch_shapes=[
            pltpu.VMEM((count, 2, half, chunk), BF16),
            pltpu.VMEM((cot_parts, chunk, wide), BF16),
            pltpu.VMEM((2, half, width), BF16),
            pltpu.VMEM((2, half, width), BF16),
            pltpu.VMEM((2, half, width), BF16),
            pltpu.VMEM((2, half, 1), F32),
            pltpu.VMEM((heads, 128, 256), BF16),
            pltpu.VMEM((8, width), F32),
            pltpu.VMEM((8, width), F32),
            pltpu.VMEM((chunk + 8, width), F32),
            pltpu.VMEM((chunk, 2 * width), F32),
            dma((count, 2)),
            dma((count, 2)),
            dma((4,)),
            dma((4,)),
            dma((4,)),
            dma((count, 2)),
            dma((count, 2)),
            dma((cot_parts,)),
            dma((cot_parts,)),
            dma((3,)),
        ],
        compiler_params=pltpu.CompilerParams(
            vmem_limit_bytes=60 * MIB, collective_id=2, has_side_effects=True
        ),
        name="recurrent_forward",
    )(tokens, cotangent, wr, wg, ow, gain, rw, iw, cw, cb, rb, ib, sp)


def norm_back_rows(rows, grad, held, cot, gain, gain_o, g1_o):
    wide = held.shape[1]
    scale = lax.rsqrt(jnp.sum(held * held, axis=1, keepdims=True) / wide + EPS)
    product = grad * held
    by_gain = product * scale
    gain_o[...] += by_gain[0:8] + by_gain[8:16]
    inner = jnp.sum(product * gain[...], axis=1, keepdims=True)
    grad_one = (
        cot.astype(F32)
        + scale * (grad * gain[...])
        - held * (scale * scale * scale * inner / wide)
    )
    g1_o[rows, :] = grad_one.astype(BF16)


def ffn_kernel(
    count, blocks,
    x, mix, lengths, gain, keep, wg0, wg1, wu0, wu1, wd0, wd1, mixed, cotangent, far_first, cot_first,
    out_o, gu_sum, gg_sum, gg0, gg1, gd0, gd1, g1_o, g1t_o, gain_o, gn_last, far_last, cot_last,
    far_s, ct_s, ctok_s, n2_s, n2t_s, hid_s, ga_s, gb_s, out_acc, gn_acc, gn_s, gn_far,
    keep_s, give_s, got_s,
    far_send, far_recv, ct_send, ct_recv, gn_send, gn_recv, up_send, up_recv, free_sem,
):
    step = pl.program_id(0)
    core, chip = lax.axis_index("rows"), lax.axis_index("cols")
    chunk, wide = n2_s.shape
    half, block = gg0.shape
    first_part = count * blocks
    slot = lax.select(core == chip, 0, 1)
    beside = {"cols": 1 - chip}

    def far_move(c):
        return pltpu.make_async_remote_copy(
            mixed.at[pl.ds(c * chunk, chunk), :], far_s.at[c], far_send.at[c], far_recv.at[c], device_id=beside
        )

    def far_load():
        return pltpu.make_async_copy(far_first, far_s.at[0], far_recv.at[0])

    def cot_moves(c):
        src = cotangent.at[:, pl.ds(c * chunk, chunk)]
        there = ct_s.at[slot, :, pl.ds(c * chunk, chunk)]
        return (
            pltpu.make_async_copy(src, there, ct_recv.at[c, slot]),
            pltpu.make_async_remote_copy(
                src, there, ct_send.at[c, 0], ct_recv.at[c, slot], device_id={"rows": 1 - core}
            ),
            pltpu.make_async_remote_copy(
                src, there, ct_send.at[c, 1], ct_recv.at[c, slot],
                device_id={"rows": chip, "cols": 1 - chip},
            ),
        )

    def cot_load(s):
        return pltpu.make_async_copy(
            cot_first.at[s], ct_s.at[s, :, pl.ds(0, chunk)], ct_recv.at[0, s]
        )

    def gn_move(c):
        return pltpu.make_async_remote_copy(
            gn_s.at[c], gn_far.at[c], gn_send.at[c], gn_recv.at[c], device_id=beside
        )

    def send_part(c):
        far_move(c).start()
        moves = cot_moves(c)
        moves[2].start()

        @pl.when(core == chip)
        def _():
            moves[0].start()

        @pl.when(core != chip)
        def _():
            moves[1].start()

    @pl.when(step == 0)
    def _():
        far_load().start()
        for s in range(2):
            cot_load(s).start()
        group_barrier(core, chip)
        gain_o[...] = jnp.zeros_like(gain_o)

    for c, at in enumerate(SEND_STEPS):

        @pl.when(step == at)
        def _():
            send_part(c + 1)

    def turned_cot(c):
        cols = pl.ds(pl.multiple_of(c * chunk, chunk), chunk)
        for s in range(2):
            ctok_s[:, s * half : (s + 1) * half] = ct_s[s, :, cols].T

    def norm_forward(c):
        cols = pl.ds(pl.multiple_of(c * chunk, chunk), chunk)
        slots = c * chunk + lax.broadcasted_iota(jnp.int32, (1, chunk), 1)
        live = (slots < lengths[core]).astype(F32).astype(BF16)
        pltpu.make_async_copy(far_first, far_s.at[c], far_recv.at[c]).wait()
        for s in range(2):
            pltpu.make_async_copy(
                cot_first.at[s], ct_s.at[s, :, cols], ct_recv.at[c, s]
            ).wait()
            ct_s[s, :, cols] = ct_s[s, :, cols] * live
        turned_cot(c)
        gn_acc[...] = jnp.zeros_like(gn_acc)

        def rows_step(i, _):
            rows = pl.ds(pl.multiple_of(i * 16, 16), 16)
            res = x[rows, :].astype(F32) + (mix[rows, :].astype(F32) + far_s[c, rows, :].astype(F32))
            out_acc[rows, :] = keep[...] * res
            scale = lax.rsqrt(jnp.sum(res * res, axis=1, keepdims=True) / wide + EPS)
            n2_s[rows, :] = (res * scale * gain[...]).astype(BF16)
            return 0

        lax.fori_loop(0, chunk // 16, rows_step, 0)
        n2t_s[:, cols] = n2_s[...].T

    @pl.when(step < first_part)
    def _():
        c = step // blocks
        blk = step % blocks
        rows = pl.ds(pl.multiple_of(c * chunk, chunk), chunk)

        @pl.when(blk == 0)
        def _():
            norm_forward(c)

        n0, n1 = n2_s[:, :half], n2_s[:, half:]
        c0, c1 = ctok_s[:, :half], ctok_s[:, half:]
        a = dot(n0, wg0[...]) + dot(n1, wg1[...])
        b = dot(n0, wu0[...]) + dot(n1, wu1[...])
        gh = dot(c0, wd0[...]) + dot(c1, wd1[...])
        act, slope = gelu_pair(a)
        hidden = (act * b).astype(BF16)
        ga = (gh * b * slope).astype(BF16)
        gb = (gh * act).astype(BF16)
        hid_s[blk, rows, :] = hidden
        ga_s[blk, rows, :] = ga
        gb_s[blk, rows, :] = gb
        out_acc[:, :half] += dot_nt(hidden, wd0[...])
        out_acc[:, half:] += dot_nt(hidden, wd1[...])
        gn_acc[:, :half] += dot_nt(ga, wg0[...]) + dot_nt(gb, wu0[...])
        gn_acc[:, half:] += dot_nt(ga, wg1[...]) + dot_nt(gb, wu1[...])

        @pl.when(blk == blocks - 1)
        def _():
            out_o[...] = out_acc[...].astype(BF16)
            gn_s[c] = gn_acc[...].astype(BF16)

        @pl.when(step == first_part - 1)
        def _():
            gn_last[...] = gn_s[count - 1]
            far_last[...] = far_s[count - 1]
            cot_last[...] = ctok_s[...]

    for c, at in enumerate(GN_STEPS):

        @pl.when(step == first_part - blocks + at)
        def _():
            gn_move(c).start()

    def norm_back(c):
        turned_cot(c)
        gn_move(c).wait_recv()

        def rows_step(i, _):
            rows = pl.ds(pl.multiple_of(i * 16, 16), 16)
            grad = gn_s[c, rows, :].astype(F32) + gn_far[c, rows, :].astype(F32)
            held = x[rows, :].astype(F32) + (mix[rows, :].astype(F32) + far_s[c, rows, :].astype(F32))
            norm_back_rows(rows, grad, held, ctok_s[rows, :], gain, gain_o, g1_o)
            return 0

        lax.fori_loop(0, chunk // 16, rows_step, 0)
        g1t_o[...] = g1_o[...].T

    def give(a, k):
        at = k % 2
        return pltpu.make_async_remote_copy(
            give_s.at[a, at], got_s.at[a, at], up_send.at[a, at], up_recv.at[a, at],
            device_id={"rows": 1 - core},
        )

    k = step - first_part
    shared = ((gb_s, gu_sum, blocks), (ga_s, gg_sum, BESIDE))
    for a, (_, total_o, many) in enumerate(shared):

        @pl.when(jnp.logical_and(k > 0, k <= many))
        def _():
            give(a, k - 1).wait()
            at = (k - 1) % 2
            total_o[...] = (keep_s[a, at].astype(F32) + got_s[a, at].astype(F32)).astype(BF16)

            @pl.when(k - 1 < many - 2)
            def _():
                pl.semaphore_signal(free_sem.at[a], inc=1, device_id={"rows": 1 - core})

        @pl.when(jnp.logical_and(k >= 0, k < many))
        def _():
            product = dot(n2t_s[...], shared[a][0][k]).astype(BF16)
            give_s[a, k % 2] = product[half:]

            @pl.when(k >= 2)
            def _():
                pl.semaphore_wait(free_sem.at[a], 1)

            give(a, k).start()
            keep_s[a, k % 2] = product[:half]

    @pl.when(jnp.logical_and(k >= BESIDE, k < blocks))
    def _():
        product = dot(n2t_s[...], ga_s[k]).astype(BF16)
        gg0[...] = product[:half]
        gg1[...] = product[half:]

    @pl.when(jnp.logical_and(k >= 0, k < blocks))
    def _():
        product = dot(ct_s[...].reshape(2 * half, ct_s.shape[2]), hid_s[k]).astype(BF16)
        gd0[...] = product[:half]
        gd1[...] = product[half:]

    for c in range(count - 1):

        @pl.when(k == 3 * (c + 1))
        def _():
            norm_back(c)

    @pl.when(k == blocks)
    def _():
        for c in range(count - 1):
            gn_move(c).wait_send()
        for c in range(1, count):
            far_move(c).wait_send()
            moves = cot_moves(c)
            moves[2].wait_send()

            @pl.when(core != chip)
            def _():
                moves[1].wait_send()


def ffn(x, mix, lengths, gain, keep, wg, wu, wd, cotangent, far_first, cot_first, chunk=256, block=BLOCK):
    tokens, wide = x.shape
    half, width = wg[0].shape
    count, blocks = tokens // chunk, width // block
    first_part = count * blocks
    whole = lambda shape: pl.BlockSpec(
        shape, lambda i: (0,) * len(shape), pipeline_mode=pl.Buffered(1)
    )
    hbm = pl.BlockSpec(memory_space=pl.ANY)

    def back_chunk(i):
        return jnp.clip((i - first_part - 1) // 3, 0, count - 2)

    def chunk_at(i):
        return jnp.where(i < first_part, i // blocks, back_chunk(i))

    rows = pl.BlockSpec((chunk, wide), lambda i: (chunk_at(i), 0))
    weight = pl.BlockSpec(
        (half, block), lambda i: (0, jnp.where(i < first_part, i % blocks, blocks - 1))
    )
    grad_at = lambda late, many: pl.BlockSpec(
        (half, block), lambda i: (0, jnp.clip(i - first_part - late, 0, many - 1))
    )
    grad = lambda many: jax.ShapeDtypeStruct((half, many * block), BF16)
    low = jax.ShapeDtypeStruct((tokens, wide), BF16)
    part = pltpu.VMEM((count, chunk, wide), BF16)
    middle = pltpu.VMEM((blocks, tokens, block), BF16)
    pair = pltpu.VMEM((2, 2, half, block), BF16)
    dma = pltpu.SemaphoreType.DMA
    return pl.pallas_call(
        functools.partial(ffn_kernel, count, blocks),
        grid=(first_part + blocks + 1,),
        in_specs=[rows, rows, pl.BlockSpec(memory_space=pltpu.SMEM), whole((1, wide)), whole((1, 1))]
        + [weight] * 6
        + [hbm] * 4,
        out_specs=[
            pl.BlockSpec((chunk, wide), lambda i: (jnp.minimum(i // blocks, count - 1), 0)),
            grad_at(1, blocks),
            grad_at(1, BESIDE),
        ]
        + [grad_at(BESIDE, blocks - BESIDE)] * 2
        + [grad_at(0, blocks)] * 2
        + [
            pl.BlockSpec((chunk, wide), lambda i: (back_chunk(i), 0)),
            pl.BlockSpec((wide, chunk), lambda i: (0, back_chunk(i))),
            whole((8, wide)),
        ]
        + [whole((chunk, wide))] * 3,
        out_shape=[low]
        + [grad(blocks), grad(BESIDE)]
        + [grad(blocks - BESIDE)] * 2
        + [grad(blocks)] * 2
        + [
            jax.ShapeDtypeStruct((tokens - chunk, wide), BF16),
            jax.ShapeDtypeStruct((wide, tokens - chunk), BF16),
            jax.ShapeDtypeStruct((8, wide), F32),
        ]
        + [jax.ShapeDtypeStruct((chunk, wide), BF16)] * 3,
        scratch_shapes=[
            part,
            pltpu.VMEM((2, half, tokens), BF16),
            pltpu.VMEM((chunk, wide), BF16),
            pltpu.VMEM((chunk, wide), BF16),
            pltpu.VMEM((wide, tokens), BF16),
            middle, middle, middle,
            pltpu.VMEM((chunk, wide), F32),
            pltpu.VMEM((chunk, wide), F32),
            part, part,
            pair, pair, pair,
            dma((count,)), dma((count,)),
            dma((count, 2)), dma((count, 2)),
            dma((count,)), dma((count,)),
            dma((2, 2)), dma((2, 2)),
            pltpu.SemaphoreType.REGULAR((2,)),
        ],
        compiler_params=pltpu.CompilerParams(
            vmem_limit_bytes=62 * MIB, collective_id=3, has_side_effects=True
        ),
        name="ffn",
    )(
        x, mix, lengths, gain, keep, wg[0], wg[1], wu[0], wu[1], wd[0], wd[1],
        mix, cotangent, far_first, cot_first,
    )


def ring_place(n, at):
    def index_of(place):
        return lax.select(place < n // 2, 2 * place, 2 * (n - 1 - place) + 1)

    me = lax.select(at % 2 == 0, at // 2, n - 1 - at // 2)
    return me, (index_of(lax.rem(me + 1, n)), index_of(lax.rem(me + n - 1, n)))


def ring_rows(n, me, total, way, s):
    size = total // n
    chunk = lax.rem(me + n - s, n) if way == 0 else lax.rem(me + s, n)
    return pl.ds(pl.multiple_of(chunk * size, size), size)


def ring_beside(n, owns, out, own_b, ring_b, own_sem, rs_send, rs_recv, ag_send, ag_recv, put_sem):
    me, nexts = ring_place(n, lax.axis_index("dp"))
    wide = out.shape[1] // 2
    cut = (wide // 128 + 1) // 2 * 128
    groups = (pl.ds(0, cut), pl.ds(cut, wide - cut))
    both = [(g, way) for g in range(2) for way in range(2)]
    per = -(-n // 8)
    per_gather = -(-(n - 2) // 6)
    rows_of = lambda way, s: ring_rows(n, me, out.shape[0], way, s)
    cols_of = lambda g, way: pl.ds(way * wide + g * cut, wide - cut if g else cut)

    def own_copies(way, s):
        moves, at = [], 0
        for m, own in enumerate(owns):
            size = own.shape[1] // 2
            moves.append(
                pltpu.make_async_copy(
                    own.at[rows_of(way, s), pl.ds(way * size, size)],
                    own_b.at[way, s % 2, :, pl.ds(at, size)],
                    own_sem.at[m, way, s % 2],
                )
            )
            at += size
        return moves

    def sum_copy(g, way, s):
        return pltpu.make_async_remote_copy(
            ring_b.at[way, s, :, groups[g]], ring_b.at[way, s + 1, :, groups[g]],
            rs_send.at[g, way], rs_recv.at[g, way, s], device_id={"dp": nexts[way]},
        )

    def first_gather(g, way):
        return pltpu.make_async_remote_copy(
            ring_b.at[way, n - 1, :, groups[g]], out.at[rows_of(way, n - 1), cols_of(g, way)],
            ag_send.at[g, way, 0], ag_recv.at[g, way, 0], device_id={"dp": nexts[way]},
        )

    def gather_copy(g, way, s):
        there = out.at[rows_of(way, s - 1), cols_of(g, way)]
        return pltpu.make_async_remote_copy(
            there, there, ag_send.at[g, way, s], ag_recv.at[g, way, s], device_id={"dp": nexts[way]}
        )

    def put_copy(g, way):
        return pltpu.make_async_copy(
            ring_b.at[way, n - 1, :, groups[g]],
            out.at[rows_of(way, n - 1), cols_of(g, way)],
            put_sem.at[g, way],
        )

    def begin(chip):
        barrier = pltpu.get_barrier_semaphore()
        for neighbour in nexts:
            pl.semaphore_signal(barrier, inc=1, device_id={"dp": neighbour})
        pl.semaphore_signal(barrier, inc=1, device_id={"cols": 1 - chip})
        for s in range(2):
            for way in range(2):
                for move in own_copies(way, s):
                    move.start()
        pl.semaphore_wait(barrier, 3)

    def sum_step(g, s):
        for way in range(2):
            if g == 0:
                for move in own_copies(way, s):
                    move.wait()

            @pl.when(s == 0)
            def _():
                ring_b[way, s, :, groups[g]] = own_b[way, s % 2, :, groups[g]]

            @pl.when(s > 0)
            def _():
                sum_copy(g, way, s - 1).wait_recv()
                total = ring_b[way, s, :, groups[g]].astype(F32) + own_b[
                    way, s % 2, :, groups[g]
                ].astype(F32)
                ring_b[way, s, :, groups[g]] = total.astype(BF16)

            @pl.when(s < n - 1)
            def _():
                sum_copy(g, way, s).start()

            @pl.when(s == n - 1)
            def _():
                first_gather(g, way).start()
                put_copy(g, way).start()

            if g == 1:

                @pl.when(s < n - 2)
                def _():
                    for move in own_copies(way, s + 2):
                        move.start()

    def gather_step(g, s):
        for way in range(2):

            @pl.when(s == 1)
            def _():
                first_gather(g, way).wait_recv()

            @pl.when(s > 1)
            def _():
                gather_copy(g, way, s - 1).wait_recv()

            gather_copy(g, way, s).start()

    def tick(g, t):
        if per > 1 and g == 0:
            return
        turns = (0, 1) if per > 1 else (g,)

        def run(step):
            def once(s, _):
                for turn in turns:
                    step(turn, s)
                return 0

            return once

        @pl.when(t < 8)
        def _():
            lax.fori_loop(t * per, jnp.minimum((t + 1) * per, n), run(sum_step), 0)

        @pl.when(t >= 8)
        def _():
            start = 1 + (t - 8) * per_gather
            lax.fori_loop(start, jnp.minimum(start + per_gather, n - 1), run(gather_step), 0)

    def end():
        for g, way in both:
            gather_copy(g, way, n - 2).wait_recv()
            put_copy(g, way).wait()
            first_gather(g, way).wait_send()
            pltpu.make_async_remote_copy(
                ring_b.at[way, pl.ds(0, n - 1), :, groups[g]],
                ring_b.at[way, pl.ds(1, n - 1), :, groups[g]],
                rs_send.at[g, way], rs_recv.at[g, way, 0], device_id={"dp": nexts[way]},
            ).wait_send()

        def drain(s, _):
            for g, way in both:
                gather_copy(g, way, s).wait_send()
            return 0

        lax.fori_loop(1, n - 1, drain, 0)

    return begin, tick, end


def rec_backward_kernel(
    tile, n,
    n1t, st, gate, r_in, i_in, cl, rec, br, ow0, ow1, wr0, wr1, wg0, wg1, rw, iw, cw, sp,
    x, gain, gain_second, gain_two, up, gate_own, g1_head, g1t_head, mixed, gn_last, far_last, cot_last,
    gn1_o, go0, go1, gr0, gr1, gg0, gg1, ggw, small0, small1, stat, up_o, g1_last,
    acc, gb_s, gc_s, ggp_s, grp_s, gip_s, grec_s, gain_s, sums, g1, g1t, gain_b,
    gn_s, gn_far, mix_s, far_s, cot_s, load_sem, gn_send, gn_recv, put_last, *ring_refs
):
    step = pl.program_id(0)
    tokens, block = gb_s.shape
    wide = n1t.shape[0]
    heads = block // 128
    half = ow0.shape[0]
    tiles = tokens // tile
    subs = tile // 8

    begin, tick, end = ring_beside(n, (up, gate_own), up_o, *ring_refs)

    chunk = gn_s.shape[0]
    head = tokens - chunk
    chip = lax.axis_index("cols")
    gn_move = pltpu.make_async_remote_copy(
        gn_last, gn_far, gn_send.at[0], gn_recv.at[0], device_id={"cols": 1 - chip}
    )
    last_put = pltpu.make_async_copy(g1.at[pl.ds(head, chunk), :], g1_last, put_last.at[0])
    beat = lambda at: tick(at % 2, 3 + step * 3 + at // 2)

    @pl.when(step == 0)
    def _():
        loads = [
            pltpu.make_async_copy(src, dst, load_sem.at[m])
            for m, (src, dst) in enumerate(
                (
                    (mixed.at[pl.ds(head, chunk), :], mix_s),
                    (far_last, far_s),
                    (cot_last, cot_s),
                    (gn_last, gn_s),
                    (g1_head, g1.at[pl.ds(0, head), :]),
                    (g1t_head, g1t.at[:, pl.ds(0, head)]),
                )
            )
        ]
        for move in loads:
            move.start()
        begin(chip)
        gn_move.start()
        acc[...] = jnp.zeros_like(acc)
        small0[...] = jnp.zeros_like(small0)
        small1[...] = jnp.zeros_like(small1)
        gain_b[...] = gain_two[...]
        for t in range(3):
            for g in range(2):
                tick(g, t)
        for move in loads:
            move.wait()
        gn_move.wait()

        def rows_step(i, _):
            base = pl.multiple_of(i * 16, 16)
            rows = pl.ds(base, 16)
            grad = gn_s[rows, :].astype(F32) + gn_far[rows, :].astype(F32)
            held = x[pl.ds(head + base, 16), :].astype(F32) + (
                mix_s[rows, :].astype(F32) + far_s[rows, :].astype(F32)
            )
            norm_back_rows(pl.ds(head + base, 16), grad, held, cot_s[rows, :], gain_second, gain_b, g1)
            return 0

        lax.fori_loop(0, chunk // 16, rows_step, 0)
        g1t[:, head:] = g1[head:, :].T
        last_put.start()

    beat(0)
    gb_s[...] = dot(g1[:, :half], ow0[...]) + dot(g1[:, half:], ow1[...])
    beat(1)
    product = dot(g1t[...], br[...]).astype(BF16)
    go0[...] = product[:half]
    go1[...] = product[half:]
    beat(2)
    sums[...] = jnp.zeros_like(sums)
    row = lax.broadcasted_iota(jnp.int32, (8, 128), 0)

    def back_step(j, held):
        @pl.when(j == tiles // 2)
        def _():
            beat(3)

        i = tiles - 1 - j
        base = pl.multiple_of(i * tile, tile)
        rows = pl.ds(base, tile)
        before = pl.ds(pl.multiple_of(jnp.maximum(base - 8, 0), 8), 8)
        out = []
        for h in range(heads):
            sl = slice(h * 128, (h + 1) * 128)
            later_decay, later_carried = held[h]
            grad_branch = gb_s[rows, sl]
            act, slope = gelu_pair(gate[rows, sl])
            state = st[rows, sl]
            ggp_s[rows, sl] = (grad_branch * state * slope).astype(BF16)
            grad_state = grad_branch * act
            r = r_in[rows, sl]
            soft = sp[:, sl]
            decay, em = decay_terms(r, soft)
            parts = [None] * subs
            for p in range(subs - 1, -1, -1):
                own = decay[p * 8 : p * 8 + 8]
                after = jnp.where(row == 7, later_decay, pltpu.roll(own, 7, 0))
                a, b = scan_tile_back(after, grad_state[p * 8 : p * 8 + 8], row)
                carried = a * later_carried + b
                later_decay = own[0:1]
                later_carried = carried[0:1]
                parts[p] = carried
            out.append((later_decay, later_carried))
            carried = jnp.concatenate(parts, axis=0)
            edge = jnp.where(i > 0, st[before, sl][7:8], 0.0)
            prev = []
            for p in range(subs):
                prev.append(jnp.where(row == 0, edge, pltpu.roll(state[p * 8 : p * 8 + 8], 1, 0)))
                edge = state[p * 8 + 7 : p * 8 + 8]
            prev = jnp.concatenate(prev, axis=0)
            g = i_in[rows, sl]
            conv = cl[rows, sl].astype(F32)
            scaling = jnp.sqrt(em)
            gated = g * conv
            grad_log = carried * (prev * decay - gated * (decay * decay) / scaling)
            grad_soft = grad_log * (-GATE_SCALE * r)
            grp = grad_soft * soft * (1.0 - r)
            cs = carried * scaling
            gc_s[rows, sl] = cs * g
            gip = cs * gated * (1.0 - g)
            grp_s[rows, sl] = grp.astype(BF16)
            gip_s[rows, sl] = gip.astype(BF16)
            for n, term in enumerate((grp, gip, grad_soft)):
                total = term[0:8]
                for p in range(1, subs):
                    total = total + term[p * 8 : p * 8 + 8]
                sums[n * 8 : n * 8 + 8, sl] += total
        return tuple(out)

    zero = jnp.zeros((1, 128), F32)
    lax.fori_loop(0, tiles, back_step, tuple((zero, zero) for _ in range(heads)))
    beat(4)
    for h in range(heads):
        sl = slice(h * 128, (h + 1) * 128)
        low = cl[:, sl]
        ggw[h, :, 0:128] = dot_tn(low, grp_s[:, sl]).astype(BF16)
        ggw[h, :, 128:256] = dot_tn(low, gip_s[:, sl]).astype(BF16)
        gc_s[:, sl] += dot_nt(grp_s[:, sl], rw[h]) + dot_nt(gip_s[:, sl], iw[h])

    def conv_step(j, held):
        i = tiles - 1 - j
        base = pl.multiple_of(i * tile, tile)
        rows = pl.ds(base, tile)
        before = pl.ds(pl.multiple_of(jnp.maximum(base - 8, 0), 8), 8)
        out = []
        for h in range(heads):
            sl = slice(h * 128, (h + 1) * 128)
            grad_conv = gc_s[rows, sl]
            window = jnp.concatenate([grad_conv, held[h]], axis=0)
            out.append(grad_conv[0:8])
            grad_rec = cw[0:1, sl] * grad_conv
            for k in range(1, KCONV):
                grad_rec = grad_rec + cw[k : k + 1, sl] * pltpu.roll(window, tile + 8 - k, 0)[:tile]
            grec_s[rows, sl] = grad_rec.astype(BF16)
            edge = jnp.where(i > 0, rec[before, sl], 0.0)
            past = jnp.concatenate([edge, rec[rows, sl]], axis=0)
            terms = [grad_conv * past[8:]]
            for k in range(1, KCONV):
                terms.append(grad_conv * pltpu.roll(past, k, 0)[8:])
            terms.append(grad_conv)
            for n, term in enumerate(terms):
                total = term[0:8]
                for p in range(1, subs):
                    total = total + term[p * 8 : p * 8 + 8]
                sums[24 + n * 8 : 32 + n * 8, sl] += total
        return tuple(out)

    lax.fori_loop(0, tiles, conv_step, tuple(jnp.zeros((8, 128), F32) for _ in range(heads)))
    beat(5)
    all_heads = small0.shape[0] // 8
    head_row = lax.broadcasted_iota(jnp.int32, (all_heads, 128), 0)
    for n in range(8):
        vector = jnp.sum(sums[n * 8 : n * 8 + 8, :], axis=0, keepdims=True)
        for h in range(heads):
            at = slice(n * all_heads, (n + 1) * all_heads)
            mine = vector[:, h * 128 : (h + 1) * 128]
            tile_now = jnp.where(head_row == step * heads + h, mine, small0[at, 0:128])
            small0[at, 0:128] = tile_now
            small1[at, 0:128] = tile_now
    grad_rec = grec_s[...]
    grad_gate = ggp_s[...]
    product = dot(n1t[...], grad_rec).astype(BF16)
    gr0[...] = product[:half]
    gr1[...] = product[half:]
    product = dot(n1t[...], grad_gate).astype(BF16)
    gg0[...] = product[:half]
    gg1[...] = product[half:]
    acc[:, :half] += dot_nt(grad_rec, wr0[...]) + dot_nt(grad_gate, wg0[...])
    acc[:, half:] += dot_nt(grad_rec, wr1[...]) + dot_nt(grad_gate, wg1[...])

    @pl.when(step == pl.num_programs(0) - 1)
    def _():
        gain_s[...] = jnp.zeros_like(gain_s)

        def stat_step(i, _):
            rows = pl.ds(pl.multiple_of(i * 32, 32), 32)
            part = acc[rows, :]
            gn1_o[rows, :] = part.astype(BF16)
            held = x[rows, :].astype(F32)
            scale = lax.rsqrt(jnp.sum(held * held, axis=1, keepdims=True) / wide + EPS)
            product = part * held
            by_gain = product * scale
            gain_s[...] += (by_gain[0:8] + by_gain[8:16]) + (by_gain[16:24] + by_gain[24:32])
            inner = jnp.sum(product * gain[...], axis=1, keepdims=True)
            stat[rows, 0:64] = jnp.broadcast_to(inner, (32, 64))
            stat[rows, 64:128] = jnp.broadcast_to(scale, (32, 64))
            return 0

        lax.fori_loop(0, tokens // 32, stat_step, 0)
        for n, held in enumerate((gain_s, gain_b)):
            vector = jnp.sum(held[...], axis=0, keepdims=True)
            for m in range(half // 128):
                at = n * 8 + m
                small0[at : at + 1, 128:] = vector[:, m * 128 : (m + 1) * 128]
                small1[at : at + 1, 128:] = vector[:, half + m * 128 : half + (m + 1) * 128]
        last_put.wait()
        end()


def rec_backward(
    n1t, st, gate, r, g, cl, rec, br, ow, wr, wg, rw, iw, cw, sp, x, gain, gain_second, gain_two,
    up, gate_own, lasts, n, block=256, tile=64
):
    wide, tokens = n1t.shape
    half, width = wr[0].shape
    heads = block // 128
    rows = up.shape[0]
    up, gate_own = (jnp.pad(a, ((0, -rows % (16 * n)), (0, 0))) for a in (up, gate_own))
    side = (up.shape[0], up.shape[1] + gate_own.shape[1])
    small = (8 * (width // 128), 256)
    chunk = lasts[-1].shape[0]
    slots = lambda many: pltpu.VMEM((2, many, side[0] // n, side[1] // 2), BF16)
    dma = pltpu.SemaphoreType.DMA
    hbm = pl.BlockSpec(memory_space=pl.ANY)
    whole = lambda shape: pl.BlockSpec(shape, lambda i: (0, 0), pipeline_mode=pl.Buffered(1))
    act = pl.BlockSpec((tokens, block), lambda i: (0, i))
    weight = pl.BlockSpec((half, block), lambda i: (0, i))
    thin = lambda n: pl.BlockSpec((n, block), lambda i: (0, i))
    gate_block = pl.BlockSpec((heads, 128, 256), lambda i: (i, 0, 0))
    grad = jax.ShapeDtypeStruct((half, width), BF16)
    outs = pl.pallas_call(
        functools.partial(rec_backward_kernel, tile, n),
        grid=(width // block,),
        in_specs=[whole((wide, tokens))]
        + [act] * 7
        + [weight] * 6
        + [pl.BlockSpec((heads, 128, 128), lambda i: (i, 0, 0))] * 2
        + [thin(KCONV), thin(1)]
        + [whole((tokens, wide)), whole((1, wide)), whole((1, wide)), whole((8, wide))]
        + [hbm] * 8,
        out_specs=[whole((tokens, wide))]
        + [weight] * 6
        + [gate_block, whole(small), whole(small), whole((tokens, 128)), hbm, hbm],
        out_shape=[jax.ShapeDtypeStruct((tokens, wide), BF16)]
        + [grad] * 6
        + [
            jax.ShapeDtypeStruct((width // 128, 128, 256), BF16),
            jax.ShapeDtypeStruct(small, F32),
            jax.ShapeDtypeStruct(small, F32),
            jax.ShapeDtypeStruct((tokens, 128), F32),
            jax.ShapeDtypeStruct(side, BF16),
            jax.ShapeDtypeStruct((chunk, wide), BF16),
        ],
        scratch_shapes=[
            pltpu.VMEM((tokens, wide), F32),
            pltpu.VMEM((tokens, block), F32),
            pltpu.VMEM((tokens, block), F32),
            pltpu.VMEM((tokens, block), BF16),
            pltpu.VMEM((tokens, block), BF16),
            pltpu.VMEM((tokens, block), BF16),
            pltpu.VMEM((tokens, block), BF16),
            pltpu.VMEM((8, wide), F32),
            pltpu.VMEM((64, block), F32),
            pltpu.VMEM((tokens, wide), BF16),
            pltpu.VMEM((wide, tokens), BF16),
            pltpu.VMEM((8, wide), F32),
        ]
        + [pltpu.VMEM((chunk, wide), BF16)] * 5
        + [
            dma((6,)), dma((1,)), dma((1,)), dma((1,)),
            slots(2), slots(n),
            dma((2, 2, 2)), dma((2, 2)), dma((2, 2, n)), dma((2, 2, n)), dma((2, 2, n)), dma((2, 2)),
        ],
        compiler_params=pltpu.CompilerParams(
            vmem_limit_bytes=62 * MIB, collective_id=6, has_side_effects=True
        ),
        name="recurrent_backward",
    )(
        n1t, st, gate, r, g, cl, rec, br,
        ow[0], ow[1], wr[0], wr[1], wg[0], wg[1], rw, iw, cw, sp, x, gain, gain_second, gain_two,
        up, gate_own, *lasts,
    )
    return (*outs[:-2], outs[-2][:rows], outs[-1])


def ring_kernel(n, count, *refs):
    own, other, refs = refs[:count], refs[count : 2 * count], refs[2 * count :]
    (gn1, out, stat, g1_head, g1_last), refs = refs[:5], refs[5:]
    outs, refs = refs[:count], refs[count:]
    (gn1_p, out_p, stat_p, g1_p), scratch = refs[:4], refs[4:]
    piece_send, piece_recv = scratch[-2:]
    scratch = scratch[:-2]
    own_b, part_b, ring_b = scratch[:count], scratch[count : 2 * count], scratch[2 * count : 3 * count]
    own_sem, part_send, part_recv, rs_send, rs_recv, ag_send, ag_recv, put_sem = scratch[3 * count :]
    at = lax.axis_index("dp")
    core = lax.axis_index("rows")
    chip = lax.axis_index("cols")

    me, nexts = ring_place(n, at)
    barrier = pltpu.get_barrier_semaphore()
    for neighbour in nexts:
        pl.semaphore_signal(barrier, inc=1, device_id={"dp": neighbour})
    for peer in ((1 - core, chip), (core, 1 - chip), (1 - core, 1 - chip)):
        pl.semaphore_signal(barrier, inc=1, device_id={"rows": peer[0], "cols": peer[1]})
    pl.semaphore_wait(barrier, 5)

    half = gn1_p.shape[2]
    first, second = slice(0, half), slice(half, 2 * half)
    everything = slice(None)
    pieces = [
        (gn1, gn1_p, slice(None), first, second),
        (out, out_p, slice(None), first, second),
        (stat, stat_p, slice(None), everything, everything),
    ]
    head = g1_head.shape[0]
    singles = [(g1_head, slice(0, head)), (g1_last, slice(head, gn1.shape[0]))]
    diag = core == chip

    def piece_moves(m):
        src, dst, rows, mine, theirs = pieces[m]
        there = dst.at[chip, rows, :]
        sems = lambda w: (piece_send.at[m, w], piece_recv.at[m, chip])
        near = src.at[:, mine]
        away = src.at[:, theirs]
        return (
            pltpu.make_async_copy(near, there, piece_recv.at[m, chip]),
            pltpu.make_async_remote_copy(near, there, *sems(0), device_id={"cols": 1 - chip}),
            pltpu.make_async_remote_copy(away, there, *sems(1), device_id={"rows": 1 - core}),
            pltpu.make_async_remote_copy(
                away, there, *sems(1), device_id={"rows": 1 - core, "cols": 1 - chip}
            ),
        )

    def single_moves(m):
        src, rows = singles[m]
        there = g1_p.at[rows, :]
        at = len(pieces) + m
        return (
            pltpu.make_async_copy(src.at[:, first], there, piece_recv.at[at, 0]),
            pltpu.make_async_remote_copy(
                src.at[:, second], there, piece_send.at[at, 1], piece_recv.at[at, 0],
                device_id={"rows": 1 - core},
            ),
        )

    @pl.when(diag)
    def _():
        for m in range(len(pieces)):
            moves = piece_moves(m)
            moves[0].start()
            moves[2].start()
        for m in range(len(singles)):
            moves = single_moves(m)
            moves[0].start()
            moves[1].start()

    @pl.when(jnp.logical_not(diag))
    def _():
        for m in range(len(pieces)):
            moves = piece_moves(m)
            moves[1].start()
            moves[3].start()

    def rows_of(k, way, s):
        return ring_rows(n, me, own[k].shape[0], way, s)

    def cols_of(k, way):
        wide = own[k].shape[1] // 2
        return pl.ds(way * wide, wide)

    def own_copy(k, way, s):
        return pltpu.make_async_copy(
            own[k].at[rows_of(k, way, s), cols_of(k, way)], own_b[k].at[way, s], own_sem.at[k, way, s]
        )

    def part_copy(k, way, s):
        return pltpu.make_async_remote_copy(
            src_ref=other[k].at[rows_of(k, way, s), cols_of(k, way)],
            dst_ref=part_b[k].at[way, s],
            send_sem=part_send.at[k, way],
            recv_sem=part_recv.at[k, way, s],
            device_id={"rows": 1 - core},
        )

    def sum_copy(k, way, s):
        return pltpu.make_async_remote_copy(
            src_ref=ring_b[k].at[way, s],
            dst_ref=ring_b[k].at[way, s + 1],
            send_sem=rs_send.at[k, way],
            recv_sem=rs_recv.at[k, way, s],
            device_id={"dp": nexts[way]},
        )

    def first_gather(k, way):
        rows = rows_of(k, way, n - 1)
        return pltpu.make_async_remote_copy(
            src_ref=ring_b[k].at[way, n - 1],
            dst_ref=outs[k].at[rows, cols_of(k, way)],
            send_sem=ag_send.at[k, way, 0],
            recv_sem=ag_recv.at[k, way, 0],
            device_id={"dp": nexts[way]},
        )

    def gather_copy(k, way, s):
        rows = rows_of(k, way, s - 1)
        there = outs[k].at[rows, cols_of(k, way)]
        return pltpu.make_async_remote_copy(
            src_ref=there,
            dst_ref=there,
            send_sem=ag_send.at[k, way, s],
            recv_sem=ag_recv.at[k, way, s],
            device_id={"dp": nexts[way]},
        )

    def put_copy(k, way):
        return pltpu.make_async_copy(
            ring_b[k].at[way, n - 1],
            outs[k].at[rows_of(k, way, n - 1), cols_of(k, way)],
            put_sem.at[k, way],
        )

    both = [(k, way) for k in range(count) for way in range(2)]

    def load_step(s, _):
        for k, way in both:
            part_copy(k, way, s).start()
            own_copy(k, way, s).start()
        return 0

    lax.fori_loop(0, n, load_step, 0)

    def add_step(k, way, s, received):
        own_copy(k, way, s).wait()
        part_copy(k, way, s).wait_recv()
        total = own_b[k][way, s].astype(F32) + part_b[k][way, s].astype(F32)
        if received:
            sum_copy(k, way, s - 1).wait_recv()
            total = total + ring_b[k][way, s].astype(F32)
        ring_b[k][way, s] = total.astype(ring_b[k].dtype)

    for k, way in both:
        add_step(k, way, 0, False)
        sum_copy(k, way, 0).start()

    def sum_step(s, _):
        for k, way in both:
            add_step(k, way, s, True)
            sum_copy(k, way, s).start()
        return 0

    lax.fori_loop(1, n - 1, sum_step, 0)
    for k, way in both:
        add_step(k, way, n - 1, True)
        first_gather(k, way).start()
        put_copy(k, way).start()

    def gather_step(s, _):
        for k, way in both:
            gather_copy(k, way, s - 1).wait_recv()
            gather_copy(k, way, s).start()
        return 0

    for k, way in both:
        first_gather(k, way).wait_recv()
        gather_copy(k, way, 1).start()
    lax.fori_loop(2, n - 1, gather_step, 0)
    for k, way in both:
        gather_copy(k, way, n - 2).wait_recv()
        put_copy(k, way).wait()
        first_gather(k, way).wait_send()

    def drain_step(s, _):
        for k, way in both:
            gather_copy(k, way, s).wait_send()
        return 0

    lax.fori_loop(1, n - 1, drain_step, 0)
    for k, way in both:
        pltpu.make_async_remote_copy(
            ring_b[k].at[way, pl.ds(0, n - 1)],
            ring_b[k].at[way, pl.ds(1, n - 1)],
            rs_send.at[k, way],
            rs_recv.at[k, way, 0],
            device_id={"dp": nexts[way]},
        ).wait_send()
        pltpu.make_async_remote_copy(
            own_b[k].at[way],
            part_b[k].at[way],
            part_send.at[k, way],
            part_recv.at[k, way, 0],
            device_id={"rows": 1 - core},
        ).wait_send()

    for m in range(len(pieces)):
        src, dst, rows, mine, _ = pieces[m]
        for c in range(2):
            pltpu.make_async_copy(src.at[:, mine], dst.at[c, rows, :], piece_recv.at[m, c]).wait()
    for m in range(len(singles)):
        single_moves(m)[0].wait()

    @pl.when(diag)
    def _():
        for m in range(len(pieces)):
            piece_moves(m)[2].wait_send()
        for m in range(len(singles)):
            single_moves(m)[1].wait_send()

    @pl.when(jnp.logical_not(diag))
    def _():
        for m in range(len(pieces)):
            moves = piece_moves(m)
            moves[1].wait_send()
            moves[3].wait_send()


def ring_sum(n, own, other, pieces):
    count = len(own)
    own, other = list(own), list(other)
    rows = [a.shape[0] for a in own]
    unit = lambda a: (16 if a.dtype == BF16 else 8) * n
    pad = [-a.shape[0] % unit(a) for a in own]
    fit = lambda a, extra: jnp.pad(a, ((0, extra), (0, 0))) if extra else a
    own = [fit(a, e) for a, e in zip(own, pad)]
    other = [fit(a, e) for a, e in zip(other, pad)]
    slots = [pltpu.VMEM((2, n, a.shape[0] // n, a.shape[1] // 2), a.dtype) for a in own]
    sems = pltpu.SemaphoreType.DMA((count, 2, n))
    pair = pltpu.SemaphoreType.DMA((count, 2))
    tokens, wide = pieces[0].shape
    piece = jax.ShapeDtypeStruct((2, tokens, wide // 2), BF16)
    hbm = pl.BlockSpec(memory_space=pl.ANY)
    outs = pl.pallas_call(
        functools.partial(ring_kernel, n, count),
        in_specs=[hbm] * (2 * count + len(pieces)),
        out_specs=[hbm] * (count + 4),
        out_shape=[jax.ShapeDtypeStruct(a.shape, a.dtype) for a in own]
        + [
            piece,
            piece,
            jax.ShapeDtypeStruct((2, tokens, 128), F32),
            jax.ShapeDtypeStruct((tokens, wide // 2), BF16),
        ],
        scratch_shapes=slots * 3
        + [sems, pair, sems, pair] + [sems] * 3 + [pair]
        + [pltpu.SemaphoreType.DMA((5, 2))] * 2,
        compiler_params=pltpu.CompilerParams(
            collective_id=0, has_side_effects=True, vmem_limit_bytes=60 * MIB
        ),
        name="ring_sum",
    )(*own, *other, *pieces)
    return [a[:r] for a, r in zip(outs, rows)], outs[count:]


def final_kernel(
    gn, out, stat, g1, tokens, gain, lengths, beside, down, gate, out_w, rec_w, gate_w,
    result_o, grad_o, up_o, gate_o, down_o, out_w_o, rec_w_o, gate_w_o,
):
    wide = 2 * tokens.shape[0]
    low = lambda ref: ref[0].astype(F32) + ref[1].astype(F32)
    chunk = tokens.shape[1]
    slots = pl.program_id(0) * chunk + lax.broadcasted_iota(jnp.int32, (1, chunk), 1)
    live = (slots < lengths[lax.axis_index("cols")]).astype(F32)
    result_o[...] = (low(out).T * live).astype(BF16)
    grad = low(gn).T
    held = tokens[...].astype(F32)
    inner = (stat[0] + stat[1]).T[0:1, :]
    scale = stat[0].T[64:65, :]
    grad_o[...] = (
        g1[...].astype(F32).T
        + (scale * gain[...]) * grad
        - held * (scale * scale * scale * inner / wide)
    ).astype(BF16)
    side = beside.shape[1] // 2
    up_half = up_o.shape[1] // 2
    gate_half = side - up_half
    for way in range(2):
        at = way * side
        up_o[:, way * up_half : (way + 1) * up_half] = beside[:, at : at + up_half].astype(F32)
        gate_o[:, way * gate_half : (way + 1) * gate_half] = beside[:, at + up_half : at + side].astype(F32)
    gate_o[:, 2 * gate_half :] = gate[...].astype(F32)
    for src, dst in ((down, down_o), (out_w, out_w_o), (rec_w, rec_w_o), (gate_w, gate_w_o)):
        dst[...] = src[...].astype(F32)


def final(gn, out, stat, g1, tokens, gain, lengths, beside, down, gate, out_w, rec_w, gate_w, steps=8):
    half, length = tokens.shape
    chunk, size = length // steps, half // steps
    pair = lambda cols: pl.BlockSpec((2, chunk, cols), lambda i: (0, i, 0))
    across = pl.BlockSpec((half, chunk), lambda i: (0, i))
    rows = lambda cols: pl.BlockSpec((size, cols), lambda i: (i, 0))
    shape = jax.ShapeDtypeStruct((half, length), BF16)
    ffn_wide, wide = down.shape[1], out_w.shape[1]
    grads = [ffn_wide] * 3 + [wide] * 3
    return pl.pallas_call(
        final_kernel,
        grid=(steps,),
        in_specs=[
            pair(half), pair(half), pair(128),
            pl.BlockSpec((chunk, half), lambda i: (i, 0)),
            across,
            pl.BlockSpec((half, 1), lambda i: (0, 0)),
            pl.BlockSpec(memory_space=pltpu.SMEM),
        ]
        + [rows(a.shape[1]) for a in (beside, down, gate, out_w, rec_w, gate_w)],
        out_specs=[across, across] + [rows(cols) for cols in grads],
        out_shape=[shape, shape] + [jax.ShapeDtypeStruct((half, cols), F32) for cols in grads],
        compiler_params=pltpu.CompilerParams(vmem_limit_bytes=56 * MIB),
        name="final",
    )(gn, out, stat, g1, tokens, gain, lengths, beside, down, gate, out_w, rec_w, gate_w)


def body(
    dp, tokens, lengths, mix_gain, rec_weight, gate_weight, conv_weight, conv_bias,
    recur_weight, recur_bias, input_weight, input_bias, decay_param, out_weight,
    ffn_gain, ffn_gate, ffn_up, ffn_down, cotangent,
):
    at_row = lax.axis_index("rows")
    at_col = lax.axis_index("cols")
    diag = at_row == at_col
    half = tokens.shape[0]
    wide = 2 * half

    both = lambda weight: (weight, swap(weight, "rows"))

    sp = jax.nn.softplus(-decay_param)[None, :]
    (x, n1t, rec, gate, cl, r, g, st, br, mixed, cot_a, far_a, wr_far, wg_far, ow_far) = rec_forward(
        tokens, cotangent, rec_weight, gate_weight, out_weight, mix_gain[:, None],
        recur_weight, input_weight, conv_weight, conv_bias[None, :], recur_bias[None, :],
        input_bias[None, :], sp,
    )
    wr = (rec_weight, wr_far)
    wg = (gate_weight, wg_far)
    ow = (out_weight, ow_far)
    fg = both(ffn_gate)
    fu = both(ffn_up)
    fd = both(ffn_down)
    gain_two = jnp.concatenate(both(ffn_gain))[None, :]
    gain_one = jnp.concatenate(both(mix_gain))[None, :]
    keep = diag.astype(F32).reshape(1, 1)

    out, up_own, gate_own, gg0, gg1, gd0, gd1, g1_head, g1t_head, grad_gain_two, *lasts = ffn(
        x, mixed, lengths, gain_two, keep, fg, fu, fd, cotangent, far_a, cot_a
    )
    gn1_part, go0, go1, gr0, gr1, gt0, gt1, ggw, small0, small1, stat, beside, g1_last = rec_backward(
        n1t, st, gate, r, g, cl, rec, br, ow, wr, wg, recur_weight, input_weight, conv_weight, sp,
        x, gain_one, gain_two, grad_gain_two, up_own, gate_own, [g1_head, g1t_head, mixed, *lasts], dp,
    )
    gates = ggw.reshape(-1, 256)
    total, moved = ring_sum(
        dp,
        [gd0, gg0, go0, gr0, gt0, gates, small0],
        [gd1, gg1, go1, gr1, gt1, gates, small1],
        [gn1_part, out, stat, g1_head, g1_last],
    )
    gates, small = total[5:]
    result, grad_tokens, sum_up, sum_gate, sum_down, sum_out, sum_rec, sum_gatew = final(
        *moved, tokens, mix_gain[:, None], lengths, beside, *total[:5]
    )
    gates = gates.astype(F32).reshape(ggw.shape)
    vec = small[:, :128].reshape(8, -1)
    gains = small[:16, 128:].reshape(2, -1)[:, :half]
    grad_gain_one = gains[0] + swap(gains[0], "cols")
    grad_decay = vec[2] * -jax.nn.sigmoid(-decay_param)
    return (
        result,
        grad_tokens,
        grad_gain_one,
        sum_rec,
        sum_gatew,
        vec[3:7],
        vec[7],
        gates[:, :, :128],
        vec[0],
        gates[:, :, 128:],
        vec[1],
        grad_decay,
        sum_out,
        gains[1],
        sum_gate,
        sum_up,
        sum_down,
    )


def solution(mesh):
    return jax.shard_map(
        functools.partial(body, mesh.shape["dp"]),
        mesh=mesh,
        in_specs=(
            P("rows", ("dp", "cols")),
            P("dp"),
            P("rows"),
            P("rows", "cols"),
            P("rows", "cols"),
            P(None, "cols"),
            P("cols"),
            P("cols", None, None),
            P("cols"),
            P("cols", None, None),
            P("cols"),
            P("cols"),
            P("rows", "cols"),
            P("rows"),
            P("rows", "cols"),
            P("rows", "cols"),
            P("rows", "cols"),
            P("rows", ("dp", "cols")),
        ),
        out_specs=(
            P("rows", ("dp", "cols")),
            P("rows", ("dp", "cols")),
            P("rows"),
            P("rows", "cols"),
            P("rows", "cols"),
            P(None, "cols"),
            P("cols"),
            P("cols", None, None),
            P("cols"),
            P("cols", None, None),
            P("cols"),
            P("cols"),
            P("rows", "cols"),
            P("rows"),
            P("rows", "cols"),
            P("rows", "cols"),
            P("rows", "cols"),
        ),
        check_vma=False,
    )
```

```python
import functools
import math

import jax
import jax.numpy as jnp
from jax import lax
from jax.experimental import pallas as pl
from jax.experimental.pallas import tpu as pltpu
from jax.sharding import PartitionSpec as P

D = 1536
KCONV = 4
LEN = 1024
BLOCK = 256
SEND_STEPS = (0, 8, 17)
GN_STEPS = (0, 6, 11)
BESIDE = 3
EPS = 1e-06
GATE_SCALE = 8.0
TANH_COEF = math.sqrt(2.0 / math.pi)
CUBIC_COEF = 0.044715
F32 = jnp.float32
BF16 = jnp.bfloat16
MIB = 1024 * 1024


def swap(value, axis):
    return lax.ppermute(value, axis, [(0, 1), (1, 0)])


def dot(left, right):
    return lax.dot_general(left, right, (((1,), (0,)), ((), ())), preferred_element_type=F32)


def dot_nt(left, right):
    return lax.dot_general(left, right, (((1,), (1,)), ((), ())), preferred_element_type=F32)


def dot_tn(left, right):
    return lax.dot_general(left, right, (((0,), (0,)), ((), ())), preferred_element_type=F32)


def gelu_act(values):
    inner_arg = TANH_COEF * (values + CUBIC_COEF * values * values * values)
    return 0.5 * values * (1.0 + jnp.tanh(inner_arg))


def gelu_pair(values):
    square = values * values
    tanh_val = jnp.tanh(values * (TANH_COEF + (TANH_COEF * CUBIC_COEF) * square))
    half_up = 0.5 + 0.5 * tanh_val
    slope = half_up + 0.5 * values * (1.0 - tanh_val * tanh_val) * (
        TANH_COEF + (3.0 * TANH_COEF * CUBIC_COEF) * square
    )
    return (values * half_up, slope)


def decay_terms(recur_gate, soft_decay):
    u = (2.0 * GATE_SCALE) * recur_gate * soft_decay
    decay = jnp.exp(-0.5 * u)
    series = u * (
        1.0
        - u
        * (0.5 - u * (1.0 / 6 - u * (1.0 / 24 - u * (1.0 / 120 - u * (1.0 / 720)))))
    )
    em = jnp.where(u < 0.25, series, 1.0 - decay * decay)
    return (decay, em)


def scan_tile(decay, drive, row):
    for shift in (1, 2, 4):
        keep = row >= shift
        before_a = jnp.where(keep, pltpu.roll(decay, shift, 0), 1.0)
        before_b = jnp.where(keep, pltpu.roll(drive, shift, 0), 0.0)
        drive = decay * before_b + drive
        decay = decay * before_a
    return (decay, drive)


def scan_tile_back(decay, drive, row):
    for shift in (1, 2, 4):
        keep = row < 8 - shift
        after_a = jnp.where(keep, pltpu.roll(decay, 8 - shift, 0), 1.0)
        after_b = jnp.where(keep, pltpu.roll(drive, 8 - shift, 0), 0.0)
        drive = decay * after_b + drive
        decay = decay * after_a
    return (decay, drive)


def group_barrier(core, chip):
    barrier = pltpu.get_barrier_semaphore()
    for peer in ((1 - core, chip), (core, 1 - chip), (1 - core, 1 - chip)):
        pl.semaphore_signal(barrier, inc=1, device_id={"rows": peer[0], "cols": peer[1]})
    pl.semaphore_wait(barrier, 3)


def rec_forward_kernel(
    chunk, count, cot_parts,
    tokens, cotangent, wr_h, wg_h, ow_h, gain_h, rw, iw, cw, cb, rb, ib, sp,
    x_o, n1t_o, rec_o, gate_o, cl_o, r_o, i_o, st_o, br_o, mix_o, cot_o, far_o, wr_o, wg_o, ow_o,
    tok_b, mix_s, wr, wg, ow, gain, gw, halo, carry, recpad, pre,
    tok_send, tok_recv, w_send, w_recv, w_own, cot_send, cot_recv, mix_send, mix_recv, put,
):
    step = pl.program_id(0)
    width = wr_h.shape[1]
    half = wr_h.shape[0]
    heads = width // 128
    core = lax.axis_index("rows")
    chip = lax.axis_index("cols")
    slot = lax.select(core == chip, 0, 1)
    near = {"rows": 1 - core}
    far = {"rows": chip, "cols": 1 - chip}

    def piece_moves(src, dst, send, recv):
        return (
            pltpu.make_async_copy(src, dst, recv),
            pltpu.make_async_remote_copy(src, dst, send.at[0], recv, device_id=near),
            pltpu.make_async_remote_copy(src, dst, send.at[1], recv, device_id=far),
        )

    def token_moves(k):
        return piece_moves(
            tokens.at[:, pl.ds(k * chunk, chunk)], tok_b.at[k, slot], tok_send.at[k], tok_recv.at[k, slot]
        )

    def cot_moves(k):
        return piece_moves(
            cotangent.at[:, pl.ds(k * chunk, chunk)],
            cot_o.at[slot, :, pl.ds(k * chunk, chunk)],
            cot_send.at[k],
            cot_recv.at[k, slot],
        )

    def mix_move(k):
        return pltpu.make_async_remote_copy(
            mix_s.at[k],
            far_o.at[pl.ds(k * chunk, chunk), :],
            mix_send.at[k],
            mix_recv.at[k],
            device_id={"cols": 1 - chip},
        )

    def start(moves):
        moves[2].start()

        @pl.when(core == chip)
        def _():
            moves[0].start()

        @pl.when(core != chip)
        def _():
            moves[1].start()

    def finish_send(moves):
        moves[2].wait_send()

        @pl.when(core != chip)
        def _():
            moves[1].wait_send()

    weights = ((wr_h, wr), (wg_h, wg), (ow_h, ow), (gain_h, gain))

    def weight_moves(n):
        src, dst = weights[n]
        return (
            pltpu.make_async_copy(src, dst.at[0], w_own.at[n]),
            pltpu.make_async_remote_copy(src, dst.at[1], w_send.at[n], w_recv.at[n], device_id=near),
        )

    def wait_weight(n):
        own, other = weight_moves(n)
        own.wait()
        other.wait_recv()

    @pl.when(step == 0)
    def _():
        group_barrier(core, chip)
        start(token_moves(0))
        for n in (3, 0, 1, 2):
            for move in weight_moves(n):
                move.start()
        for k in range(1, count):
            start(token_moves(k))
        halo[...] = jnp.zeros_like(halo)
        carry[...] = jnp.zeros_like(carry)
        for h in range(heads):
            gw[h, :, 0:128] = rw[h]
            gw[h, :, 128:256] = iw[h]
        wait_weight(3)

    for s in range(2):
        pltpu.make_async_copy(
            tokens.at[:, pl.ds(0, chunk)], tok_b.at[step, s], tok_recv.at[step, s]
        ).wait()

    @pl.when(step == count - 2)
    def _():
        for k in range(cot_parts):
            start(cot_moves(k))

    xt0 = tok_b[step, 0].astype(F32)
    xt1 = tok_b[step, 1].astype(F32)
    squares = jnp.sum(xt0 * xt0, axis=0, keepdims=True) + jnp.sum(xt1 * xt1, axis=0, keepdims=True)
    scale = lax.rsqrt(squares / (2 * half) + EPS)
    nt0 = (xt0 * scale * gain[0]).astype(BF16)
    nt1 = (xt1 * scale * gain[1]).astype(BF16)
    n1t_o[0:half, :] = nt0
    n1t_o[half:, :] = nt1
    x_o[:, 0:half] = tok_b[step, 0].T
    x_o[:, half:] = tok_b[step, 1].T
    low0 = nt0.T
    low1 = nt1.T

    @pl.when(step == 0)
    def _():
        wait_weight(0)
        wait_weight(1)

    rec = dot(low0, wr[0]) + dot(low1, wr[1])
    recpad[0:8, :] = halo[...]
    recpad[8:, :] = rec
    halo[...] = rec[chunk - 8 :, :]
    rec_o[...] = rec
    gate_o[...] = dot(low0, wg[0]) + dot(low1, wg[1])

    def conv_step(i, _):
        base = pl.multiple_of(i * 16, 16)
        for h in range(heads):
            sl = slice(h * 128, (h + 1) * 128)
            window = recpad[pl.ds(base, 24), sl]
            out = cb[:, sl] + cw[0:1, sl] * window[8:]
            for k in range(1, KCONV):
                out = out + cw[k : k + 1, sl] * pltpu.roll(window, k, 0)[8:]
            cl_o[pl.ds(base, 16), sl] = out.astype(BF16)
        return 0

    lax.fori_loop(0, chunk // 16, conv_step, 0)
    for h in range(heads):
        pre[:, h * 256 : (h + 1) * 256] = dot(cl_o[:, h * 128 : (h + 1) * 128], gw[h])
    row = lax.broadcasted_iota(jnp.int32, (8, 128), 0)

    def main_step(i, _):
        base = pl.multiple_of(i * 16, 16)
        rows = pl.ds(base, 16)
        for h in range(heads):
            sl = slice(h * 128, (h + 1) * 128)
            r = jax.nn.sigmoid(pre[rows, h * 256 : h * 256 + 128] + rb[:, sl])
            g = jax.nn.sigmoid(pre[rows, h * 256 + 128 : (h + 1) * 256] + ib[:, sl])
            conv = cl_o[rows, sl].astype(F32)
            decay, em = decay_terms(r, sp[:, sl])
            drive = jnp.sqrt(em) * g * conv
            r_o[rows, sl] = r
            i_o[rows, sl] = g
            held = carry[0:1, sl]
            parts = []
            for p in range(2):
                a, b = scan_tile(decay[p * 8 : p * 8 + 8], drive[p * 8 : p * 8 + 8], row)
                state = a * held + b
                held = state[7:8]
                parts.append(state)
            carry[0:1, sl] = held
            state = jnp.concatenate(parts, axis=0)
            st_o[rows, sl] = state
            br_o[rows, sl] = (state * gelu_act(gate_o[rows, sl])).astype(BF16)
        return 0

    lax.fori_loop(0, chunk // 16, main_step, 0)

    @pl.when(step == 0)
    def _():
        wait_weight(2)

    def put_moves():
        return [
            pltpu.make_async_copy(held.at[1], out, put.at[n])
            for n, (held, out) in enumerate(((wr, wr_o), (wg, wg_o), (ow, ow_o)))
        ]

    @pl.when(step == 0)
    def _():
        for move in put_moves():
            move.start()

    branch = br_o[...]
    mix_o[:, :half] = dot_nt(branch, ow[0]).astype(BF16)
    mix_o[:, half:] = dot_nt(branch, ow[1]).astype(BF16)

    for k in range(cot_parts):

        @pl.when(step == k)
        def _():
            mix_s[k] = mix_o[...]
            mix_move(k).start()

    @pl.when(step == count - 1)
    def _():
        for k in range(cot_parts):
            for s in range(2):
                pltpu.make_async_copy(
                    cotangent.at[:, pl.ds(0, chunk)],
                    cot_o.at[s, :, pl.ds(k * chunk, chunk)],
                    cot_recv.at[k, s],
                ).wait()
            finish_send(cot_moves(k))
            mix_move(k).wait()
        for k in range(count):
            finish_send(token_moves(k))
        for n in range(4):
            weight_moves(n)[1].wait_send()
        for move in put_moves():
            move.wait()


def rec_forward(tokens, cotangent, wr, wg, ow, gain, rw, iw, cw, cb, rb, ib, sp, chunk=256):
    half, length = tokens.shape
    width = wr.shape[1]
    heads = width // 128
    count = length // chunk
    cot_parts = 1
    wide = 2 * half
    row_block = lambda cols: pl.BlockSpec((chunk, cols), lambda i: (i, 0))
    whole = lambda shape: pl.BlockSpec(
        shape, lambda i: (0,) * len(shape), pipeline_mode=pl.Buffered(1)
    )
    hbm = pl.BlockSpec(memory_space=pl.ANY)
    f32 = jax.ShapeDtypeStruct((length, width), F32)
    low = jax.ShapeDtypeStruct((length, width), BF16)
    dma = pltpu.SemaphoreType.DMA
    return pl.pallas_call(
        functools.partial(rec_forward_kernel, chunk, count, cot_parts),
        grid=(count,),
        in_specs=[hbm] * 6
        + [whole((heads, 128, 128))] * 2
        + [whole((KCONV, width))]
        + [whole((1, width))] * 4,
        out_specs=[row_block(wide), pl.BlockSpec((wide, chunk), lambda i: (0, i))]
        + [row_block(width)] * 7
        + [row_block(wide)]
        + [hbm] * 5,
        out_shape=[
            jax.ShapeDtypeStruct((length, wide), BF16),
            jax.ShapeDtypeStruct((wide, length), BF16),
            f32, f32, low, f32, f32, f32, low,
            jax.ShapeDtypeStruct((length, wide), BF16),
            jax.ShapeDtypeStruct((2, half, cot_parts * chunk), BF16),
            jax.ShapeDtypeStruct((cot_parts * chunk, wide), BF16),
        ]
        + [jax.ShapeDtypeStruct((half, width), BF16)] * 3,
        scratch_shapes=[
            pltpu.VMEM((count, 2, half, chunk), BF16),
            pltpu.VMEM((cot_parts, chunk, wide), BF16),
            pltpu.VMEM((2, half, width), BF16),
            pltpu.VMEM((2, half, width), BF16),
            pltpu.VMEM((2, half, width), BF16),
            pltpu.VMEM((2, half, 1), F32),
            pltpu.VMEM((heads, 128, 256), BF16),
            pltpu.VMEM((8, width), F32),
            pltpu.VMEM((8, width), F32),
            pltpu.VMEM((chunk + 8, width), F32),
            pltpu.VMEM((chunk, 2 * width), F32),
            dma((count, 2)),
            dma((count, 2)),
            dma((4,)),
            dma((4,)),
            dma((4,)),
            dma((count, 2)),
            dma((count, 2)),
            dma((cot_parts,)),
            dma((cot_parts,)),
            dma((3,)),
        ],
        compiler_params=pltpu.CompilerParams(
            vmem_limit_bytes=60 * MIB, collective_id=2, has_side_effects=True
        ),
        name="recurrent_forward",
    )(tokens, cotangent, wr, wg, ow, gain, rw, iw, cw, cb, rb, ib, sp)


def norm_back_rows(rows, grad, held, cot, gain, gain_o, g1_o):
    wide = held.shape[1]
    scale = lax.rsqrt(jnp.sum(held * held, axis=1, keepdims=True) / wide + EPS)
    product = grad * held
    by_gain = product * scale
    gain_o[...] += by_gain[0:8] + by_gain[8:16]
    inner = jnp.sum(product * gain[...], axis=1, keepdims=True)
    grad_one = (
        cot.astype(F32)
        + scale * (grad * gain[...])
        - held * (scale * scale * scale * inner / wide)
    )
    g1_o[rows, :] = grad_one.astype(BF16)


def ffn_kernel(
    count, blocks,
    x, mix, lengths, gain, keep, wg0, wg1, wu0, wu1, wd0, wd1, mixed, cotangent, far_first, cot_first,
    out_o, gu_sum, gg_sum, gg0, gg1, gd0, gd1, g1_o, g1t_o, gain_o, gn_last, far_last, cot_last,
    far_s, ct_s, ctok_s, n2_s, n2t_s, hid_s, ga_s, gb_s, out_acc, gn_acc, gn_s, gn_far,
    keep_s, give_s, got_s,
    far_send, far_recv, ct_send, ct_recv, gn_send, gn_recv, up_send, up_recv, free_sem,
):
    step = pl.program_id(0)
    core, chip = lax.axis_index("rows"), lax.axis_index("cols")
    chunk, wide = n2_s.shape
    half, block = gg0.shape
    first_part = count * blocks
    slot = lax.select(core == chip, 0, 1)
    beside = {"cols": 1 - chip}

    def far_move(c):
        return pltpu.make_async_remote_copy(
            mixed.at[pl.ds(c * chunk, chunk), :], far_s.at[c], far_send.at[c], far_recv.at[c], device_id=beside
        )

    def far_load():
        return pltpu.make_async_copy(far_first, far_s.at[0], far_recv.at[0])

    def cot_moves(c):
        src = cotangent.at[:, pl.ds(c * chunk, chunk)]
        there = ct_s.at[slot, :, pl.ds(c * chunk, chunk)]
        return (
            pltpu.make_async_copy(src, there, ct_recv.at[c, slot]),
            pltpu.make_async_remote_copy(
                src, there, ct_send.at[c, 0], ct_recv.at[c, slot], device_id={"rows": 1 - core}
            ),
            pltpu.make_async_remote_copy(
                src, there, ct_send.at[c, 1], ct_recv.at[c, slot],
                device_id={"rows": chip, "cols": 1 - chip},
            ),
        )

    def cot_load(s):
        return pltpu.make_async_copy(
            cot_first.at[s], ct_s.at[s, :, pl.ds(0, chunk)], ct_recv.at[0, s]
        )

    def gn_move(c):
        return pltpu.make_async_remote_copy(
            gn_s.at[c], gn_far.at[c], gn_send.at[c], gn_recv.at[c], device_id=beside
        )

    def send_part(c):
        far_move(c).start()
        moves = cot_moves(c)
        moves[2].start()

        @pl.when(core == chip)
        def _():
            moves[0].start()

        @pl.when(core != chip)
        def _():
            moves[1].start()

    @pl.when(step == 0)
    def _():
        far_load().start()
        for s in range(2):
            cot_load(s).start()
        group_barrier(core, chip)
        gain_o[...] = jnp.zeros_like(gain_o)

    for c, at in enumerate(SEND_STEPS):

        @pl.when(step == at)
        def _():
            send_part(c + 1)

    def turned_cot(c):
        cols = pl.ds(pl.multiple_of(c * chunk, chunk), chunk)
        for s in range(2):
            ctok_s[:, s * half : (s + 1) * half] = ct_s[s, :, cols].T

    def norm_forward(c):
        cols = pl.ds(pl.multiple_of(c * chunk, chunk), chunk)
        slots = c * chunk + lax.broadcasted_iota(jnp.int32, (1, chunk), 1)
        live = (slots < lengths[core]).astype(F32).astype(BF16)
        pltpu.make_async_copy(far_first, far_s.at[c], far_recv.at[c]).wait()
        for s in range(2):
            pltpu.make_async_copy(
                cot_first.at[s], ct_s.at[s, :, cols], ct_recv.at[c, s]
            ).wait()
            ct_s[s, :, cols] = ct_s[s, :, cols] * live
        turned_cot(c)
        gn_acc[...] = jnp.zeros_like(gn_acc)

        def rows_step(i, _):
            rows = pl.ds(pl.multiple_of(i * 16, 16), 16)
            res = x[rows, :].astype(F32) + (mix[rows, :].astype(F32) + far_s[c, rows, :].astype(F32))
            out_acc[rows, :] = keep[...] * res
            scale = lax.rsqrt(jnp.sum(res * res, axis=1, keepdims=True) / wide + EPS)
            n2_s[rows, :] = (res * scale * gain[...]).astype(BF16)
            return 0

        lax.fori_loop(0, chunk // 16, rows_step, 0)
        n2t_s[:, cols] = n2_s[...].T

    @pl.when(step < first_part)
    def _():
        c = step // blocks
        blk = step % blocks
        rows = pl.ds(pl.multiple_of(c * chunk, chunk), chunk)

        @pl.when(blk == 0)
        def _():
            norm_forward(c)

        n0, n1 = n2_s[:, :half], n2_s[:, half:]
        c0, c1 = ctok_s[:, :half], ctok_s[:, half:]
        a = dot(n0, wg0[...]) + dot(n1, wg1[...])
        b = dot(n0, wu0[...]) + dot(n1, wu1[...])
        gh = dot(c0, wd0[...]) + dot(c1, wd1[...])
        act, slope = gelu_pair(a)
        hidden = (act * b).astype(BF16)
        ga = (gh * b * slope).astype(BF16)
        gb = (gh * act).astype(BF16)
        hid_s[blk, rows, :] = hidden
        ga_s[blk, rows, :] = ga
        gb_s[blk, rows, :] = gb
        out_acc[:, :half] += dot_nt(hidden, wd0[...])
        out_acc[:, half:] += dot_nt(hidden, wd1[...])
        gn_acc[:, :half] += dot_nt(ga, wg0[...]) + dot_nt(gb, wu0[...])
        gn_acc[:, half:] += dot_nt(ga, wg1[...]) + dot_nt(gb, wu1[...])

        @pl.when(blk == blocks - 1)
        def _():
            out_o[...] = out_acc[...].astype(BF16)
            gn_s[c] = gn_acc[...].astype(BF16)

        @pl.when(step == first_part - 1)
        def _():
            gn_last[...] = gn_s[count - 1]
            far_last[...] = far_s[count - 1]
            cot_last[...] = ctok_s[...]

    for c, at in enumerate(GN_STEPS):

        @pl.when(step == first_part - blocks + at)
        def _():
            gn_move(c).start()

    def norm_back(c):
        turned_cot(c)
        gn_move(c).wait_recv()

        def rows_step(i, _):
            rows = pl.ds(pl.multiple_of(i * 16, 16), 16)
            grad = gn_s[c, rows, :].astype(F32) + gn_far[c, rows, :].astype(F32)
            held = x[rows, :].astype(F32) + (mix[rows, :].astype(F32) + far_s[c, rows, :].astype(F32))
            norm_back_rows(rows, grad, held, ctok_s[rows, :], gain, gain_o, g1_o)
            return 0

        lax.fori_loop(0, chunk // 16, rows_step, 0)
        g1t_o[...] = g1_o[...].T

    def give(a, k):
        at = k % 2
        return pltpu.make_async_remote_copy(
            give_s.at[a, at], got_s.at[a, at], up_send.at[a, at], up_recv.at[a, at],
            device_id={"rows": 1 - core},
        )

    k = step - first_part
    shared = ((gb_s, gu_sum, blocks), (ga_s, gg_sum, BESIDE))
    for a, (_, total_o, many) in enumerate(shared):

        @pl.when(jnp.logical_and(k > 0, k <= many))
        def _():
            give(a, k - 1).wait()
            at = (k - 1) % 2
            total_o[...] = (keep_s[a, at].astype(F32) + got_s[a, at].astype(F32)).astype(BF16)

            @pl.when(k - 1 < many - 2)
            def _():
                pl.semaphore_signal(free_sem.at[a], inc=1, device_id={"rows": 1 - core})

        @pl.when(jnp.logical_and(k >= 0, k < many))
        def _():
            product = dot(n2t_s[...], shared[a][0][k]).astype(BF16)
            give_s[a, k % 2] = product[half:]

            @pl.when(k >= 2)
            def _():
                pl.semaphore_wait(free_sem.at[a], 1)

            give(a, k).start()
            keep_s[a, k % 2] = product[:half]

    @pl.when(jnp.logical_and(k >= BESIDE, k < blocks))
    def _():
        product = dot(n2t_s[...], ga_s[k]).astype(BF16)
        gg0[...] = product[:half]
        gg1[...] = product[half:]

    @pl.when(jnp.logical_and(k >= 0, k < blocks))
    def _():
        product = dot(ct_s[...].reshape(2 * half, ct_s.shape[2]), hid_s[k]).astype(BF16)
        gd0[...] = product[:half]
        gd1[...] = product[half:]

    for c in range(count - 1):

        @pl.when(k == 3 * (c + 1))
        def _():
            norm_back(c)

    @pl.when(k == blocks)
    def _():
        for c in range(count - 1):
            gn_move(c).wait_send()
        for c in range(1, count):
            far_move(c).wait_send()
            moves = cot_moves(c)
            moves[2].wait_send()

            @pl.when(core != chip)
            def _():
                moves[1].wait_send()


def ffn(x, mix, lengths, gain, keep, wg, wu, wd, cotangent, far_first, cot_first, chunk=256, block=BLOCK):
    tokens, wide = x.shape
    half, width = wg[0].shape
    count, blocks = tokens // chunk, width // block
    first_part = count * blocks
    whole = lambda shape: pl.BlockSpec(
        shape, lambda i: (0,) * len(shape), pipeline_mode=pl.Buffered(1)
    )
    hbm = pl.BlockSpec(memory_space=pl.ANY)

    def back_chunk(i):
        return jnp.clip((i - first_part - 1) // 3, 0, count - 2)

    def chunk_at(i):
        return jnp.where(i < first_part, i // blocks, back_chunk(i))

    rows = pl.BlockSpec((chunk, wide), lambda i: (chunk_at(i), 0))
    weight = pl.BlockSpec(
        (half, block), lambda i: (0, jnp.where(i < first_part, i % blocks, blocks - 1))
    )
    grad_at = lambda late, many: pl.BlockSpec(
        (half, block), lambda i: (0, jnp.clip(i - first_part - late, 0, many - 1))
    )
    grad = lambda many: jax.ShapeDtypeStruct((half, many * block), BF16)
    low = jax.ShapeDtypeStruct((tokens, wide), BF16)
    part = pltpu.VMEM((count, chunk, wide), BF16)
    middle = pltpu.VMEM((blocks, tokens, block), BF16)
    pair = pltpu.VMEM((2, 2, half, block), BF16)
    dma = pltpu.SemaphoreType.DMA
    return pl.pallas_call(
        functools.partial(ffn_kernel, count, blocks),
        grid=(first_part + blocks + 1,),
        in_specs=[rows, rows, pl.BlockSpec(memory_space=pltpu.SMEM), whole((1, wide)), whole((1, 1))]
        + [weight] * 6
        + [hbm] * 4,
        out_specs=[
            pl.BlockSpec((chunk, wide), lambda i: (jnp.minimum(i // blocks, count - 1), 0)),
            grad_at(1, blocks),
            grad_at(1, BESIDE),
        ]
        + [grad_at(BESIDE, blocks - BESIDE)] * 2
        + [grad_at(0, blocks)] * 2
        + [
            pl.BlockSpec((chunk, wide), lambda i: (back_chunk(i), 0)),
            pl.BlockSpec((wide, chunk), lambda i: (0, back_chunk(i))),
            whole((8, wide)),
        ]
        + [whole((chunk, wide))] * 3,
        out_shape=[low]
        + [grad(blocks), grad(BESIDE)]
        + [grad(blocks - BESIDE)] * 2
        + [grad(blocks)] * 2
        + [
            jax.ShapeDtypeStruct((tokens - chunk, wide), BF16),
            jax.ShapeDtypeStruct((wide, tokens - chunk), BF16),
            jax.ShapeDtypeStruct((8, wide), F32),
        ]
        + [jax.ShapeDtypeStruct((chunk, wide), BF16)] * 3,
        scratch_shapes=[
            part,
            pltpu.VMEM((2, half, tokens), BF16),
            pltpu.VMEM((chunk, wide), BF16),
            pltpu.VMEM((chunk, wide), BF16),
            pltpu.VMEM((wide, tokens), BF16),
            middle, middle, middle,
            pltpu.VMEM((chunk, wide), F32),
            pltpu.VMEM((chunk, wide), F32),
            part, part,
            pair, pair, pair,
            dma((count,)), dma((count,)),
            dma((count, 2)), dma((count, 2)),
            dma((count,)), dma((count,)),
            dma((2, 2)), dma((2, 2)),
            pltpu.SemaphoreType.REGULAR((2,)),
        ],
        compiler_params=pltpu.CompilerParams(
            vmem_limit_bytes=62 * MIB, collective_id=3, has_side_effects=True
        ),
        name="ffn",
    )(
        x, mix, lengths, gain, keep, wg[0], wg[1], wu[0], wu[1], wd[0], wd[1],
        mix, cotangent, far_first, cot_first,
    )


def ring_place(n, at):
    def index_of(place):
        return lax.select(place < n // 2, 2 * place, 2 * (n - 1 - place) + 1)

    me = lax.select(at % 2 == 0, at // 2, n - 1 - at // 2)
    return me, (index_of(lax.rem(me + 1, n)), index_of(lax.rem(me + n - 1, n)))


def ring_rows(n, me, total, way, s):
    size = total // n
    chunk = lax.rem(me + n - s, n) if way == 0 else lax.rem(me + s, n)
    return pl.ds(pl.multiple_of(chunk * size, size), size)


def ring_beside(n, owns, out, own_b, ring_b, own_sem, rs_send, rs_recv, ag_send, ag_recv, put_sem):
    me, nexts = ring_place(n, lax.axis_index("dp"))
    wide = out.shape[1] // 2
    cut = (wide // 128 + 1) // 2 * 128
    groups = (pl.ds(0, cut), pl.ds(cut, wide - cut))
    both = [(g, way) for g in range(2) for way in range(2)]
    per = -(-n // 8)
    per_gather = -(-(n - 2) // 6)
    rows_of = lambda way, s: ring_rows(n, me, out.shape[0], way, s)
    cols_of = lambda g, way: pl.ds(way * wide + g * cut, wide - cut if g else cut)

    def own_copies(way, s):
        moves, at = [], 0
        for m, own in enumerate(owns):
            size = own.shape[1] // 2
            moves.append(
                pltpu.make_async_copy(
                    own.at[rows_of(way, s), pl.ds(way * size, size)],
                    own_b.at[way, s % 2, :, pl.ds(at, size)],
                    own_sem.at[m, way, s % 2],
                )
            )
            at += size
        return moves

    def sum_copy(g, way, s):
        return pltpu.make_async_remote_copy(
            ring_b.at[way, s, :, groups[g]], ring_b.at[way, s + 1, :, groups[g]],
            rs_send.at[g, way], rs_recv.at[g, way, s], device_id={"dp": nexts[way]},
        )

    def first_gather(g, way):
        return pltpu.make_async_remote_copy(
            ring_b.at[way, n - 1, :, groups[g]], out.at[rows_of(way, n - 1), cols_of(g, way)],
            ag_send.at[g, way, 0], ag_recv.at[g, way, 0], device_id={"dp": nexts[way]},
        )

    def gather_copy(g, way, s):
        there = out.at[rows_of(way, s - 1), cols_of(g, way)]
        return pltpu.make_async_remote_copy(
            there, there, ag_send.at[g, way, s], ag_recv.at[g, way, s], device_id={"dp": nexts[way]}
        )

    def put_copy(g, way):
        return pltpu.make_async_copy(
            ring_b.at[way, n - 1, :, groups[g]],
            out.at[rows_of(way, n - 1), cols_of(g, way)],
            put_sem.at[g, way],
        )

    def begin(chip):
        barrier = pltpu.get_barrier_semaphore()
        for neighbour in nexts:
            pl.semaphore_signal(barrier, inc=1, device_id={"dp": neighbour})
        pl.semaphore_signal(barrier, inc=1, device_id={"cols": 1 - chip})
        for s in range(2):
            for way in range(2):
                for move in own_copies(way, s):
                    move.start()
        pl.semaphore_wait(barrier, 3)

    def sum_step(g, s):
        for way in range(2):
            if g == 0:
                for move in own_copies(way, s):
                    move.wait()

            @pl.when(s == 0)
            def _():
                ring_b[way, s, :, groups[g]] = own_b[way, s % 2, :, groups[g]]

            @pl.when(s > 0)
            def _():
                sum_copy(g, way, s - 1).wait_recv()
                total = ring_b[way, s, :, groups[g]].astype(F32) + own_b[
                    way, s % 2, :, groups[g]
                ].astype(F32)
                ring_b[way, s, :, groups[g]] = total.astype(BF16)

            @pl.when(s < n - 1)
            def _():
                sum_copy(g, way, s).start()

            @pl.when(s == n - 1)
            def _():
                first_gather(g, way).start()
                put_copy(g, way).start()

            if g == 1:

                @pl.when(s < n - 2)
                def _():
                    for move in own_copies(way, s + 2):
                        move.start()

    def gather_step(g, s):
        for way in range(2):

            @pl.when(s == 1)
            def _():
                first_gather(g, way).wait_recv()

            @pl.when(s > 1)
            def _():
                gather_copy(g, way, s - 1).wait_recv()

            gather_copy(g, way, s).start()

    def tick(g, t):
        if per > 1 and g == 0:
            return
        turns = (0, 1) if per > 1 else (g,)

        def run(step):
            def once(s, _):
                for turn in turns:
                    step(turn, s)
                return 0

            return once

        @pl.when(t < 8)
        def _():
            lax.fori_loop(t * per, jnp.minimum((t + 1) * per, n), run(sum_step), 0)

        @pl.when(t >= 8)
        def _():
            start = 1 + (t - 8) * per_gather
            lax.fori_loop(start, jnp.minimum(start + per_gather, n - 1), run(gather_step), 0)

    def end():
        for g, way in both:
            gather_copy(g, way, n - 2).wait_recv()
            put_copy(g, way).wait()
            first_gather(g, way).wait_send()
            pltpu.make_async_remote_copy(
                ring_b.at[way, pl.ds(0, n - 1), :, groups[g]],
                ring_b.at[way, pl.ds(1, n - 1), :, groups[g]],
                rs_send.at[g, way], rs_recv.at[g, way, 0], device_id={"dp": nexts[way]},
            ).wait_send()

        def drain(s, _):
            for g, way in both:
                gather_copy(g, way, s).wait_send()
            return 0

        lax.fori_loop(1, n - 1, drain, 0)

    return begin, tick, end


def rec_backward_kernel(
    tile, n,
    n1t, st, gate, r_in, i_in, cl, rec, br, ow0, ow1, wr0, wr1, wg0, wg1, rw, iw, cw, sp,
    x, gain, gain_second, gain_two, up, gate_own, g1_head, g1t_head, mixed, gn_last, far_last, cot_last,
    gn1_o, go0, go1, gr0, gr1, gg0, gg1, ggw, small0, small1, stat, up_o, g1_last,
    acc, gb_s, gc_s, ggp_s, grp_s, gip_s, grec_s, gain_s, sums, g1, g1t, gain_b,
    gn_s, gn_far, mix_s, far_s, cot_s, load_sem, gn_send, gn_recv, put_last, *ring_refs
):
    step = pl.program_id(0)
    tokens, block = gb_s.shape
    wide = n1t.shape[0]
    heads = block // 128
    half = ow0.shape[0]
    tiles = tokens // tile
    subs = tile // 8

    begin, tick, end = ring_beside(n, (up, gate_own), up_o, *ring_refs)

    chunk = gn_s.shape[0]
    head = tokens - chunk
    chip = lax.axis_index("cols")
    gn_move = pltpu.make_async_remote_copy(
        gn_last, gn_far, gn_send.at[0], gn_recv.at[0], device_id={"cols": 1 - chip}
    )
    last_put = pltpu.make_async_copy(g1.at[pl.ds(head, chunk), :], g1_last, put_last.at[0])
    beat = lambda at: tick(at % 2, 3 + step * 3 + at // 2)

    @pl.when(step == 0)
    def _():
        loads = [
            pltpu.make_async_copy(src, dst, load_sem.at[m])
            for m, (src, dst) in enumerate(
                (
                    (mixed.at[pl.ds(head, chunk), :], mix_s),
                    (far_last, far_s),
                    (cot_last, cot_s),
                    (gn_last, gn_s),
                    (g1_head, g1.at[pl.ds(0, head), :]),
                    (g1t_head, g1t.at[:, pl.ds(0, head)]),
                )
            )
        ]
        for move in loads:
            move.start()
        begin(chip)
        gn_move.start()
        acc[...] = jnp.zeros_like(acc)
        small0[...] = jnp.zeros_like(small0)
        small1[...] = jnp.zeros_like(small1)
        gain_b[...] = gain_two[...]
        for t in range(3):
            for g in range(2):
                tick(g, t)
        for move in loads:
            move.wait()
        gn_move.wait()

        def rows_step(i, _):
            base = pl.multiple_of(i * 16, 16)
            rows = pl.ds(base, 16)
            grad = gn_s[rows, :].astype(F32) + gn_far[rows, :].astype(F32)
            held = x[pl.ds(head + base, 16), :].astype(F32) + (
                mix_s[rows, :].astype(F32) + far_s[rows, :].astype(F32)
            )
            norm_back_rows(pl.ds(head + base, 16), grad, held, cot_s[rows, :], gain_second, gain_b, g1)
            return 0

        lax.fori_loop(0, chunk // 16, rows_step, 0)
        g1t[:, head:] = g1[head:, :].T
        last_put.start()

    beat(0)
    gb_s[...] = dot(g1[:, :half], ow0[...]) + dot(g1[:, half:], ow1[...])
    beat(1)
    product = dot(g1t[...], br[...]).astype(BF16)
    go0[...] = product[:half]
    go1[...] = product[half:]
    beat(2)
    sums[...] = jnp.zeros_like(sums)
    row = lax.broadcasted_iota(jnp.int32, (8, 128), 0)

    def back_step(j, held):
        @pl.when(j == tiles // 2)
        def _():
            beat(3)

        i = tiles - 1 - j
        base = pl.multiple_of(i * tile, tile)
        rows = pl.ds(base, tile)
        before = pl.ds(pl.multiple_of(jnp.maximum(base - 8, 0), 8), 8)
        out = []
        for h in range(heads):
            sl = slice(h * 128, (h + 1) * 128)
            later_decay, later_carried = held[h]
            grad_branch = gb_s[rows, sl]
            act, slope = gelu_pair(gate[rows, sl])
            state = st[rows, sl]
            ggp_s[rows, sl] = (grad_branch * state * slope).astype(BF16)
            grad_state = grad_branch * act
            r = r_in[rows, sl]
            soft = sp[:, sl]
            decay, em = decay_terms(r, soft)
            parts = [None] * subs
            for p in range(subs - 1, -1, -1):
                own = decay[p * 8 : p * 8 + 8]
                after = jnp.where(row == 7, later_decay, pltpu.roll(own, 7, 0))
                a, b = scan_tile_back(after, grad_state[p * 8 : p * 8 + 8], row)
                carried = a * later_carried + b
                later_decay = own[0:1]
                later_carried = carried[0:1]
                parts[p] = carried
            out.append((later_decay, later_carried))
            carried = jnp.concatenate(parts, axis=0)
            edge = jnp.where(i > 0, st[before, sl][7:8], 0.0)
            prev = []
            for p in range(subs):
                prev.append(jnp.where(row == 0, edge, pltpu.roll(state[p * 8 : p * 8 + 8], 1, 0)))
                edge = state[p * 8 + 7 : p * 8 + 8]
            prev = jnp.concatenate(prev, axis=0)
            g = i_in[rows, sl]
            conv = cl[rows, sl].astype(F32)
            scaling = jnp.sqrt(em)
            gated = g * conv
            grad_log = carried * (prev * decay - gated * (decay * decay) / scaling)
            grad_soft = grad_log * (-GATE_SCALE * r)
            grp = grad_soft * soft * (1.0 - r)
            cs = carried * scaling
            gc_s[rows, sl] = cs * g
            gip = cs * gated * (1.0 - g)
            grp_s[rows, sl] = grp.astype(BF16)
            gip_s[rows, sl] = gip.astype(BF16)
            for n, term in enumerate((grp, gip, grad_soft)):
                total = term[0:8]
                for p in range(1, subs):
                    total = total + term[p * 8 : p * 8 + 8]
                sums[n * 8 : n * 8 + 8, sl] += total
        return tuple(out)

    zero = jnp.zeros((1, 128), F32)
    lax.fori_loop(0, tiles, back_step, tuple((zero, zero) for _ in range(heads)))
    beat(4)
    for h in range(heads):
        sl = slice(h * 128, (h + 1) * 128)
        low = cl[:, sl]
        ggw[h, :, 0:128] = dot_tn(low, grp_s[:, sl]).astype(BF16)
        ggw[h, :, 128:256] = dot_tn(low, gip_s[:, sl]).astype(BF16)
        gc_s[:, sl] += dot_nt(grp_s[:, sl], rw[h]) + dot_nt(gip_s[:, sl], iw[h])

    def conv_step(j, held):
        i = tiles - 1 - j
        base = pl.multiple_of(i * tile, tile)
        rows = pl.ds(base, tile)
        before = pl.ds(pl.multiple_of(jnp.maximum(base - 8, 0), 8), 8)
        out = []
        for h in range(heads):
            sl = slice(h * 128, (h + 1) * 128)
            grad_conv = gc_s[rows, sl]
            window = jnp.concatenate([grad_conv, held[h]], axis=0)
            out.append(grad_conv[0:8])
            grad_rec = cw[0:1, sl] * grad_conv
            for k in range(1, KCONV):
                grad_rec = grad_rec + cw[k : k + 1, sl] * pltpu.roll(window, tile + 8 - k, 0)[:tile]
            grec_s[rows, sl] = grad_rec.astype(BF16)
            edge = jnp.where(i > 0, rec[before, sl], 0.0)
            past = jnp.concatenate([edge, rec[rows, sl]], axis=0)
            terms = [grad_conv * past[8:]]
            for k in range(1, KCONV):
                terms.append(grad_conv * pltpu.roll(past, k, 0)[8:])
            terms.append(grad_conv)
            for n, term in enumerate(terms):
                total = term[0:8]
                for p in range(1, subs):
                    total = total + term[p * 8 : p * 8 + 8]
                sums[24 + n * 8 : 32 + n * 8, sl] += total
        return tuple(out)

    lax.fori_loop(0, tiles, conv_step, tuple(jnp.zeros((8, 128), F32) for _ in range(heads)))
    beat(5)
    all_heads = small0.shape[0] // 8
    head_row = lax.broadcasted_iota(jnp.int32, (all_heads, 128), 0)
    for n in range(8):
        vector = jnp.sum(sums[n * 8 : n * 8 + 8, :], axis=0, keepdims=True)
        for h in range(heads):
            at = slice(n * all_heads, (n + 1) * all_heads)
            mine = vector[:, h * 128 : (h + 1) * 128]
            tile_now = jnp.where(head_row == step * heads + h, mine, small0[at, 0:128])
            small0[at, 0:128] = tile_now
            small1[at, 0:128] = tile_now
    grad_rec = grec_s[...]
    grad_gate = ggp_s[...]
    product = dot(n1t[...], grad_rec).astype(BF16)
    gr0[...] = product[:half]
    gr1[...] = product[half:]
    product = dot(n1t[...], grad_gate).astype(BF16)
    gg0[...] = product[:half]
    gg1[...] = product[half:]
    acc[:, :half] += dot_nt(grad_rec, wr0[...]) + dot_nt(grad_gate, wg0[...])
    acc[:, half:] += dot_nt(grad_rec, wr1[...]) + dot_nt(grad_gate, wg1[...])

    @pl.when(step == pl.num_programs(0) - 1)
    def _():
        gain_s[...] = jnp.zeros_like(gain_s)

        def stat_step(i, _):
            rows = pl.ds(pl.multiple_of(i * 32, 32), 32)
            part = acc[rows, :]
            gn1_o[rows, :] = part.astype(BF16)
            held = x[rows, :].astype(F32)
            scale = lax.rsqrt(jnp.sum(held * held, axis=1, keepdims=True) / wide + EPS)
            product = part * held
            by_gain = product * scale
            gain_s[...] += (by_gain[0:8] + by_gain[8:16]) + (by_gain[16:24] + by_gain[24:32])
            inner = jnp.sum(product * gain[...], axis=1, keepdims=True)
            stat[rows, 0:64] = jnp.broadcast_to(inner, (32, 64))
            stat[rows, 64:128] = jnp.broadcast_to(scale, (32, 64))
            return 0

        lax.fori_loop(0, tokens // 32, stat_step, 0)
        for n, held in enumerate((gain_s, gain_b)):
            vector = jnp.sum(held[...], axis=0, keepdims=True)
            for m in range(half // 128):
                at = n * 8 + m
                small0[at : at + 1, 128:] = vector[:, m * 128 : (m + 1) * 128]
                small1[at : at + 1, 128:] = vector[:, half + m * 128 : half + (m + 1) * 128]
        last_put.wait()
        end()


def rec_backward(
    n1t, st, gate, r, g, cl, rec, br, ow, wr, wg, rw, iw, cw, sp, x, gain, gain_second, gain_two,
    up, gate_own, lasts, n, block=256, tile=64
):
    wide, tokens = n1t.shape
    half, width = wr[0].shape
    heads = block // 128
    rows = up.shape[0]
    up, gate_own = (jnp.pad(a, ((0, -rows % (16 * n)), (0, 0))) for a in (up, gate_own))
    side = (up.shape[0], up.shape[1] + gate_own.shape[1])
    small = (8 * (width // 128), 256)
    chunk = lasts[-1].shape[0]
    slots = lambda many: pltpu.VMEM((2, many, side[0] // n, side[1] // 2), BF16)
    dma = pltpu.SemaphoreType.DMA
    hbm = pl.BlockSpec(memory_space=pl.ANY)
    whole = lambda shape: pl.BlockSpec(shape, lambda i: (0, 0), pipeline_mode=pl.Buffered(1))
    act = pl.BlockSpec((tokens, block), lambda i: (0, i))
    weight = pl.BlockSpec((half, block), lambda i: (0, i))
    thin = lambda n: pl.BlockSpec((n, block), lambda i: (0, i))
    gate_block = pl.BlockSpec((heads, 128, 256), lambda i: (i, 0, 0))
    grad = jax.ShapeDtypeStruct((half, width), BF16)
    outs = pl.pallas_call(
        functools.partial(rec_backward_kernel, tile, n),
        grid=(width // block,),
        in_specs=[whole((wide, tokens))]
        + [act] * 7
        + [weight] * 6
        + [pl.BlockSpec((heads, 128, 128), lambda i: (i, 0, 0))] * 2
        + [thin(KCONV), thin(1)]
        + [whole((tokens, wide)), whole((1, wide)), whole((1, wide)), whole((8, wide))]
        + [hbm] * 8,
        out_specs=[whole((tokens, wide))]
        + [weight] * 6
        + [gate_block, whole(small), whole(small), whole((tokens, 128)), hbm, hbm],
        out_shape=[jax.ShapeDtypeStruct((tokens, wide), BF16)]
        + [grad] * 6
        + [
            jax.ShapeDtypeStruct((width // 128, 128, 256), BF16),
            jax.ShapeDtypeStruct(small, F32),
            jax.ShapeDtypeStruct(small, F32),
            jax.ShapeDtypeStruct((tokens, 128), F32),
            jax.ShapeDtypeStruct(side, BF16),
            jax.ShapeDtypeStruct((chunk, wide), BF16),
        ],
        scratch_shapes=[
            pltpu.VMEM((tokens, wide), F32),
            pltpu.VMEM((tokens, block), F32),
            pltpu.VMEM((tokens, block), F32),
            pltpu.VMEM((tokens, block), BF16),
            pltpu.VMEM((tokens, block), BF16),
            pltpu.VMEM((tokens, block), BF16),
            pltpu.VMEM((tokens, block), BF16),
            pltpu.VMEM((8, wide), F32),
            pltpu.VMEM((64, block), F32),
            pltpu.VMEM((tokens, wide), BF16),
            pltpu.VMEM((wide, tokens), BF16),
            pltpu.VMEM((8, wide), F32),
        ]
        + [pltpu.VMEM((chunk, wide), BF16)] * 5
        + [
            dma((6,)), dma((1,)), dma((1,)), dma((1,)),
            slots(2), slots(n),
            dma((2, 2, 2)), dma((2, 2)), dma((2, 2, n)), dma((2, 2, n)), dma((2, 2, n)), dma((2, 2)),
        ],
        compiler_params=pltpu.CompilerParams(
            vmem_limit_bytes=62 * MIB, collective_id=6, has_side_effects=True
        ),
        name="recurrent_backward",
    )(
        n1t, st, gate, r, g, cl, rec, br,
        ow[0], ow[1], wr[0], wr[1], wg[0], wg[1], rw, iw, cw, sp, x, gain, gain_second, gain_two,
        up, gate_own, *lasts,
    )
    return (*outs[:-2], outs[-2][:rows], outs[-1])


def ring_kernel(n, count, *refs):
    own, other, refs = refs[:count], refs[count : 2 * count], refs[2 * count :]
    (gn1, out, stat, g1_head, g1_last), refs = refs[:5], refs[5:]
    outs, refs = refs[:count], refs[count:]
    (gn1_p, out_p, stat_p, g1_p), scratch = refs[:4], refs[4:]
    piece_send, piece_recv = scratch[-2:]
    scratch = scratch[:-2]
    own_b, part_b, ring_b = scratch[:count], scratch[count : 2 * count], scratch[2 * count : 3 * count]
    own_sem, part_send, part_recv, rs_send, rs_recv, ag_send, ag_recv, put_sem = scratch[3 * count :]
    at = lax.axis_index("dp")
    core = lax.axis_index("rows")
    chip = lax.axis_index("cols")

    me, nexts = ring_place(n, at)
    barrier = pltpu.get_barrier_semaphore()
    for neighbour in nexts:
        pl.semaphore_signal(barrier, inc=1, device_id={"dp": neighbour})
    for peer in ((1 - core, chip), (core, 1 - chip), (1 - core, 1 - chip)):
        pl.semaphore_signal(barrier, inc=1, device_id={"rows": peer[0], "cols": peer[1]})
    pl.semaphore_wait(barrier, 5)

    half = gn1_p.shape[2]
    first, second = slice(0, half), slice(half, 2 * half)
    everything = slice(None)
    pieces = [
        (gn1, gn1_p, slice(None), first, second),
        (out, out_p, slice(None), first, second),
        (stat, stat_p, slice(None), everything, everything),
    ]
    head = g1_head.shape[0]
    singles = [(g1_head, slice(0, head)), (g1_last, slice(head, gn1.shape[0]))]
    diag = core == chip

    def piece_moves(m):
        src, dst, rows, mine, theirs = pieces[m]
        there = dst.at[chip, rows, :]
        sems = lambda w: (piece_send.at[m, w], piece_recv.at[m, chip])
        near = src.at[:, mine]
        away = src.at[:, theirs]
        return (
            pltpu.make_async_copy(near, there, piece_recv.at[m, chip]),
            pltpu.make_async_remote_copy(near, there, *sems(0), device_id={"cols": 1 - chip}),
            pltpu.make_async_remote_copy(away, there, *sems(1), device_id={"rows": 1 - core}),
            pltpu.make_async_remote_copy(
                away, there, *sems(1), device_id={"rows": 1 - core, "cols": 1 - chip}
            ),
        )

    def single_moves(m):
        src, rows = singles[m]
        there = g1_p.at[rows, :]
        at = len(pieces) + m
        return (
            pltpu.make_async_copy(src.at[:, first], there, piece_recv.at[at, 0]),
            pltpu.make_async_remote_copy(
                src.at[:, second], there, piece_send.at[at, 1], piece_recv.at[at, 0],
                device_id={"rows": 1 - core},
            ),
        )

    @pl.when(diag)
    def _():
        for m in range(len(pieces)):
            moves = piece_moves(m)
            moves[0].start()
            moves[2].start()
        for m in range(len(singles)):
            moves = single_moves(m)
            moves[0].start()
            moves[1].start()

    @pl.when(jnp.logical_not(diag))
    def _():
        for m in range(len(pieces)):
            moves = piece_moves(m)
            moves[1].start()
            moves[3].start()

    def rows_of(k, way, s):
        return ring_rows(n, me, own[k].shape[0], way, s)

    def cols_of(k, way):
        wide = own[k].shape[1] // 2
        return pl.ds(way * wide, wide)

    def own_copy(k, way, s):
        return pltpu.make_async_copy(
            own[k].at[rows_of(k, way, s), cols_of(k, way)], own_b[k].at[way, s], own_sem.at[k, way, s]
        )

    def part_copy(k, way, s):
        return pltpu.make_async_remote_copy(
            src_ref=other[k].at[rows_of(k, way, s), cols_of(k, way)],
            dst_ref=part_b[k].at[way, s],
            send_sem=part_send.at[k, way],
            recv_sem=part_recv.at[k, way, s],
            device_id={"rows": 1 - core},
        )

    def sum_copy(k, way, s):
        return pltpu.make_async_remote_copy(
            src_ref=ring_b[k].at[way, s],
            dst_ref=ring_b[k].at[way, s + 1],
            send_sem=rs_send.at[k, way],
            recv_sem=rs_recv.at[k, way, s],
            device_id={"dp": nexts[way]},
        )

    def first_gather(k, way):
        rows = rows_of(k, way, n - 1)
        return pltpu.make_async_remote_copy(
            src_ref=ring_b[k].at[way, n - 1],
            dst_ref=outs[k].at[rows, cols_of(k, way)],
            send_sem=ag_send.at[k, way, 0],
            recv_sem=ag_recv.at[k, way, 0],
            device_id={"dp": nexts[way]},
        )

    def gather_copy(k, way, s):
        rows = rows_of(k, way, s - 1)
        there = outs[k].at[rows, cols_of(k, way)]
        return pltpu.make_async_remote_copy(
            src_ref=there,
            dst_ref=there,
            send_sem=ag_send.at[k, way, s],
            recv_sem=ag_recv.at[k, way, s],
            device_id={"dp": nexts[way]},
        )

    def put_copy(k, way):
        return pltpu.make_async_copy(
            ring_b[k].at[way, n - 1],
            outs[k].at[rows_of(k, way, n - 1), cols_of(k, way)],
            put_sem.at[k, way],
        )

    both = [(k, way) for k in range(count) for way in range(2)]

    def load_step(s, _):
        for k, way in both:
            part_copy(k, way, s).start()
            own_copy(k, way, s).start()
        return 0

    lax.fori_loop(0, n, load_step, 0)

    def add_step(k, way, s, received):
        own_copy(k, way, s).wait()
        part_copy(k, way, s).wait_recv()
        total = own_b[k][way, s].astype(F32) + part_b[k][way, s].astype(F32)
        if received:
            sum_copy(k, way, s - 1).wait_recv()
            total = total + ring_b[k][way, s].astype(F32)
        ring_b[k][way, s] = total.astype(ring_b[k].dtype)

    for k, way in both:
        add_step(k, way, 0, False)
        sum_copy(k, way, 0).start()

    def sum_step(s, _):
        for k, way in both:
            add_step(k, way, s, True)
            sum_copy(k, way, s).start()
        return 0

    lax.fori_loop(1, n - 1, sum_step, 0)
    for k, way in both:
        add_step(k, way, n - 1, True)
        first_gather(k, way).start()
        put_copy(k, way).start()

    def gather_step(s, _):
        for k, way in both:
            gather_copy(k, way, s - 1).wait_recv()
            gather_copy(k, way, s).start()
        return 0

    for k, way in both:
        first_gather(k, way).wait_recv()
        gather_copy(k, way, 1).start()
    lax.fori_loop(2, n - 1, gather_step, 0)
    for k, way in both:
        gather_copy(k, way, n - 2).wait_recv()
        put_copy(k, way).wait()
        first_gather(k, way).wait_send()

    def drain_step(s, _):
        for k, way in both:
            gather_copy(k, way, s).wait_send()
        return 0

    lax.fori_loop(1, n - 1, drain_step, 0)
    for k, way in both:
        pltpu.make_async_remote_copy(
            ring_b[k].at[way, pl.ds(0, n - 1)],
            ring_b[k].at[way, pl.ds(1, n - 1)],
            rs_send.at[k, way],
            rs_recv.at[k, way, 0],
            device_id={"dp": nexts[way]},
        ).wait_send()
        pltpu.make_async_remote_copy(
            own_b[k].at[way],
            part_b[k].at[way],
            part_send.at[k, way],
            part_recv.at[k, way, 0],
            device_id={"rows": 1 - core},
        ).wait_send()

    for m in range(len(pieces)):
        src, dst, rows, mine, _ = pieces[m]
        for c in range(2):
            pltpu.make_async_copy(src.at[:, mine], dst.at[c, rows, :], piece_recv.at[m, c]).wait()
    for m in range(len(singles)):
        single_moves(m)[0].wait()

    @pl.when(diag)
    def _():
        for m in range(len(pieces)):
            piece_moves(m)[2].wait_send()
        for m in range(len(singles)):
            single_moves(m)[1].wait_send()

    @pl.when(jnp.logical_not(diag))
    def _():
        for m in range(len(pieces)):
            moves = piece_moves(m)
            moves[1].wait_send()
            moves[3].wait_send()


def ring_sum(n, own, other, pieces):
    count = len(own)
    own, other = list(own), list(other)
    rows = [a.shape[0] for a in own]
    unit = lambda a: (16 if a.dtype == BF16 else 8) * n
    pad = [-a.shape[0] % unit(a) for a in own]
    fit = lambda a, extra: jnp.pad(a, ((0, extra), (0, 0))) if extra else a
    own = [fit(a, e) for a, e in zip(own, pad)]
    other = [fit(a, e) for a, e in zip(other, pad)]
    slots = [pltpu.VMEM((2, n, a.shape[0] // n, a.shape[1] // 2), a.dtype) for a in own]
    sems = pltpu.SemaphoreType.DMA((count, 2, n))
    pair = pltpu.SemaphoreType.DMA((count, 2))
    tokens, wide = pieces[0].shape
    piece = jax.ShapeDtypeStruct((2, tokens, wide // 2), BF16)
    hbm = pl.BlockSpec(memory_space=pl.ANY)
    outs = pl.pallas_call(
        functools.partial(ring_kernel, n, count),
        in_specs=[hbm] * (2 * count + len(pieces)),
        out_specs=[hbm] * (count + 4),
        out_shape=[jax.ShapeDtypeStruct(a.shape, a.dtype) for a in own]
        + [
            piece,
            piece,
            jax.ShapeDtypeStruct((2, tokens, 128), F32),
            jax.ShapeDtypeStruct((tokens, wide // 2), BF16),
        ],
        scratch_shapes=slots * 3
        + [sems, pair, sems, pair] + [sems] * 3 + [pair]
        + [pltpu.SemaphoreType.DMA((5, 2))] * 2,
        compiler_params=pltpu.CompilerParams(
            collective_id=0, has_side_effects=True, vmem_limit_bytes=60 * MIB
        ),
        name="ring_sum",
    )(*own, *other, *pieces)
    return [a[:r] for a, r in zip(outs, rows)], outs[count:]


def final_kernel(
    gn, out, stat, g1, tokens, gain, lengths, beside, down, gate, out_w, rec_w, gate_w, blocks,
    result_o, grad_o, up_o, gate_o, down_o, out_w_o, rec_w_o, gate_w_o, recur_o, input_o,
):
    wide = 2 * tokens.shape[0]
    low = lambda ref: ref[0].astype(F32) + ref[1].astype(F32)
    chunk = tokens.shape[1]
    slots = pl.program_id(0) * chunk + lax.broadcasted_iota(jnp.int32, (1, chunk), 1)
    live = (slots < lengths[lax.axis_index("cols")]).astype(F32)
    result_o[...] = (low(out).T * live).astype(BF16)
    grad = low(gn).T
    held = tokens[...].astype(F32)
    inner = (stat[0] + stat[1]).T[0:1, :]
    scale = stat[0].T[64:65, :]
    grad_o[...] = (
        g1[...].astype(F32).T
        + (scale * gain[...]) * grad
        - held * (scale * scale * scale * inner / wide)
    ).astype(BF16)
    side = beside.shape[1] // 2
    up_half = up_o.shape[1] // 2
    gate_half = side - up_half
    for way in range(2):
        at = way * side
        up_o[:, way * up_half : (way + 1) * up_half] = beside[:, at : at + up_half].astype(F32)
        gate_o[:, way * gate_half : (way + 1) * gate_half] = beside[:, at + up_half : at + side].astype(F32)
    gate_o[:, 2 * gate_half :] = gate[...].astype(F32)
    for src, dst in ((down, down_o), (out_w, out_w_o), (rec_w, rec_w_o), (gate_w, gate_w_o)):
        dst[...] = src[...].astype(F32)
    both = blocks[...].astype(F32).reshape(recur_o.shape[0], 128, 256)
    recur_o[...] = both[:, :, :128]
    input_o[...] = both[:, :, 128:]


def final(gn, out, stat, g1, tokens, gain, lengths, beside, down, gate, out_w, rec_w, gate_w, blocks, steps=8):
    half, length = tokens.shape
    chunk, size = length // steps, half // steps
    pair = lambda cols: pl.BlockSpec((2, chunk, cols), lambda i: (0, i, 0))
    across = pl.BlockSpec((half, chunk), lambda i: (0, i))
    rows = lambda cols: pl.BlockSpec((size, cols), lambda i: (i, 0))
    shape = jax.ShapeDtypeStruct((half, length), BF16)
    ffn_wide, wide = down.shape[1], out_w.shape[1]
    grads = [ffn_wide] * 3 + [wide] * 3
    heads = blocks.shape[0] // 128
    return pl.pallas_call(
        final_kernel,
        grid=(steps,),
        in_specs=[
            pair(half), pair(half), pair(128),
            pl.BlockSpec((chunk, half), lambda i: (i, 0)),
            across,
            pl.BlockSpec((half, 1), lambda i: (0, 0)),
            pl.BlockSpec(memory_space=pltpu.SMEM),
        ]
        + [rows(a.shape[1]) for a in (beside, down, gate, out_w, rec_w, gate_w)]
        + [pl.BlockSpec((blocks.shape[0] // steps, 256), lambda i: (i, 0))],
        out_specs=[across, across]
        + [rows(cols) for cols in grads]
        + [pl.BlockSpec((heads // steps, 128, 128), lambda i: (i, 0, 0))] * 2,
        out_shape=[shape, shape] + [jax.ShapeDtypeStruct((half, cols), F32) for cols in grads]
        + [jax.ShapeDtypeStruct((heads, 128, 128), F32)] * 2,
        compiler_params=pltpu.CompilerParams(vmem_limit_bytes=56 * MIB),
        name="final",
    )(gn, out, stat, g1, tokens, gain, lengths, beside, down, gate, out_w, rec_w, gate_w, blocks)


def body(
    dp, tokens, lengths, mix_gain, rec_weight, gate_weight, conv_weight, conv_bias,
    recur_weight, recur_bias, input_weight, input_bias, decay_param, out_weight,
    ffn_gain, ffn_gate, ffn_up, ffn_down, cotangent,
):
    at_row = lax.axis_index("rows")
    at_col = lax.axis_index("cols")
    diag = at_row == at_col
    half = tokens.shape[0]
    wide = 2 * half

    both = lambda weight: (weight, swap(weight, "rows"))

    sp = jax.nn.softplus(-decay_param)[None, :]
    (x, n1t, rec, gate, cl, r, g, st, br, mixed, cot_a, far_a, wr_far, wg_far, ow_far) = rec_forward(
        tokens, cotangent, rec_weight, gate_weight, out_weight, mix_gain[:, None],
        recur_weight, input_weight, conv_weight, conv_bias[None, :], recur_bias[None, :],
        input_bias[None, :], sp,
    )
    wr = (rec_weight, wr_far)
    wg = (gate_weight, wg_far)
    ow = (out_weight, ow_far)
    fg = both(ffn_gate)
    fu = both(ffn_up)
    fd = both(ffn_down)
    gain_two = jnp.concatenate(both(ffn_gain))[None, :]
    gain_one = jnp.concatenate(both(mix_gain))[None, :]
    keep = diag.astype(F32).reshape(1, 1)

    out, up_own, gate_own, gg0, gg1, gd0, gd1, g1_head, g1t_head, grad_gain_two, *lasts = ffn(
        x, mixed, lengths, gain_two, keep, fg, fu, fd, cotangent, far_a, cot_a
    )
    gn1_part, go0, go1, gr0, gr1, gt0, gt1, ggw, small0, small1, stat, beside, g1_last = rec_backward(
        n1t, st, gate, r, g, cl, rec, br, ow, wr, wg, recur_weight, input_weight, conv_weight, sp,
        x, gain_one, gain_two, grad_gain_two, up_own, gate_own, [g1_head, g1t_head, mixed, *lasts], dp,
    )
    gates = ggw.reshape(-1, 256)
    total, moved = ring_sum(
        dp,
        [gd0, gg0, go0, gr0, gt0, gates, small0],
        [gd1, gg1, go1, gr1, gt1, gates, small1],
        [gn1_part, out, stat, g1_head, g1_last],
    )
    small = total[6]
    result, grad_tokens, sum_up, sum_gate, sum_down, sum_out, sum_rec, sum_gatew, grad_recur, grad_input = final(
        *moved, tokens, mix_gain[:, None], lengths, beside, *total[:6]
    )
    vec = small[:, :128].reshape(8, -1)
    gains = small[:16, 128:].reshape(2, -1)[:, :half]
    grad_gain_one = gains[0] + swap(gains[0], "cols")
    grad_decay = vec[2] * -jax.nn.sigmoid(-decay_param)
    return (
        result,
        grad_tokens,
        grad_gain_one,
        sum_rec,
        sum_gatew,
        vec[3:7],
        vec[7],
        grad_recur,
        vec[0],
        grad_input,
        vec[1],
        grad_decay,
        sum_out,
        gains[1],
        sum_gate,
        sum_up,
        sum_down,
    )


def solution(mesh):
    return jax.shard_map(
        functools.partial(body, mesh.shape["dp"]),
        mesh=mesh,
        in_specs=(
            P("rows", ("dp", "cols")),
            P("dp"),
            P("rows"),
            P("rows", "cols"),
            P("rows", "cols"),
            P(None, "cols"),
            P("cols"),
            P("cols", None, None),
            P("cols"),
            P("cols", None, None),
            P("cols"),
            P("cols"),
            P("rows", "cols"),
            P("rows"),
            P("rows", "cols"),
            P("rows", "cols"),
            P("rows", "cols"),
            P("rows", ("dp", "cols")),
        ),
        out_specs=(
            P("rows", ("dp", "cols")),
            P("rows", ("dp", "cols")),
            P("rows"),
            P("rows", "cols"),
            P("rows", "cols"),
            P(None, "cols"),
            P("cols"),
            P("cols", None, None),
            P("cols"),
            P("cols", None, None),
            P("cols"),
            P("cols"),
            P("rows", "cols"),
            P("rows"),
            P("rows", "cols"),
            P("rows", "cols"),
            P("rows", "cols"),
        ),
        check_vma=False,
    )
```
